32 devices in a mesh: seq: 8 (over z, y), head: 4 (over x, core).
Axes of the slice: x: 2, y: 2, z: 4, core: 2. Of those that a mesh axis runs over, the one named last changes fastest.
Arguments:
- tokens: bfloat16 [12288, 2048], P('seq'), may hold values from -6 to 6
- boundary: int32 [12288], P('seq'), may hold values from 0 to 1, as said below
- norm_gain: float32 [2048], replicated, may hold values from 0.5 to 1.5
- w_gate: bfloat16 [2048, 4096], P(None, 'head'), may hold values from -0.125 to 0.125
- w_inner: bfloat16 [2048, 4096], P(None, 'head'), may hold values from -0.125 to 0.125
- w_pair: bfloat16 [2048, 256], P(None, 'head'), may hold values from -0.125 to 0.125
- w_step: bfloat16 [2048, 64], P(None, 'head'), may hold values from -0.125 to 0.125
- conv_inner: float32 [4, 4096], P(None, 'head'), may hold values from -3 to 3
- conv_pair: float32 [4, 256], P(None, 'head'), may hold values from -3 to 3
- bias_inner: float32 [4096], P('head'), may hold values from -2 to 2
- bias_pair: float32 [256], P('head'), may hold values from -2 to 2
- step_bias: float32 [64], P('head')
- decay_log: float32 [64], P('head'), may hold values from 0 to 1.4
- skip_gain: float32 [64], P('head'), may hold values from 0.5 to 1.5
- gate_gain: float32 [4096], P('head'), may hold values from 0.5 to 1.5
- w_output: bfloat16 [4096, 2048], P('head'), may hold values from -0.09375 to 0.09375
- cotangent: bfloat16 [12288, 2048], P('seq'), may hold values from -6 to 6
Outputs:
- result: bfloat16 [12288, 2048], P('seq', 'head')
- grad_tokens: float32 [12288, 2048], P('seq', 'head')
- grad_norm_gain: float32 [2048], P('head')
- grad_w_gate: float32 [2048, 4096], P('seq', 'head')
- grad_w_inner: float32 [2048, 4096], P('seq', 'head')
- grad_w_pair: float32 [2048, 256], P('seq', 'head')
- grad_w_step: float32 [2048, 64], P('seq', 'head')
- grad_conv_inner: float32 [4, 4096], P(None, 'head')
- grad_conv_pair: float32 [4, 256], P(None, 'head')
- grad_bias_inner: float32 [4096], P('head')
- grad_bias_pair: float32 [256], P('head')
- grad_step_bias: float32 [64], P('head')
- grad_decay_log: float32 [64], P('head')
- grad_skip_gain: float32 [64], P('head')
- grad_gate_gain: float32 [4096], P('head')
- grad_w_output: float32 [4096, 2048], P('head', 'seq')
The draws below stay inside these ranges and needn't reach their ends.
Inputs may be any that keep to these rules, and one draw needn't show every extreme that they name: `boundary`: 1 marks a token that starts a document and token 0 is marked; one document starts among the first 1536 tokens and runs, with no start in between, into the last 1536 tokens; other starts lie only before it or after it.
All inputs are finite; a program needn't handle non-finite values.
Results may differ from the reference program's by a relative error of at most 0.011.
Values may be sent and summed in bfloat16 or wider, within the bound.
No kernel may reach another device: no remote copies, remote signals or barrier semaphores. Data moves between devices by JAX's collectives and lax.ppermute only.
A program may use at most 256 MiB of HBM per device.

```python
import jax
import jax.numpy as jnp
from jax import lax

D = 2048
H = 64
P_SIZE = 64
N = 128
CONV = 4
GROUP = 256
TOK_DEV = 1536
DI = 4096
TOKENS = 12288


def draw_boundary(key, part):
    key = jax.random.fold_in(key, 11)
    first_key, second_key, third_key = jax.random.split(key, 3)
    position = jnp.arange(TOKENS)
    opening = jax.random.randint(first_key, (), 1, TOK_DEV)
    closing = TOKENS - TOK_DEV + jax.random.randint(second_key, (), 1, TOK_DEV)
    scatter_bits = jax.random.randint(third_key, (TOKENS,), 0, 16) == 0
    inside = (position > opening) & (position < closing)
    marked = jnp.where(inside, False, scatter_bits) | (position == opening) | (position == closing) | (position == 0)
    return marked.astype(jnp.int32)


def draw_step_bias(key, part):
    key = jax.random.fold_in(key, 5)
    low_end = jnp.log(0.3 / TOKENS)
    high_end = jnp.log(1.0 / 40.0)
    return jax.random.uniform(key, (H,), jnp.float32, low_end, high_end)


def block_scale(key, dims, shards, smallest, high):
    loudness = 1.0
    for dim, shards_of in shards:
        draws = jax.random.uniform(jax.random.fold_in(jax.random.fold_in(key, 6), dim), (shards_of,), jnp.float32, smallest / len(shards), high / len(shards))
        loudness = loudness * jnp.repeat(jnp.exp(draws), dims[dim] // shards_of).reshape((-1,) + (1,) * (len(dims) - 1 - dim))
    return loudness


def centred(stream_key, shape, scale, bound, cuts=(), dtype=jnp.bfloat16):
    gain = block_scale(stream_key, shape, cuts, -0.22, 0.18) if cuts else 1.0
    result = jax.random.normal(stream_key, shape, jnp.float32) * scale * gain
    return jnp.minimum(jnp.maximum(result, -bound), bound).astype(dtype)


def setup_inputs(seed: int = 0) -> dict:
    splits = jax.random.split(jax.random.key(seed), 18)
    return {
        "tokens": centred(splits[0], (TOKENS, D), 1.0, 6.0, ((0, 8),)),
        "boundary": draw_boundary(jax.random.fold_in(splits[17], 71), 0),
        "norm_gain": jnp.clip(1.0 + 0.1 * jax.random.normal(splits[2], (D,), jnp.float32), 0.5, 1.5),
        "w_gate": centred(splits[3], (D, DI), D ** -0.5, 0.125, ((1, 4),)),
        "w_inner": centred(splits[4], (D, DI), D ** -0.5, 0.125, ((1, 4),)),
        "w_pair": centred(splits[5], (D, 2 * N), D ** -0.5, 0.125, ((1, 4),)),
        "w_step": centred(splits[6], (D, H), D ** -0.5, 0.125, ((1, 4),)),
        "conv_inner": centred(splits[7], (CONV, DI), 0.5, 3.0, ((1, 4),), jnp.float32),
        "conv_pair": centred(splits[8], (CONV, 2 * N), 0.5, 3.0, ((1, 4),), jnp.float32),
        "bias_inner": centred(splits[9], (DI,), 0.3, 2.0, ((0, 4),), jnp.float32),
        "bias_pair": centred(splits[10], (2 * N,), 0.3, 2.0, ((0, 4),), jnp.float32),
        "step_bias": draw_step_bias(jax.random.fold_in(splits[17], 71), 0),
        "decay_log": jnp.clip(1.4 * jax.random.uniform(splits[12], (H,), jnp.float32) ** block_scale(splits[12], (H,), ((0, 4),), -0.2, 0.2), 0.0, 1.4),
        "skip_gain": jnp.clip(0.5 + 1.0 * jax.random.uniform(splits[13], (H,), jnp.float32) ** block_scale(splits[13], (H,), ((0, 4),), -0.2, 0.2), 0.5, 1.5),
        "gate_gain": jnp.clip(1.0 + 0.1 * jax.random.normal(splits[14], (DI,), jnp.float32), 0.5, 1.5),
        "w_output": centred(splits[15], (DI, D), DI ** -0.5, 0.09375, ((0, 4),)),
        "cotangent": centred(splits[16], (TOKENS, D), 1.0, 6.0, ((0, 8),)),
    }


HIGH = lax.Precision.HIGHEST
EPS = 1e-05

@jax.custom_vjp
def low(v):
    return lax.optimization_barrier(v.astype(jnp.bfloat16)).astype(jnp.float32)

@jax.custom_vjp
def low_back(v):
    return v

def low_keep(v):
    return (low(v), None)

def low_pass(kept, grad):
    return (grad,)

def back_keep(v):
    return (v, None)

def back_low(kept, grad):
    return (low(grad),)
low.defvjp(low_keep, low_pass)
low_back.defvjp(back_keep, back_low)

def mult(left, right):
    return jnp.dot(left, right, precision=HIGH, preferred_element_type=jnp.float32)

def group_ssd(carry_state, pieces, decay_rate):
    values, step_sizes, key_rows, query_rows, starts = pieces
    length = starts.shape[0]
    segment = jnp.cumsum(starts).astype(jnp.int32)
    decay_sum = jnp.cumsum(step_sizes * decay_rate[None, :], axis=0)
    position = jnp.arange(length)
    linked = (segment[:, None] == segment[None, :]) & (position[:, None] >= position[None, :])
    linked_three = linked[:, :, None]
    spread = decay_sum[:, None, :] - decay_sum[None, :, :]
    factor = jnp.where(linked_three, jnp.exp(jnp.where(linked_three, spread, 0.0)), 0.0)
    scores = jnp.einsum('tn,sn->ts', query_rows, key_rows, precision=HIGH)
    weights = scores[:, :, None] * factor * step_sizes[None, :, :]
    output = jnp.einsum('tsh,shp->thp', weights, values, precision=HIGH)
    opened = (segment == 0).astype(jnp.float32)[:, None] * jnp.exp(decay_sum)
    output = output + opened[:, :, None] * jnp.einsum('tn,hpn->thp', query_rows, carry_state, precision=HIGH)
    closing = decay_sum[-1]
    tail_keep = (segment == segment[-1]).astype(jnp.float32)[:, None] * jnp.exp(closing[None, :] - decay_sum) * step_sizes
    carried = jnp.exp(closing) * (segment[-1] == 0).astype(jnp.float32)
    added_state = jnp.einsum('sh,shp,sn->hpn', tail_keep, values, key_rows, precision=HIGH)
    return (carried[:, None, None] * carry_state + added_state, output)

def run_ssd(values, step_sizes, key_rows, query_rows, starts, decay_rate, initial, block_rows):
    total_blocks = starts.shape[0] // block_rows
    pieces = (values.reshape(total_blocks, block_rows, values.shape[1], values.shape[2]), step_sizes.reshape(total_blocks, block_rows, step_sizes.shape[1]), key_rows.reshape(total_blocks, block_rows, key_rows.shape[1]), query_rows.reshape(total_blocks, block_rows, query_rows.shape[1]), starts.reshape(total_blocks, block_rows))

    def advance(carry_state, piece):
        return group_ssd(carry_state, piece, decay_rate)
    closing, outputs = lax.scan(jax.checkpoint(advance), initial, pieces)
    return (outputs.reshape(values.shape), closing)

def causal_conv(signal, kernel, offset_bias, segment):
    summed = offset_bias[None, :] + kernel[0] * signal
    for back_step in range(1, CONV):
        moved = jnp.concatenate([jnp.zeros((back_step, signal.shape[1]), jnp.float32), signal[:-back_step]], 0)
        earlier = jnp.concatenate([jnp.full((back_step,), -1, jnp.int32), segment[:-back_step]], 0)
        linked = (earlier == segment).astype(jnp.float32)[:, None]
        summed = summed + kernel[back_step] * moved * linked
    return summed

def reference(tokens, boundary, norm_gain, w_gate, w_inner, w_pair, w_step, conv_inner, conv_pair, bias_inner, bias_pair, step_bias, decay_log, skip_gain, gate_gain, w_output, cotangent):
    segment = jnp.cumsum(boundary).astype(jnp.int32)

    def forward(tokens, norm_gain, w_gate, w_inner, w_pair, w_step, conv_inner, conv_pair, bias_inner, bias_pair, step_bias, decay_log, skip_gain, gate_gain, w_output):
        scale_in = lax.rsqrt(lax.optimization_barrier(jnp.mean(tokens * tokens, axis=-1, keepdims=True)) + EPS)
        normed = low(tokens * scale_in * norm_gain)
        gate_pre = low_back(mult(normed, w_gate))
        inner_raw = low(low_back(mult(normed, w_inner)))
        pair_raw = low(low_back(mult(normed, w_pair)))
        step_raw = low_back(mult(normed, w_step))
        inner_act = low(jax.nn.silu(causal_conv(inner_raw, conv_inner, bias_inner, segment)))
        pair_act = low(jax.nn.silu(causal_conv(pair_raw, conv_pair, bias_pair, segment)))
        step_sizes = jax.nn.softplus(step_raw + step_bias)
        decay_rate = -jnp.exp(decay_log)
        values = inner_act.reshape(TOKENS, H, P_SIZE)
        mixed, _ = run_ssd(values, step_sizes, pair_act[:, :N], pair_act[:, N:], boundary, decay_rate, jnp.zeros((H, P_SIZE, N), jnp.float32), GROUP)
        mixed = mixed.reshape(TOKENS, H * P_SIZE) + jnp.repeat(skip_gain, P_SIZE) * inner_act
        gated = mixed * jax.nn.silu(gate_pre)
        scale_out = lax.rsqrt(lax.optimization_barrier(jnp.mean(gated * gated, axis=-1, keepdims=True)) + EPS)
        gate_normed = low(gated * scale_out * gate_gain)
        return tokens + mult(gate_normed, w_output)
    outcome, pullback = jax.vjp(forward, tokens.astype(jnp.float32), norm_gain.astype(jnp.float32), w_gate.astype(jnp.float32), w_inner.astype(jnp.float32), w_pair.astype(jnp.float32), w_step.astype(jnp.float32), conv_inner.astype(jnp.float32), conv_pair.astype(jnp.float32), bias_inner.astype(jnp.float32), bias_pair.astype(jnp.float32), step_bias.astype(jnp.float32), decay_log.astype(jnp.float32), skip_gain.astype(jnp.float32), gate_gain.astype(jnp.float32), w_output.astype(jnp.float32))
    grads = pullback(cotangent.astype(jnp.float32))
    return (outcome.astype(jnp.bfloat16), grads[0], grads[1], grads[2], grads[3], grads[4], grads[5], grads[6], grads[7], grads[8], grads[9], grads[10], grads[11], grads[12], grads[13], grads[14])
```

```python
import jax
import jax.numpy as jnp
from jax import lax
from jax.experimental import pallas as pl
from jax.experimental.pallas import tpu as pltpu
from jax.sharding import PartitionSpec as P

N = 128
HP = 64
DI = 4096
EPS = 1e-05
L = 128
LANES = 128
HALO = 16
F32 = jnp.float32
BF = jnp.bfloat16
VMEM_LIMIT = 56 * 1024 * 1024
FIRST = (((0,), (0,)), ((), ()))
LAST = (((1,), (1,)), ((), ()))


def dot(a, b):
    return jnp.dot(a, b, preferred_element_type=F32)


def dotg(a, b, dims):
    return lax.dot_general(a, b, dims, preferred_element_type=F32)


def split2(v):
    hi = v.astype(BF)
    return hi, (v - hi.astype(F32)).astype(BF)


def split3(v):
    hi = v.astype(BF)
    rest = v - hi.astype(F32)
    mid = rest.astype(BF)
    return hi, mid, (rest - mid.astype(F32)).astype(BF)


def exact_sum(tri, v):
    hi, mid, lo = split3(v)
    return dot(tri, hi) + dot(tri, mid) + dot(tri, lo)


def expand(v, spread2):
    hi, lo = split2(v)
    return dot(jnp.concatenate([hi, lo], 1), spread2)


def fold8(v):
    return jnp.sum(v.reshape(v.shape[0] // 8, 8, v.shape[1]), axis=0)


def stacked_pair(v, left):
    zero = jnp.zeros_like(v)
    return jnp.concatenate([jnp.where(left, v, zero), jnp.where(left, zero, v)], 0)


def lane_is_left(shape):
    return lax.broadcasted_iota(jnp.int32, shape, 1) < HP


def mask_of(info, seg_row):
    rows = lax.broadcasted_iota(jnp.int32, (L, L), 0)
    cols = lax.broadcasted_iota(jnp.int32, (L, L), 1)
    linked = (info[:, 0:1] == seg_row) & (rows >= cols)
    return jnp.where(linked, 0.0, -1e30).astype(F32)


def sigmoid(v):
    return 1.0 / (1.0 + jnp.exp(-v))


def chunk_spec(width, place):
    return pl.BlockSpec((L, width), lambda c: (place(c), 0))


def slab_spec(rows, width, place):
    return pl.BlockSpec((1, rows, width), lambda c: (place(c), 0, 0))


def whole_spec(shape):
    return pl.BlockSpec(shape, lambda c: (0,) * len(shape))


def ahead(c):
    return c


def call(kernel, steps, in_specs, out_specs, out_shape, scratch, args, flops, traffic):
    return pl.pallas_call(
        kernel,
        grid=(steps,),
        in_specs=in_specs,
        out_specs=out_specs,
        out_shape=out_shape,
        scratch_shapes=scratch,
        compiler_params=pltpu.CompilerParams(
            dimension_semantics=("arbitrary",), vmem_limit_bytes=VMEM_LIMIT
        ),
        cost_estimate=pl.CostEstimate(flops=flops, bytes_accessed=traffic, transcendentals=0),
    )(*args)


def conv_kernel(
    raw_ref, pair_ref, step_ref, info_ref, halo_ref, taps_ref, head_ref, tri_ref, spread_ref,
    act_ref, pact_ref, dt_ref, cs_ref, state_ref, total_ref, buf,
):
    c = pl.program_id(0)
    inner = raw_ref.shape[1]
    groups = inner // LANES
    pair_groups = pair_ref.shape[1] // LANES

    @pl.when(c == 0)
    def _():
        buf[0:8, :] = halo_ref[HALO - 8 :, :].astype(F32)
        state_ref[...] = jnp.zeros_like(state_ref)
        total_ref[...] = jnp.zeros_like(total_ref)

    info = info_ref[...]
    masks = [None] + [jnp.broadcast_to(info[:, 2 + k : 3 + k], (L, LANES)) for k in (1, 2, 3)]
    dt = jax.nn.softplus(step_ref[...] + head_ref[0:1, :])
    dt_ref[...] = dt
    cs = exact_sum(tri_ref[...], dt * head_ref[1:2, :])
    cs_ref[...] = cs
    closing = cs[L - 1 :, :]
    total_ref[...] += jnp.broadcast_to(closing, total_ref.shape)
    tail = jnp.exp(closing - cs) * info[:, 2:3] * dt
    tail_wide = expand(tail, spread_ref[...])
    keep = jnp.exp(closing) * info[0:1, 9:10]
    keep_wide = expand(jnp.broadcast_to(keep, (8, LANES)), spread_ref[...])[0:1, :]
    acts = []
    for j in range(groups + pair_groups):
        cols = slice(j * LANES, (j + 1) * LANES)
        if j < groups:
            raw = raw_ref[:, cols].astype(F32)
        else:
            raw = pair_ref[:, (j - groups) * LANES : (j - groups + 1) * LANES].astype(F32)
        buf[8 : 8 + L, cols] = raw
        pre = taps_ref[4:5, cols] + taps_ref[0:1, cols] * raw
        for k in (1, 2, 3):
            pre = pre + taps_ref[k : k + 1, cols] * buf[8 - k : 8 - k + L, cols] * masks[k]
        act = (pre * sigmoid(pre)).astype(BF)
        buf[0:8, cols] = raw[L - 8 :, :]
        if j < groups:
            act_ref[:, cols] = act
        else:
            pact_ref[:, (j - groups) * LANES : (j - groups + 1) * LANES] = act
    key = pact_ref[:, :N]
    for j in range(groups):
        cols = slice(j * LANES, (j + 1) * LANES)
        weighted = (act_ref[:, cols].astype(F32) * tail_wide[:, cols]).astype(BF)
        state_ref[:, cols] = keep_wide[:, cols] * state_ref[:, cols] + dotg(key, weighted, FIRST)


def out_kernel(
    act_ref, pact_ref, dt_ref, cs_ref, info_ref, seg_ref, gate_ref, dgn_ref, state_in_ref,
    gains_ref, spread_ref,
    mixed_ref, gg_ref, sums_ref, entry_ref, state,
):
    c = pl.program_id(0)
    inner = act_ref.shape[1]
    groups = inner // LANES

    @pl.when(c == 0)
    def _():
        state[...] = state_in_ref[...]

    info = info_ref[...]
    mask = mask_of(info, seg_ref[0])
    key = pact_ref[:, :N]
    query = pact_ref[:, N:]
    scores = dotg(query, key, LAST)
    dt = dt_ref[...]
    cs = cs_ref[...]
    cs_rows = cs.T
    closing = cs[L - 1 :, :]
    spread = spread_ref[...]
    dt_wide = expand(dt, spread)
    open_wide = expand(jnp.exp(cs) * info[:, 1:2], spread)
    tail_wide = expand(jnp.exp(closing - cs) * info[:, 2:3], spread)
    keep = jnp.exp(closing) * info[0:1, 9:10]
    keep_wide = expand(jnp.broadcast_to(keep, (8, LANES)), spread)[0:1, :]
    left = lane_is_left((L, LANES))
    square = jnp.zeros((L, LANES), F32)
    cross = jnp.zeros((L, LANES), F32)
    for j in range(groups):
        cols = slice(j * LANES, (j + 1) * LANES)
        x = act_ref[:, cols].astype(F32)
        xd = x * dt_wide[:, cols]
        xd_low = xd.astype(BF)
        weights = []
        for h in (2 * j, 2 * j + 1):
            factor = jnp.exp(cs[:, h : h + 1] - cs_rows[h : h + 1, :] + mask)
            weights.append((scores * factor).astype(BF))
        entry = state[:, cols].astype(BF)
        entry_ref[0, :, cols] = entry
        y = dot(jnp.concatenate(weights, 1), stacked_pair(xd_low, left))
        y = y + open_wide[:, cols] * dot(query, entry)
        mixed = y + gains_ref[0:1, cols] * x
        mixed_ref[:, cols] = mixed.astype(BF)
        gate = gate_ref[:, cols].astype(F32)
        gated = mixed * (gate * sigmoid(gate))
        gg = gated * gains_ref[1:2, cols]
        gg_ref[:, cols] = gg.astype(BF)
        square = square + gated * gated
        cross = cross + gg * dgn_ref[:, cols].astype(F32)
        weighted = (xd * tail_wide[:, cols]).astype(BF)
        state[:, cols] = keep_wide[:, cols] * state[:, cols] + dotg(key, weighted, FIRST)
    lane = lax.broadcasted_iota(jnp.int32, (L, LANES), 1)
    both = jnp.where(
        lane == 0,
        jnp.sum(square, axis=1, keepdims=True),
        jnp.sum(cross, axis=1, keepdims=True),
    )
    sums_ref[0] = both.T[0:8, :]


def gate_kernel(
    mixed_ref, gate_ref, dgn_ref, act_ref, pact_ref, cs_ref, info_ref, stats_ref, gains_ref, spread_ref,
    dmix_ref, dgate_ref, stat_ref, dstate_ref, dgain_ref, dskip_ref,
):
    c = pl.program_id(0)
    inner = act_ref.shape[1]
    groups = inner // LANES

    @pl.when(c == 0)
    def _():
        dstate_ref[...] = jnp.zeros_like(dstate_ref)
        dgain_ref[...] = jnp.zeros_like(dgain_ref)
        dskip_ref[...] = jnp.zeros_like(dskip_ref)

    info = info_ref[...]
    stats = jnp.concatenate([stats_ref[0]] * (LANES // 8), 0).T
    scale = jnp.broadcast_to(stats[:, 0:1], (L, LANES))
    coef = jnp.broadcast_to(stats[:, 1:2], (L, LANES))
    cs = cs_ref[...]
    spread = spread_ref[...]
    open_wide = expand(jnp.exp(cs) * info[:, 1:2], spread)
    keep = jnp.exp(cs[L - 1 :, :]) * info[0:1, 9:10]
    keep_wide = expand(jnp.broadcast_to(keep, (8, LANES)), spread)[0:1, :]
    query = pact_ref[:, N:]
    row = jnp.zeros((L, LANES), F32)
    for j in range(groups):
        cols = slice(j * LANES, (j + 1) * LANES)
        mixed = mixed_ref[:, cols].astype(F32)
        gate = gate_ref[:, cols].astype(F32)
        dgn = dgn_ref[:, cols].astype(F32)
        x = act_ref[:, cols].astype(F32)
        sig = sigmoid(gate)
        act = gate * sig
        gated = mixed * act
        scaled = dgn * scale
        dgain_ref[:, cols] += fold8(scaled * gated)
        dgated = scaled * gains_ref[1:2, cols] - gated * coef
        dmix = dgated * act
        dgate = dgated * mixed * (sig + act * (1.0 - sig))
        dskip_ref[:, cols] += fold8(dmix * x)
        row = row + dgate * gate
        dgate_ref[:, cols] = dgate.astype(BF)
        low = dmix.astype(BF)
        dmix_ref[:, cols] = low
        opened = (low.astype(F32) * open_wide[:, cols]).astype(BF)
        dstate_ref[:, cols] = keep_wide[:, cols] * dstate_ref[:, cols] + dotg(query, opened, FIRST)
    stat_ref[0] = jnp.broadcast_to(jnp.sum(row, axis=1, keepdims=True), (L, LANES)).T[0:8, :]


def back_kernel(
    act_ref, pact_ref, dt_ref, cs_ref, info_ref, seg_ref, dmix_ref, entry_ref, dstate_in_ref,
    raw_ref, pair_ref, raw_prev_ref, pair_prev_ref, step_ref, halo_ref, near_ref,
    taps_ref, head_ref, gains_ref, tri_ref, spread_ref, gather_ref,
    d_ref, stat_ref, dtaps_ref, dhead_ref, dhalo_ref,
    dstate, buf, dbuf,
):
    c = pl.program_id(0)
    last = pl.num_programs(0) - 1
    inner = act_ref.shape[1]
    groups = inner // LANES
    wide = inner + 2 * N

    @pl.when(c == 0)
    def _():
        dstate[...] = dstate_in_ref[...]
        dbuf[L:, :] = jnp.zeros((8, wide), F32)
        dtaps_ref[...] = jnp.zeros_like(dtaps_ref)
        dhead_ref[...] = jnp.zeros_like(dhead_ref)

    @pl.when(c == last)
    def _():
        buf[0:8, :] = halo_ref[HALO - 8 :, :].astype(F32)

    @pl.when(c < last)
    def _():
        buf[0:8, :inner] = raw_prev_ref[HALO - 8 :, :].astype(F32)
        buf[0:8, inner:] = pair_prev_ref[HALO - 8 :, :].astype(F32)

    info = info_ref[...]
    masks = [None] + [jnp.broadcast_to(info[:, 2 + k : 3 + k], (L, LANES)) for k in (1, 2, 3)]
    afters = [None] + [jnp.broadcast_to(info[:, 5 + k : 6 + k], (L, LANES)) for k in (1, 2, 3)]
    mask = mask_of(info, seg_ref[0])
    key = pact_ref[:, :N]
    query = pact_ref[:, N:]
    scores = dotg(query, key, LAST)
    dt = dt_ref[...]
    cs = cs_ref[...]
    cs_rows = cs.T
    closing = cs[L - 1 :, :]
    spread = spread_ref[...]
    dt_wide = expand(dt, spread)
    open_wide = expand(jnp.exp(cs) * info[:, 1:2], spread)
    tail_wide = expand(jnp.exp(closing - cs) * info[:, 2:3], spread)
    keep = jnp.exp(closing) * info[0:1, 9:10]
    keep_wide = expand(jnp.broadcast_to(keep, (8, LANES)), spread)[0:1, :]
    left = lane_is_left((L, LANES))

    def conv_back(j, raw, dact):
        cols = slice(j * LANES, (j + 1) * LANES)
        buf[8 : 8 + L, cols] = raw
        pre = taps_ref[4:5, cols] + taps_ref[0:1, cols] * raw
        moved = [raw]
        for k in (1, 2, 3):
            moved.append(buf[8 - k : 8 - k + L, cols] * masks[k])
            pre = pre + taps_ref[k : k + 1, cols] * moved[k]
        sig = sigmoid(pre)
        dpre = dact * (sig * (1.0 + pre * (1.0 - sig)))
        for k in range(4):
            dtaps_ref[8 * k : 8 * k + 8, cols] += fold8(dpre * moved[k])
        dtaps_ref[32:40, cols] += fold8(dpre)
        dbuf[0:L, cols] = dpre
        draw = taps_ref[0:1, cols] * dpre
        for k in (1, 2, 3):
            draw = draw + taps_ref[k : k + 1, cols] * dbuf[k : k + L, cols] * afters[k]
        dbuf[L : L + 8, cols] = dpre[0:8, :]
        d_ref[:, cols] = draw.astype(BF)
        return draw * raw

    row = jnp.zeros((L, LANES), F32)
    dscores = jnp.zeros((L, L), F32)
    dkey = jnp.zeros((L, N), F32)
    dquery = jnp.zeros((L, N), F32)
    dcs = jnp.zeros((L, LANES), F32)
    ddt = jnp.zeros((L, LANES), F32)
    dclose = jnp.zeros((8, LANES), F32)
    for j in range(groups):
        cols = slice(j * LANES, (j + 1) * LANES)
        x = act_ref[:, cols].astype(F32)
        xd = (x * dt_wide[:, cols]).astype(BF)
        dm = dmix_ref[:, cols]
        dmf = dm.astype(F32)
        xdf = xd.astype(F32)
        factors = []
        weights = []
        for h in (2 * j, 2 * j + 1):
            factor = jnp.exp(cs[:, h : h + 1] - cs_rows[h : h + 1, :] + mask)
            factors.append(factor)
            weights.append((scores * factor).astype(BF))
        pair_x = stacked_pair(xd, left)
        pair_d = stacked_pair(dm, left)
        dweights = dotg(dm, pair_x, LAST)
        dscores = dscores + dweights[:, :L] * factors[0] + dweights[:, L:] * factors[1]
        y = dot(jnp.concatenate(weights, 1), pair_x)
        dxd = dotg(jnp.concatenate(weights, 0), pair_d, FIRST)
        entry = entry_ref[0, :, cols]
        dst = dstate[:, cols]
        dst_low = dst.astype(BF)
        opened = (dmf * open_wide[:, cols]).astype(BF)
        tailed = (xdf * tail_wide[:, cols]).astype(BF)
        from_state = dot(query, entry)
        to_state = dot(key, dst_low)
        out_part = tailed.astype(F32) * to_state
        diff = dmf * y + opened.astype(F32) * from_state - xdf * dxd - out_part
        dxd = dxd + to_state * tail_wide[:, cols]
        hi, lo = split2(diff)
        gather = gather_ref[cols, :]
        dcs = dcs + dot(hi, gather) + dot(lo, gather)
        ddt = ddt + dot((dxd * x).astype(BF), gather)
        close = fold8(out_part) + keep_wide[:, cols] * fold8(dst * entry.astype(F32))
        hi, lo = split2(close)
        dclose = dclose + dot(hi, gather) + dot(lo, gather)
        dquery = dquery + dotg(opened, entry, LAST)
        dkey = dkey + dotg(tailed, dst_low, LAST)
        dstate[:, cols] = keep_wide[:, cols] * dst + dotg(query, opened, FIRST)
        dx = dxd * dt_wide[:, cols] + gains_ref[0:1, cols] * dmf
        row = row + conv_back(j, raw_ref[:, cols].astype(F32), dx)
    dscores = dscores.astype(BF)
    dquery = dquery + dot(dscores, key)
    dkey = dkey + dotg(dscores, query, FIRST)
    row = row + conv_back(groups, pair_ref[:, :N].astype(F32), dkey)
    row = row + conv_back(groups + 1, pair_ref[:, N:].astype(F32), dquery)
    later = dcs
    hi, mid, lo = split3(later)
    tri = tri_ref[...]
    da = dotg(tri, hi, FIRST) + dotg(tri, mid, FIRST) + dotg(tri, lo, FIRST)
    da = da + jnp.sum(dclose, axis=0, keepdims=True)
    ddt = ddt + head_ref[1:2, :] * da
    step = step_ref[...]
    dstep = ddt * sigmoid(step + head_ref[0:1, :])
    dhead_ref[0:8, :] += fold8(dstep)
    dhead_ref[8:16, :] += fold8(dt * da)
    d_ref[:, wide:] = dstep.astype(BF)
    row = row + dstep * step
    stat_ref[0] = jnp.broadcast_to(jnp.sum(row, axis=1, keepdims=True), (L, LANES)).T[0:8, :]

    @pl.when(c == last)
    def _():
        near = near_ref[...]
        for j in range(groups + 2):
            cols = slice(j * LANES, (j + 1) * LANES)
            head_rows = jnp.concatenate([jnp.zeros((8, LANES), F32), dbuf[0:8, cols]], 0)
            dbuf[0:16, cols] = head_rows
            total = jnp.zeros((8, LANES), F32)
            for k in (1, 2, 3):
                total = total + taps_ref[k : k + 1, cols] * dbuf[k : k + 8, cols] * near[:, 5 + k : 6 + k]
            dhalo_ref[:, cols] = total


def flip(block, axis, bit):
    count = lax.axis_size(axis)
    route = [(i, i ^ bit) for i in range(count)]
    return jax.tree.map(lambda a: lax.ppermute(a, axis, route), block)


def sum_over(block, axis):
    bit = 1
    while bit < lax.axis_size(axis):
        block = jax.tree.map(jnp.add, block, flip(block, axis, bit))
        bit *= 2
    return block


def gather_over(block, axis, dim):
    count = lax.axis_size(axis)
    place = lax.axis_index(axis)
    pieces = jnp.stack([block] + [flip(block, axis, d) for d in range(1, count)], 0)
    return jnp.concatenate(
        [lax.dynamic_index_in_dim(pieces, place ^ q, 0, False) for q in range(count)], dim
    )


def shift_over(block, axis, distance):
    devices = range(lax.axis_size(axis))
    route = [(i, i + distance) for i in devices if i + distance in devices]
    return lax.ppermute(block, axis, route)


def entering(through, state, axis, reverse):
    count = lax.axis_size(axis)
    place = lax.axis_index(axis)
    before_decay = jnp.ones_like(through)
    before = jnp.zeros_like(state)
    bit = 1
    while bit < count:
        other_decay = flip(through, axis, bit)
        other = flip(state.astype(BF), axis, bit).astype(F32)
        upper = (place & bit) != 0
        follows = jnp.logical_not(upper) if reverse else upper
        before = jnp.where(follows, before + before_decay * other, before)
        before_decay = jnp.where(follows, before_decay * other_decay, before_decay)
        state = jnp.where(follows, state + through * other, other + other_decay * state)
        through = through * other_decay
        bit *= 2
    return before


def body(
    tokens, boundary, norm_gain, w_gate, w_inner, w_pair, w_step, conv_inner, conv_pair,
    bias_inner, bias_pair, step_bias, decay_log, skip_gain, gate_gain, w_output, cotangent,
):
    rows, width = tokens.shape
    inner = w_gate.shape[1]
    heads = w_step.shape[1]
    head_count = lax.axis_size("head")
    place = lax.axis_index("head")
    quarter = width // head_count
    pair_cols = w_pair.shape[1]
    pair = pair_cols * head_count
    wide = inner + pair
    steps = rows // L
    margin = conv_inner.shape[0] - 1
    sds = jax.ShapeDtypeStruct

    def behind(c):
        return steps - 1 - c

    starts = boundary.reshape(steps, L).astype(F32)
    upper = jnp.triu(jnp.ones((L, L), BF))
    seg = dot(starts.astype(BF), upper)
    seg_last = seg[:, L - 1 :]
    m1 = 1.0 - boundary.astype(F32)
    m2 = m1 * jnp.concatenate([jnp.ones((1,), F32), m1[:-1]])
    m3 = m2 * jnp.concatenate([jnp.ones((2,), F32), m1[:-2]])
    afters = []
    for k, m in ((1, m1), (2, m2), (3, m3)):
        ext = jnp.concatenate([jnp.zeros((8,), F32), m, jnp.zeros((3,), F32)])
        afters.append(ext[k : k + 8 + rows])
    zero = jnp.zeros((rows,), F32)
    opened = (seg == 0).astype(F32).reshape(rows)
    tail = (seg == seg_last).astype(F32).reshape(rows)
    keep = jnp.broadcast_to((seg_last == 0).astype(F32), (steps, L)).reshape(rows)
    info = jnp.stack(
        [seg.reshape(rows), opened, tail, m1, m2, m3]
        + [a[8:] for a in afters]
        + [keep]
        + [zero] * 6,
        1,
    )
    near = jnp.stack([jnp.zeros((8,), F32)] * 6 + [a[:8] for a in afters] + [jnp.zeros((8,), F32)] * 7, 1)
    seg_rows = seg.reshape(steps, 1, L)
    no_start = (jnp.max(boundary) == 0).astype(F32)
    tail_starts = boundary[rows - HALO :].astype(F32)
    after_it = jnp.sum(jnp.triu(jnp.ones((HALO, HALO), F32), 1) * tail_starts[None, :], axis=1)
    is_margin = jnp.arange(HALO) >= HALO - margin
    keep_tail = jnp.where(is_margin & (after_it == 0), 1.0, 0.0)[:, None]

    head_of = jnp.arange(inner)[None, :] // HP
    spread = (head_of == jnp.arange(LANES)[:, None]).astype(BF)
    spread2 = jnp.concatenate([spread, spread], 0)
    gather = (head_of.T == jnp.arange(LANES)[None, :]).astype(BF)
    lower = jnp.tril(jnp.ones((L, L), BF))

    pair_small = jnp.concatenate([conv_pair, bias_pair[None, :], jnp.zeros((3, pair_cols), F32)], 0)
    pair_small = gather_over(pair_small, "head", 1)
    w_pair_all = gather_over(w_pair, "head", 1)
    taps = jnp.concatenate(
        [jnp.concatenate([conv_inner, bias_inner[None, :], jnp.zeros((3, inner), F32)], 0), pair_small], 1
    )
    pad = LANES - heads
    rate = -jnp.exp(decay_log)
    head_rows = jnp.pad(jnp.stack([step_bias, rate] + [jnp.zeros_like(rate)] * 6, 0), ((0, 0), (0, pad)))
    skip_cols = jnp.repeat(skip_gain, HP)
    gains = jnp.stack([skip_cols, gate_gain] + [jnp.zeros_like(gate_gain)] * 6, 0)
    w_step_pad = jnp.pad(w_step, ((0, 0), (0, pad)))

    def norm(t):
        t = t.astype(F32)
        s = lax.rsqrt(jnp.mean(t * t, axis=-1, keepdims=True) + EPS)
        return s, (t * s * norm_gain).astype(BF)

    sent = (tokens[rows - HALO :].astype(F32) * keep_tail).astype(BF)
    token_halo = shift_over(sent, "seq", 1)
    scale_in, normed = norm(tokens)
    _, normed_halo = norm(token_halo)
    inner_raw = dot(normed, w_inner).astype(BF)
    pair_raw = dot(normed, w_pair_all).astype(BF)
    step_raw = dot(normed, w_step_pad)
    halo = jnp.concatenate([dot(normed_halo, w_inner), dot(normed_halo, w_pair_all)], 1).astype(BF)

    wide_flops = 2 * rows * N * inner
    act, pact, dt, cs, closing, total = call(
        conv_kernel,
        steps,
        [
            chunk_spec(inner, ahead), chunk_spec(pair, ahead), chunk_spec(LANES, ahead), chunk_spec(16, ahead),
            whole_spec((HALO, wide)), whole_spec((8, wide)), whole_spec((8, LANES)), whole_spec((L, L)),
            whole_spec((2 * LANES, inner)),
        ],
        [
            chunk_spec(inner, ahead), chunk_spec(pair, ahead), chunk_spec(LANES, ahead), chunk_spec(LANES, ahead),
            whole_spec((N, inner)), whole_spec((8, LANES)),
        ],
        [
            sds((rows, inner), BF), sds((rows, pair), BF), sds((rows, LANES), F32), sds((rows, LANES), F32),
            sds((N, inner), F32), sds((8, LANES), F32),
        ],
        [pltpu.VMEM((8 + L, wide), F32)],
        (inner_raw, pair_raw, step_raw, info, halo, taps, head_rows, lower, spread2),
        2 * wide_flops,
        rows * inner * 5,
    )
    through = jnp.repeat(jnp.exp(total[0, :heads]) * no_start, HP)[None, :]
    state_in = entering(through, closing, "seq", False)

    gate_pre = dot(normed, w_gate).astype(BF)
    dgn = dotg(cotangent, w_output, LAST).astype(BF)

    mixed, gg, sums, entries = call(
        out_kernel,
        steps,
        [
            chunk_spec(inner, ahead), chunk_spec(pair, ahead), chunk_spec(LANES, ahead), chunk_spec(LANES, ahead),
            chunk_spec(16, ahead), slab_spec(1, L, ahead), chunk_spec(inner, ahead), chunk_spec(inner, ahead),
            whole_spec((N, inner)), whole_spec((8, inner)), whole_spec((2 * LANES, inner)),
        ],
        [chunk_spec(inner, ahead), chunk_spec(inner, ahead), slab_spec(8, L, ahead), slab_spec(N, inner, ahead)],
        [
            sds((rows, inner), BF), sds((rows, inner), BF), sds((steps, 8, L), F32), sds((steps, N, inner), BF),
        ],
        [pltpu.VMEM((N, inner), F32)],
        (act, pact, dt, cs, info, seg_rows, gate_pre, dgn, state_in, gains, spread2),
        6 * wide_flops,
        rows * inner * 14,
    )
    sums = sum_over(sums[:, 0:2, :], "head")
    scale_rows = lax.rsqrt(sums[:, 0:1, :] / DI + EPS)
    coef_rows = scale_rows * scale_rows * scale_rows * sums[:, 1:2, :] / DI
    stats = jnp.concatenate([scale_rows, coef_rows, jnp.zeros((steps, 6, L), F32)], 1)
    scale_out = scale_rows.reshape(rows, 1)

    partial_out = dot(gg, w_output).astype(BF)
    branch = lax.psum_scatter(partial_out, "head", scatter_dimension=1, tiled=True).astype(F32)
    token_cols = lax.dynamic_slice_in_dim(tokens, place * quarter, quarter, 1).astype(F32)
    result = (token_cols + scale_out * branch).astype(BF)

    cot_scaled = (cotangent.astype(F32) * scale_out).astype(BF)
    dw_out = dotg(cot_scaled, gg, FIRST).astype(BF)
    dw_out = lax.psum_scatter(dw_out, "seq", scatter_dimension=0, tiled=True).astype(F32)

    dmix, dgate, stat_gate, dstate_local, dgain, dskip = call(
        gate_kernel,
        steps,
        [
            chunk_spec(inner, behind), chunk_spec(inner, behind), chunk_spec(inner, behind), chunk_spec(inner, behind),
            chunk_spec(pair, behind), chunk_spec(LANES, behind), chunk_spec(16, behind), slab_spec(8, L, behind),
            whole_spec((8, inner)), whole_spec((2 * LANES, inner)),
        ],
        [
            chunk_spec(inner, behind), chunk_spec(inner, behind), slab_spec(8, L, behind), whole_spec((N, inner)),
            whole_spec((8, inner)), whole_spec((8, inner)),
        ],
        [
            sds((rows, inner), BF), sds((rows, inner), BF), sds((steps, 8, L), F32), sds((N, inner), F32),
            sds((8, inner), F32), sds((8, inner), F32),
        ],
        [],
        (mixed, gate_pre, dgn, act, pact, cs, info, stats, gains, spread2),
        2 * wide_flops,
        rows * inner * 14,
    )
    dclosing = entering(through, dstate_local, "seq", True)

    dw_gate = dotg(normed, dgate, FIRST).astype(BF)
    dw_gate = lax.psum_scatter(dw_gate, "seq", scatter_dimension=0, tiled=True).astype(F32)
    dn_gate = dotg(dgate, w_gate, LAST)

    def before_spec(width):
        return pl.BlockSpec((HALO, width), lambda c: (jnp.maximum(behind(c) * (L // HALO) - 1, 0), 0))

    d_all, stat_back, dtaps, dhead, dhalo = call(
        back_kernel,
        steps,
        [
            chunk_spec(inner, behind), chunk_spec(pair, behind), chunk_spec(LANES, behind), chunk_spec(LANES, behind),
            chunk_spec(16, behind), slab_spec(1, L, behind), chunk_spec(inner, behind), slab_spec(N, inner, behind),
            whole_spec((N, inner)),
            chunk_spec(inner, behind), chunk_spec(pair, behind), before_spec(inner), before_spec(pair),
            chunk_spec(LANES, behind), whole_spec((HALO, wide)), whole_spec((8, 16)),
            whole_spec((8, wide)), whole_spec((8, LANES)), whole_spec((8, inner)), whole_spec((L, L)),
            whole_spec((2 * LANES, inner)), whole_spec((inner, LANES)),
        ],
        [
            chunk_spec(wide + LANES, behind), slab_spec(8, L, behind), whole_spec((40, wide)),
            whole_spec((16, LANES)), whole_spec((8, wide)),
        ],
        [
            sds((rows, wide + LANES), BF), sds((steps, 8, L), F32), sds((40, wide), F32),
            sds((16, LANES), F32), sds((8, wide), F32),
        ],
        [pltpu.VMEM((N, inner), F32), pltpu.VMEM((8 + L, wide), F32), pltpu.VMEM((L + 8, wide), F32)],
        (
            act, pact, dt, cs, info, seg_rows, dmix, entries, dclosing, inner_raw, pair_raw, inner_raw, pair_raw,
            step_raw, halo, near, taps, head_rows, gains, lower, spread2, gather,
        ),
        14 * wide_flops,
        rows * inner * 14,
    )
    returned = shift_over(dhalo, "seq", -1)
    returned = jnp.concatenate([jnp.zeros((HALO - 8, wide), F32), returned], 0) * keep_tail
    tail_rows = slice(rows - HALO, rows)
    d_all = d_all.at[tail_rows, :wide].set((d_all[tail_rows, :wide].astype(F32) + returned).astype(BF))
    raw_tail = jnp.concatenate([inner_raw[tail_rows], pair_raw[tail_rows]], 1).astype(F32)
    stat_tail = jnp.sum(raw_tail * returned, axis=1)

    w_rest = jnp.concatenate([w_inner, w_pair_all, w_step_pad], 1)
    dw_rest = dotg(normed, d_all, FIRST).astype(BF)
    dw_rest = lax.psum_scatter(dw_rest, "seq", scatter_dimension=0, tiled=True).astype(F32)
    d_normed = (dn_gate + dotg(d_all, w_rest, LAST)).astype(BF)
    d_cols = lax.psum_scatter(d_normed, "head", scatter_dimension=1, tiled=True).astype(F32)
    row_stat = (stat_gate[:, 0, :] + stat_back[:, 0, :]).reshape(rows)
    row_stat = row_stat.at[tail_rows].add(stat_tail)
    row_stat = sum_over(row_stat.reshape(steps, L), "head").reshape(rows, 1)
    gain_cols = lax.dynamic_slice_in_dim(norm_gain, place * quarter, quarter, 0)
    cot_cols = lax.dynamic_slice_in_dim(cotangent, place * quarter, quarter, 1).astype(F32)
    grad_tokens = (
        cot_cols + scale_in * d_cols * gain_cols - token_cols * scale_in * scale_in * row_stat / width
    )
    d_norm_gain = jnp.sum(d_cols * token_cols * scale_in, axis=0)

    dtaps = jnp.sum(dtaps.reshape(5, 8, wide), axis=1)
    dhead = jnp.sum(dhead.reshape(2, 8, LANES), axis=1)
    dgain = jnp.sum(dgain, axis=0)
    dskip = jnp.sum(jnp.sum(dskip, axis=0).reshape(heads, HP), axis=1)
    pair_taps = sum_over(dtaps[:, inner:], "head")
    small = sum_over((dtaps[:, :inner], pair_taps, dhead, dgain, dskip, d_norm_gain), "seq")
    taps_sum, pair_sum, head_sum, gain_sum, skip_sum, norm_sum = small
    pair_sum = lax.dynamic_slice_in_dim(pair_sum, place * pair_cols, pair_cols, 1)
    dw_pair = lax.psum_scatter(dw_rest[:, inner:wide], "head", scatter_dimension=1, tiled=True)
    return (
        result,
        grad_tokens,
        norm_sum,
        dw_gate,
        dw_rest[:, :inner],
        dw_pair,
        dw_rest[:, wide : wide + heads],
        taps_sum[:4],
        pair_sum[:4],
        taps_sum[4],
        pair_sum[4],
        head_sum[0, :heads],
        head_sum[1, :heads] * rate,
        skip_sum,
        gain_sum,
        jnp.transpose(dw_out),
    )


def solution(mesh):
    return jax.shard_map(
        body,
        mesh=mesh,
        in_specs=(
            P("seq", None),
            P("seq"),
            P(),
            P(None, "head"),
            P(None, "head"),
            P(None, "head"),
            P(None, "head"),
            P(None, "head"),
            P(None, "head"),
            P("head"),
            P("head"),
            P("head"),
            P("head"),
            P("head"),
            P("head"),
            P("head", None),
            P("seq", None),
        ),
        out_specs=(
            P("seq", "head"),
            P("seq", "head"),
            P("head"),
            P("seq", "head"),
            P("seq", "head"),
            P("seq", "head"),
            P("seq", "head"),
            P(None, "head"),
            P(None, "head"),
            P("head"),
            P("head"),
            P("head"),
            P("head"),
            P("head"),
            P("head"),
            P("head", "seq"),
        ),
        check_vma=False,
    )
```

```python
import functools

import jax
import jax.numpy as jnp
import numpy as np
from jax import lax
from jax.experimental import pallas as pl
from jax.experimental.pallas import tpu as pltpu
from jax.sharding import PartitionSpec as P

N = 128
HP = 64
DI = 4096
EPS = 1e-05
L = 128
LANES = 128
HALO = 16
F32 = jnp.float32
BF = jnp.bfloat16
VMEM_LIMIT = 56 * 1024 * 1024
FIRST = (((0,), (0,)), ((), ()))
LAST = (((1,), (1,)), ((), ()))


def dot(a, b):
    return jnp.dot(a, b, preferred_element_type=F32)


def dotg(a, b, dims):
    return lax.dot_general(a, b, dims, preferred_element_type=F32)


def split2(v):
    hi = v.astype(BF)
    return hi, (v - hi.astype(F32)).astype(BF)


def split3(v):
    hi = v.astype(BF)
    rest = v - hi.astype(F32)
    mid = rest.astype(BF)
    return hi, mid, (rest - mid.astype(F32)).astype(BF)


def exact_sum(tri, v):
    hi, mid, lo = split3(v)
    return dot(tri, hi) + dot(tri, mid) + dot(tri, lo)


def expand(v, spread2):
    hi, lo = split2(v)
    return dot(jnp.concatenate([hi, lo], 1), spread2)


def fold8(v):
    return jnp.sum(v.reshape(v.shape[0] // 8, 8, v.shape[1]), axis=0)


def stacked_pair(v, left):
    zero = jnp.zeros_like(v)
    return jnp.concatenate([jnp.where(left, v, zero), jnp.where(left, zero, v)], 0)


def lane_is_left(shape):
    return lax.broadcasted_iota(jnp.int32, shape, 1) < HP


def columns(slab):
    pad = LANES - slab.shape[0]
    return jnp.concatenate([slab, jnp.zeros((pad, L), F32)], 0).T


def mask_of(info, seg_row):
    rows = lax.broadcasted_iota(jnp.int32, (L, L), 0)
    cols = lax.broadcasted_iota(jnp.int32, (L, L), 1)
    linked = (info[:, 0:1] == seg_row) & (rows >= cols)
    return jnp.where(linked, 0.0, -1e30).astype(F32)


def sigmoid(v):
    return 0.5 * jnp.tanh(0.5 * v) + 0.5


def chunk_spec(width, place):
    return pl.BlockSpec((L, width), lambda c: (place(c), 0))


def slab_spec(rows, width, place):
    return pl.BlockSpec((1, rows, width), lambda c: (place(c), 0, 0))


def whole_spec(shape):
    return pl.BlockSpec(shape, lambda c: (0,) * len(shape))


def ahead(c):
    return c


ANY = pl.BlockSpec(memory_space=pl.ANY)


class Chain:
    def __init__(self):
        self.last = None

    def run(self, kernel, grid, ins, outs, after=(), scratch=(), ids=None, aliases=None, us=5.0):
        given = [array for array, _ in ins]
        after = [a for a in list(after) + [self.last] if a is not None and not any(a is g for g in given)]
        lead = 0 if ids is None else 1
        keep_in = lead + len(ins)

        def inner(*refs):
            kernel(*refs[:keep_in], *refs[keep_in + len(after) :])

        result = pl.pallas_call(
            inner,
            grid_spec=pltpu.PrefetchScalarGridSpec(
                num_scalar_prefetch=lead,
                grid=grid,
                in_specs=[spec for _, spec in ins] + [ANY] * len(after),
                out_specs=[spec for spec, _, _ in outs],
                scratch_shapes=list(scratch),
            ),
            out_shape=[jax.ShapeDtypeStruct(shape, dtype) for _, shape, dtype in outs],
            input_output_aliases={lead + i: o for i, o in (aliases or {}).items()},
            compiler_params=pltpu.CompilerParams(
                dimension_semantics=("arbitrary",) * len(grid), vmem_limit_bytes=VMEM_LIMIT
            ),
            cost_estimate=pl.CostEstimate(flops=int(us * 1.15e9), bytes_accessed=10**4, transcendentals=0),
        )(*(() if ids is None else (ids,)), *given, *after)
        self.last = min(result, key=lambda r: r.size)
        return result


def whole(array):
    zeros = (0,) * array.ndim
    return array, pl.BlockSpec(array.shape, lambda *_: zeros)


def norm_rows(block, gain):
    t = block.astype(F32)
    scale = lax.rsqrt(jnp.mean(t * t, axis=-1, keepdims=True) + EPS)
    return scale, (t * scale * gain).astype(BF)


def proj_kernel(tokens_ref, gain_ref, w_ref, normed_ref, scale_ref, inner_ref):
    scale, normed = norm_rows(tokens_ref[...], gain_ref[...])
    scale_ref[...] = scale
    normed_ref[...] = normed
    inner_ref[...] = dot(normed, w_ref[...]).astype(BF)


def along(v, k):
    zero = jnp.zeros((1, v.shape[1]), v.dtype)
    if k > 0:
        other = jnp.concatenate([zero, v[:-1]], 0)
        return jnp.concatenate([other[:, L - k :], v[:, : L - k]], 1)
    other = jnp.concatenate([v[1:], zero], 0)
    return jnp.concatenate([v[:, -k:], other[:, :-k]], 1)


def prep_kernel(
    starts_ref, upper_ref, tokens_ref, step_bias_ref, decay_ref, skip_ref, gate_gain_ref, spread_ref,
    info_ref, sent_ref, keep_ref, head_ref, gains_ref,
):
    starts = starts_ref[...].astype(F32)
    seg = dot(starts.astype(BF), upper_ref[...])
    m1 = 1.0 - starts
    m2 = m1 * (1.0 - along(starts, 1))
    m3 = m2 * (1.0 - along(starts, 2))
    seg_last = jnp.broadcast_to(seg[:, L - 1 :], seg.shape)
    one = jnp.ones_like(seg)
    zero = jnp.zeros_like(seg)
    fields = [
        seg, jnp.where(seg == 0, one, zero), jnp.where(seg == seg_last, one, zero), m1, m2, m3,
        along(m1, -1), along(m2, -2), along(m3, -3), jnp.where(seg_last == 0, one, zero),
    ]
    for i in range(16):
        info_ref[:, i, :] = fields[i] if i < len(fields) else zero
    rows = lax.broadcasted_iota(jnp.int32, (HALO, L), 0)
    lanes = lax.broadcasted_iota(jnp.int32, (HALO, L), 1)
    last = jnp.broadcast_to(starts[starts.shape[0] - 1 :, :], (HALO, L))
    later = jnp.sum(jnp.where(lanes > rows + L - HALO, last, 0.0), axis=1, keepdims=True)
    place = lax.broadcasted_iota(jnp.int32, (HALO, 1), 0)
    keep = jnp.where((later == 0) & (place >= HALO - 3), 1.0, 0.0)
    keep_ref[...] = keep
    sent_ref[...] = (tokens_ref[...].astype(F32) * keep).astype(BF)
    heads = step_bias_ref.shape[1]
    head_ref[...] = jnp.zeros_like(head_ref)
    head_ref[0:1, 0:heads] = step_bias_ref[...]
    head_ref[1:2, 0:heads] = -jnp.exp(decay_ref[...])
    head_ref[2:3, 0:heads] = skip_ref[...]
    gains_ref[...] = expand(jnp.broadcast_to(head_ref[2:3, :], (8, LANES)), spread_ref[...])
    gains_ref[1:2, :] = gate_gain_ref[...]


def side_kernel(
    swap_ref, normed_ref, own_ref, one_ref, two_ref, three_ref, w_step_ref, halo_ref, gain_ref, w_ref,
    conv_ref, bias_ref,
    side_ref, halo_out_ref, w_side_ref, taps_ref,
):
    @pl.when(pl.program_id(0) == 0)
    def _():
        width = w_ref.shape[0]
        near = jnp.concatenate([own_ref[...], one_ref[...]], 1)
        far = jnp.concatenate([two_ref[...], three_ref[...]], 1)
        swap = swap_ref[0] != 0
        first = jnp.where(swap, far, near)
        second = jnp.where(swap, near, far)
        w_side_ref[:, 0:N] = first[:width]
        w_side_ref[:, N : 2 * N] = second[:width]
        w_side_ref[:, 2 * N :] = jnp.zeros((width, LANES), BF)
        w_side_ref[:, 2 * N : 2 * N + w_step_ref.shape[1]] = w_step_ref[...]
        inner = w_ref.shape[1]
        taps_ref[0:4, :inner] = conv_ref[...]
        taps_ref[4:5, :inner] = bias_ref[...]
        taps_ref[5:8, :inner] = jnp.zeros((3, inner), F32)
        for i, part in enumerate((first, second)):
            extra = part[width:].astype(F32)
            taps_ref[:, inner + i * N : inner + (i + 1) * N] = extra[0:8] + extra[8:16] + extra[16:24]
        _, halo = norm_rows(halo_ref[...], gain_ref[...])
        halo_out_ref[:, :inner] = dot(halo, w_ref[...])
        halo_out_ref[:, inner:] = dot(halo, w_side_ref[...])

    side_ref[...] = dot(normed_ref[...], w_side_ref[...])


def combine_kernel(
    reverse, first, known, final,
    follows_ref, arrived_ref, state_ref, rows_ref, *rest,
):
    rest = list(rest)
    before_ref = None if first else rest.pop(0)
    factor_ref = rest.pop(0) if known else None
    follows = follows_ref[0] != 0
    n = state_ref.shape[0]
    other = arrived_ref[0:n, :].astype(F32)
    if known:
        factor = factor_ref[2:3, :]
    else:
        extra = arrived_ref[n : n + 3, :].astype(F32)
        factor = extra[0:1] + extra[1:2] + extra[2:3]
    through = rows_ref[0:1, :]
    past = jnp.ones_like(through) if first else rows_ref[1:2, :]
    before = jnp.zeros_like(other) if first else before_ref[...]
    rest.pop(0)[...] = jnp.where(follows, before + past * other, before)
    new_rows = rest.pop(0)
    if first:
        new_rows[...] = jnp.zeros_like(new_rows)
    else:
        new_rows[...] = rows_ref[...]
    product = through * factor
    new_rows[0:1, :] = product
    new_rows[1:2, :] = jnp.where(follows, past * factor, past)
    new_rows[2:3, :] = factor
    if not final:
        state = state_ref[...]
        state = jnp.where(follows, state + through * other, other + factor * state)
        rest.pop(0)[...] = state
        low_ref = rest.pop(0)
        low_ref[0:n, :] = state.astype(BF)
        if not known:
            low_ref[n:, :] = factor_rows(product)


def factor_rows(row):
    hi, mid, lo = split3(row)
    return jnp.concatenate([hi, mid, lo, jnp.zeros((HALO - 3, row.shape[1]), BF)], 0)


def meet_kernel(_, *refs):
    for i in range(4):
        total = refs[2 * i][...].astype(F32) + refs[2 * i + 1][...].astype(F32)
        refs[8 + i][...] = total.astype(refs[8 + i].dtype)


def settle_kernel(mine, one, two, three, *rest):
    out_ref = rest[-1]
    total = mine[...] + one[...].astype(F32) + two[...].astype(F32) + three[...].astype(F32)
    out_ref[...] = total.T if out_ref.shape != total.shape else total


def add_kernel(count, *refs):
    for i in range(count):
        refs[2 * count + i][...] = refs[2 * i][...] + refs[2 * i + 1][...]


def share_kernel(swap_ref, kept_ref, got_ref, mine_ref, sent_ref):
    total = kept_ref[...].astype(F32) + got_ref[...].astype(F32)
    half = total.shape[1] // 2
    left, right = total[:, :half], total[:, half:]
    swap = swap_ref[0] != 0
    mine_ref[...] = jnp.where(swap, right, left)
    sent_ref[...] = jnp.where(swap, left, right).astype(BF)


def join_kernel(mine_ref, got_ref, step_ref, out_ref):
    half = mine_ref.shape[1]
    out_ref[:, :half] = (mine_ref[...] + got_ref[...].astype(F32)).astype(BF)
    out_ref[:, half:] = step_ref[:, :half]


def fix_kernel(
    raw_ref, side_ref, keep_ref, back_ref, small_ref, small_got_ref, d_in, dside_in, stat_in,
    d_ref, dside_ref, stat_ref, small_out_ref,
):
    small_out_ref[...] = small_ref[...] + small_got_ref[...]
    inner = raw_ref.shape[1]
    pair = 2 * N
    back = jnp.concatenate([jnp.zeros((HALO - 8, inner + pair), F32), back_ref[...]], 0) * keep_ref[...]
    d_ref[...] = (d_in[...].astype(F32) + back[:, :inner]).astype(BF)
    dside_ref[...] = dside_in[...]
    dside_ref[:, :pair] = (dside_in[:, :pair].astype(F32) + back[:, inner:]).astype(BF)
    row = jnp.sum(back[:, :inner] * raw_ref[...].astype(F32), axis=1, keepdims=True)
    row = row + jnp.sum(back[:, inner:] * side_ref[:, :pair].astype(BF).astype(F32), axis=1, keepdims=True)
    tall = jnp.concatenate([jnp.zeros((L - HALO, LANES), F32), jnp.broadcast_to(row, (HALO, LANES))], 0)
    stat_ref[...] = stat_in[...]
    stat_ref[0] += tall.T[0:8, :]


def nn_kernel(x_ref, w_ref, *rest):
    rest[-1][...] = dot(x_ref[...], w_ref[...]).astype(BF)


def nt_kernel(x_ref, w_ref, *rest):
    rest[-1][...] = dotg(x_ref[...], w_ref[...], LAST).astype(BF)


def cols_kernel(_, x_ref, w_ref, out_ref):
    out_ref[...] = dot(x_ref[...], w_ref[...]).astype(out_ref.dtype)


def cols_add_kernel(_, x_ref, w_ref, got_ref, out_ref):
    out_ref[...] = (dot(x_ref[...], w_ref[...]) + got_ref[...].astype(F32)).astype(out_ref.dtype)


def gate_back_kernel(_, x_ref, w_ref, out_ref):
    out_ref[0] = dotg(x_ref[...], w_ref[...], LAST).astype(BF)


def normed_back_kernel(_, x_ref, w_ref, y_ref, v_ref, base_ref, *rest):
    total = dotg(x_ref[...], w_ref[...], LAST) + dotg(y_ref[...], v_ref[...], LAST) + base_ref[0].astype(F32)
    if len(rest) == 2:
        total = total + rest[0][...].astype(F32)
    rest[-1][...] = total.astype(rest[-1].dtype)


def weight_kernel(scaled, count, grown, _, x_ref, *rest):
    x = x_ref[...]
    if scaled:
        x = (x.astype(F32) * rest[0][...]).astype(BF)
        rest = rest[1:]
    outs = rest[count + grown :]
    for y_ref, out_ref in zip(rest[:count], outs):
        total = dotg(x, y_ref[...], FIRST)
        if len(outs) > count and y_ref is rest[count - 1]:
            half = N // 2
            out_ref[...] = jnp.concatenate([total[:, half:N], total[:, N + half : 2 * N]], 1).astype(BF)
            outs[-2][...] = jnp.concatenate([total[:, :half], total[:, N : N + half]], 1).astype(BF)
            outs[-1][...] = total[:, 2 * N :].astype(BF)
        else:
            out_ref[...] = total.astype(BF)


def conv_kernel(
    raw_ref, side_ref, info_ref, halo_ref, taps_ref, head_ref, tri_ref, spread_ref,
    act_ref, pact_ref, dt_ref, cs_ref, state_ref, low_ref, rows_ref, buf, total_ref,
):
    c = pl.program_id(0)
    inner = raw_ref.shape[1]
    groups = inner // LANES
    pair = pact_ref.shape[1]
    pair_groups = pair // LANES

    @pl.when(c == 0)
    def _():
        buf[0:8, :] = halo_ref[HALO - 8 :, : inner + pair].astype(BF).astype(F32)
        state_ref[...] = jnp.zeros_like(state_ref)
        total_ref[...] = jnp.zeros_like(total_ref)

    info = columns(info_ref[0])
    masks = [None] + [jnp.broadcast_to(info[:, 2 + k : 3 + k], (L, LANES)) for k in (1, 2, 3)]
    dt = jax.nn.softplus(side_ref[:, pair:] + head_ref[0:1, :])
    dt_ref[...] = dt
    cs = exact_sum(tri_ref[...], dt * head_ref[1:2, :])
    cs_ref[...] = cs
    closing = cs[L - 1 :, :]
    total_ref[0:1, :] += closing
    total_ref[1:2, :] = jnp.where(c == 0, 1.0, total_ref[1:2, :]) * info[0:1, 9:10]
    tail = jnp.exp(closing - cs) * info[:, 2:3] * dt
    tail_wide = expand(tail, spread_ref[...])
    keep = jnp.exp(closing) * info[0:1, 9:10]
    keep_wide = expand(jnp.broadcast_to(keep, (8, LANES)), spread_ref[...])[0:1, :]
    acts = []
    for j in range(groups + pair_groups):
        cols = slice(j * LANES, (j + 1) * LANES)
        if j < groups:
            raw = raw_ref[:, cols].astype(F32)
        else:
            raw = side_ref[:, (j - groups) * LANES : (j - groups + 1) * LANES].astype(BF).astype(F32)
        buf[8 : 8 + L, cols] = raw
        pre = taps_ref[4:5, cols] + taps_ref[0:1, cols] * raw
        for k in (1, 2, 3):
            pre = pre + taps_ref[k : k + 1, cols] * buf[8 - k : 8 - k + L, cols] * masks[k]
        act = (pre * sigmoid(pre)).astype(BF)
        buf[0:8, cols] = raw[L - 8 :, :]
        if j < groups:
            act_ref[:, cols] = act
        else:
            pact_ref[:, (j - groups) * LANES : (j - groups + 1) * LANES] = act
    key = pact_ref[:, :N]
    for j in range(groups):
        cols = slice(j * LANES, (j + 1) * LANES)
        weighted = (act_ref[:, cols].astype(F32) * tail_wide[:, cols]).astype(BF)
        state_ref[:, cols] = keep_wide[:, cols] * state_ref[:, cols] + dotg(key, weighted, FIRST)

    @pl.when(c == pl.num_programs(0) - 1)
    def _():
        through = jnp.exp(total_ref[0:1, :]) * total_ref[1:2, :]
        rows_ref[...] = expand(jnp.broadcast_to(through, (8, LANES)), spread_ref[...])
        low_ref[0:N, :] = state_ref[...].astype(BF)
        low_ref[N:, :] = factor_rows(rows_ref[0:1, :])


def out_kernel(
    act_ref, pact_ref, dt_ref, cs_ref, info_ref, gate_ref, dgn_ref, state_in_ref,
    gains_ref, spread_ref,
    mixed_ref, gg_ref, sums_ref, entry_ref, state,
):
    c = pl.program_id(0)
    inner = act_ref.shape[1]
    groups = inner // LANES

    @pl.when(c == 0)
    def _():
        state[...] = state_in_ref[...]

    info = columns(info_ref[0])
    mask = mask_of(info, info_ref[0, 0:1, :])
    key = pact_ref[:, :N]
    query = pact_ref[:, N:]
    scores = dotg(query, key, LAST)
    dt = dt_ref[...]
    cs = cs_ref[...]
    cs_rows = cs.T
    closing = cs[L - 1 :, :]
    spread = spread_ref[...]
    dt_wide = expand(dt, spread)
    open_wide = expand(jnp.exp(cs) * info[:, 1:2], spread)
    tail_wide = expand(jnp.exp(closing - cs) * info[:, 2:3], spread)
    keep = jnp.exp(closing) * info[0:1, 9:10]
    keep_wide = expand(jnp.broadcast_to(keep, (8, LANES)), spread)[0:1, :]
    left = lane_is_left((L, LANES))
    square = jnp.zeros((L, LANES), F32)
    cross = jnp.zeros((L, LANES), F32)
    for j in range(groups):
        cols = slice(j * LANES, (j + 1) * LANES)
        x = act_ref[:, cols].astype(F32)
        xd = x * dt_wide[:, cols]
        xd_low = xd.astype(BF)
        weights = []
        for h in (2 * j, 2 * j + 1):
            factor = jnp.exp(cs[:, h : h + 1] - cs_rows[h : h + 1, :] + mask)
            weights.append((scores * factor).astype(BF))
        entry = state[:, cols].astype(BF)
        entry_ref[0, :, cols] = entry
        y = dot(jnp.concatenate(weights, 1), stacked_pair(xd_low, left))
        y = y + open_wide[:, cols] * dot(query, entry)
        mixed = y + gains_ref[0:1, cols] * x
        mixed_ref[:, cols] = mixed.astype(BF)
        gate = gate_ref[:, cols].astype(F32)
        gated = mixed * (gate * sigmoid(gate))
        gg = gated * gains_ref[1:2, cols]
        gg_ref[:, cols] = gg.astype(BF)
        square = square + gated * gated
        cross = cross + gg * dgn_ref[:, cols].astype(F32)
        weighted = (xd * tail_wide[:, cols]).astype(BF)
        state[:, cols] = keep_wide[:, cols] * state[:, cols] + dotg(key, weighted, FIRST)
    lane = lax.broadcasted_iota(jnp.int32, (L, LANES), 1)
    both = jnp.where(
        lane == 0,
        jnp.sum(square, axis=1, keepdims=True),
        jnp.sum(cross, axis=1, keepdims=True),
    )
    sums_ref[0] = both.T[0:2, :]


def gate_kernel(
    mixed_ref, gate_ref, dgn_ref, act_ref, pact_ref, cs_ref, info_ref, near_ref, far_ref, gains_ref, spread_ref,
    dmix_ref, dgate_ref, stat_ref, dstate_ref, low_ref, dgain_ref, dskip_ref,
):
    c = pl.program_id(0)
    inner = act_ref.shape[1]
    groups = inner // LANES

    @pl.when(c == 0)
    def _():
        dstate_ref[...] = jnp.zeros_like(dstate_ref)
        dgain_ref[...] = jnp.zeros_like(dgain_ref)
        dskip_ref[...] = jnp.zeros_like(dskip_ref)

    info = columns(info_ref[0])
    both = near_ref[0] + far_ref[0]
    scale_row = lax.rsqrt(both[0:1, :] / DI + EPS)
    coef_row = scale_row * scale_row * scale_row * both[1:2, :] / DI
    stats = columns(jnp.concatenate([scale_row, coef_row, jnp.zeros((6, L), F32)], 0))
    scale = jnp.broadcast_to(stats[:, 0:1], (L, LANES))
    coef = jnp.broadcast_to(stats[:, 1:2], (L, LANES))
    cs = cs_ref[...]
    spread = spread_ref[...]
    open_wide = expand(jnp.exp(cs) * info[:, 1:2], spread)
    keep = jnp.exp(cs[L - 1 :, :]) * info[0:1, 9:10]
    keep_wide = expand(jnp.broadcast_to(keep, (8, LANES)), spread)[0:1, :]
    query = pact_ref[:, N:]
    row = jnp.zeros((L, LANES), F32)
    for j in range(groups):
        cols = slice(j * LANES, (j + 1) * LANES)
        mixed = mixed_ref[:, cols].astype(F32)
        gate = gate_ref[:, cols].astype(F32)
        dgn = dgn_ref[:, cols].astype(F32)
        x = act_ref[:, cols].astype(F32)
        sig = sigmoid(gate)
        act = gate * sig
        gated = mixed * act
        scaled = dgn * scale
        dgain_ref[:, cols] += fold8(scaled * gated)
        dgated = scaled * gains_ref[1:2, cols] - gated * coef
        dmix = dgated * act
        dgate = dgated * mixed * (sig + act * (1.0 - sig))
        dskip_ref[:, cols] += fold8(dmix * x)
        row = row + dgate * gate
        dgate_ref[:, cols] = dgate.astype(BF)
        low = dmix.astype(BF)
        dmix_ref[:, cols] = low
        opened = (low.astype(F32) * open_wide[:, cols]).astype(BF)
        dstate_ref[:, cols] = keep_wide[:, cols] * dstate_ref[:, cols] + dotg(query, opened, FIRST)
    stat_ref[0] = jnp.broadcast_to(jnp.sum(row, axis=1, keepdims=True), (L, LANES)).T[0:8, :]

    @pl.when(c == pl.num_programs(0) - 1)
    def _():
        low_ref[...] = dstate_ref[...].astype(BF)


def back_kernel(
    grown, final,
    act_ref, pact_ref, dt_ref, cs_ref, info_ref, dmix_ref, entry_ref,
    raw_ref, side_ref, raw_prev_ref, side_prev_ref, halo_ref,
    taps_ref, head_ref, gains_ref, tri_ref, spread_ref, gather_ref,
    dstate_in_ref, carried_in_ref, dtaps_in_ref, dhead_in_ref, dgain_ref, dskip_ref, stat_in_ref, *rest,
):
    rest = list(rest[grown:])
    d_ref, dside_ref, stat_ref, dstate, carried_ref, dtaps_ref, dhead_ref = rest[:7]
    small_ref, dhalo_ref = rest[7:9] if final else (None, None)
    buf, dbuf = rest[-2:]
    c = pl.program_id(0)
    last = pl.num_programs(0) - 1
    inner = act_ref.shape[1]
    groups = inner // LANES
    pair = 2 * N
    wide = inner + pair

    @pl.when(c == 0)
    def _():
        dstate[...] = dstate_in_ref[...]
        dbuf[L:, :] = carried_in_ref[...]
        dtaps_ref[...] = dtaps_in_ref[...]
        dhead_ref[...] = dhead_in_ref[...]

    def before():
        buf[0:8, :inner] = raw_prev_ref[HALO - 8 :, :].astype(F32)
        buf[0:8, inner:] = side_prev_ref[HALO - 8 :, :pair].astype(BF).astype(F32)

    if final:

        @pl.when(c == last)
        def _():
            buf[0:8, :] = halo_ref[HALO - 8 :, :wide].astype(BF).astype(F32)

        pl.when(c < last)(before)
    else:
        before()

    info = columns(info_ref[0])
    masks = [None] + [jnp.broadcast_to(info[:, 2 + k : 3 + k], (L, LANES)) for k in (1, 2, 3)]
    afters = [None] + [jnp.broadcast_to(info[:, 5 + k : 6 + k], (L, LANES)) for k in (1, 2, 3)]
    mask = mask_of(info, info_ref[0, 0:1, :])
    key = pact_ref[:, :N]
    query = pact_ref[:, N:]
    scores = dotg(query, key, LAST)
    dt = dt_ref[...]
    cs = cs_ref[...]
    cs_rows = cs.T
    closing = cs[L - 1 :, :]
    spread = spread_ref[...]
    dt_wide = expand(dt, spread)
    open_wide = expand(jnp.exp(cs) * info[:, 1:2], spread)
    tail_wide = expand(jnp.exp(closing - cs) * info[:, 2:3], spread)
    keep = jnp.exp(closing) * info[0:1, 9:10]
    keep_wide = expand(jnp.broadcast_to(keep, (8, LANES)), spread)[0:1, :]
    left = lane_is_left((L, LANES))

    def conv_back(j, raw, dact):
        cols = slice(j * LANES, (j + 1) * LANES)
        buf[8 : 8 + L, cols] = raw
        pre = taps_ref[4:5, cols] + taps_ref[0:1, cols] * raw
        moved = [raw]
        for k in (1, 2, 3):
            moved.append(buf[8 - k : 8 - k + L, cols] * masks[k])
            pre = pre + taps_ref[k : k + 1, cols] * moved[k]
        sig = sigmoid(pre)
        dpre = dact * (sig * (1.0 + pre * (1.0 - sig)))
        for k in range(4):
            dtaps_ref[8 * k : 8 * k + 8, cols] += fold8(dpre * moved[k])
        dtaps_ref[32:40, cols] += fold8(dpre)
        dbuf[0:L, cols] = dpre
        draw = taps_ref[0:1, cols] * dpre
        for k in (1, 2, 3):
            draw = draw + taps_ref[k : k + 1, cols] * dbuf[k : k + L, cols] * afters[k]
        dbuf[L : L + 8, cols] = dpre[0:8, :]
        if j < groups:
            d_ref[:, cols] = draw.astype(BF)
        else:
            dside_ref[:, (j - groups) * LANES : (j - groups + 1) * LANES] = draw.astype(BF)
        return draw * raw

    row = jnp.zeros((L, LANES), F32)
    dscores = jnp.zeros((L, L), F32)
    dkey = jnp.zeros((L, N), F32)
    dquery = jnp.zeros((L, N), F32)
    dcs = jnp.zeros((L, LANES), F32)
    ddt = jnp.zeros((L, LANES), F32)
    dclose = jnp.zeros((8, LANES), F32)
    for j in range(groups):
        cols = slice(j * LANES, (j + 1) * LANES)
        x = act_ref[:, cols].astype(F32)
        xd = (x * dt_wide[:, cols]).astype(BF)
        dm = dmix_ref[:, cols]
        dmf = dm.astype(F32)
        xdf = xd.astype(F32)
        factors = []
        weights = []
        for h in (2 * j, 2 * j + 1):
            factor = jnp.exp(cs[:, h : h + 1] - cs_rows[h : h + 1, :] + mask)
            factors.append(factor)
            weights.append((scores * factor).astype(BF))
        pair_x = stacked_pair(xd, left)
        pair_d = stacked_pair(dm, left)
        dweights = dotg(dm, pair_x, LAST)
        dscores = dscores + dweights[:, :L] * factors[0] + dweights[:, L:] * factors[1]
        y = dot(jnp.concatenate(weights, 1), pair_x)
        dxd = dotg(jnp.concatenate(weights, 0), pair_d, FIRST)
        entry = entry_ref[0, :, cols]
        dst = dstate[:, cols]
        dst_low = dst.astype(BF)
        opened = (dmf * open_wide[:, cols]).astype(BF)
        tailed = (xdf * tail_wide[:, cols]).astype(BF)
        from_state = dot(query, entry)
        to_state = dot(key, dst_low)
        out_part = tailed.astype(F32) * to_state
        diff = dmf * y + opened.astype(F32) * from_state - xdf * dxd - out_part
        dxd = dxd + to_state * tail_wide[:, cols]
        hi, lo = split2(diff)
        gather = gather_ref[cols, :]
        dcs = dcs + dot(hi, gather) + dot(lo, gather)
        ddt = ddt + dot((dxd * x).astype(BF), gather)
        close = fold8(out_part) + keep_wide[:, cols] * fold8(dst * entry.astype(F32))
        hi, lo = split2(close)
        dclose = dclose + dot(hi, gather) + dot(lo, gather)
        dquery = dquery + dotg(opened, entry, LAST)
        dkey = dkey + dotg(tailed, dst_low, LAST)
        dstate[:, cols] = keep_wide[:, cols] * dst + dotg(query, opened, FIRST)
        dx = dxd * dt_wide[:, cols] + gains_ref[0:1, cols] * dmf
        row = row + conv_back(j, raw_ref[:, cols].astype(F32), dx)
    dscores = dscores.astype(BF)
    dquery = dquery + dot(dscores, key)
    dkey = dkey + dotg(dscores, query, FIRST)
    row = row + conv_back(groups, side_ref[:, :N].astype(BF).astype(F32), dkey)
    row = row + conv_back(groups + 1, side_ref[:, N:pair].astype(BF).astype(F32), dquery)
    later = dcs
    hi, mid, lo = split3(later)
    tri = tri_ref[...]
    da = dotg(tri, hi, FIRST) + dotg(tri, mid, FIRST) + dotg(tri, lo, FIRST)
    da = da + jnp.sum(dclose, axis=0, keepdims=True)
    ddt = ddt + head_ref[1:2, :] * da
    step = side_ref[:, pair:]
    dstep = ddt * sigmoid(step + head_ref[0:1, :])
    dhead_ref[0:8, :] += fold8(dstep)
    dhead_ref[8:16, :] += fold8(dt * da)
    dside_ref[:, pair:] = dstep.astype(BF)
    row = row + dstep * step
    stat_ref[0] = stat_in_ref[0] + jnp.broadcast_to(jnp.sum(row, axis=1, keepdims=True), (L, LANES)).T[0:8, :]

    @pl.when(c == last)
    def _():
        carried_ref[...] = dbuf[L:, :]

    if final:

        @pl.when(c == last)
        def _():
            for k in range(5):
                small_ref[k : k + 1, :] = jnp.sum(dtaps_ref[8 * k : 8 * k + 8, :], axis=0, keepdims=True)
            small_ref[5:8, :] = jnp.zeros((3, wide), F32)
            small_ref[5:6, :inner] = jnp.sum(dgain_ref[...], axis=0, keepdims=True)
            skip = jnp.broadcast_to(jnp.sum(dskip_ref[...], axis=0, keepdims=True), (8, inner))
            hi, lo = split2(skip)
            skip = dot(hi, gather_ref[...]) + dot(lo, gather_ref[...])
            small_ref[6:7, 0:LANES] = skip[0:1, :]
            small_ref[6:7, LANES : 2 * LANES] = jnp.sum(dhead_ref[0:8, :], axis=0, keepdims=True)
            small_ref[6:7, 2 * LANES : 3 * LANES] = (
                jnp.sum(dhead_ref[8:16, :], axis=0, keepdims=True) * head_ref[1:2, :]
            )
            dhalo_ref[...] = jnp.zeros((8, wide), F32)
            for j in range(groups + 2):
                cols = slice(j * LANES, (j + 1) * LANES)
                for k in (1, 2, 3):
                    reach = dbuf[L : L + 8, cols] * masks[k][0:8, :] * taps_ref[k : k + 1, cols]
                    dhalo_ref[8 - k :, cols] += reach[0:k, :]


def flip(block, axis, bit):
    count = lax.axis_size(axis)
    route = [(i, i ^ bit) for i in range(count)]
    return jax.tree.map(lambda a: lax.ppermute(a, axis, route), block)


def sum_over(block, axis):
    bit = 1
    while bit < lax.axis_size(axis):
        block = block + flip(block, axis, bit)
        bit *= 2
    return block


def shift_over(block, axis, distance):
    devices = range(lax.axis_size(axis))
    route = [(i, i + distance) for i in devices if i + distance in devices]
    return lax.ppermute(block, axis, route)


def body(
    tokens, boundary, norm_gain, w_gate, w_inner, w_pair, w_step, conv_inner, conv_pair,
    bias_inner, bias_pair, step_bias, decay_log, skip_gain, gate_gain, w_output, cotangent,
):
    rows, width = tokens.shape
    inner = w_gate.shape[1]
    heads = w_step.shape[1]
    head_count = lax.axis_size("head")
    place = lax.axis_index("head")
    quarter = width // head_count
    pair_cols = w_pair.shape[1]
    pair = pair_cols * head_count
    wide = inner + pair
    side = pair + LANES
    steps = rows // L
    chain = Chain()
    run = chain.run

    def behind(c):
        return steps - 1 - c

    def row_of(v):
        return v.reshape(1, -1)

    head_of = np.arange(inner)[None, :] // HP == np.arange(LANES)[:, None]
    spread2 = jnp.asarray(np.concatenate([head_of, head_of], 0), BF)
    gather = jnp.asarray(head_of.T, BF)
    lower = jnp.asarray(np.tril(np.ones((L, L))), BF)
    upper = jnp.asarray(np.triu(np.ones((L, L))), BF)

    def split_low(v):
        hi, mid, lo = split3(v)
        return [hi, mid, lo]

    swap = (place & 2) != 0

    def own_columns(block):
        near = jnp.where(swap, block[:, N:], block[:, :N])
        far = jnp.where(swap, block[:, :N], block[:, N:])
        kept = jnp.concatenate([near[:, :pair_cols], far[:, :pair_cols]], 1)
        sent = jnp.concatenate([near[:, pair_cols:], far[:, pair_cols:]], 1)
        total = kept.astype(F32) + flip(sent, "head", 1).astype(F32)
        return total[:, :pair_cols] + flip(total[:, pair_cols:].astype(block.dtype), "head", 2).astype(F32)

    pair_small = jnp.concatenate([conv_pair, row_of(bias_pair), jnp.zeros((3, pair_cols), F32)], 0)
    pair_own = jnp.concatenate([w_pair, *split_low(pair_small), jnp.zeros((8, pair_cols), BF)], 0)
    pair_pieces = [pair_own] + [flip(pair_own, "head", d) for d in (1, 2, 3)]
    gain_row = row_of(norm_gain)

    info_spec = slab_spec(16, L, ahead)
    info_back = slab_spec(16, L, behind)
    one_step = (1,)
    info, sent, keep_tail, head_rows, gains = run(
        prep_kernel,
        one_step,
        [
            whole(boundary.reshape(steps, L)), whole(upper),
            (tokens, pl.BlockSpec((HALO, width), lambda c: (rows // HALO - 1, 0))),
            whole(row_of(step_bias)), whole(row_of(decay_log)), whole(row_of(skip_gain)), whole(row_of(gate_gain)),
            whole(spread2),
        ],
        [
            (whole_spec((steps, 16, L)), (steps, 16, L), F32), (whole_spec((HALO, width)), (HALO, width), BF),
            (whole_spec((HALO, 1)), (HALO, 1), F32), (whole_spec((8, LANES)), (8, LANES), F32),
            (whole_spec((8, inner)), (8, inner), F32),
        ],
        us=2,
    )
    token_halo = shift_over(sent, "seq", 1)

    big = 512
    blocks = rows // big

    def rows_spec(cols, start=0, size=big):
        return pl.BlockSpec((size, cols), lambda i, *_: (i + start, 0))

    def fixed(shape):
        return pl.BlockSpec(shape, lambda i, *_: (0,) * len(shape))

    normed, scale_in, inner_raw = run(
        proj_kernel,
        (blocks,),
        [(tokens, rows_spec(width)), whole(gain_row), whole(w_inner)],
        [
            (rows_spec(width), (rows, width), BF),
            (rows_spec(1), (rows, 1), F32),
            (rows_spec(inner), (rows, inner), BF),
        ],
        us=12,
    )
    halo_shape = (HALO, inner + side)
    side_raw, halo, w_side, taps = run(
        side_kernel,
        (blocks,),
        [(normed, rows_spec(width))]
        + [whole(p) for p in pair_pieces]
        + [whole(w_step), whole(token_halo), whole(gain_row), whole(w_inner), whole(conv_inner), whole(row_of(bias_inner))],
        [
            (rows_spec(side), (rows, side), F32),
            (fixed(halo_shape), halo_shape, F32),
            (fixed((width, side)), (width, side), BF),
            (fixed((8, wide)), (8, wide), F32),
        ],
        ids=swap.astype(jnp.int32).reshape(1),
        us=10,
    )

    low_rows = N + HALO
    act, pact, dt, cs, closing, closing_low, through = run(
        conv_kernel,
        (steps,),
        [
            (inner_raw, chunk_spec(inner, ahead)), (side_raw, chunk_spec(side, ahead)), (info, info_spec),
            whole(halo), whole(taps), whole(head_rows), whole(lower), whole(spread2),
        ],
        [
            (chunk_spec(inner, ahead), (rows, inner), BF), (chunk_spec(pair, ahead), (rows, pair), BF),
            (chunk_spec(LANES, ahead), (rows, LANES), F32), (chunk_spec(LANES, ahead), (rows, LANES), F32),
            (whole_spec((N, inner)), (N, inner), F32), (whole_spec((low_rows, inner)), (low_rows, inner), BF),
            (whole_spec((8, inner)), (8, inner), F32),
        ],
        scratch=[pltpu.VMEM((8 + L, wide), F32), pltpu.VMEM((8, LANES), F32)],
        us=17,
    )

    seq_count = lax.axis_size("seq")
    seq_place = lax.axis_index("seq")

    def exchange(state, low, rows0, known, reverse, between):
        before, row, factors = None, rows0, []
        bit = 1
        while bit < seq_count:
            arrived = flip(low, "seq", bit)
            if between:
                between.pop(0)()
            follows = (seq_place & bit) != 0
            if reverse:
                follows = jnp.logical_not(follows)
            final = bit * 2 >= seq_count
            has = known is not None
            ins = [whole(arrived), whole(state), whole(row)]
            if before is not None:
                ins.append(whole(before))
            if has:
                ins.append(whole(known[len(factors)]))
            big_out = (fixed((N, inner)), (N, inner), F32)
            outs = [big_out, (fixed((8, inner)), (8, inner), F32)]
            if not final:
                height = N if has else low_rows
                outs += [big_out, (fixed((height, inner)), (height, inner), BF)]
            got = run(
                functools.partial(combine_kernel, reverse, before is None, has, final),
                one_step,
                ins,
                outs,
                ids=follows.astype(jnp.int32).reshape(1),
                us=2,
            )
            before, row = got[0], got[1]
            factors.append(row)
            if not final:
                state, low = got[2], got[3]
            bit *= 2
        for work in between:
            work()
        return before, factors

    def product(kernel, x, w, start, size, into):
        out = [] if into is None else [(into, ANY)]
        return run(
            kernel,
            (size,),
            [(x, rows_spec(x.shape[1], start)), whole(w)] + out,
            [(rows_spec(inner, start), (rows, inner), BF)],
            aliases={2: 0} if out else None,
            us=2.9 * size,
        )[0]

    third = max(blocks // 3, 1)
    held = {}

    def gate_one():
        held["gate"] = product(nn_kernel, normed, w_gate, 0, blocks - third, None)

    def gate_two():
        held["gate"] = product(nn_kernel, normed, w_gate, blocks - third, third, held["gate"])
        held["dgn"] = product(nt_kernel, cotangent, w_output, 0, third, None)

    def gate_three():
        held["dgn"] = product(nt_kernel, cotangent, w_output, third, blocks - third, held["dgn"])

    state_in, factors = exchange(closing, closing_low, through, None, False, [gate_one, gate_two, gate_three])
    gate_pre, dgn = held["gate"], held["dgn"]

    mixed, gg, sums, entries = run(
        out_kernel,
        (steps,),
        [
            (act, chunk_spec(inner, ahead)), (pact, chunk_spec(pair, ahead)), (dt, chunk_spec(LANES, ahead)),
            (cs, chunk_spec(LANES, ahead)), (info, info_spec),
            (gate_pre, chunk_spec(inner, ahead)), (dgn, chunk_spec(inner, ahead)),
            whole(state_in), whole(gains), whole(spread2),
        ],
        [
            (chunk_spec(inner, ahead), (rows, inner), BF), (chunk_spec(inner, ahead), (rows, inner), BF),
            (slab_spec(2, L, ahead), (steps, 2, L), F32), (slab_spec(N, inner, ahead), (steps, N, inner), BF),
        ],
        scratch=[pltpu.VMEM((N, inner), F32)],
        us=18,
    )

    order = [place ^ 3, place ^ 1, place ^ 2, place]

    def quarter_spec():
        return pl.BlockSpec((big, quarter), lambda i, ids: (i, 0))

    def out_quarter(which, got, dtype, after=()):
        ins = [
            (gg, pl.BlockSpec((big, inner), lambda i, ids: (i, 0))),
            (w_output, pl.BlockSpec((inner, quarter), lambda i, ids: (0, ids[0]))),
        ]
        if got is not None:
            ins.append((got, quarter_spec()))
        return run(
            cols_kernel if got is None else cols_add_kernel,
            (blocks,),
            ins,
            [(quarter_spec(), (rows, quarter), dtype)],
            after=after,
            ids=order[which].reshape(1),
            us=5,
        )[0]

    sums_core = flip(sums, "head", 1)
    out_a = out_quarter(0, None, BF)
    sums = sums + sums_core
    got_a = flip(out_a, "head", 1)
    sums_x = flip(sums, "head", 2)
    out_b = out_quarter(1, None, BF, [sums_core])
    got_b = flip(out_b, "head", 1)
    scale_out = lax.rsqrt((sums + sums_x)[:, 0, :] / DI + EPS).reshape(rows, 1)

    share = width // seq_count
    manual = seq_count == 8
    half = seq_count // 2
    seq_core = seq_place % 2
    if manual:
        row_ids = [jnp.arange(half) * 2 + (1 - seq_core), jnp.arange(half) * 2 + seq_core]
    else:
        share = 256
        row_ids = [jnp.arange(width // share)]

    def weight_rows(which, x, ys, scale=None, into=()):
        ids = row_ids[which].astype(jnp.int32)
        count = ids.shape[0]
        ins = [(x, pl.BlockSpec((rows, share), lambda i, ids: (0, ids[i])))]
        if scale is not None:
            ins.append(whole(scale))
        outs = []
        lead = count * which
        for y, cols, at in ys:
            ins.append((y, pl.BlockSpec((rows, cols), lambda i, ids, at=at: (0, at))))
            if cols == side:
                spec = pl.BlockSpec((share, LANES), lambda i, ids: (i + lead, 0))
                outs += [(spec, (width, LANES), BF)] * 3
            else:
                outs.append((pl.BlockSpec((share, cols), lambda i, ids: (i, 0)), (count * share, cols), BF))
        aliases = {len(ins) + k: len(outs) - 3 + k for k in range(len(into))}
        return run(
            functools.partial(weight_kernel, scale is not None, len(ys), len(into)),
            (count,),
            ins + [(a, ANY) for a in into],
            outs,
            ids=ids,
            aliases=aliases,
            us=8,
        )

    class Spread:
        def __init__(self, kept, got):
            cols = kept.shape[1]
            part = share // 2
            z = seq_place // 2
            ids = jnp.stack([z ^ d for d in range(4)]).astype(jnp.int32)
            ins = []
            for d in range(4):
                spec = pl.BlockSpec((part, cols), lambda i, ids, d=d: (ids[d] * 2 + i, 0))
                ins += [(kept, spec), (got, spec)]
            out = pl.BlockSpec((part, cols), lambda i, ids: (i, 0))
            sums = run(
                meet_kernel,
                (2,),
                ins,
                [(out, (share, cols), BF if d else F32) for d in range(4)],
                ids=ids,
                us=4,
            )
            self.parts = [sums[0]] + [flip(sums[d], "seq", 2 * d) for d in (1, 2, 3)]
            self.shape = (share, cols)

        def settle(self, turned=False, into=None, place=0, total=1):
            rows_, cols = self.shape
            count = 1 if turned else 2
            step = (rows_ // count, cols)
            spec = pl.BlockSpec(step, lambda i: (i, 0))
            if turned:
                out = (pl.BlockSpec((cols, rows_), lambda i: (0, 0)), (cols, rows_), F32)
            else:
                out = (pl.BlockSpec(step, lambda i: (i, place)), (rows_, cols * total), F32)
            return run(
                settle_kernel,
                (count,),
                [(p, spec) for p in self.parts] + ([] if into is None else [(into, ANY)]),
                [out],
                aliases=None if into is None else {4: 0},
                us=2,
            )[0]

    (out_first,) = weight_rows(0, cotangent, [(gg, inner, 0)], scale_out)
    if manual:
        out_got = flip(out_first, "seq", 1)
    away = out_quarter(2, got_a, BF)
    away_got = flip(away, "head", 2)
    mine = out_quarter(3, got_b, F32)
    if manual:
        (out_second,) = weight_rows(1, cotangent, [(gg, inner, 0)], scale_out)

    dmix, dgate, stat, dstate_local, dstate_low, dgain, dskip = run(
        gate_kernel,
        (steps,),
        [
            (mixed, chunk_spec(inner, behind)), (gate_pre, chunk_spec(inner, behind)), (dgn, chunk_spec(inner, behind)),
            (act, chunk_spec(inner, behind)), (pact, chunk_spec(pair, behind)), (cs, chunk_spec(LANES, behind)),
            (info, info_back), (sums, slab_spec(2, L, behind)), (sums_x, slab_spec(2, L, behind)),
            whole(gains), whole(spread2),
        ],
        [
            (chunk_spec(inner, behind), (rows, inner), BF), (chunk_spec(inner, behind), (rows, inner), BF),
            (slab_spec(8, L, behind), (steps, 8, L), F32), (whole_spec((N, inner)), (N, inner), F32),
            (whole_spec((N, inner)), (N, inner), BF),
            (whole_spec((8, inner)), (8, inner), F32), (whole_spec((8, inner)), (8, inner), F32),
        ],
        us=17,
    )

    order_ids = jnp.stack(order).astype(jnp.int32)

    def gate_first():
        held["first"] = weight_rows(0, normed, [(dgate, inner, 0)])[0]

    def gate_second():
        if manual:
            held["got"] = flip(held["first"], "seq", 1)
            held["second"] = weight_rows(1, normed, [(dgate, inner, 0)])[0]

    def gate_third():
        held["dn"] = run(
            gate_back_kernel,
            (4, blocks),
            [
                (dgate, pl.BlockSpec((big, inner), lambda n, i, ids: (i, 0))),
                (w_gate, pl.BlockSpec((quarter, inner), lambda n, i, ids: (ids[n], 0))),
            ],
            [(pl.BlockSpec((1, big, quarter), lambda n, i, ids: (n, i, 0)), (4, rows, quarter), BF)],
            ids=order_ids,
            us=17,
        )[0]

    dstate, _ = exchange(
        dstate_local, dstate_low, through, factors, True, [gate_first, gate_second, gate_third]
    )
    dn_gate = held["dn"]

    parts = 1
    each = steps // parts
    carried = jnp.zeros((8, wide), F32)
    dtaps = jnp.zeros((40, wide), F32)
    dhead = jnp.zeros((16, LANES), F32)
    d_inner = d_side = small = dhalo = None
    if manual:
        out_sum = Spread(out_second, out_got)
        gate_sum = Spread(held["second"], held["got"])
    for part in range(parts):
        first = steps - 1 - part * each

        def at(c, first=first):
            return first - c

        def near_end(c, at=at):
            return jnp.maximum(at(c) * (L // HALO) - 1, 0)

        final = part == parts - 1
        grown = [] if d_inner is None else [(d_inner, ANY), (d_side, ANY)]
        state_specs = [
            (whole_spec((N, inner)), (N, inner), F32), (whole_spec((8, wide)), (8, wide), F32),
            (whole_spec((40, wide)), (40, wide), F32), (whole_spec((16, LANES)), (16, LANES), F32),
        ]
        if final:
            state_specs += [(whole_spec((8, wide)), (8, wide), F32)] * 2
        ins = [
            (act, chunk_spec(inner, at)), (pact, chunk_spec(pair, at)), (dt, chunk_spec(LANES, at)),
            (cs, chunk_spec(LANES, at)), (info, slab_spec(16, L, at)),
            (dmix, chunk_spec(inner, at)), (entries, slab_spec(N, inner, at)),
            (inner_raw, chunk_spec(inner, at)), (side_raw, chunk_spec(side, at)),
            (inner_raw, pl.BlockSpec((HALO, inner), lambda c, p=near_end: (p(c), 0))),
            (side_raw, pl.BlockSpec((HALO, side), lambda c, p=near_end: (p(c), 0))),
            whole(halo), whole(taps), whole(head_rows), whole(gains), whole(lower), whole(spread2), whole(gather),
            whole(dstate), whole(carried), whole(dtaps), whole(dhead), whole(dgain), whole(dskip),
            (stat, slab_spec(8, L, at)), *grown,
        ]
        aliases = {24: 2}
        if grown:
            aliases.update({25: 0, 26: 1})
        got = run(
            functools.partial(back_kernel, len(grown), final),
            (each,),
            ins,
            [
                (chunk_spec(inner, at), (rows, inner), BF), (chunk_spec(side, at), (rows, side), BF),
                (slab_spec(8, L, at), (steps, 8, L), F32), *state_specs,
            ],
            after=[away_got] if part == min(1, parts - 1) else [],
            scratch=[pltpu.VMEM((8 + L, wide), F32), pltpu.VMEM((L + 8, wide), F32)],
            aliases=aliases,
            us=64 / parts,
        )
        d_inner, d_side, stat, dstate, carried, dtaps, dhead = got[:7]
        if final:
            small, dhalo = got[7:]

    returned = shift_over(dhalo, "seq", -1)
    small_got = flip(small, "seq", 1)

    def last_rows(cols):
        return pl.BlockSpec((HALO, cols), lambda c: (rows // HALO - 1, 0))

    last_slab = slab_spec(8, L, lambda c: steps - 1)
    if manual:
        dw_out = out_sum.settle(True)
    d_inner, d_side, stat, small = run(
        fix_kernel,
        one_step,
        [
            (inner_raw, last_rows(inner)), (side_raw, last_rows(side)), whole(keep_tail), whole(returned),
            whole(small), whole(small_got),
            (d_inner, last_rows(inner)), (d_side, last_rows(side)), (stat, last_slab),
        ],
        [
            (last_rows(inner), (rows, inner), BF), (last_rows(side), (rows, side), BF), (last_slab, (steps, 8, L), F32),
            (whole_spec((8, wide)), (8, wide), F32),
        ],
        aliases={6: 0, 7: 1, 8: 2},
        us=2,
    )

    def add(pairs):
        return run(
            functools.partial(add_kernel, len(pairs)),
            one_step,
            [whole(a) for pair_ in pairs for a in pair_],
            [(pl.BlockSpec(a.shape, lambda i, n=a.ndim: (0,) * n), a.shape, a.dtype) for a, _ in pairs],
            us=1,
        )

    def normed_quarter(which, got, dtype):
        ins = [
            (d_inner, pl.BlockSpec((big, inner), lambda i, ids: (i, 0))),
            (w_inner, pl.BlockSpec((quarter, inner), lambda i, ids: (ids[0], 0))),
            (d_side, pl.BlockSpec((big, side), lambda i, ids: (i, 0))),
            (w_side, pl.BlockSpec((quarter, side), lambda i, ids: (ids[0], 0))),
            (dn_gate, pl.BlockSpec((1, big, quarter), lambda i, ids: (which, i, 0))),
        ]
        if got is not None:
            ins.append((got, quarter_spec()))
        return run(
            normed_back_kernel,
            (blocks,),
            ins,
            [(quarter_spec(), (rows, quarter), dtype)],
            ids=order[which].reshape(1),
            us=6.5,
        )[0]

    token_cols = lax.dynamic_slice_in_dim(tokens, place * quarter, quarter, 1).astype(F32)
    half_inner = inner // 2
    inner_parts = [(d_inner, half_inner, 0), (d_inner, half_inner, 1), (d_side, side, 0)]

    swap_id = swap.astype(jnp.int32).reshape(1)
    first_a, first_b, sent, kept, step = weight_rows(0, normed, inner_parts)
    stat = stat[:, 0, :]
    stat_got = flip(stat, "head", 1)
    small_got = flip(small, "seq", 2)
    if manual:
        got_first = [flip(block, "seq", 1) for block in (first_a, first_b)]
        second_a, second_b, sent, kept, step = weight_rows(1, normed, inner_parts, None, [sent, kept, step])
    side_got = flip(sent, "head", 1)
    dn_a = normed_quarter(0, None, BF)
    dn_got_a = flip(dn_a, "head", 1)
    tall = pl.BlockSpec((256, LANES), lambda i, *_: (i, 0))
    thin = pl.BlockSpec((256, pair_cols), lambda i, *_: (i, 0))
    side_mine, side_sent = run(
        share_kernel,
        (width // 256,),
        [(kept, tall), (side_got, tall)],
        [(thin, (width, pair_cols), F32), (thin, (width, pair_cols), BF)],
        ids=swap_id,
        us=3,
    )
    side_got = flip(side_sent, "head", 2)
    if manual:
        dw_gate = gate_sum.settle()
    stat, small = add([(stat, stat_got), (small, small_got)])
    stat_got = flip(stat, "head", 2)
    small_got = flip(small, "seq", 4)
    dn_b = normed_quarter(1, None, BF)
    dn_got_b = flip(dn_b, "head", 1)
    if manual:
        sum_a = Spread(second_a, got_first[0])
    rest = run(
        join_kernel,
        (width // 256,),
        [(side_mine, thin), (side_got, thin), (step, tall)],
        [(tall, (width, LANES), BF)],
        us=3,
    )[0]
    if manual:
        rest_got = flip(rest[: half * share], "seq", 1)
    dn_away = normed_quarter(2, dn_got_a, BF)
    dn_away_got = flip(dn_away, "head", 2)
    dn_mine = normed_quarter(3, dn_got_b, F32)
    stat, small = add([(stat, stat_got), (small, small_got)])
    bit = 8
    while bit < seq_count:
        small = small + flip(small, "seq", bit)
        bit *= 2
    if manual:
        sum_b = Spread(second_b, got_first[1])
        sum_rest = Spread(rest[half * share :], rest_got)
        dw_inner = sum_a.settle(total=2)
        dw_inner = sum_b.settle(into=dw_inner, place=1, total=2)
        dw_side = sum_rest.settle()
    else:
        dw_out, dw_gate, dw_inner, dw_side = [
            lax.psum_scatter(block, "seq", scatter_dimension=0, tiled=True).astype(F32)
            for block in (out_first, held["first"], jnp.concatenate([first_a, first_b], 1), rest)
        ]
        dw_out = jnp.transpose(dw_out)
    row_stat = stat.reshape(rows, 1)
    result = (token_cols + scale_out * (mine + away_got.astype(F32))).astype(BF)
    d_cols = dn_mine + dn_away_got.astype(F32)
    gain_cols = lax.dynamic_slice_in_dim(norm_gain, place * quarter, quarter, 0)
    cot_cols = lax.dynamic_slice_in_dim(cotangent, place * quarter, quarter, 1).astype(F32)
    grad_tokens = (
        cot_cols + scale_in * d_cols * gain_cols - token_cols * scale_in * scale_in * row_stat / width
    )
    d_norm_gain = jnp.sum(d_cols * token_cols * scale_in, axis=0)
    norm_sum = sum_over(d_norm_gain.reshape(-1, LANES), "seq").reshape(-1)
    pair_sum = own_columns(small[:, inner:])
    return (
        result,
        grad_tokens,
        norm_sum,
        dw_gate,
        dw_inner,
        dw_side[:, :pair_cols],
        dw_side[:, pair_cols : pair_cols + heads],
        small[:4, :inner],
        pair_sum[:4],
        small[4, :inner],
        pair_sum[4],
        small[6, LANES : LANES + heads],
        small[6, 2 * LANES : 2 * LANES + heads],
        small[6, :heads],
        small[5, :inner],
        dw_out,
    )


def solution(mesh):
    return jax.shard_map(
        body,
        mesh=mesh,
        in_specs=(
            P("seq", None),
            P("seq"),
            P(),
            P(None, "head"),
            P(None, "head"),
            P(None, "head"),
            P(None, "head"),
            P(None, "head"),
            P(None, "head"),
            P("head"),
            P("head"),
            P("head"),
            P("head"),
            P("head"),
            P("head"),
            P("head", None),
            P("seq", None),
        ),
        out_specs=(
            P("seq", "head"),
            P("seq", "head"),
            P("head"),
            P("seq", "head"),
            P("seq", "head"),
            P("seq", "head"),
            P("seq", "head"),
            P(None, "head"),
            P(None, "head"),
            P("head"),
            P("head"),
            P("head"),
            P("head"),
            P("head"),
            P("head"),
            P("head", "seq"),
        ),
        check_vma=False,
    )
```

```python
import functools

import jax
import jax.numpy as jnp
import numpy as np
from jax import lax
from jax.experimental import pallas as pl
from jax.experimental.pallas import tpu as pltpu
from jax.sharding import PartitionSpec as P

N = 128
HP = 64
DI = 4096
EPS = 1e-05
L = 128
LANES = 128
HALO = 16
F32 = jnp.float32
BF = jnp.bfloat16
VMEM_LIMIT = 64 * 1024 * 1024 - 65536
FIRST = (((0,), (0,)), ((), ()))
LAST = (((1,), (1,)), ((), ()))


def dot(a, b):
    return jnp.dot(a, b, preferred_element_type=F32)


def dotg(a, b, dims):
    return lax.dot_general(a, b, dims, preferred_element_type=F32)


def split2(v):
    hi = v.astype(BF)
    return hi, (v - hi.astype(F32)).astype(BF)


def split3(v):
    hi = v.astype(BF)
    rest = v - hi.astype(F32)
    mid = rest.astype(BF)
    return hi, mid, (rest - mid.astype(F32)).astype(BF)


def exact_sum(tri, v):
    hi, mid, lo = split3(v)
    return dot(tri, hi) + dot(tri, mid) + dot(tri, lo)


def expand(v, spread2):
    hi, lo = split2(v)
    return dot(jnp.concatenate([hi, lo], 1), spread2)


def fold8(v):
    return jnp.sum(v.reshape(v.shape[0] // 8, 8, v.shape[1]), axis=0)


def stacked_pair(v, left):
    zero = jnp.zeros_like(v)
    return jnp.concatenate([jnp.where(left, v, zero), jnp.where(left, zero, v)], 0)


def lane_is_left(shape):
    return lax.broadcasted_iota(jnp.int32, shape, 1) < HP


def columns(slab):
    pad = LANES - slab.shape[0]
    return jnp.concatenate([slab, jnp.zeros((pad, L), F32)], 0).T


def mask_of(info, seg_row):
    rows = lax.broadcasted_iota(jnp.int32, (L, L), 0)
    cols = lax.broadcasted_iota(jnp.int32, (L, L), 1)
    linked = (info[:, 0:1] == seg_row) & (rows >= cols)
    return jnp.where(linked, 0.0, -1e30).astype(F32)


def sigmoid(v):
    return 0.5 * jnp.tanh(0.5 * v) + 0.5


def chunk_spec(width, place):
    return pl.BlockSpec((L, width), lambda c: (place(c), 0))


def slab_spec(rows, width, place):
    return pl.BlockSpec((1, rows, width), lambda c: (place(c), 0, 0))


def whole_spec(shape):
    return pl.BlockSpec(shape, lambda c: (0,) * len(shape))


def ahead(c):
    return c


ANY = pl.BlockSpec(memory_space=pl.ANY)


class Chain:
    def __init__(self):
        self.last = None
        self.factor = 1.0

    def run(self, kernel, grid, ins, outs, after=(), scratch=(), ids=None, aliases=None, us=5.0):
        given = [array for array, _ in ins]
        after = [a for a in list(after) + [self.last] if a is not None and not any(a is g for g in given)]
        lead = 0 if ids is None else 1
        keep_in = lead + len(ins)

        def inner(*refs):
            kernel(*refs[:keep_in], *refs[keep_in + len(after) :])

        result = pl.pallas_call(
            inner,
            grid_spec=pltpu.PrefetchScalarGridSpec(
                num_scalar_prefetch=lead,
                grid=grid,
                in_specs=[spec for _, spec in ins] + [ANY] * len(after),
                out_specs=[spec for spec, _, _ in outs],
                scratch_shapes=list(scratch),
            ),
            out_shape=[jax.ShapeDtypeStruct(shape, dtype) for _, shape, dtype in outs],
            input_output_aliases={lead + i: o for i, o in (aliases or {}).items()},
            compiler_params=pltpu.CompilerParams(
                dimension_semantics=("arbitrary",) * len(grid), vmem_limit_bytes=VMEM_LIMIT
            ),
            cost_estimate=pl.CostEstimate(flops=int(us * self.factor * 1.15e9), bytes_accessed=10**4, transcendentals=0),
        )(*(() if ids is None else (ids,)), *given, *after)
        self.last = min(result, key=lambda r: r.size)
        return result


def whole(array):
    zeros = (0,) * array.ndim
    return array, pl.BlockSpec(array.shape, lambda *_: zeros)


def norm_rows(block, gain):
    t = block.astype(F32)
    scale = lax.rsqrt(jnp.mean(t * t, axis=-1, keepdims=True) + EPS)
    return scale, (t * scale * gain).astype(BF)


def proj_kernel(tokens_ref, gain_ref, w_ref, normed_ref, scale_ref, inner_ref):
    scale, normed = norm_rows(tokens_ref[...], gain_ref[...])
    scale_ref[...] = scale
    normed_ref[...] = normed
    inner_ref[...] = dot(normed, w_ref[...]).astype(BF)


def along(v, k):
    zero = jnp.zeros((1, v.shape[1]), v.dtype)
    if k > 0:
        other = jnp.concatenate([zero, v[:-1]], 0)
        return jnp.concatenate([other[:, L - k :], v[:, : L - k]], 1)
    other = jnp.concatenate([v[1:], zero], 0)
    return jnp.concatenate([v[:, -k:], other[:, :-k]], 1)


def prep_kernel(
    starts_ref, upper_ref, tokens_ref, step_bias_ref, decay_ref, skip_ref, gate_gain_ref, spread_ref,
    info_ref, sent_ref, keep_ref, head_ref, gains_ref,
):
    starts = starts_ref[...].astype(F32)
    seg = dot(starts.astype(BF), upper_ref[...])
    m1 = 1.0 - starts
    m2 = m1 * (1.0 - along(starts, 1))
    m3 = m2 * (1.0 - along(starts, 2))
    seg_last = jnp.broadcast_to(seg[:, L - 1 :], seg.shape)
    one = jnp.ones_like(seg)
    zero = jnp.zeros_like(seg)
    fields = [
        seg, jnp.where(seg == 0, one, zero), jnp.where(seg == seg_last, one, zero), m1, m2, m3,
        along(m1, -1), along(m2, -2), along(m3, -3), jnp.where(seg_last == 0, one, zero),
    ]
    for i in range(16):
        info_ref[:, i, :] = fields[i] if i < len(fields) else zero
    rows = lax.broadcasted_iota(jnp.int32, (HALO, L), 0)
    lanes = lax.broadcasted_iota(jnp.int32, (HALO, L), 1)
    last = jnp.broadcast_to(starts[starts.shape[0] - 1 :, :], (HALO, L))
    later = jnp.sum(jnp.where(lanes > rows + L - HALO, last, 0.0), axis=1, keepdims=True)
    place = lax.broadcasted_iota(jnp.int32, (HALO, 1), 0)
    keep = jnp.where((later == 0) & (place >= HALO - 3), 1.0, 0.0)
    keep_ref[...] = keep
    sent_ref[...] = (tokens_ref[...].astype(F32) * keep).astype(BF)
    heads = step_bias_ref.shape[1]
    head_ref[...] = jnp.zeros_like(head_ref)
    head_ref[0:1, 0:heads] = step_bias_ref[...]
    head_ref[1:2, 0:heads] = -jnp.exp(decay_ref[...])
    head_ref[2:3, 0:heads] = skip_ref[...]
    gains_ref[...] = expand(jnp.broadcast_to(head_ref[2:3, :], (8, LANES)), spread_ref[...])
    gains_ref[1:2, :] = gate_gain_ref[...]


def side_kernel(
    swap_ref, normed_ref, own_ref, one_ref, two_ref, three_ref, w_step_ref, halo_ref, gain_ref, w_ref,
    conv_ref, bias_ref,
    side_ref, halo_out_ref, w_side_ref, taps_ref,
):
    @pl.when(pl.program_id(0) == 0)
    def _():
        width, inner = w_ref.shape
        near = jnp.concatenate([own_ref[...], one_ref[...]], 0)
        far = jnp.concatenate([two_ref[...], three_ref[...]], 0)
        swap = swap_ref[0] != 0
        first = jnp.where(swap, far, near)
        second = jnp.where(swap, near, far)
        w_side_ref[0:N, :] = first[:, :width]
        w_side_ref[N : 2 * N, :] = second[:, :width]
        heads = w_step_ref.shape[0]
        w_side_ref[2 * N : 2 * N + heads, :] = w_step_ref[...]
        w_side_ref[2 * N + heads :, :] = jnp.zeros((LANES - heads, width), BF)
        taps_ref[0:4, :inner] = conv_ref[...]
        taps_ref[4:5, :inner] = bias_ref[...]
        taps_ref[5:8, :inner] = jnp.zeros((3, inner), F32)
        for i, part in enumerate((first, second)):
            extra = part[:, width:].astype(F32).T
            taps_ref[:, inner + i * N : inner + (i + 1) * N] = extra[0:8] + extra[8:16] + extra[16:24]
        _, halo = norm_rows(halo_ref[...], gain_ref[...])
        halo_out_ref[:, :inner] = dot(halo, w_ref[...])
        halo_out_ref[:, inner:] = dotg(halo, w_side_ref[...], LAST)

    side_ref[...] = dotg(normed_ref[...], w_side_ref[...], LAST)


def combine_kernel(
    reverse, first, known, final,
    follows_ref, arrived_ref, state_ref, rows_ref, *rest,
):
    rest = list(rest)
    before_ref = None if first else rest.pop(0)
    factor_ref = rest.pop(0) if known else None
    follows = follows_ref[0] != 0
    n = state_ref.shape[0]
    other = arrived_ref[0:n, :].astype(F32)
    if known:
        factor = factor_ref[2:3, :]
    else:
        extra = arrived_ref[n : n + 3, :].astype(F32)
        factor = extra[0:1] + extra[1:2] + extra[2:3]
    through = rows_ref[0:1, :]
    past = jnp.ones_like(through) if first else rows_ref[1:2, :]
    before = jnp.zeros_like(other) if first else before_ref[...]
    rest.pop(0)[...] = jnp.where(follows, before + past * other, before)
    new_rows = rest.pop(0)
    if first:
        new_rows[...] = jnp.zeros_like(new_rows)
    else:
        new_rows[...] = rows_ref[...]
    product = through * factor
    new_rows[0:1, :] = product
    new_rows[1:2, :] = jnp.where(follows, past * factor, past)
    new_rows[2:3, :] = factor
    if not final:
        state = state_ref[...]
        state = jnp.where(follows, state + through * other, other + factor * state)
        rest.pop(0)[...] = state
        low_ref = rest.pop(0)
        low_ref[0:n, :] = state.astype(BF)
        if not known:
            low_ref[n:, :] = factor_rows(product)


def factor_rows(row):
    hi, mid, lo = split3(row)
    return jnp.concatenate([hi, mid, lo, jnp.zeros((HALO - 3, row.shape[1]), BF)], 0)


def split_kernel(count, _, *refs):
    sent, kept = refs[4 * count :]
    at = 0
    for i in range(count):
        sent_kept, sent_got, kept_kept, kept_got = refs[4 * i : 4 * i + 4]
        cols = slice(at, at + sent_kept.shape[1])
        at = cols.stop
        sent[:, cols] = (sent_kept[...].astype(F32) + sent_got[...].astype(F32)).astype(BF)
        kept[:, cols] = kept_kept[...].astype(F32) + kept_got[...].astype(F32)


def end_kernel(kept, got, *rest):
    total = kept[...] + got[...].astype(F32)
    rest[-1][...] = total.T if rest[-1].shape != total.shape else total


def add_kernel(count, *refs):
    for i in range(count):
        refs[2 * count + i][...] = refs[2 * i][...] + refs[2 * i + 1][...]


def share_kernel(swap_ref, kept_ref, got_ref, mine_ref, sent_ref):
    total = kept_ref[...].astype(F32) + got_ref[...].astype(F32)
    half = total.shape[1] // 2
    left, right = total[:, :half], total[:, half:]
    swap = swap_ref[0] != 0
    mine_ref[...] = jnp.where(swap, right, left)
    sent_ref[...] = jnp.where(swap, left, right).astype(sent_ref.dtype)


def join_kernel(kept_ref, got_ref, step_ref, first_ref, second_ref):
    def write(out_ref):
        out_ref[:, :LANES] = (kept_ref[...].astype(F32) + got_ref[...].astype(F32)).astype(BF)
        out_ref[:, LANES:] = step_ref[...]

    pl.when(pl.program_id(0) == 0)(lambda: write(first_ref))
    pl.when(pl.program_id(0) == 1)(lambda: write(second_ref))


def close_kernel(
    swap_ref, kept_a, got_a, kept_b, got_b, kept_s, got_s, inner_ref, mine_ref, sent_ref, step_ref
):
    half = kept_a.shape[1]
    inner_ref[:, :half] = kept_a[...] + got_a[...].astype(F32)
    inner_ref[:, half:] = kept_b[...] + got_b[...].astype(F32)
    rest = kept_s[...] + got_s[...].astype(F32)
    left, right = rest[:, : LANES // 2], rest[:, LANES // 2 : LANES]
    swap = swap_ref[0] != 0
    mine_ref[...] = jnp.where(swap, right, left)
    sent_ref[...] = jnp.where(swap, left, right)
    step_ref[...] = rest[:, LANES:]


def unpack_kernel(
    small_ref, pair_ref, pair_got, norm_ref, norm_got, side_ref, side_got,
    norm_out, taps_out, bias_out, pair_taps_out, pair_bias_out, step_out, decay_out, skip_out, gain_out, side_out,
):
    inner = taps_out.shape[1]
    heads = step_out.shape[1]
    pair = pair_ref[...] + pair_got[...]
    norm_out[...] = jnp.sum(norm_ref[...] + norm_got[...], axis=0, keepdims=True)
    taps_out[...] = small_ref[0:4, :inner]
    bias_out[...] = small_ref[4:5, :inner]
    gain_out[...] = small_ref[5:6, :inner]
    pair_taps_out[...] = pair[0:4]
    pair_bias_out[...] = pair[4:5]
    skip_out[...] = small_ref[6:7, 0:heads]
    step_out[...] = small_ref[6:7, LANES : LANES + heads]
    decay_out[...] = small_ref[6:7, 2 * LANES : 2 * LANES + heads]
    side_out[...] = side_ref[...] + side_got[...]


def result_kernel(_, tokens_ref, scale_ref, mine_ref, away_ref, out_ref):
    branch = mine_ref[...] + away_ref[...].astype(F32)
    out_ref[...] = (tokens_ref[...].astype(F32) + scale_ref[...] * branch).astype(BF)


def final_kernel(
    _, tokens_ref, cot_ref, scale_ref, stat_ref, gain_ref, mine_ref, away_ref, grad_ref, norm_ref
):
    scale = scale_ref[...]
    scaled = (mine_ref[...] + away_ref[...].astype(F32)) * scale
    tokens = tokens_ref[...].astype(F32)
    factor = scale * scale * stat_ref[...] * (1.0 / (mine_ref.shape[1] * lax.axis_size("head")))
    grad_ref[...] = cot_ref[...].astype(F32) + scaled * gain_ref[...] - tokens * factor

    @pl.when(pl.program_id(0) == 0)
    def _():
        norm_ref[...] = jnp.zeros_like(norm_ref)

    norm_ref[...] += fold8(scaled * tokens)


def fix_kernel(
    raw_ref, side_ref, keep_ref, back_ref, small_ref, small_got_ref, d_in, dside_in, stat_in,
    d_ref, dside_ref, stat_ref, small_out_ref,
):
    small_out_ref[...] = small_ref[...] + small_got_ref[...]
    inner = raw_ref.shape[1]
    pair = 2 * N
    back = jnp.concatenate([jnp.zeros((HALO - 8, inner + pair), F32), back_ref[...]], 0) * keep_ref[...]
    d_ref[...] = (d_in[...].astype(F32) + back[:, :inner]).astype(BF)
    dside_ref[...] = dside_in[...]
    dside_ref[:, :pair] = (dside_in[:, :pair].astype(F32) + back[:, inner:]).astype(BF)
    row = jnp.sum(back[:, :inner] * raw_ref[...].astype(F32), axis=1, keepdims=True)
    row = row + jnp.sum(back[:, inner:] * side_ref[:, :pair].astype(BF).astype(F32), axis=1, keepdims=True)
    tall = jnp.concatenate([jnp.zeros((L - HALO, LANES), F32), jnp.broadcast_to(row, (HALO, LANES))], 0)
    stat_ref[...] = stat_in[...]
    stat_ref[0] += tall.T[0:8, :]


def nn_kernel(x_ref, w_ref, *rest):
    rest[-1][...] = dot(x_ref[...], w_ref[...]).astype(BF)


def nt_kernel(x_ref, w_ref, *rest):
    rest[-1][...] = dotg(x_ref[...], w_ref[...], LAST).astype(BF)


def cols_kernel(_, x_ref, w_ref, out_ref):
    out_ref[...] = dot(x_ref[...], w_ref[...]).astype(out_ref.dtype)


def cols_add_kernel(_, x_ref, w_ref, got_ref, out_ref):
    out_ref[...] = (dot(x_ref[...], w_ref[...]) + got_ref[...].astype(F32)).astype(out_ref.dtype)


def gate_back_kernel(_, x_ref, w_ref, out_ref):
    out_ref[0] = dotg(x_ref[...], w_ref[...], LAST).astype(BF)


def weight_kernel(scaled, count, grown, _, x_ref, *rest):
    x = x_ref[...]
    if scaled:
        x = (x.astype(F32) * rest[0][...]).astype(BF)
        rest = rest[1:]
    outs = rest[count + grown :]
    for y_ref, out_ref in zip(rest[:count], outs):
        total = dotg(x, y_ref[...], FIRST)
        if len(outs) > count and y_ref is rest[count - 1]:
            half = N // 2
            out_ref[...] = jnp.concatenate([total[:, half:N], total[:, N + half : 2 * N]], 1).astype(BF)
            outs[-2][...] = jnp.concatenate([total[:, :half], total[:, N : N + half]], 1).astype(BF)
            outs[-1][...] = total[:, 2 * N :].astype(BF)
        else:
            out_ref[...] = total.astype(BF)


def twin_kernel(lead, blocks, adds, _, *refs):
    refs = list(refs)
    x_ref, d_ref, side_ref, w_ref, v_ref, base_ref = refs[:6]
    got = refs[6 : 6 + adds]
    outs = refs[-2 - (5 if lead else 0) :]
    step = pl.program_id(0)
    if lead:

        @pl.when(step < lead)
        def _():
            x = x_ref[...]
            half = N // 2
            cols = outs[0].shape[1]
            outs[0][...] = dotg(x, d_ref[:, :cols], FIRST).astype(BF)
            outs[1][...] = dotg(x, d_ref[:, cols:], FIRST).astype(BF)
            total = dotg(x, side_ref[...], FIRST)
            outs[2][...] = jnp.concatenate([total[:, half:N], total[:, N + half : 2 * N]], 1).astype(BF)
            outs[3][...] = jnp.concatenate([total[:, :half], total[:, N : N + half]], 1).astype(BF)
            outs[4][...] = total[:, 2 * N :].astype(BF)

    for which in (0, 1):

        @pl.when((step >= lead + which * blocks) & (step < lead + (which + 1) * blocks))
        def _():
            big = base_ref.shape[1]
            rows = pl.ds(pl.multiple_of((step - lead - which * blocks) * big, big), big)
            total = dotg(d_ref[rows, :], w_ref[...], LAST) + dot(side_ref[rows, :], v_ref[...])
            total = total + base_ref[0].astype(F32)
            if adds:
                total = total + got[which][...].astype(F32)
            out = outs[which - 2]
            out[...] = total.astype(out.dtype)


def conv_kernel(
    raw_ref, side_ref, info_ref, halo_ref, taps_ref, head_ref, tri_ref, spread_ref,
    act_ref, pact_ref, dt_ref, cs_ref, state_ref, low_ref, rows_ref, buf, total_ref,
):
    c = pl.program_id(0)
    inner = raw_ref.shape[1]
    groups = inner // LANES
    pair = pact_ref.shape[1]
    pair_groups = pair // LANES

    @pl.when(c == 0)
    def _():
        buf[0:8, :] = halo_ref[HALO - 8 :, : inner + pair].astype(BF).astype(F32)
        state_ref[...] = jnp.zeros_like(state_ref)
        total_ref[...] = jnp.zeros_like(total_ref)

    info = columns(info_ref[0])
    masks = [None] + [jnp.broadcast_to(info[:, 2 + k : 3 + k], (L, LANES)) for k in (1, 2, 3)]
    dt = jax.nn.softplus(side_ref[:, pair:] + head_ref[0:1, :])
    dt_ref[...] = dt
    cs = exact_sum(tri_ref[...], dt * head_ref[1:2, :])
    cs_ref[...] = cs
    closing = cs[L - 1 :, :]
    total_ref[0:1, :] += closing
    total_ref[1:2, :] = jnp.where(c == 0, 1.0, total_ref[1:2, :]) * info[0:1, 9:10]
    tail = jnp.exp(closing - cs) * info[:, 2:3] * dt
    tail_wide = expand(tail, spread_ref[...])
    keep = jnp.exp(closing) * info[0:1, 9:10]
    keep_wide = expand(jnp.broadcast_to(keep, (8, LANES)), spread_ref[...])[0:1, :]
    acts = []
    for j in range(groups + pair_groups):
        cols = slice(j * LANES, (j + 1) * LANES)
        if j < groups:
            raw = raw_ref[:, cols].astype(F32)
        else:
            raw = side_ref[:, (j - groups) * LANES : (j - groups + 1) * LANES].astype(BF).astype(F32)
        buf[8 : 8 + L, cols] = raw
        pre = taps_ref[4:5, cols] + taps_ref[0:1, cols] * raw
        for k in (1, 2, 3):
            pre = pre + taps_ref[k : k + 1, cols] * buf[8 - k : 8 - k + L, cols] * masks[k]
        act = (pre * sigmoid(pre)).astype(BF)
        buf[0:8, cols] = raw[L - 8 :, :]
        if j < groups:
            act_ref[:, cols] = act
        else:
            pact_ref[:, (j - groups) * LANES : (j - groups + 1) * LANES] = act
    key = pact_ref[:, :N]
    for j in range(groups):
        cols = slice(j * LANES, (j + 1) * LANES)
        weighted = (act_ref[:, cols].astype(F32) * tail_wide[:, cols]).astype(BF)
        state_ref[:, cols] = keep_wide[:, cols] * state_ref[:, cols] + dotg(key, weighted, FIRST)

    @pl.when(c == pl.num_programs(0) - 1)
    def _():
        through = jnp.exp(total_ref[0:1, :]) * total_ref[1:2, :]
        rows_ref[...] = expand(jnp.broadcast_to(through, (8, LANES)), spread_ref[...])
        low_ref[0:N, :] = state_ref[...].astype(BF)
        low_ref[N:, :] = factor_rows(rows_ref[0:1, :])


def out_kernel(
    act_ref, pact_ref, dt_ref, cs_ref, info_ref, gate_ref, dgn_ref, state_in_ref,
    gains_ref, spread_ref,
    mixed_ref, gg_ref, sums_ref, entry_ref, state,
):
    c = pl.program_id(0)
    inner = act_ref.shape[1]
    groups = inner // LANES

    @pl.when(c == 0)
    def _():
        state[...] = state_in_ref[...]

    info = columns(info_ref[0])
    mask = mask_of(info, info_ref[0, 0:1, :])
    key = pact_ref[:, :N]
    query = pact_ref[:, N:]
    scores = dotg(query, key, LAST)
    dt = dt_ref[...]
    cs = cs_ref[...]
    cs_rows = cs.T
    closing = cs[L - 1 :, :]
    spread = spread_ref[...]
    dt_wide = expand(dt, spread)
    open_wide = expand(jnp.exp(cs) * info[:, 1:2], spread)
    tail_wide = expand(jnp.exp(closing - cs) * info[:, 2:3], spread)
    keep = jnp.exp(closing) * info[0:1, 9:10]
    keep_wide = expand(jnp.broadcast_to(keep, (8, LANES)), spread)[0:1, :]
    left = lane_is_left((L, LANES))
    square = jnp.zeros((L, LANES), F32)
    cross = jnp.zeros((L, LANES), F32)
    for j in range(groups):
        cols = slice(j * LANES, (j + 1) * LANES)
        x = act_ref[:, cols].astype(F32)
        xd = x * dt_wide[:, cols]
        xd_low = xd.astype(BF)
        weights = []
        for h in (2 * j, 2 * j + 1):
            factor = jnp.exp(cs[:, h : h + 1] - cs_rows[h : h + 1, :] + mask)
            weights.append((scores * factor).astype(BF))
        entry = state[:, cols].astype(BF)
        entry_ref[0, :, cols] = entry
        y = dot(jnp.concatenate(weights, 1), stacked_pair(xd_low, left))
        y = y + open_wide[:, cols] * dot(query, entry)
        mixed = y + gains_ref[0:1, cols] * x
        mixed_ref[:, cols] = mixed.astype(BF)
        gate = gate_ref[:, cols].astype(F32)
        gated = mixed * (gate * sigmoid(gate))
        gg = gated * gains_ref[1:2, cols]
        gg_ref[:, cols] = gg.astype(BF)
        square = square + gated * gated
        cross = cross + gg * dgn_ref[:, cols].astype(F32)
        weighted = (xd * tail_wide[:, cols]).astype(BF)
        state[:, cols] = keep_wide[:, cols] * state[:, cols] + dotg(key, weighted, FIRST)
    lane = lax.broadcasted_iota(jnp.int32, (L, LANES), 1)
    both = jnp.where(
        lane == 0,
        jnp.sum(square, axis=1, keepdims=True),
        jnp.sum(cross, axis=1, keepdims=True),
    )
    sums_ref[0] = both.T[0:2, :]


def gate_kernel(
    mixed_ref, gate_ref, dgn_ref, act_ref, pact_ref, cs_ref, info_ref, near_ref, far_ref, gains_ref, spread_ref,
    dmix_ref, dgate_ref, stat_ref, dstate_ref, low_ref, dgain_ref, dskip_ref,
):
    c = pl.program_id(0)
    inner = act_ref.shape[1]
    groups = inner // LANES

    @pl.when(c == 0)
    def _():
        dstate_ref[...] = jnp.zeros_like(dstate_ref)
        dgain_ref[...] = jnp.zeros_like(dgain_ref)
        dskip_ref[...] = jnp.zeros_like(dskip_ref)

    info = columns(info_ref[0])
    both = near_ref[0] + far_ref[0]
    scale_row = lax.rsqrt(both[0:1, :] / DI + EPS)
    coef_row = scale_row * scale_row * scale_row * both[1:2, :] / DI
    stats = columns(jnp.concatenate([scale_row, coef_row, jnp.zeros((6, L), F32)], 0))
    scale = jnp.broadcast_to(stats[:, 0:1], (L, LANES))
    coef = jnp.broadcast_to(stats[:, 1:2], (L, LANES))
    cs = cs_ref[...]
    spread = spread_ref[...]
    open_wide = expand(jnp.exp(cs) * info[:, 1:2], spread)
    keep = jnp.exp(cs[L - 1 :, :]) * info[0:1, 9:10]
    keep_wide = expand(jnp.broadcast_to(keep, (8, LANES)), spread)[0:1, :]
    query = pact_ref[:, N:]
    row = jnp.zeros((L, LANES), F32)
    for j in range(groups):
        cols = slice(j * LANES, (j + 1) * LANES)
        mixed = mixed_ref[:, cols].astype(F32)
        gate = gate_ref[:, cols].astype(F32)
        dgn = dgn_ref[:, cols].astype(F32)
        x = act_ref[:, cols].astype(F32)
        sig = sigmoid(gate)
        act = gate * sig
        gated = mixed * act
        scaled = dgn * scale
        dgain_ref[:, cols] += fold8(scaled * gated)
        dgated = scaled * gains_ref[1:2, cols] - gated * coef
        dmix = dgated * act
        dgate = dgated * mixed * (sig + act * (1.0 - sig))
        dskip_ref[:, cols] += fold8(dmix * x)
        row = row + dgate * gate
        dgate_ref[:, cols] = dgate.astype(BF)
        low = dmix.astype(BF)
        dmix_ref[:, cols] = low
        opened = (low.astype(F32) * open_wide[:, cols]).astype(BF)
        dstate_ref[:, cols] = keep_wide[:, cols] * dstate_ref[:, cols] + dotg(query, opened, FIRST)
    stat_ref[0] = jnp.broadcast_to(jnp.sum(row, axis=1, keepdims=True), (L, LANES)).T[0:8, :]

    @pl.when(c == pl.num_programs(0) - 1)
    def _():
        low_ref[...] = dstate_ref[...].astype(BF)


def back_kernel(
    grown, final,
    act_ref, pact_ref, dt_ref, cs_ref, info_ref, dmix_ref, entry_ref,
    raw_ref, side_ref, raw_prev_ref, side_prev_ref, halo_ref,
    taps_ref, head_ref, gains_ref, tri_ref, spread_ref, gather_ref,
    dstate_in_ref, carried_in_ref, dtaps_in_ref, dhead_in_ref, dgain_ref, dskip_ref, stat_in_ref, *rest,
):
    rest = list(rest[grown:])
    d_ref, dside_ref, stat_ref, dstate, carried_ref, dtaps_ref, dhead_ref = rest[:7]
    small_ref, dhalo_ref = rest[7:9] if final else (None, None)
    buf, dbuf = rest[-2:]
    c = pl.program_id(0)
    last = pl.num_programs(0) - 1
    inner = act_ref.shape[1]
    groups = inner // LANES
    pair = 2 * N
    wide = inner + pair

    @pl.when(c == 0)
    def _():
        dstate[...] = dstate_in_ref[...]
        dbuf[L:, :] = carried_in_ref[...]
        dtaps_ref[...] = dtaps_in_ref[...]
        dhead_ref[...] = dhead_in_ref[...]

    def before():
        buf[0:8, :inner] = raw_prev_ref[HALO - 8 :, :].astype(F32)
        buf[0:8, inner:] = side_prev_ref[HALO - 8 :, :pair].astype(BF).astype(F32)

    if final:

        @pl.when(c == last)
        def _():
            buf[0:8, :] = halo_ref[HALO - 8 :, :wide].astype(BF).astype(F32)

        pl.when(c < last)(before)
    else:
        before()

    info = columns(info_ref[0])
    masks = [None] + [jnp.broadcast_to(info[:, 2 + k : 3 + k], (L, LANES)) for k in (1, 2, 3)]
    afters = [None] + [jnp.broadcast_to(info[:, 5 + k : 6 + k], (L, LANES)) for k in (1, 2, 3)]
    mask = mask_of(info, info_ref[0, 0:1, :])
    key = pact_ref[:, :N]
    query = pact_ref[:, N:]
    scores = dotg(query, key, LAST)
    dt = dt_ref[...]
    cs = cs_ref[...]
    cs_rows = cs.T
    closing = cs[L - 1 :, :]
    spread = spread_ref[...]
    dt_wide = expand(dt, spread)
    open_wide = expand(jnp.exp(cs) * info[:, 1:2], spread)
    tail_wide = expand(jnp.exp(closing - cs) * info[:, 2:3], spread)
    keep = jnp.exp(closing) * info[0:1, 9:10]
    keep_wide = expand(jnp.broadcast_to(keep, (8, LANES)), spread)[0:1, :]
    left = lane_is_left((L, LANES))

    def conv_back(j, raw, dact):
        cols = slice(j * LANES, (j + 1) * LANES)
        buf[8 : 8 + L, cols] = raw
        pre = taps_ref[4:5, cols] + taps_ref[0:1, cols] * raw
        moved = [raw]
        for k in (1, 2, 3):
            moved.append(buf[8 - k : 8 - k + L, cols] * masks[k])
            pre = pre + taps_ref[k : k + 1, cols] * moved[k]
        sig = sigmoid(pre)
        dpre = dact * (sig * (1.0 + pre * (1.0 - sig)))
        for k in range(4):
            dtaps_ref[8 * k : 8 * k + 8, cols] += fold8(dpre * moved[k])
        dtaps_ref[32:40, cols] += fold8(dpre)
        dbuf[0:L, cols] = dpre
        draw = taps_ref[0:1, cols] * dpre
        for k in (1, 2, 3):
            draw = draw + taps_ref[k : k + 1, cols] * dbuf[k : k + L, cols] * afters[k]
        dbuf[L : L + 8, cols] = dpre[0:8, :]
        if j < groups:
            d_ref[:, cols] = draw.astype(BF)
        else:
            dside_ref[:, (j - groups) * LANES : (j - groups + 1) * LANES] = draw.astype(BF)
        return draw * raw

    row = jnp.zeros((L, LANES), F32)
    dscores = jnp.zeros((L, L), F32)
    dkey = jnp.zeros((L, N), F32)
    dquery = jnp.zeros((L, N), F32)
    dcs = jnp.zeros((L, LANES), F32)
    ddt = jnp.zeros((L, LANES), F32)
    dclose = jnp.zeros((8, LANES), F32)
    for j in range(groups):
        cols = slice(j * LANES, (j + 1) * LANES)
        x = act_ref[:, cols].astype(F32)
        xd = (x * dt_wide[:, cols]).astype(BF)
        dm = dmix_ref[:, cols]
        dmf = dm.astype(F32)
        xdf = xd.astype(F32)
        factors = []
        weights = []
        for h in (2 * j, 2 * j + 1):
            factor = jnp.exp(cs[:, h : h + 1] - cs_rows[h : h + 1, :] + mask)
            factors.append(factor)
            weights.append((scores * factor).astype(BF))
        pair_x = stacked_pair(xd, left)
        pair_d = stacked_pair(dm, left)
        dweights = dotg(dm, pair_x, LAST)
        dscores = dscores + dweights[:, :L] * factors[0] + dweights[:, L:] * factors[1]
        y = dot(jnp.concatenate(weights, 1), pair_x)
        dxd = dotg(jnp.concatenate(weights, 0), pair_d, FIRST)
        entry = entry_ref[0, :, cols]
        dst = dstate[:, cols]
        dst_low = dst.astype(BF)
        opened = (dmf * open_wide[:, cols]).astype(BF)
        tailed = (xdf * tail_wide[:, cols]).astype(BF)
        from_state = dot(query, entry)
        to_state = dot(key, dst_low)
        out_part = tailed.astype(F32) * to_state
        diff = dmf * y + opened.astype(F32) * from_state - xdf * dxd - out_part
        dxd = dxd + to_state * tail_wide[:, cols]
        hi, lo = split2(diff)
        gather = gather_ref[cols, :]
        dcs = dcs + dot(hi, gather) + dot(lo, gather)
        ddt = ddt + dot((dxd * x).astype(BF), gather)
        close = fold8(out_part) + keep_wide[:, cols] * fold8(dst * entry.astype(F32))
        hi, lo = split2(close)
        dclose = dclose + dot(hi, gather) + dot(lo, gather)
        dquery = dquery + dotg(opened, entry, LAST)
        dkey = dkey + dotg(tailed, dst_low, LAST)
        dstate[:, cols] = keep_wide[:, cols] * dst + dotg(query, opened, FIRST)
        dx = dxd * dt_wide[:, cols] + gains_ref[0:1, cols] * dmf
        row = row + conv_back(j, raw_ref[:, cols].astype(F32), dx)
    dscores = dscores.astype(BF)
    dquery = dquery + dot(dscores, key)
    dkey = dkey + dotg(dscores, query, FIRST)
    row = row + conv_back(groups, side_ref[:, :N].astype(BF).astype(F32), dkey)
    row = row + conv_back(groups + 1, side_ref[:, N:pair].astype(BF).astype(F32), dquery)
    later = dcs
    hi, mid, lo = split3(later)
    tri = tri_ref[...]
    da = dotg(tri, hi, FIRST) + dotg(tri, mid, FIRST) + dotg(tri, lo, FIRST)
    da = da + jnp.sum(dclose, axis=0, keepdims=True)
    ddt = ddt + head_ref[1:2, :] * da
    step = side_ref[:, pair:]
    dstep = ddt * sigmoid(step + head_ref[0:1, :])
    dhead_ref[0:8, :] += fold8(dstep)
    dhead_ref[8:16, :] += fold8(dt * da)
    dside_ref[:, pair:] = dstep.astype(BF)
    row = row + dstep * step
    stat_ref[0] = stat_in_ref[0] + jnp.broadcast_to(jnp.sum(row, axis=1, keepdims=True), (L, LANES)).T[0:8, :]

    @pl.when(c == last)
    def _():
        carried_ref[...] = dbuf[L:, :]

    if final:

        @pl.when(c == last)
        def _():
            for k in range(5):
                small_ref[k : k + 1, :] = jnp.sum(dtaps_ref[8 * k : 8 * k + 8, :], axis=0, keepdims=True)
            small_ref[5:8, :] = jnp.zeros((3, wide), F32)
            small_ref[5:6, :inner] = jnp.sum(dgain_ref[...], axis=0, keepdims=True)
            skip = jnp.broadcast_to(jnp.sum(dskip_ref[...], axis=0, keepdims=True), (8, inner))
            hi, lo = split2(skip)
            skip = dot(hi, gather_ref[...]) + dot(lo, gather_ref[...])
            small_ref[6:7, 0:LANES] = skip[0:1, :]
            small_ref[6:7, LANES : 2 * LANES] = jnp.sum(dhead_ref[0:8, :], axis=0, keepdims=True)
            small_ref[6:7, 2 * LANES : 3 * LANES] = (
                jnp.sum(dhead_ref[8:16, :], axis=0, keepdims=True) * head_ref[1:2, :]
            )
            dhalo_ref[...] = jnp.zeros((8, wide), F32)
            for j in range(groups + 2):
                cols = slice(j * LANES, (j + 1) * LANES)
                for k in (1, 2, 3):
                    reach = dbuf[L : L + 8, cols] * masks[k][0:8, :] * taps_ref[k : k + 1, cols]
                    dhalo_ref[8 - k :, cols] += reach[0:k, :]


def flip(block, axis, bit):
    count = lax.axis_size(axis)
    route = [(i, i ^ bit) for i in range(count)]
    return jax.tree.map(lambda a: lax.ppermute(a, axis, route), block)


def sum_over(block, axis):
    bit = 1
    while bit < lax.axis_size(axis):
        block = block + flip(block, axis, bit)
        bit *= 2
    return block


def shift_over(block, axis, distance):
    devices = range(lax.axis_size(axis))
    route = [(i, i + distance) for i in devices if i + distance in devices]
    return lax.ppermute(block, axis, route)


def body(
    tokens, boundary, norm_gain, w_gate, w_inner, w_pair, w_step, conv_inner, conv_pair,
    bias_inner, bias_pair, step_bias, decay_log, skip_gain, gate_gain, w_output, cotangent,
):
    rows, width = tokens.shape
    inner = w_gate.shape[1]
    heads = w_step.shape[1]
    head_count = lax.axis_size("head")
    place = lax.axis_index("head")
    quarter = width // head_count
    pair_cols = w_pair.shape[1]
    pair = pair_cols * head_count
    wide = inner + pair
    side = pair + LANES
    steps = rows // L
    chain = Chain()
    run = chain.run

    def behind(c):
        return steps - 1 - c

    def row_of(v):
        return v.reshape(1, -1)

    head_of = np.arange(inner)[None, :] // HP == np.arange(LANES)[:, None]
    spread2 = jnp.asarray(np.concatenate([head_of, head_of], 0), BF)
    gather = jnp.asarray(head_of.T, BF)
    lower = jnp.asarray(np.tril(np.ones((L, L))), BF)
    upper = jnp.asarray(np.triu(np.ones((L, L))), BF)

    def split_low(v):
        hi, mid, lo = split3(v)
        return [hi, mid, lo]

    swap = (place & 2) != 0

    pair_small = jnp.concatenate([conv_pair, row_of(bias_pair), jnp.zeros((3, pair_cols), F32)], 0).T
    pair_own = jnp.concatenate([w_pair.T, *split_low(pair_small), jnp.zeros((pair_cols, LANES - 24), BF)], 1)
    pair_pieces = [pair_own] + [flip(pair_own, "head", d) for d in (1, 2, 3)]
    gain_row = row_of(norm_gain)

    info_spec = slab_spec(16, L, ahead)
    info_back = slab_spec(16, L, behind)
    one_step = (1,)
    info, sent, keep_tail, head_rows, gains = run(
        prep_kernel,
        one_step,
        [
            whole(boundary.reshape(steps, L)), whole(upper),
            (tokens, pl.BlockSpec((HALO, width), lambda c: (rows // HALO - 1, 0))),
            whole(row_of(step_bias)), whole(row_of(decay_log)), whole(row_of(skip_gain)), whole(row_of(gate_gain)),
            whole(spread2),
        ],
        [
            (whole_spec((steps, 16, L)), (steps, 16, L), F32), (whole_spec((HALO, width)), (HALO, width), BF),
            (whole_spec((HALO, 1)), (HALO, 1), F32), (whole_spec((8, LANES)), (8, LANES), F32),
            (whole_spec((8, inner)), (8, inner), F32),
        ],
        us=2,
    )
    token_halo = shift_over(sent, "seq", 1)

    big = 512
    blocks = rows // big

    def rows_spec(cols, start=0, size=big):
        return pl.BlockSpec((size, cols), lambda i, *_: (i + start, 0))

    def fixed(shape):
        return pl.BlockSpec(shape, lambda i, *_: (0,) * len(shape))

    normed, scale_in, inner_raw = run(
        proj_kernel,
        (blocks,),
        [(tokens, rows_spec(width)), whole(gain_row), whole(w_inner)],
        [
            (rows_spec(width), (rows, width), BF),
            (rows_spec(1), (rows, 1), F32),
            (rows_spec(inner), (rows, inner), BF),
        ],
        us=12,
    )
    halo_shape = (HALO, inner + side)
    side_raw, halo, w_side, taps = run(
        side_kernel,
        (blocks,),
        [(normed, rows_spec(width))]
        + [whole(p) for p in pair_pieces]
        + [whole(w_step.T), whole(token_halo), whole(gain_row), whole(w_inner), whole(conv_inner), whole(row_of(bias_inner))],
        [
            (rows_spec(side), (rows, side), F32),
            (fixed(halo_shape), halo_shape, F32),
            (fixed((side, width)), (side, width), BF),
            (fixed((8, wide)), (8, wide), F32),
        ],
        ids=swap.astype(jnp.int32).reshape(1),
        us=10,
    )

    low_rows = N + HALO
    act, pact, dt, cs, closing, closing_low, through = run(
        conv_kernel,
        (steps,),
        [
            (inner_raw, chunk_spec(inner, ahead)), (side_raw, chunk_spec(side, ahead)), (info, info_spec),
            whole(halo), whole(taps), whole(head_rows), whole(lower), whole(spread2),
        ],
        [
            (chunk_spec(inner, ahead), (rows, inner), BF), (chunk_spec(pair, ahead), (rows, pair), BF),
            (chunk_spec(LANES, ahead), (rows, LANES), F32), (chunk_spec(LANES, ahead), (rows, LANES), F32),
            (whole_spec((N, inner)), (N, inner), F32), (whole_spec((low_rows, inner)), (low_rows, inner), BF),
            (whole_spec((8, inner)), (8, inner), F32),
        ],
        scratch=[pltpu.VMEM((8 + L, wide), F32), pltpu.VMEM((8, LANES), F32)],
        us=17,
    )

    seq_count = lax.axis_size("seq")
    seq_place = lax.axis_index("seq")

    def exchange(state, low, rows0, known, reverse, between):
        before, row, factors = None, rows0, []
        bit = 1
        while bit < seq_count:
            arrived = flip(low, "seq", bit)
            if between:
                between.pop(0)()
            follows = (seq_place & bit) != 0
            if reverse:
                follows = jnp.logical_not(follows)
            final = bit * 2 >= seq_count
            has = known is not None
            ins = [whole(arrived), whole(state), whole(row)]
            if before is not None:
                ins.append(whole(before))
            if has:
                ins.append(whole(known[len(factors)]))
            big_out = (fixed((N, inner)), (N, inner), F32)
            outs = [big_out, (fixed((8, inner)), (8, inner), F32)]
            if not final:
                height = N if has else low_rows
                outs += [big_out, (fixed((height, inner)), (height, inner), BF)]
            got = run(
                functools.partial(combine_kernel, reverse, before is None, has, final),
                one_step,
                ins,
                outs,
                ids=follows.astype(jnp.int32).reshape(1),
                us=2,
            )
            before, row = got[0], got[1]
            factors.append(row)
            if not final:
                state, low = got[2], got[3]
            bit *= 2
        for work in between:
            work()
        return before, factors

    def product(kernel, x, w, start, size, into):
        out = [] if into is None else [(into, ANY)]
        return run(
            kernel,
            (size,),
            [(x, rows_spec(x.shape[1], start)), whole(w)] + out,
            [(rows_spec(inner, start), (rows, inner), BF)],
            aliases={2: 0} if out else None,
            us=2.9 * size,
        )[0]

    third = max(blocks // 3, 1)
    held = {}

    def gate_one():
        held["gate"] = product(nn_kernel, normed, w_gate, 0, blocks - third, None)

    def gate_two():
        held["gate"] = product(nn_kernel, normed, w_gate, blocks - third, third, held["gate"])
        held["dgn"] = product(nt_kernel, cotangent, w_output, 0, third, None)

    def gate_three():
        held["dgn"] = product(nt_kernel, cotangent, w_output, third, blocks - third, held["dgn"])

    state_in, factors = exchange(closing, closing_low, through, None, False, [gate_one, gate_two, gate_three])
    gate_pre, dgn = held["gate"], held["dgn"]

    mixed, gg, sums, entries = run(
        out_kernel,
        (steps,),
        [
            (act, chunk_spec(inner, ahead)), (pact, chunk_spec(pair, ahead)), (dt, chunk_spec(LANES, ahead)),
            (cs, chunk_spec(LANES, ahead)), (info, info_spec),
            (gate_pre, chunk_spec(inner, ahead)), (dgn, chunk_spec(inner, ahead)),
            whole(state_in), whole(gains), whole(spread2),
        ],
        [
            (chunk_spec(inner, ahead), (rows, inner), BF), (chunk_spec(inner, ahead), (rows, inner), BF),
            (slab_spec(2, L, ahead), (steps, 2, L), F32), (slab_spec(N, inner, ahead), (steps, N, inner), BF),
        ],
        scratch=[pltpu.VMEM((N, inner), F32)],
        us=18,
    )

    order = [place ^ 3, place ^ 1, place ^ 2, place]

    def quarter_spec():
        return pl.BlockSpec((big, quarter), lambda i, ids: (i, 0))

    def out_quarter(which, got, dtype, after=()):
        ins = [
            (gg, pl.BlockSpec((big, inner), lambda i, ids: (i, 0))),
            (w_output, pl.BlockSpec((inner, quarter), lambda i, ids: (0, ids[0]))),
        ]
        if got is not None:
            ins.append((got, quarter_spec()))
        return run(
            cols_kernel if got is None else cols_add_kernel,
            (blocks,),
            ins,
            [(quarter_spec(), (rows, quarter), dtype)],
            after=after,
            ids=order[which].reshape(1),
            us=5,
        )[0]

    sums_core = flip(sums, "head", 1)
    out_a = out_quarter(0, None, BF)
    sums = sums + sums_core
    got_a = flip(out_a, "head", 1)
    sums_x = flip(sums, "head", 2)
    out_b = out_quarter(1, None, BF, [sums_core])
    got_b = flip(out_b, "head", 1)
    scale_out = lax.rsqrt((sums + sums_x)[:, 0, :] / DI + EPS).reshape(rows, 1)

    share = width // seq_count
    manual = seq_count == 8
    half = seq_count // 2
    seq_core = seq_place % 2
    if manual:
        row_ids = [jnp.arange(half) * 2 + (1 - seq_core), jnp.arange(half) * 2 + seq_core]
    else:
        share = 256
        row_ids = [jnp.arange(width // share)]

    def weight_rows(which, x, ys, scale=None, into=()):
        ids = row_ids[which].astype(jnp.int32)
        count = ids.shape[0]
        ins = [(x, pl.BlockSpec((rows, share), lambda i, ids: (0, ids[i])))]
        if scale is not None:
            ins.append(whole(scale))
        outs = []
        lead = count * which
        for y, cols, at in ys:
            ins.append((y, pl.BlockSpec((rows, cols), lambda i, ids, at=at: (0, at))))
            if cols == side:
                spec = pl.BlockSpec((share, LANES), lambda i, ids: (i + lead, 0))
                outs += [(spec, (width, LANES), BF)] * 3
            else:
                outs.append((pl.BlockSpec((share, cols), lambda i, ids: (i, 0)), (count * share, cols), BF))
        aliases = {len(ins) + k: len(outs) - 3 + k for k in range(len(into))}
        return run(
            functools.partial(weight_kernel, scale is not None, len(ys), len(into)),
            (count,),
            ins + [(a, ANY) for a in into],
            outs,
            ids=ids,
            aliases=aliases,
            us=8,
        )

    z = seq_place // 2

    class Halving:
        def __init__(self, pieces):
            low = z % 2
            ids = jnp.stack([1 - low, 3 - low, low, 2 + low]).astype(jnp.int32)
            ins = []
            for kept, got in pieces:
                cols = kept.shape[1]
                for first in (0, 2):
                    spec = pl.BlockSpec((share, cols), lambda i, ids, f=first: (ids[f + i], 0))
                    ins += [(kept, spec), (got, spec)]
            self.cols = sum(kept.shape[1] for kept, _ in pieces)
            self.count = len(pieces)
            out = pl.BlockSpec((share, self.cols), lambda i, ids: (i, 0))
            sent, self.kept = run(
                functools.partial(split_kernel, self.count),
                (2,),
                ins,
                [(out, (2 * share, self.cols), BF), (out, (2 * share, self.cols), F32)],
                ids=ids,
                us=3,
            )
            self.got = flip(sent, "seq", 2)

        def middle(self):
            high = z // 2
            ids = jnp.stack([1 - high, high]).astype(jnp.int32)
            part = share // 2
            ins = []
            for w in (0, 1):
                spec = pl.BlockSpec((part, self.cols), lambda i, ids, w=w: (ids[w] * 2 + i, 0))
                ins += [(self.kept, spec), (self.got, spec)]
            out = pl.BlockSpec((part, self.cols), lambda i, ids: (i, 0))
            sent, self.kept = run(
                functools.partial(split_kernel, 1),
                (2,),
                ins,
                [(out, (share, self.cols), BF), (out, (share, self.cols), F32)],
                ids=ids,
                us=2,
            )
            self.got = flip(sent, "seq", 4)

        def end(self, into=None, place=0, total=1, turned=False):
            if turned:
                shape = block = (self.cols, share)
            else:
                shape, block = (share, self.cols * total), (share, self.cols)
            ins = [whole(self.kept), whole(self.got)] + ([] if into is None else [(into, ANY)])
            return run(
                end_kernel,
                one_step,
                ins,
                [(pl.BlockSpec(block, lambda i: (0, place)), shape, F32)],
                aliases=None if into is None else {2: 0},
                us=2,
            )[0]

    (out_first,) = weight_rows(0, cotangent, [(gg, inner, 0)], scale_out)
    if manual:
        out_got = flip(out_first, "seq", 1)
    away = out_quarter(2, got_a, BF)
    away_got = flip(away, "head", 2)
    mine = out_quarter(3, got_b, F32)
    if manual:
        (out_second,) = weight_rows(1, cotangent, [(gg, inner, 0)], scale_out)

    dmix, dgate, stat, dstate_local, dstate_low, dgain, dskip = run(
        gate_kernel,
        (steps,),
        [
            (mixed, chunk_spec(inner, behind)), (gate_pre, chunk_spec(inner, behind)), (dgn, chunk_spec(inner, behind)),
            (act, chunk_spec(inner, behind)), (pact, chunk_spec(pair, behind)), (cs, chunk_spec(LANES, behind)),
            (info, info_back), (sums, slab_spec(2, L, behind)), (sums_x, slab_spec(2, L, behind)),
            whole(gains), whole(spread2),
        ],
        [
            (chunk_spec(inner, behind), (rows, inner), BF), (chunk_spec(inner, behind), (rows, inner), BF),
            (slab_spec(8, L, behind), (steps, 8, L), F32), (whole_spec((N, inner)), (N, inner), F32),
            (whole_spec((N, inner)), (N, inner), BF),
            (whole_spec((8, inner)), (8, inner), F32), (whole_spec((8, inner)), (8, inner), F32),
        ],
        us=17,
    )

    order_ids = jnp.stack(order).astype(jnp.int32)

    def gate_first():
        held["first"] = weight_rows(0, normed, [(dgate, inner, 0)])[0]

    def gate_second():
        if manual:
            held["got"] = flip(held["first"], "seq", 1)
            held["second"] = weight_rows(1, normed, [(dgate, inner, 0)])[0]

    def gate_third():
        held["dn"] = run(
            gate_back_kernel,
            (4, blocks),
            [
                (dgate, pl.BlockSpec((big, inner), lambda n, i, ids: (i, 0))),
                (w_gate, pl.BlockSpec((quarter, inner), lambda n, i, ids: (ids[n], 0))),
            ],
            [(pl.BlockSpec((1, big, quarter), lambda n, i, ids: (n, i, 0)), (4, rows, quarter), BF)],
            ids=order_ids,
            us=17,
        )[0]

    dstate, _ = exchange(
        dstate_local, dstate_low, through, factors, True, [gate_first, gate_second, gate_third]
    )
    dn_gate = held["dn"]

    parts = 3 if steps % 3 == 0 else 1
    each = steps // parts
    carried = jnp.zeros((8, wide), F32)
    dtaps = jnp.zeros((40, wide), F32)
    dhead = jnp.zeros((16, LANES), F32)
    d_inner = d_side = small = dhalo = None
    if manual:
        out_sum = Halving([(out_second, out_got)])
    for part in range(parts):
        first = steps - 1 - part * each

        def at(c, first=first):
            return first - c

        def near_end(c, at=at):
            return jnp.maximum(at(c) * (L // HALO) - 1, 0)

        final = part == parts - 1
        if manual and part == 1:
            out_sum.middle()
        if manual and part == 2:
            dw_out = out_sum.end(turned=True)
            gate_sum = Halving([(held["second"], held["got"])])
        grown = [] if d_inner is None else [(d_inner, ANY), (d_side, ANY)]
        state_specs = [
            (whole_spec((N, inner)), (N, inner), F32), (whole_spec((8, wide)), (8, wide), F32),
            (whole_spec((40, wide)), (40, wide), F32), (whole_spec((16, LANES)), (16, LANES), F32),
        ]
        if final:
            state_specs += [(whole_spec((8, wide)), (8, wide), F32)] * 2
        ins = [
            (act, chunk_spec(inner, at)), (pact, chunk_spec(pair, at)), (dt, chunk_spec(LANES, at)),
            (cs, chunk_spec(LANES, at)), (info, slab_spec(16, L, at)),
            (dmix, chunk_spec(inner, at)), (entries, slab_spec(N, inner, at)),
            (inner_raw, chunk_spec(inner, at)), (side_raw, chunk_spec(side, at)),
            (inner_raw, pl.BlockSpec((HALO, inner), lambda c, p=near_end: (p(c), 0))),
            (side_raw, pl.BlockSpec((HALO, side), lambda c, p=near_end: (p(c), 0))),
            whole(halo), whole(taps), whole(head_rows), whole(gains), whole(lower), whole(spread2), whole(gather),
            whole(dstate), whole(carried), whole(dtaps), whole(dhead), whole(dgain), whole(dskip),
            (stat, slab_spec(8, L, at)), *grown,
        ]
        aliases = {24: 2}
        if grown:
            aliases.update({25: 0, 26: 1})
        got = run(
            functools.partial(back_kernel, len(grown), final),
            (each,),
            ins,
            [
                (chunk_spec(inner, at), (rows, inner), BF), (chunk_spec(side, at), (rows, side), BF),
                (slab_spec(8, L, at), (steps, 8, L), F32), *state_specs,
            ],
            after=[away_got] if part == min(1, parts - 1) else [],
            scratch=[pltpu.VMEM((8 + L, wide), F32), pltpu.VMEM((L + 8, wide), F32)],
            aliases=aliases,
            us=64 / parts,
        )
        d_inner, d_side, stat, dstate, carried, dtaps, dhead = got[:7]
        if final:
            small, dhalo = got[7:]

    if manual:
        gate_sum.middle()
    returned = shift_over(dhalo, "seq", -1)
    small_got = flip(small, "seq", 1)

    def last_rows(cols):
        return pl.BlockSpec((HALO, cols), lambda c: (rows // HALO - 1, 0))

    last_slab = slab_spec(8, L, lambda c: steps - 1)
    d_inner, d_side, stat, small = run(
        fix_kernel,
        one_step,
        [
            (inner_raw, last_rows(inner)), (side_raw, last_rows(side)), whole(keep_tail), whole(returned),
            whole(small), whole(small_got),
            (d_inner, last_rows(inner)), (d_side, last_rows(side)), (stat, last_slab),
        ],
        [
            (last_rows(inner), (rows, inner), BF), (last_rows(side), (rows, side), BF), (last_slab, (steps, 8, L), F32),
            (whole_spec((8, wide)), (8, wide), F32),
        ],
        aliases={6: 0, 7: 1, 8: 2},
        us=2,
    )

    def add(pairs):
        return run(
            functools.partial(add_kernel, len(pairs)),
            one_step,
            [whole(a) for pair_ in pairs for a in pair_],
            [(pl.BlockSpec(a.shape, lambda i, n=a.ndim: (0,) * n), a.shape, a.dtype) for a, _ in pairs],
            us=1,
        )

    half_inner = inner // 2
    swap_id = swap.astype(jnp.int32).reshape(1)
    inner_parts = [(d_inner, half_inner, 0), (d_inner, half_inner, 1), (d_side, side, 0)]

    swap_id = swap.astype(jnp.int32).reshape(1)
    stat = stat[:, 0, :]

    def twin(pair_at, got, dtypes, into=None):
        lead = half if into is not None else 0
        ids = [order[pair_at], order[pair_at + 1]]
        ids = jnp.concatenate([jnp.stack(ids)] + ([row_ids[1]] if lead else [])).astype(jnp.int32)

        def which(s):
            return jnp.clip((s - lead) // blocks, 0, 1)

        def row(s):
            return jnp.where(s < lead, 0, (s - lead) % blocks)

        def x_at(s, ids):
            return (0, ids[2 + jnp.minimum(s, lead - 1)]) if lead else (0, 0)

        def out_at(s, w):
            return jnp.clip(s - lead - w * blocks, 0, blocks - 1)

        ins = [
            (normed, pl.BlockSpec((rows if lead else 256, 256), x_at)),
            whole(d_inner), whole(d_side),
            (w_inner, pl.BlockSpec((quarter, inner), lambda s, ids: (ids[which(s)], 0))),
            (w_side, pl.BlockSpec((side, quarter), lambda s, ids: (0, ids[which(s)]))),
            (dn_gate, pl.BlockSpec((1, big, quarter), lambda s, ids: (pair_at + which(s), row(s), 0))),
        ]
        for w, block in enumerate(got):
            ins.append((block, pl.BlockSpec((big, quarter), lambda s, ids, w=w: (out_at(s, w), 0))))
        aliases = {}
        outs = []
        if lead:
            last = lead - 1
            aliases = {len(ins) + k: 2 + k for k in range(3)}
            ins += [(a, ANY) for a in into]
            wide_spec = pl.BlockSpec((share, inner // 2), lambda s, ids: (jnp.minimum(s, last), 0))
            side_spec = pl.BlockSpec((share, LANES), lambda s, ids: (lead + jnp.minimum(s, last), 0))
            outs += [(wide_spec, (lead * share, inner // 2), BF)] * 2 + [(side_spec, (width, LANES), BF)] * 3
        for w in (0, 1):
            spec = pl.BlockSpec((big, quarter), lambda s, ids, w=w: (out_at(s, w), 0))
            outs.append((spec, (rows, quarter), dtypes[w]))
        return run(
            functools.partial(twin_kernel, lead, blocks, len(got)),
            (lead + 2 * blocks,),
            ins,
            outs,
            ids=ids,
            aliases=aliases,
            us=22 if lead else 14,
        )

    first_a, first_b, sent, kept, step = weight_rows(0, normed, inner_parts)
    here = place.astype(jnp.int32).reshape(1)
    own_spec = pl.BlockSpec((big, quarter), lambda i, ids: (i, ids[0]))
    column = pl.BlockSpec((big, 1), lambda i, ids: (i, 0))
    result = run(
        result_kernel,
        (blocks,),
        [(tokens, own_spec), (scale_out, column), (mine, quarter_spec()), (away_got, quarter_spec())],
        [(quarter_spec(), (rows, quarter), BF)],
        ids=here,
        us=4,
    )[0]
    if manual:
        dw_gate = gate_sum.end()
    tall = pl.BlockSpec((1024, LANES), lambda i, *_: (i, 0))
    stat_got = flip(stat, "head", 1)
    small_got = flip(small, "seq", 2)
    if manual:
        got_a = flip(first_a, "seq", 1)
        got_b = flip(first_b, "seq", 1)
        second_a, second_b, sent, kept, step, dn_a, dn_b = twin(0, [], [BF, BF], [sent, kept, step])
    else:
        dn_a, dn_b = twin(0, [], [BF, BF])
    side_got = flip(sent, "head", 1)
    dn_got_a = flip(dn_a, "head", 1)
    dn_got_b = flip(dn_b, "head", 1)
    if manual:
        sum_a = Halving([(second_a, got_a)])
    joined = (pl.BlockSpec((width // 2, 2 * LANES), lambda i: (0, 0)), (width // 2, 2 * LANES), BF)
    rest_first, rest_second = run(
        join_kernel,
        (2,),
        [(kept, tall), (side_got, tall), (step, tall)],
        [joined, joined],
        us=3,
    )
    stat, small = add([(stat, stat_got), (small, small_got)])
    stat_got = flip(stat, "head", 2)
    small_got = flip(small, "seq", 4)
    if manual:
        rest_got = flip(rest_first, "seq", 1)
        sum_b = Halving([(second_b, got_b)])
    (stat,) = add([(stat, stat_got)])
    dn_away, dn_mine = twin(2, [dn_got_a, dn_got_b], [BF, F32])
    dn_away_got = flip(dn_away, "head", 2)
    if manual:
        sum_a.middle()
    (small,) = add([(small, small_got)])
    bit = 8
    while bit < seq_count:
        small = small + flip(small, "seq", bit)
        bit *= 2
    if manual:
        sum_b.middle()
        sum_s = Halving([(rest_second, rest_got)])
    small_pair = small[:, inner:]
    low_half, high_half = small_pair[:, : N // 2], small_pair[:, N // 2 : N]
    pair_kept = jnp.concatenate([low_half, small_pair[:, N : N + N // 2]], 1)
    pair_sent = jnp.concatenate([high_half, small_pair[:, N + N // 2 :]], 1)
    pair_got = flip(pair_sent, "head", 1)
    grad_tokens, norm_sum = run(
        final_kernel,
        (blocks,),
        [
            (tokens, own_spec), (cotangent, own_spec), (scale_in, column), (stat.reshape(rows, 1), column),
            (gain_row, pl.BlockSpec((1, quarter), lambda i, ids: (0, ids[0]))),
            (dn_mine, quarter_spec()), (dn_away_got, quarter_spec()),
        ],
        [
            (quarter_spec(), (rows, quarter), F32),
            (pl.BlockSpec((8, quarter), lambda i, ids: (0, 0)), (8, quarter), F32),
        ],
        ids=here,
        us=6,
    )
    norm_got = flip(norm_sum, "seq", 1)
    if manual:
        sum_s.middle()
    norm_sum = add([(norm_sum, norm_got)])[0]
    norm_got = flip(norm_sum, "seq", 2)
    pair_half = pl.BlockSpec((8, pair_cols), lambda i, *_: (0, 0))
    pair_full = pl.BlockSpec((8, N), lambda i, *_: (0, 0))
    pair_mine, pair_away = run(
        share_kernel,
        one_step,
        [(pair_kept, pair_full), (pair_got, pair_full)],
        [(pair_half, (8, pair_cols), F32)] * 2,
        ids=swap_id,
        us=1,
    )
    pair_got = flip(pair_away, "head", 2)
    norm_sum = add([(norm_sum, norm_got)])[0]
    norm_got = flip(norm_sum, "seq", 4)
    if manual:
        own_rows = (share, pair_cols)
        thin = (pl.BlockSpec(own_rows, lambda i, *_: (0, 0)), own_rows, F32)
        dw_inner, side_mine, side_sent, dw_step = run(
            close_kernel,
            one_step,
            [whole(block) for sum_ in (sum_a, sum_b, sum_s) for block in (sum_.kept, sum_.got)],
            [
                (pl.BlockSpec((share, inner), lambda i, *_: (0, 0)), (share, inner), F32), thin, thin,
                (pl.BlockSpec((share, LANES), lambda i, *_: (0, 0)), (share, LANES), F32),
            ],
            ids=swap_id,
            us=3,
        )
    else:
        dw_out, dw_gate, dw_inner, rest = [
            lax.psum_scatter(block, "seq", scatter_dimension=0, tiled=True).astype(F32)
            for block in (
                out_first,
                held["first"],
                jnp.concatenate([first_a, first_b], 1),
                jnp.concatenate([rest_first, rest_second], 0),
            )
        ]
        dw_out = jnp.transpose(dw_out)
        left, right = rest[:, :pair_cols], rest[:, pair_cols : 2 * pair_cols]
        side_mine, side_sent = jnp.where(swap, right, left), jnp.where(swap, left, right)
        dw_step = rest[:, LANES:]
    side_got = flip(side_sent, "head", 2)
    bit = 8
    while bit < seq_count:
        norm_sum = norm_sum + norm_got
        norm_got = flip(norm_sum, "seq", bit)
        bit *= 2
    shapes = [
        (1, quarter), (4, inner), (1, inner), (4, pair_cols), (1, pair_cols), (1, heads), (1, heads), (1, heads),
        (1, inner), side_mine.shape,
    ]
    outs = run(
        unpack_kernel,
        one_step,
        [whole(a) for a in (small, pair_mine, pair_got, norm_sum, norm_got, side_mine, side_got)],
        [(pl.BlockSpec(shape, lambda i: (0, 0)), shape, F32) for shape in shapes],
        us=1,
    )
    norm_sum, taps_sum, bias_sum, pair_taps, pair_bias, step_sum, decay_sum, skip_sum, gain_sum, dw_pair = outs
    return (
        result,
        grad_tokens,
        norm_sum.reshape(-1),
        dw_gate,
        dw_inner,
        dw_pair,
        dw_step[:, :heads],
        taps_sum,
        pair_taps,
        bias_sum.reshape(-1),
        pair_bias.reshape(-1),
        step_sum.reshape(-1),
        decay_sum.reshape(-1),
        skip_sum.reshape(-1),
        gain_sum.reshape(-1),
        dw_out,
    )


def solution(mesh):
    return jax.shard_map(
        body,
        mesh=mesh,
        in_specs=(
            P("seq", None),
            P("seq"),
            P(),
            P(None, "head"),
            P(None, "head"),
            P(None, "head"),
            P(None, "head"),
            P(None, "head"),
            P(None, "head"),
            P("head"),
            P("head"),
            P("head"),
            P("head"),
            P("head"),
            P("head"),
            P("head", None),
            P("seq", None),
        ),
        out_specs=(
            P("seq", "head"),
            P("seq", "head"),
            P("head"),
            P("seq", "head"),
            P("seq", "head"),
            P("seq", "head"),
            P("seq", "head"),
            P(None, "head"),
            P(None, "head"),
            P("head"),
            P("head"),
            P("head"),
            P("head"),
            P("head"),
            P("head"),
            P("head", "seq"),
        ),
        check_vma=False,
    )
```

```python
import functools

import jax
import jax.numpy as jnp
import numpy as np
from jax import lax
from jax.experimental import pallas as pl
from jax.experimental.pallas import tpu as pltpu
from jax.sharding import PartitionSpec as P

N = 128
HP = 64
DI = 4096
EPS = 1e-05
L = 128
LANES = 128
U = 2
HALO = 16
F32 = jnp.float32
BF = jnp.bfloat16
VMEM_LIMIT = 64 * 1024 * 1024 - 65536
FIRST = (((0,), (0,)), ((), ()))
LAST = (((1,), (1,)), ((), ()))


def dot(a, b):
    return jnp.dot(a, b, preferred_element_type=F32)


def dotg(a, b, dims):
    return lax.dot_general(a, b, dims, preferred_element_type=F32)


def split2(v):
    hi = v.astype(BF)
    return hi, (v - hi.astype(F32)).astype(BF)


def split3(v):
    hi = v.astype(BF)
    rest = v - hi.astype(F32)
    mid = rest.astype(BF)
    return hi, mid, (rest - mid.astype(F32)).astype(BF)


def exact_sum(tri, v):
    hi, mid, lo = split3(v)
    return dot(tri, hi) + dot(tri, mid) + dot(tri, lo)


def expand(v, spread2):
    hi, lo = split2(v)
    return dot(jnp.concatenate([hi, lo], 1), spread2)


def fold8(v):
    return jnp.sum(v.reshape(v.shape[0] // 8, 8, v.shape[1]), axis=0)


def stacked_pair(v, left):
    zero = jnp.zeros_like(v)
    return jnp.concatenate([jnp.where(left, v, zero), jnp.where(left, zero, v)], 0)


def lane_is_left(shape):
    return lax.broadcasted_iota(jnp.int32, shape, 1) < HP


def columns(slab):
    pad = LANES - slab.shape[0]
    return jnp.concatenate([slab, jnp.zeros((pad, L), F32)], 0).T


def mask_of(info, seg_row):
    rows = lax.broadcasted_iota(jnp.int32, (L, L), 0)
    cols = lax.broadcasted_iota(jnp.int32, (L, L), 1)
    linked = (info[:, 0:1] == seg_row) & (rows >= cols)
    return jnp.where(linked, 0.0, -1e30).astype(F32)


def turned(v):
    return v.astype(F32).T.astype(BF)


def sigmoid(v):
    return 0.5 * jnp.tanh(0.5 * v) + 0.5


def chunk_spec(width, place):
    return pl.BlockSpec((U * L, width), lambda c: (place(c), 0))


def slab_spec(rows, width, place, count=U):
    return pl.BlockSpec((count, rows, width), lambda c: (place(c), 0, 0))


class Turn:
    def __init__(self, i, sub):
        self.i, self.sub = i, sub

    def first(self, work):
        if self.i == 0:
            pl.when(pl.program_id(0) == 0)(work)

    def last(self, work):
        if self.i == U - 1:
            pl.when(pl.program_id(0) == pl.num_programs(0) - 1)(work)


def chunked(kernel, kinds, reverse):
    def run_all(*refs):
        for i in range(U):
            sub = U - 1 - i if reverse else i
            views = []
            for n, ref in enumerate(refs):
                kind = kinds[n] if n < len(kinds) else "-"
                if kind == "r":
                    ref = ref.at[pl.ds(sub * L, L), :]
                elif kind == "s":
                    ref = ref.at[pl.ds(sub, 1)]
                views.append(ref)
            kernel(Turn(i, sub), *views)

    return run_all


def whole_spec(shape):
    return pl.BlockSpec(shape, lambda c: (0,) * len(shape))


def ahead(c):
    return c


ANY = pl.BlockSpec(memory_space=pl.ANY)


class Chain:
    def __init__(self):
        self.last = None
        self.factor = 1.0

    def run(self, kernel, grid, ins, outs, after=(), scratch=(), ids=None, aliases=None, us=5.0):
        given = [array for array, _ in ins]
        after = [a for a in list(after) + [self.last] if a is not None and not any(a is g for g in given)]
        lead = 0 if ids is None else 1
        keep_in = lead + len(ins)

        def inner(*refs):
            kernel(*refs[:keep_in], *refs[keep_in + len(after) :])

        result = pl.pallas_call(
            inner,
            grid_spec=pltpu.PrefetchScalarGridSpec(
                num_scalar_prefetch=lead,
                grid=grid,
                in_specs=[spec for _, spec in ins] + [ANY] * len(after),
                out_specs=[spec for spec, _, _ in outs],
                scratch_shapes=list(scratch),
            ),
            out_shape=[jax.ShapeDtypeStruct(shape, dtype) for _, shape, dtype in outs],
            input_output_aliases={lead + i: o for i, o in (aliases or {}).items()},
            compiler_params=pltpu.CompilerParams(
                dimension_semantics=("arbitrary",) * len(grid), vmem_limit_bytes=VMEM_LIMIT
            ),
            cost_estimate=pl.CostEstimate(flops=int(us * self.factor * 1.15e9), bytes_accessed=10**4, transcendentals=0),
        )(*(() if ids is None else (ids,)), *given, *after)
        self.last = min(result, key=lambda r: r.size)
        return result


def whole(array):
    zeros = (0,) * array.ndim
    return array, pl.BlockSpec(array.shape, lambda *_: zeros)


def norm_rows(block, gain):
    t = block.astype(F32)
    scale = lax.rsqrt(jnp.mean(t * t, axis=-1, keepdims=True) + EPS)
    return scale, (t * scale * gain).astype(BF)


def proj_kernel(tokens_ref, gain_ref, w_ref, normed_ref, scale_ref, inner_ref):
    scale, normed = norm_rows(tokens_ref[...], gain_ref[...])
    scale_ref[...] = scale
    normed_ref[...] = normed
    inner_ref[...] = dot(normed, w_ref[...]).astype(BF)


def along(v, k):
    zero = jnp.zeros((1, v.shape[1]), v.dtype)
    if k > 0:
        other = jnp.concatenate([zero, v[:-1]], 0)
        return jnp.concatenate([other[:, L - k :], v[:, : L - k]], 1)
    other = jnp.concatenate([v[1:], zero], 0)
    return jnp.concatenate([v[:, -k:], other[:, :-k]], 1)


def prep_kernel(
    starts_ref, upper_ref, tokens_ref, step_bias_ref, decay_ref, skip_ref, gate_gain_ref, spread_ref,
    info_ref, sent_ref, keep_ref, head_ref, gains_ref,
):
    starts = starts_ref[...].astype(F32)
    seg = dot(starts.astype(BF), upper_ref[...])
    m1 = 1.0 - starts
    m2 = m1 * (1.0 - along(starts, 1))
    m3 = m2 * (1.0 - along(starts, 2))
    seg_last = jnp.broadcast_to(seg[:, L - 1 :], seg.shape)
    one = jnp.ones_like(seg)
    zero = jnp.zeros_like(seg)
    fields = [
        seg, jnp.where(seg == 0, one, zero), jnp.where(seg == seg_last, one, zero), m1, m2, m3,
        along(m1, -1), along(m2, -2), along(m3, -3), jnp.where(seg_last == 0, one, zero),
    ]
    for i in range(16):
        info_ref[:, i, :] = fields[i] if i < len(fields) else zero
    rows = lax.broadcasted_iota(jnp.int32, (HALO, L), 0)
    lanes = lax.broadcasted_iota(jnp.int32, (HALO, L), 1)
    last = jnp.broadcast_to(starts[starts.shape[0] - 1 :, :], (HALO, L))
    later = jnp.sum(jnp.where(lanes > rows + L - HALO, last, 0.0), axis=1, keepdims=True)
    place = lax.broadcasted_iota(jnp.int32, (HALO, 1), 0)
    keep = jnp.where((later == 0) & (place >= HALO - 3), 1.0, 0.0)
    keep_ref[...] = keep
    sent_ref[...] = (tokens_ref[...].astype(F32) * keep).astype(BF)
    heads = step_bias_ref.shape[1]
    head_ref[...] = jnp.zeros_like(head_ref)
    head_ref[0:1, 0:heads] = step_bias_ref[...]
    head_ref[1:2, 0:heads] = -jnp.exp(decay_ref[...])
    head_ref[2:3, 0:heads] = skip_ref[...]
    gains_ref[...] = expand(jnp.broadcast_to(head_ref[2:3, :], (8, LANES)), spread_ref[...])
    gains_ref[1:2, :] = gate_gain_ref[...]


def side_kernel(
    swap_ref, normed_ref, own_ref, one_ref, two_ref, three_ref, w_step_ref, halo_ref, gain_ref, w_ref,
    conv_ref, bias_ref,
    side_ref, halo_out_ref, w_side_ref, taps_ref,
):
    @pl.when(pl.program_id(0) == 0)
    def _():
        width, inner = w_ref.shape
        near = jnp.concatenate([own_ref[...], one_ref[...]], 0)
        far = jnp.concatenate([two_ref[...], three_ref[...]], 0)
        swap = swap_ref[0] != 0
        first = jnp.where(swap, far, near)
        second = jnp.where(swap, near, far)
        w_side_ref[0:N, :] = first[:, :width]
        w_side_ref[N : 2 * N, :] = second[:, :width]
        heads = w_step_ref.shape[0]
        w_side_ref[2 * N : 2 * N + heads, :] = w_step_ref[...]
        w_side_ref[2 * N + heads :, :] = jnp.zeros((LANES - heads, width), BF)
        taps_ref[0:4, :inner] = conv_ref[...]
        taps_ref[4:5, :inner] = bias_ref[...]
        taps_ref[5:8, :inner] = jnp.zeros((3, inner), F32)
        for i, part in enumerate((first, second)):
            extra = part[:, width:].astype(F32).T
            taps_ref[:, inner + i * N : inner + (i + 1) * N] = extra[0:8] + extra[8:16] + extra[16:24]
        _, halo = norm_rows(halo_ref[...], gain_ref[...])
        halo_out_ref[:, :inner] = dot(halo, w_ref[...])
        halo_out_ref[:, inner:] = dotg(halo, w_side_ref[...], LAST)

    side_ref[...] = dotg(normed_ref[...], w_side_ref[...], LAST)


def combine_kernel(
    reverse, first, known, final,
    follows_ref, arrived_ref, state_ref, rows_ref, *rest,
):
    rest = list(rest)
    before_ref = None if first else rest.pop(0)
    factor_ref = rest.pop(0) if known else None
    follows = follows_ref[0] != 0
    n = state_ref.shape[0]
    other = arrived_ref[0:n, :].astype(F32)
    if known:
        factor = factor_ref[2:3, :]
    else:
        extra = arrived_ref[n : n + 3, :].astype(F32)
        factor = extra[0:1] + extra[1:2] + extra[2:3]
    through = rows_ref[0:1, :]
    past = jnp.ones_like(through) if first else rows_ref[1:2, :]
    before = jnp.zeros_like(other) if first else before_ref[...]
    rest.pop(0)[...] = jnp.where(follows, before + past * other, before)
    new_rows = rest.pop(0)
    if first:
        new_rows[...] = jnp.zeros_like(new_rows)
    else:
        new_rows[...] = rows_ref[...]
    product = through * factor
    new_rows[0:1, :] = product
    new_rows[1:2, :] = jnp.where(follows, past * factor, past)
    new_rows[2:3, :] = factor
    if not final:
        state = state_ref[...]
        state = jnp.where(follows, state + through * other, other + factor * state)
        rest.pop(0)[...] = state
        low_ref = rest.pop(0)
        low_ref[0:n, :] = state.astype(BF)
        if not known:
            low_ref[n:, :] = factor_rows(product)


def factor_rows(row):
    hi, mid, lo = split3(row)
    return jnp.concatenate([hi, mid, lo, jnp.zeros((HALO - 3, row.shape[1]), BF)], 0)


def split_kernel(count, _, *refs):
    sent, kept = refs[4 * count :]
    at = 0
    for i in range(count):
        sent_kept, sent_got, kept_kept, kept_got = refs[4 * i : 4 * i + 4]
        cols = slice(at, at + sent_kept.shape[1])
        at = cols.stop
        sent[:, cols] = (sent_kept[...].astype(F32) + sent_got[...].astype(F32)).astype(BF)
        kept[:, cols] = kept_kept[...].astype(F32) + kept_got[...].astype(F32)


def end_kernel(kept, got, *rest):
    total = kept[...] + got[...].astype(F32)
    rest[-1][...] = total.T if rest[-1].shape != total.shape else total


def add_kernel(count, *refs):
    for i in range(count):
        refs[2 * count + i][...] = refs[2 * i][...] + refs[2 * i + 1][...]


def share_kernel(swap_ref, kept_ref, got_ref, mine_ref, sent_ref):
    total = kept_ref[...].astype(F32) + got_ref[...].astype(F32)
    half = total.shape[1] // 2
    left, right = total[:, :half], total[:, half:]
    swap = swap_ref[0] != 0
    mine_ref[...] = jnp.where(swap, right, left)
    sent_ref[...] = jnp.where(swap, left, right).astype(sent_ref.dtype)


def join_kernel(kept_ref, got_ref, step_ref, first_ref, second_ref):
    def write(out_ref):
        out_ref[:, :LANES] = (kept_ref[...].astype(F32) + got_ref[...].astype(F32)).astype(BF)
        out_ref[:, LANES:] = step_ref[...]

    pl.when(pl.program_id(0) == 0)(lambda: write(first_ref))
    pl.when(pl.program_id(0) == 1)(lambda: write(second_ref))


def close_kernel(
    swap_ref, kept_a, got_a, kept_b, got_b, kept_s, got_s, inner_ref, mine_ref, sent_ref, step_ref
):
    half = kept_a.shape[1]
    inner_ref[:, :half] = kept_a[...] + got_a[...].astype(F32)
    inner_ref[:, half:] = kept_b[...] + got_b[...].astype(F32)
    rest = kept_s[...] + got_s[...].astype(F32)
    left, right = rest[:, : LANES // 2], rest[:, LANES // 2 : LANES]
    swap = swap_ref[0] != 0
    mine_ref[...] = jnp.where(swap, right, left)
    sent_ref[...] = jnp.where(swap, left, right)
    step_ref[...] = rest[:, LANES:]


def unpack_kernel(
    small_ref, pair_ref, pair_got, norm_ref, norm_got, side_ref, side_got,
    norm_out, taps_out, bias_out, pair_taps_out, pair_bias_out, step_out, decay_out, skip_out, gain_out, side_out,
):
    inner = taps_out.shape[1]
    heads = step_out.shape[1]
    pair = pair_ref[...] + pair_got[...]
    norm_out[...] = jnp.sum(norm_ref[...] + norm_got[...], axis=0, keepdims=True)
    taps_out[...] = small_ref[0:4, :inner]
    bias_out[...] = small_ref[4:5, :inner]
    gain_out[...] = small_ref[5:6, :inner]
    pair_taps_out[...] = pair[0:4]
    pair_bias_out[...] = pair[4:5]
    skip_out[...] = small_ref[6:7, 0:heads]
    step_out[...] = small_ref[6:7, LANES : LANES + heads]
    decay_out[...] = small_ref[6:7, 2 * LANES : 2 * LANES + heads]
    side_out[...] = side_ref[...] + side_got[...]


def result_kernel(_, tokens_ref, scale_ref, mine_ref, away_ref, out_ref):
    branch = mine_ref[...] + away_ref[...].astype(F32)
    out_ref[...] = (tokens_ref[...].astype(F32) + scale_ref[...] * branch).astype(BF)


def final_kernel(
    _, tokens_ref, cot_ref, scale_ref, stat_ref, gain_ref, mine_ref, away_ref, grad_ref, norm_ref
):
    scale = scale_ref[...]
    scaled = (mine_ref[...] + away_ref[...].astype(F32)) * scale
    tokens = tokens_ref[...].astype(F32)
    factor = scale * scale * stat_ref[...] * (1.0 / (mine_ref.shape[1] * lax.axis_size("head")))
    grad_ref[...] = cot_ref[...].astype(F32) + scaled * gain_ref[...] - tokens * factor

    @pl.when(pl.program_id(0) == 0)
    def _():
        norm_ref[...] = jnp.zeros_like(norm_ref)

    norm_ref[...] += fold8(scaled * tokens)


def fix_kernel(
    raw_ref, side_ref, keep_ref, back_ref, small_ref, small_got_ref, d_in, dside_in, stat_in,
    d_ref, dside_ref, stat_ref, small_out_ref,
):
    small_out_ref[...] = small_ref[...] + small_got_ref[...]
    inner = raw_ref.shape[1]
    pair = 2 * N
    back = jnp.concatenate([jnp.zeros((HALO - 8, inner + pair), F32), back_ref[...]], 0) * keep_ref[...]
    d_ref[...] = (d_in[...].astype(F32) + back[:, :inner]).astype(BF)
    dside_ref[...] = dside_in[...]
    dside_ref[:, :pair] = (dside_in[:, :pair].astype(F32) + back[:, inner:]).astype(BF)
    row = jnp.sum(back[:, :inner] * raw_ref[...].astype(F32), axis=1, keepdims=True)
    row = row + jnp.sum(back[:, inner:] * side_ref[:, :pair].astype(BF).astype(F32), axis=1, keepdims=True)
    tall = jnp.concatenate([jnp.zeros((L - HALO, LANES), F32), jnp.broadcast_to(row, (HALO, LANES))], 0)
    stat_ref[...] = stat_in[...]
    stat_ref[0] += tall.T[0:8, :]


def nn_kernel(x_ref, w_ref, *rest):
    rest[-1][...] = dot(x_ref[...], w_ref[...]).astype(BF)


def nt_kernel(x_ref, w_ref, *rest):
    rest[-1][...] = dotg(x_ref[...], w_ref[...], LAST).astype(BF)


def cols_kernel(_, x_ref, w_ref, out_ref):
    out_ref[...] = dot(x_ref[...], w_ref[...]).astype(out_ref.dtype)


def cols_add_kernel(_, x_ref, w_ref, got_ref, out_ref):
    out_ref[...] = (dot(x_ref[...], w_ref[...]) + got_ref[...].astype(F32)).astype(out_ref.dtype)


def gate_back_kernel(_, x_ref, w_ref, out_ref):
    out_ref[0] = dotg(x_ref[...], w_ref[...], LAST).astype(BF)


def weight_kernel(scaled, count, grown, _, x_ref, *rest):
    x = x_ref[...]
    if scaled:
        x = (x.astype(F32) * rest[0][...]).astype(BF)
        rest = rest[1:]
    outs = rest[count + grown :]
    for y_ref, out_ref in zip(rest[:count], outs):
        total = dotg(x, y_ref[...], FIRST)
        if len(outs) > count and y_ref is rest[count - 1]:
            half = N // 2
            out_ref[...] = jnp.concatenate([total[:, half:N], total[:, N + half : 2 * N]], 1).astype(BF)
            outs[-2][...] = jnp.concatenate([total[:, :half], total[:, N : N + half]], 1).astype(BF)
            outs[-1][...] = total[:, 2 * N :].astype(BF)
        else:
            out_ref[...] = total.astype(BF)


def twin_kernel(lead, blocks, adds, _, *refs):
    refs = list(refs)
    x_ref, d_ref, side_ref, w_ref, v_ref, base_ref = refs[:6]
    got = refs[6 : 6 + adds]
    outs = refs[-2 - (5 if lead else 0) :]
    step = pl.program_id(0)
    if lead:

        @pl.when(step < lead)
        def _():
            x = x_ref[...]
            half = N // 2
            cols = outs[0].shape[1]
            outs[0][...] = dotg(x, d_ref[:, :cols], FIRST).astype(BF)
            outs[1][...] = dotg(x, d_ref[:, cols:], FIRST).astype(BF)
            total = dotg(x, side_ref[...], FIRST)
            outs[2][...] = jnp.concatenate([total[:, half:N], total[:, N + half : 2 * N]], 1).astype(BF)
            outs[3][...] = jnp.concatenate([total[:, :half], total[:, N : N + half]], 1).astype(BF)
            outs[4][...] = total[:, 2 * N :].astype(BF)

    for which in (0, 1):

        @pl.when((step >= lead + which * blocks) & (step < lead + (which + 1) * blocks))
        def _():
            big = base_ref.shape[1]
            rows = pl.ds(pl.multiple_of((step - lead - which * blocks) * big, big), big)
            total = dotg(d_ref[rows, :], w_ref[...], LAST) + dot(side_ref[rows, :], v_ref[...])
            total = total + base_ref[0].astype(F32)
            if adds:
                total = total + got[which][...].astype(F32)
            out = outs[which - 2]
            out[...] = total.astype(out.dtype)


def conv_kernel(
    turn, raw_ref, side_ref, info_ref, halo_ref, taps_ref, head_ref, tri_ref, spread_ref,
    act_ref, pact_ref, dt_ref, cs_ref, state_ref, low_ref, rows_ref, buf, total_ref,
):
    inner = raw_ref.shape[1]
    groups = inner // LANES
    pair = pact_ref.shape[1]
    pair_groups = pair // LANES

    @turn.first
    def _():
        buf[0:8, :] = halo_ref[HALO - 8 :, : inner + pair].astype(BF).astype(F32)
        state_ref[...] = jnp.zeros_like(state_ref)
        total_ref[0:1, :] = jnp.zeros((1, LANES), F32)
        total_ref[1:8, :] = jnp.ones((7, LANES), F32)

    info = columns(info_ref[0])
    masks = [None] + [jnp.broadcast_to(info[:, 2 + k : 3 + k], (L, LANES)) for k in (1, 2, 3)]
    dt = jax.nn.softplus(side_ref[:, pair:] + head_ref[0:1, :])
    dt_ref[...] = dt
    cs = exact_sum(tri_ref[...], dt * head_ref[1:2, :])
    cs_ref[...] = cs
    closing = cs[L - 1 :, :]
    total_ref[0:1, :] += closing
    total_ref[1:2, :] = total_ref[1:2, :] * info[0:1, 9:10]
    tail = jnp.exp(closing - cs) * info[:, 2:3] * dt
    tail_wide = expand(tail, spread_ref[...])
    keep = jnp.exp(closing) * info[0:1, 9:10]
    keep_wide = expand(jnp.broadcast_to(keep, (8, LANES)), spread_ref[...])[0:1, :]
    acts = []
    for j in range(groups + pair_groups):
        cols = slice(j * LANES, (j + 1) * LANES)
        if j < groups:
            raw = raw_ref[:, cols].astype(F32)
        else:
            raw = side_ref[:, (j - groups) * LANES : (j - groups + 1) * LANES].astype(BF).astype(F32)
        buf[8 : 8 + L, cols] = raw
        pre = taps_ref[4:5, cols] + taps_ref[0:1, cols] * raw
        for k in (1, 2, 3):
            pre = pre + taps_ref[k : k + 1, cols] * buf[8 - k : 8 - k + L, cols] * masks[k]
        act = (pre * sigmoid(pre)).astype(BF)
        buf[0:8, cols] = raw[L - 8 :, :]
        if j < groups:
            act_ref[:, cols] = act
        else:
            pact_ref[:, (j - groups) * LANES : (j - groups + 1) * LANES] = act
    key_turned = turned(pact_ref[:, :N])
    for j in range(groups):
        cols = slice(j * LANES, (j + 1) * LANES)
        weighted = (act_ref[:, cols].astype(F32) * tail_wide[:, cols]).astype(BF)
        state_ref[:, cols] = keep_wide[:, cols] * state_ref[:, cols] + dot(key_turned, weighted)

    @turn.last
    def _():
        through = jnp.exp(total_ref[0:1, :]) * total_ref[1:2, :]
        rows_ref[...] = expand(jnp.broadcast_to(through, (8, LANES)), spread_ref[...])
        low_ref[0:N, :] = state_ref[...].astype(BF)
        low_ref[N:, :] = factor_rows(rows_ref[0:1, :])


def out_kernel(
    turn, act_ref, pact_ref, dt_ref, cs_ref, info_ref, gate_ref, dgn_ref, state_in_ref,
    gains_ref, spread_ref,
    mixed_ref, gg_ref, sums_ref, entry_ref, state,
):
    inner = act_ref.shape[1]
    groups = inner // LANES

    @turn.first
    def _():
        state[...] = state_in_ref[...]

    info = columns(info_ref[0])
    mask = mask_of(info, info_ref[0, 0:1, :])
    key = pact_ref[:, :N]
    key_turned = turned(key)
    query = pact_ref[:, N:]
    scores = dotg(query, key, LAST)
    dt = dt_ref[...]
    cs = cs_ref[...]
    cs_rows = cs.T
    closing = cs[L - 1 :, :]
    spread = spread_ref[...]
    dt_wide = expand(dt, spread)
    open_wide = expand(jnp.exp(cs) * info[:, 1:2], spread)
    tail_wide = expand(jnp.exp(closing - cs) * info[:, 2:3], spread)
    keep = jnp.exp(closing) * info[0:1, 9:10]
    keep_wide = expand(jnp.broadcast_to(keep, (8, LANES)), spread)[0:1, :]
    left = lane_is_left((L, LANES))
    square = jnp.zeros((L, LANES), F32)
    cross = jnp.zeros((L, LANES), F32)
    for j in range(groups):
        cols = slice(j * LANES, (j + 1) * LANES)
        x = act_ref[:, cols].astype(F32)
        xd = x * dt_wide[:, cols]
        xd_low = xd.astype(BF)
        weights = []
        for h in (2 * j, 2 * j + 1):
            factor = jnp.exp(cs[:, h : h + 1] - cs_rows[h : h + 1, :] + mask)
            weights.append((scores * factor).astype(BF))
        entry = state[:, cols].astype(BF)
        entry_ref[0, :, cols] = entry
        y = dot(jnp.concatenate(weights, 1), stacked_pair(xd_low, left))
        y = y + open_wide[:, cols] * dot(query, entry)
        mixed = y + gains_ref[0:1, cols] * x
        mixed_ref[:, cols] = mixed.astype(BF)
        gate = gate_ref[:, cols].astype(F32)
        gated = mixed * (gate * sigmoid(gate))
        gg = gated * gains_ref[1:2, cols]
        gg_ref[:, cols] = gg.astype(BF)
        square = square + gated * gated
        cross = cross + gg * dgn_ref[:, cols].astype(F32)
        weighted = (xd * tail_wide[:, cols]).astype(BF)
        state[:, cols] = keep_wide[:, cols] * state[:, cols] + dot(key_turned, weighted)
    lane = lax.broadcasted_iota(jnp.int32, (L, LANES), 1)
    both = jnp.where(
        lane == 0,
        jnp.sum(square, axis=1, keepdims=True),
        jnp.sum(cross, axis=1, keepdims=True),
    )
    sums_ref[0] = both.T[0:2, :]


def gate_kernel(
    turn, mixed_ref, gate_ref, dgn_ref, act_ref, pact_ref, cs_ref, info_ref, near_ref, far_ref, gains_ref, spread_ref,
    dmix_ref, dgate_ref, stat_ref, dstate_ref, low_ref, dgain_ref, dskip_ref,
):
    inner = act_ref.shape[1]
    groups = inner // LANES

    @turn.first
    def _():
        dstate_ref[...] = jnp.zeros_like(dstate_ref)
        dgain_ref[...] = jnp.zeros_like(dgain_ref)
        dskip_ref[...] = jnp.zeros_like(dskip_ref)

    info = columns(info_ref[0])
    both = near_ref[0] + far_ref[0]
    scale_row = lax.rsqrt(both[0:1, :] / DI + EPS)
    coef_row = scale_row * scale_row * scale_row * both[1:2, :] / DI
    stats = columns(jnp.concatenate([scale_row, coef_row, jnp.zeros((6, L), F32)], 0))
    scale = jnp.broadcast_to(stats[:, 0:1], (L, LANES))
    coef = jnp.broadcast_to(stats[:, 1:2], (L, LANES))
    cs = cs_ref[...]
    spread = spread_ref[...]
    open_wide = expand(jnp.exp(cs) * info[:, 1:2], spread)
    keep = jnp.exp(cs[L - 1 :, :]) * info[0:1, 9:10]
    keep_wide = expand(jnp.broadcast_to(keep, (8, LANES)), spread)[0:1, :]
    query_turned = turned(pact_ref[:, N:])
    row = jnp.zeros((L, LANES), F32)
    for j in range(groups):
        cols = slice(j * LANES, (j + 1) * LANES)
        mixed = mixed_ref[:, cols].astype(F32)
        gate = gate_ref[:, cols].astype(F32)
        dgn = dgn_ref[:, cols].astype(F32)
        x = act_ref[:, cols].astype(F32)
        sig = sigmoid(gate)
        act = gate * sig
        gated = mixed * act
        scaled = dgn * scale
        dgain_ref[:, cols] += fold8(scaled * gated)
        dgated = scaled * gains_ref[1:2, cols] - gated * coef
        dmix = dgated * act
        dgate = dgated * mixed * (sig + act * (1.0 - sig))
        dskip_ref[:, cols] += fold8(dmix * x)
        row = row + dgate * gate
        dgate_ref[:, cols] = dgate.astype(BF)
        low = dmix.astype(BF)
        dmix_ref[:, cols] = low
        opened = (low.astype(F32) * open_wide[:, cols]).astype(BF)
        dstate_ref[:, cols] = keep_wide[:, cols] * dstate_ref[:, cols] + dot(query_turned, opened)
    stat_ref[0] = jnp.broadcast_to(jnp.sum(row, axis=1, keepdims=True), (L, LANES)).T[0:8, :]

    @turn.last
    def _():
        low_ref[...] = dstate_ref[...].astype(BF)


def back_kernel(
    grown, final, turn,
    act_ref, pact_ref, dt_ref, cs_ref, info_ref, dmix_ref, entry_ref,
    raw_ref, side_ref, raw_prev_ref, side_prev_ref, halo_ref,
    taps_ref, head_ref, gains_ref, tri_ref, spread_ref, gather_ref,
    dstate_in_ref, carried_in_ref, dtaps_in_ref, dhead_in_ref, dgain_ref, dskip_ref, stat_in_ref, *rest,
):
    rest = list(rest[grown:])
    d_ref, dside_ref, stat_ref, dstate, carried_ref, dtaps_ref, dhead_ref = rest[:7]
    small_ref, dhalo_ref = rest[7:9] if final else (None, None)
    buf, dbuf = rest[-2:]
    inner = act_ref.shape[1]
    groups = inner // LANES
    pair = 2 * N
    wide = inner + pair

    @turn.first
    def _():
        dstate[...] = dstate_in_ref[...]
        dbuf[L:, :] = carried_in_ref[...]
        dtaps_ref[...] = dtaps_in_ref[...]
        dhead_ref[...] = dhead_in_ref[...]

    if turn.sub:
        whole_raw, whole_side = rest[-4], rest[-3]
        start = turn.sub * L - HALO
        buf[0:8, :inner] = whole_raw[start + HALO - 8 : start + HALO, :].astype(F32)
        buf[0:8, inner:] = whole_side[start + HALO - 8 : start + HALO, :pair].astype(BF).astype(F32)
    else:
        near_inner = raw_prev_ref[HALO - 8 :, :].astype(F32)
        near_side = side_prev_ref[HALO - 8 :, :pair].astype(BF).astype(F32)
        if final:
            start = pl.program_id(0) == pl.num_programs(0) - 1
            halo = halo_ref[HALO - 8 :, :wide].astype(BF).astype(F32)
            near_inner = jnp.where(start, halo[:, :inner], near_inner)
            near_side = jnp.where(start, halo[:, inner:], near_side)
        buf[0:8, :inner] = near_inner
        buf[0:8, inner:] = near_side

    info = columns(info_ref[0])
    masks = [None] + [jnp.broadcast_to(info[:, 2 + k : 3 + k], (L, LANES)) for k in (1, 2, 3)]
    afters = [None] + [jnp.broadcast_to(info[:, 5 + k : 6 + k], (L, LANES)) for k in (1, 2, 3)]
    mask = mask_of(info, info_ref[0, 0:1, :])
    key = pact_ref[:, :N]
    query = pact_ref[:, N:]
    query_turned = turned(query)
    scores = dotg(query, key, LAST)
    dt = dt_ref[...]
    cs = cs_ref[...]
    cs_rows = cs.T
    closing = cs[L - 1 :, :]
    spread = spread_ref[...]
    dt_wide = expand(dt, spread)
    open_wide = expand(jnp.exp(cs) * info[:, 1:2], spread)
    tail_wide = expand(jnp.exp(closing - cs) * info[:, 2:3], spread)
    keep = jnp.exp(closing) * info[0:1, 9:10]
    keep_wide = expand(jnp.broadcast_to(keep, (8, LANES)), spread)[0:1, :]
    left = lane_is_left((L, LANES))

    def conv_back(j, raw, dact):
        cols = slice(j * LANES, (j + 1) * LANES)
        buf[8 : 8 + L, cols] = raw
        pre = taps_ref[4:5, cols] + taps_ref[0:1, cols] * raw
        moved = [raw]
        for k in (1, 2, 3):
            moved.append(buf[8 - k : 8 - k + L, cols] * masks[k])
            pre = pre + taps_ref[k : k + 1, cols] * moved[k]
        sig = sigmoid(pre)
        dpre = dact * (sig * (1.0 + pre * (1.0 - sig)))
        for k in range(4):
            dtaps_ref[8 * k : 8 * k + 8, cols] += fold8(dpre * moved[k])
        dtaps_ref[32:40, cols] += fold8(dpre)
        dbuf[0:L, cols] = dpre
        draw = taps_ref[0:1, cols] * dpre
        for k in (1, 2, 3):
            draw = draw + taps_ref[k : k + 1, cols] * dbuf[k : k + L, cols] * afters[k]
        dbuf[L : L + 8, cols] = dpre[0:8, :]
        if j < groups:
            d_ref[:, cols] = draw.astype(BF)
        else:
            dside_ref[:, (j - groups) * LANES : (j - groups + 1) * LANES] = draw.astype(BF)
        return draw * raw

    row = jnp.zeros((L, LANES), F32)
    dscores = jnp.zeros((L, L), F32)
    dkey = jnp.zeros((L, N), F32)
    dquery = jnp.zeros((L, N), F32)
    dcs = jnp.zeros((L, LANES), F32)
    ddt = jnp.zeros((L, LANES), F32)
    dclose = jnp.zeros((8, LANES), F32)
    for j in range(groups):
        cols = slice(j * LANES, (j + 1) * LANES)
        x = act_ref[:, cols].astype(F32)
        xd = (x * dt_wide[:, cols]).astype(BF)
        dm = dmix_ref[:, cols]
        dmf = dm.astype(F32)
        xdf = xd.astype(F32)
        factors = []
        weights = []
        for h in (2 * j, 2 * j + 1):
            factor = jnp.exp(cs[:, h : h + 1] - cs_rows[h : h + 1, :] + mask)
            factors.append(factor)
            weights.append((scores * factor).astype(BF))
        pair_x = stacked_pair(xd, left)
        pair_d = stacked_pair(dm, left)
        dweights = dotg(dm, pair_x, LAST)
        dscores = dscores + dweights[:, :L] * factors[0] + dweights[:, L:] * factors[1]
        y = dot(jnp.concatenate(weights, 1), pair_x)
        dxd = dotg(jnp.concatenate(weights, 0), pair_d, FIRST)
        entry = entry_ref[0, :, cols]
        dst = dstate[:, cols]
        dst_low = dst.astype(BF)
        opened = (dmf * open_wide[:, cols]).astype(BF)
        tailed = (xdf * tail_wide[:, cols]).astype(BF)
        from_state = dot(query, entry)
        to_state = dot(key, dst_low)
        out_part = tailed.astype(F32) * to_state
        diff = dmf * y + opened.astype(F32) * from_state - xdf * dxd - out_part
        dxd = dxd + to_state * tail_wide[:, cols]
        hi, lo = split2(diff)
        gather = gather_ref[cols, :]
        dcs = dcs + dot(hi, gather) + dot(lo, gather)
        ddt = ddt + dot((dxd * x).astype(BF), gather)
        close = fold8(out_part) + keep_wide[:, cols] * fold8(dst * entry.astype(F32))
        hi, lo = split2(close)
        dclose = dclose + dot(hi, gather) + dot(lo, gather)
        dquery = dquery + dotg(opened, entry, LAST)
        dkey = dkey + dotg(tailed, dst_low, LAST)
        dstate[:, cols] = keep_wide[:, cols] * dst + dot(query_turned, opened)
        dx = dxd * dt_wide[:, cols] + gains_ref[0:1, cols] * dmf
        row = row + conv_back(j, raw_ref[:, cols].astype(F32), dx)
    dscores = dscores.astype(BF)
    dquery = dquery + dot(dscores, key)
    dkey = dkey + dotg(dscores, query, FIRST)
    row = row + conv_back(groups, side_ref[:, :N].astype(BF).astype(F32), dkey)
    row = row + conv_back(groups + 1, side_ref[:, N:pair].astype(BF).astype(F32), dquery)
    later = dcs
    hi, mid, lo = split3(later)
    tri = tri_ref[...]
    da = dotg(tri, hi, FIRST) + dotg(tri, mid, FIRST) + dotg(tri, lo, FIRST)
    da = da + jnp.sum(dclose, axis=0, keepdims=True)
    ddt = ddt + head_ref[1:2, :] * da
    step = side_ref[:, pair:]
    dstep = ddt * sigmoid(step + head_ref[0:1, :])
    dhead_ref[0:8, :] += fold8(dstep)
    dhead_ref[8:16, :] += fold8(dt * da)
    dside_ref[:, pair:] = dstep.astype(BF)
    row = row + dstep * step
    stat_ref[0] = stat_in_ref[0] + jnp.broadcast_to(jnp.sum(row, axis=1, keepdims=True), (L, LANES)).T[0:8, :]

    @turn.last
    def _():
        carried_ref[...] = dbuf[L:, :]

    if final:

        @turn.last
        def _():
            for k in range(5):
                small_ref[k : k + 1, :] = jnp.sum(dtaps_ref[8 * k : 8 * k + 8, :], axis=0, keepdims=True)
            small_ref[5:8, :] = jnp.zeros((3, wide), F32)
            small_ref[5:6, :inner] = jnp.sum(dgain_ref[...], axis=0, keepdims=True)
            skip = jnp.broadcast_to(jnp.sum(dskip_ref[...], axis=0, keepdims=True), (8, inner))
            hi, lo = split2(skip)
            skip = dot(hi, gather_ref[...]) + dot(lo, gather_ref[...])
            small_ref[6:7, 0:LANES] = skip[0:1, :]
            small_ref[6:7, LANES : 2 * LANES] = jnp.sum(dhead_ref[0:8, :], axis=0, keepdims=True)
            small_ref[6:7, 2 * LANES : 3 * LANES] = (
                jnp.sum(dhead_ref[8:16, :], axis=0, keepdims=True) * head_ref[1:2, :]
            )
            dhalo_ref[...] = jnp.zeros((8, wide), F32)
            for j in range(groups + 2):
                cols = slice(j * LANES, (j + 1) * LANES)
                for k in (1, 2, 3):
                    reach = dbuf[L : L + 8, cols] * masks[k][0:8, :] * taps_ref[k : k + 1, cols]
                    dhalo_ref[8 - k :, cols] += reach[0:k, :]


def flip(block, axis, bit):
    count = lax.axis_size(axis)
    route = [(i, i ^ bit) for i in range(count)]
    return jax.tree.map(lambda a: lax.ppermute(a, axis, route), block)


def sum_over(block, axis):
    bit = 1
    while bit < lax.axis_size(axis):
        block = block + flip(block, axis, bit)
        bit *= 2
    return block


def shift_over(block, axis, distance):
    devices = range(lax.axis_size(axis))
    route = [(i, i + distance) for i in devices if i + distance in devices]
    return lax.ppermute(block, axis, route)


def body(
    tokens, boundary, norm_gain, w_gate, w_inner, w_pair, w_step, conv_inner, conv_pair,
    bias_inner, bias_pair, step_bias, decay_log, skip_gain, gate_gain, w_output, cotangent,
):
    rows, width = tokens.shape
    inner = w_gate.shape[1]
    heads = w_step.shape[1]
    head_count = lax.axis_size("head")
    place = lax.axis_index("head")
    quarter = width // head_count
    pair_cols = w_pair.shape[1]
    pair = pair_cols * head_count
    wide = inner + pair
    side = pair + LANES
    steps = rows // L
    chain = Chain()
    run = chain.run

    def behind(c):
        return steps // U - 1 - c

    def row_of(v):
        return v.reshape(1, -1)

    head_of = np.arange(inner)[None, :] // HP == np.arange(LANES)[:, None]
    spread2 = jnp.asarray(np.concatenate([head_of, head_of], 0), BF)
    gather = jnp.asarray(head_of.T, BF)
    lower = jnp.asarray(np.tril(np.ones((L, L))), BF)
    upper = jnp.asarray(np.triu(np.ones((L, L))), BF)

    def split_low(v):
        hi, mid, lo = split3(v)
        return [hi, mid, lo]

    swap = (place & 2) != 0

    pair_small = jnp.concatenate([conv_pair, row_of(bias_pair), jnp.zeros((3, pair_cols), F32)], 0).T
    pair_own = jnp.concatenate([w_pair.T, *split_low(pair_small), jnp.zeros((pair_cols, LANES - 24), BF)], 1)
    pair_pieces = [pair_own] + [flip(pair_own, "head", d) for d in (1, 2, 3)]
    gain_row = row_of(norm_gain)

    info_spec = slab_spec(16, L, ahead)
    info_back = slab_spec(16, L, behind)
    one_step = (1,)
    info, sent, keep_tail, head_rows, gains = run(
        prep_kernel,
        one_step,
        [
            whole(boundary.reshape(steps, L)), whole(upper),
            (tokens, pl.BlockSpec((HALO, width), lambda c: (rows // HALO - 1, 0))),
            whole(row_of(step_bias)), whole(row_of(decay_log)), whole(row_of(skip_gain)), whole(row_of(gate_gain)),
            whole(spread2),
        ],
        [
            (whole_spec((steps, 16, L)), (steps, 16, L), F32), (whole_spec((HALO, width)), (HALO, width), BF),
            (whole_spec((HALO, 1)), (HALO, 1), F32), (whole_spec((8, LANES)), (8, LANES), F32),
            (whole_spec((8, inner)), (8, inner), F32),
        ],
        us=2,
    )
    token_halo = shift_over(sent, "seq", 1)

    big = 512
    blocks = rows // big

    def rows_spec(cols, start=0, size=big):
        return pl.BlockSpec((size, cols), lambda i, *_: (i + start, 0))

    def fixed(shape):
        return pl.BlockSpec(shape, lambda i, *_: (0,) * len(shape))

    normed, scale_in, inner_raw = run(
        proj_kernel,
        (blocks,),
        [(tokens, rows_spec(width)), whole(gain_row), whole(w_inner)],
        [
            (rows_spec(width), (rows, width), BF),
            (rows_spec(1), (rows, 1), F32),
            (rows_spec(inner), (rows, inner), BF),
        ],
        us=12,
    )
    halo_shape = (HALO, inner + side)
    side_raw, halo, w_side, taps = run(
        side_kernel,
        (blocks,),
        [(normed, rows_spec(width))]
        + [whole(p) for p in pair_pieces]
        + [whole(w_step.T), whole(token_halo), whole(gain_row), whole(w_inner), whole(conv_inner), whole(row_of(bias_inner))],
        [
            (rows_spec(side), (rows, side), F32),
            (fixed(halo_shape), halo_shape, F32),
            (fixed((side, width)), (side, width), BF),
            (fixed((8, wide)), (8, wide), F32),
        ],
        ids=swap.astype(jnp.int32).reshape(1),
        us=10,
    )

    low_rows = N + HALO
    act, pact, dt, cs, closing, closing_low, through = run(
        chunked(conv_kernel, "rrs-----rrrr", False),
        (steps // U,),
        [
            (inner_raw, chunk_spec(inner, ahead)), (side_raw, chunk_spec(side, ahead)), (info, info_spec),
            whole(halo), whole(taps), whole(head_rows), whole(lower), whole(spread2),
        ],
        [
            (chunk_spec(inner, ahead), (rows, inner), BF), (chunk_spec(pair, ahead), (rows, pair), BF),
            (chunk_spec(LANES, ahead), (rows, LANES), F32), (chunk_spec(LANES, ahead), (rows, LANES), F32),
            (whole_spec((N, inner)), (N, inner), F32), (whole_spec((low_rows, inner)), (low_rows, inner), BF),
            (whole_spec((8, inner)), (8, inner), F32),
        ],
        scratch=[pltpu.VMEM((8 + L, wide), F32), pltpu.VMEM((8, LANES), F32)],
        us=17,
    )

    seq_count = lax.axis_size("seq")
    seq_place = lax.axis_index("seq")

    def exchange(state, low, rows0, known, reverse, between):
        before, row, factors = None, rows0, []
        bit = 1
        while bit < seq_count:
            arrived = flip(low, "seq", bit)
            if between:
                between.pop(0)()
            follows = (seq_place & bit) != 0
            if reverse:
                follows = jnp.logical_not(follows)
            final = bit * 2 >= seq_count
            has = known is not None
            ins = [whole(arrived), whole(state), whole(row)]
            if before is not None:
                ins.append(whole(before))
            if has:
                ins.append(whole(known[len(factors)]))
            big_out = (fixed((N, inner)), (N, inner), F32)
            outs = [big_out, (fixed((8, inner)), (8, inner), F32)]
            if not final:
                height = N if has else low_rows
                outs += [big_out, (fixed((height, inner)), (height, inner), BF)]
            got = run(
                functools.partial(combine_kernel, reverse, before is None, has, final),
                one_step,
                ins,
                outs,
                ids=follows.astype(jnp.int32).reshape(1),
                us=2,
            )
            before, row = got[0], got[1]
            factors.append(row)
            if not final:
                state, low = got[2], got[3]
            bit *= 2
        for work in between:
            work()
        return before, factors

    def product(kernel, x, w, start, size, into):
        out = [] if into is None else [(into, ANY)]
        return run(
            kernel,
            (size,),
            [(x, rows_spec(x.shape[1], start)), whole(w)] + out,
            [(rows_spec(inner, start), (rows, inner), BF)],
            aliases={2: 0} if out else None,
            us=2.9 * size,
        )[0]

    third = max(blocks // 3, 1)
    held = {}

    def gate_one():
        held["gate"] = product(nn_kernel, normed, w_gate, 0, blocks - third, None)

    def gate_two():
        held["gate"] = product(nn_kernel, normed, w_gate, blocks - third, third, held["gate"])
        held["dgn"] = product(nt_kernel, cotangent, w_output, 0, third, None)

    def gate_three():
        held["dgn"] = product(nt_kernel, cotangent, w_output, third, blocks - third, held["dgn"])

    state_in, factors = exchange(closing, closing_low, through, None, False, [gate_one, gate_two, gate_three])
    gate_pre, dgn = held["gate"], held["dgn"]

    mixed, gg, sums, entries = run(
        chunked(out_kernel, "rrrrsrr---rrss", False),
        (steps // U,),
        [
            (act, chunk_spec(inner, ahead)), (pact, chunk_spec(pair, ahead)), (dt, chunk_spec(LANES, ahead)),
            (cs, chunk_spec(LANES, ahead)), (info, info_spec),
            (gate_pre, chunk_spec(inner, ahead)), (dgn, chunk_spec(inner, ahead)),
            whole(state_in), whole(gains), whole(spread2),
        ],
        [
            (chunk_spec(inner, ahead), (rows, inner), BF), (chunk_spec(inner, ahead), (rows, inner), BF),
            (slab_spec(2, L, ahead), (steps, 2, L), F32), (slab_spec(N, inner, ahead), (steps, N, inner), BF),
        ],
        scratch=[pltpu.VMEM((N, inner), F32)],
        us=18,
    )

    order = [place ^ 3, place ^ 1, place ^ 2, place]

    def quarter_spec():
        return pl.BlockSpec((big, quarter), lambda i, ids: (i, 0))

    def out_quarter(which, got, dtype, after=()):
        ins = [
            (gg, pl.BlockSpec((big, inner), lambda i, ids: (i, 0))),
            (w_output, pl.BlockSpec((inner, quarter), lambda i, ids: (0, ids[0]))),
        ]
        if got is not None:
            ins.append((got, quarter_spec()))
        return run(
            cols_kernel if got is None else cols_add_kernel,
            (blocks,),
            ins,
            [(quarter_spec(), (rows, quarter), dtype)],
            after=after,
            ids=order[which].reshape(1),
            us=5,
        )[0]

    sums_core = flip(sums, "head", 1)
    out_a = out_quarter(0, None, BF)
    sums = sums + sums_core
    got_a = flip(out_a, "head", 1)
    sums_x = flip(sums, "head", 2)
    out_b = out_quarter(1, None, BF, [sums_core])
    got_b = flip(out_b, "head", 1)
    scale_out = lax.rsqrt((sums + sums_x)[:, 0, :] / DI + EPS).reshape(rows, 1)

    share = width // seq_count
    manual = seq_count == 8
    half = seq_count // 2
    seq_core = seq_place % 2
    if manual:
        row_ids = [jnp.arange(half) * 2 + (1 - seq_core), jnp.arange(half) * 2 + seq_core]
    else:
        share = 256
        row_ids = [jnp.arange(width // share)]

    def weight_rows(which, x, ys, scale=None, into=()):
        ids = row_ids[which].astype(jnp.int32)
        count = ids.shape[0]
        ins = [(x, pl.BlockSpec((rows, share), lambda i, ids: (0, ids[i])))]
        if scale is not None:
            ins.append(whole(scale))
        outs = []
        lead = count * which
        for y, cols, at in ys:
            ins.append((y, pl.BlockSpec((rows, cols), lambda i, ids, at=at: (0, at))))
            if cols == side:
                spec = pl.BlockSpec((share, LANES), lambda i, ids: (i + lead, 0))
                outs += [(spec, (width, LANES), BF)] * 3
            else:
                outs.append((pl.BlockSpec((share, cols), lambda i, ids: (i, 0)), (count * share, cols), BF))
        aliases = {len(ins) + k: len(outs) - 3 + k for k in range(len(into))}
        return run(
            functools.partial(weight_kernel, scale is not None, len(ys), len(into)),
            (count,),
            ins + [(a, ANY) for a in into],
            outs,
            ids=ids,
            aliases=aliases,
            us=8,
        )

    z = seq_place // 2

    class Halving:
        def __init__(self, pieces):
            low = z % 2
            ids = jnp.stack([1 - low, 3 - low, low, 2 + low]).astype(jnp.int32)
            ins = []
            for kept, got in pieces:
                cols = kept.shape[1]
                for first in (0, 2):
                    spec = pl.BlockSpec((share, cols), lambda i, ids, f=first: (ids[f + i], 0))
                    ins += [(kept, spec), (got, spec)]
            self.cols = sum(kept.shape[1] for kept, _ in pieces)
            self.count = len(pieces)
            out = pl.BlockSpec((share, self.cols), lambda i, ids: (i, 0))
            sent, self.kept = run(
                functools.partial(split_kernel, self.count),
                (2,),
                ins,
                [(out, (2 * share, self.cols), BF), (out, (2 * share, self.cols), F32)],
                ids=ids,
                us=3,
            )
            self.got = flip(sent, "seq", 2)

        def middle(self):
            high = z // 2
            ids = jnp.stack([1 - high, high]).astype(jnp.int32)
            part = share // 2
            ins = []
            for w in (0, 1):
                spec = pl.BlockSpec((part, self.cols), lambda i, ids, w=w: (ids[w] * 2 + i, 0))
                ins += [(self.kept, spec), (self.got, spec)]
            out = pl.BlockSpec((part, self.cols), lambda i, ids: (i, 0))
            sent, self.kept = run(
                functools.partial(split_kernel, 1),
                (2,),
                ins,
                [(out, (share, self.cols), BF), (out, (share, self.cols), F32)],
                ids=ids,
                us=2,
            )
            self.got = flip(sent, "seq", 4)

        def end(self, into=None, place=0, total=1, turned=False):
            if turned:
                shape = block = (self.cols, share)
            else:
                shape, block = (share, self.cols * total), (share, self.cols)
            ins = [whole(self.kept), whole(self.got)] + ([] if into is None else [(into, ANY)])
            return run(
                end_kernel,
                one_step,
                ins,
                [(pl.BlockSpec(block, lambda i: (0, place)), shape, F32)],
                aliases=None if into is None else {2: 0},
                us=2,
            )[0]

    (out_first,) = weight_rows(0, cotangent, [(gg, inner, 0)], scale_out)
    if manual:
        out_got = flip(out_first, "seq", 1)
    away = out_quarter(2, got_a, BF)
    away_got = flip(away, "head", 2)
    mine = out_quarter(3, got_b, F32)
    if manual:
        (out_second,) = weight_rows(1, cotangent, [(gg, inner, 0)], scale_out)

    dmix, dgate, stat, dstate_local, dstate_low, dgain, dskip = run(
        chunked(gate_kernel, "rrrrrrsss--" + "rrs", True),
        (steps // U,),
        [
            (mixed, chunk_spec(inner, behind)), (gate_pre, chunk_spec(inner, behind)), (dgn, chunk_spec(inner, behind)),
            (act, chunk_spec(inner, behind)), (pact, chunk_spec(pair, behind)), (cs, chunk_spec(LANES, behind)),
            (info, info_back), (sums, slab_spec(2, L, behind)), (sums_x, slab_spec(2, L, behind)),
            whole(gains), whole(spread2),
        ],
        [
            (chunk_spec(inner, behind), (rows, inner), BF), (chunk_spec(inner, behind), (rows, inner), BF),
            (slab_spec(8, L, behind), (steps, 8, L), F32), (whole_spec((N, inner)), (N, inner), F32),
            (whole_spec((N, inner)), (N, inner), BF),
            (whole_spec((8, inner)), (8, inner), F32), (whole_spec((8, inner)), (8, inner), F32),
        ],
        us=17,
    )

    order_ids = jnp.stack(order).astype(jnp.int32)

    def gate_first():
        held["first"] = weight_rows(0, normed, [(dgate, inner, 0)])[0]

    def gate_second():
        if manual:
            held["got"] = flip(held["first"], "seq", 1)
            held["second"] = weight_rows(1, normed, [(dgate, inner, 0)])[0]

    def gate_third():
        held["dn"] = run(
            gate_back_kernel,
            (4, blocks),
            [
                (dgate, pl.BlockSpec((big, inner), lambda n, i, ids: (i, 0))),
                (w_gate, pl.BlockSpec((quarter, inner), lambda n, i, ids: (ids[n], 0))),
            ],
            [(pl.BlockSpec((1, big, quarter), lambda n, i, ids: (n, i, 0)), (4, rows, quarter), BF)],
            ids=order_ids,
            us=17,
        )[0]

    dstate, _ = exchange(
        dstate_local, dstate_low, through, factors, True, [gate_first, gate_second, gate_third]
    )
    dn_gate = held["dn"]

    def back_chunks(count, final):
        kinds = "rrrrsrsrr" + "-" * 15 + "s" + "-" * count + "rrs"
        kernel = functools.partial(back_kernel, count, final)

        def run_all(*refs):
            chunked(lambda turn, *views: kernel(turn, *views[:-2], refs[7], refs[8], *views[-2:]), kinds, True)(*refs)

        return run_all

    parts = 3 if steps % (3 * U) == 0 else 1
    each = steps // parts // U
    carried = jnp.zeros((8, wide), F32)
    dtaps = jnp.zeros((40, wide), F32)
    dhead = jnp.zeros((16, LANES), F32)
    d_inner = d_side = small = dhalo = None
    if manual:
        out_sum = Halving([(out_second, out_got)])
    for part in range(parts):
        first = steps // U - 1 - part * each

        def at(c, first=first):
            return first - c

        def near_end(c, at=at):
            return jnp.maximum(at(c) * (U * L // HALO) - 1, 0)

        final = part == parts - 1
        if manual and part == 1:
            out_sum.middle()
        if manual and part == 2:
            dw_out = out_sum.end(turned=True)
            gate_sum = Halving([(held["second"], held["got"])])
        grown = [] if d_inner is None else [(d_inner, ANY), (d_side, ANY)]
        state_specs = [
            (whole_spec((N, inner)), (N, inner), F32), (whole_spec((8, wide)), (8, wide), F32),
            (whole_spec((40, wide)), (40, wide), F32), (whole_spec((16, LANES)), (16, LANES), F32),
        ]
        if final:
            state_specs += [(whole_spec((8, wide)), (8, wide), F32)] * 2
        ins = [
            (act, chunk_spec(inner, at)), (pact, chunk_spec(pair, at)), (dt, chunk_spec(LANES, at)),
            (cs, chunk_spec(LANES, at)), (info, slab_spec(16, L, at)),
            (dmix, chunk_spec(inner, at)), (entries, slab_spec(N, inner, at)),
            (inner_raw, chunk_spec(inner, at)), (side_raw, chunk_spec(side, at)),
            (inner_raw, pl.BlockSpec((HALO, inner), lambda c, p=near_end: (p(c), 0))),
            (side_raw, pl.BlockSpec((HALO, side), lambda c, p=near_end: (p(c), 0))),
            whole(halo), whole(taps), whole(head_rows), whole(gains), whole(lower), whole(spread2), whole(gather),
            whole(dstate), whole(carried), whole(dtaps), whole(dhead), whole(dgain), whole(dskip),
            (stat, slab_spec(8, L, at)), *grown,
        ]
        aliases = {24: 2}
        if grown:
            aliases.update({25: 0, 26: 1})
        got = run(
            back_chunks(len(grown), final),
            (each,),
            ins,
            [
                (chunk_spec(inner, at), (rows, inner), BF), (chunk_spec(side, at), (rows, side), BF),
                (slab_spec(8, L, at), (steps, 8, L), F32), *state_specs,
            ],
            after=[away_got] if part == min(1, parts - 1) else [],
            scratch=[pltpu.VMEM((8 + L, wide), F32), pltpu.VMEM((L + 8, wide), F32)],
            aliases=aliases,
            us=64 / parts,
        )
        d_inner, d_side, stat, dstate, carried, dtaps, dhead = got[:7]
        if final:
            small, dhalo = got[7:]

    if manual:
        gate_sum.middle()
    returned = shift_over(dhalo, "seq", -1)
    small_got = flip(small, "seq", 1)

    def last_rows(cols):
        return pl.BlockSpec((HALO, cols), lambda c: (rows // HALO - 1, 0))

    last_slab = slab_spec(8, L, lambda c: steps - 1, 1)
    d_inner, d_side, stat, small = run(
        fix_kernel,
        one_step,
        [
            (inner_raw, last_rows(inner)), (side_raw, last_rows(side)), whole(keep_tail), whole(returned),
            whole(small), whole(small_got),
            (d_inner, last_rows(inner)), (d_side, last_rows(side)), (stat, last_slab),
        ],
        [
            (last_rows(inner), (rows, inner), BF), (last_rows(side), (rows, side), BF), (last_slab, (steps, 8, L), F32),
            (whole_spec((8, wide)), (8, wide), F32),
        ],
        aliases={6: 0, 7: 1, 8: 2},
        us=2,
    )

    def add(pairs):
        return run(
            functools.partial(add_kernel, len(pairs)),
            one_step,
            [whole(a) for pair_ in pairs for a in pair_],
            [(pl.BlockSpec(a.shape, lambda i, n=a.ndim: (0,) * n), a.shape, a.dtype) for a, _ in pairs],
            us=1,
        )

    half_inner = inner // 2
    swap_id = swap.astype(jnp.int32).reshape(1)
    inner_parts = [(d_inner, half_inner, 0), (d_inner, half_inner, 1), (d_side, side, 0)]

    swap_id = swap.astype(jnp.int32).reshape(1)
    stat = stat[:, 0, :]

    def twin(pair_at, got, dtypes, into=None):
        lead = half if into is not None else 0
        ids = [order[pair_at], order[pair_at + 1]]
        ids = jnp.concatenate([jnp.stack(ids)] + ([row_ids[1]] if lead else [])).astype(jnp.int32)

        def which(s):
            return jnp.clip((s - lead) // blocks, 0, 1)

        def row(s):
            return jnp.where(s < lead, 0, (s - lead) % blocks)

        def x_at(s, ids):
            return (0, ids[2 + jnp.minimum(s, lead - 1)]) if lead else (0, 0)

        def out_at(s, w):
            return jnp.clip(s - lead - w * blocks, 0, blocks - 1)

        ins = [
            (normed, pl.BlockSpec((rows if lead else 256, 256), x_at)),
            whole(d_inner), whole(d_side),
            (w_inner, pl.BlockSpec((quarter, inner), lambda s, ids: (ids[which(s)], 0))),
            (w_side, pl.BlockSpec((side, quarter), lambda s, ids: (0, ids[which(s)]))),
            (dn_gate, pl.BlockSpec((1, big, quarter), lambda s, ids: (pair_at + which(s), row(s), 0))),
        ]
        for w, block in enumerate(got):
            ins.append((block, pl.BlockSpec((big, quarter), lambda s, ids, w=w: (out_at(s, w), 0))))
        aliases = {}
        outs = []
        if lead:
            last = lead - 1
            aliases = {len(ins) + k: 2 + k for k in range(3)}
            ins += [(a, ANY) for a in into]
            wide_spec = pl.BlockSpec((share, inner // 2), lambda s, ids: (jnp.minimum(s, last), 0))
            side_spec = pl.BlockSpec((share, LANES), lambda s, ids: (lead + jnp.minimum(s, last), 0))
            outs += [(wide_spec, (lead * share, inner // 2), BF)] * 2 + [(side_spec, (width, LANES), BF)] * 3
        for w in (0, 1):
            spec = pl.BlockSpec((big, quarter), lambda s, ids, w=w: (out_at(s, w), 0))
            outs.append((spec, (rows, quarter), dtypes[w]))
        return run(
            functools.partial(twin_kernel, lead, blocks, len(got)),
            (lead + 2 * blocks,),
            ins,
            outs,
            ids=ids,
            aliases=aliases,
            us=22 if lead else 14,
        )

    first_a, first_b, sent, kept, step = weight_rows(0, normed, inner_parts)
    here = place.astype(jnp.int32).reshape(1)
    own_spec = pl.BlockSpec((big, quarter), lambda i, ids: (i, ids[0]))
    column = pl.BlockSpec((big, 1), lambda i, ids: (i, 0))
    result = run(
        result_kernel,
        (blocks,),
        [(tokens, own_spec), (scale_out, column), (mine, quarter_spec()), (away_got, quarter_spec())],
        [(quarter_spec(), (rows, quarter), BF)],
        ids=here,
        us=4,
    )[0]
    if manual:
        dw_gate = gate_sum.end()
    tall = pl.BlockSpec((1024, LANES), lambda i, *_: (i, 0))
    stat_got = flip(stat, "head", 1)
    small_got = flip(small, "seq", 2)
    if manual:
        got_a = flip(first_a, "seq", 1)
        got_b = flip(first_b, "seq", 1)
        second_a, second_b, sent, kept, step, dn_a, dn_b = twin(0, [], [BF, BF], [sent, kept, step])
    else:
        dn_a, dn_b = twin(0, [], [BF, BF])
    side_got = flip(sent, "head", 1)
    dn_got_a = flip(dn_a, "head", 1)
    dn_got_b = flip(dn_b, "head", 1)
    if manual:
        sum_a = Halving([(second_a, got_a)])
    joined = (pl.BlockSpec((width // 2, 2 * LANES), lambda i: (0, 0)), (width // 2, 2 * LANES), BF)
    rest_first, rest_second = run(
        join_kernel,
        (2,),
        [(kept, tall), (side_got, tall), (step, tall)],
        [joined, joined],
        us=3,
    )
    stat, small = add([(stat, stat_got), (small, small_got)])
    stat_got = flip(stat, "head", 2)
    small_got = flip(small, "seq", 4)
    if manual:
        rest_got = flip(rest_first, "seq", 1)
    (stat,) = add([(stat, stat_got)])
    dn_away, dn_mine = twin(2, [dn_got_a, dn_got_b], [BF, F32])
    dn_away_got = flip(dn_away, "head", 2)
    if manual:
        sum_a.middle()
        sum_b = Halving([(second_b, got_b)])
        sum_s = Halving([(rest_second, rest_got)])
    (small,) = add([(small, small_got)])
    bit = 8
    while bit < seq_count:
        small = small + flip(small, "seq", bit)
        bit *= 2
    if manual:
        sum_b.middle()
    small_pair = small[:, inner:]
    low_half, high_half = small_pair[:, : N // 2], small_pair[:, N // 2 : N]
    pair_kept = jnp.concatenate([low_half, small_pair[:, N : N + N // 2]], 1)
    pair_sent = jnp.concatenate([high_half, small_pair[:, N + N // 2 :]], 1)
    pair_got = flip(pair_sent, "head", 1)
    grad_tokens, norm_sum = run(
        final_kernel,
        (blocks,),
        [
            (tokens, own_spec), (cotangent, own_spec), (scale_in, column), (stat.reshape(rows, 1), column),
            (gain_row, pl.BlockSpec((1, quarter), lambda i, ids: (0, ids[0]))),
            (dn_mine, quarter_spec()), (dn_away_got, quarter_spec()),
        ],
        [
            (quarter_spec(), (rows, quarter), F32),
            (pl.BlockSpec((8, quarter), lambda i, ids: (0, 0)), (8, quarter), F32),
        ],
        ids=here,
        us=6,
    )
    norm_got = flip(norm_sum, "seq", 1)
    if manual:
        sum_s.middle()
    norm_sum = add([(norm_sum, norm_got)])[0]
    norm_got = flip(norm_sum, "seq", 2)
    pair_half = pl.BlockSpec((8, pair_cols), lambda i, *_: (0, 0))
    pair_full = pl.BlockSpec((8, N), lambda i, *_: (0, 0))
    pair_mine, pair_away = run(
        share_kernel,
        one_step,
        [(pair_kept, pair_full), (pair_got, pair_full)],
        [(pair_half, (8, pair_cols), F32)] * 2,
        ids=swap_id,
        us=1,
    )
    pair_got = flip(pair_away, "head", 2)
    norm_sum = add([(norm_sum, norm_got)])[0]
    norm_got = flip(norm_sum, "seq", 4)
    if manual:
        own_rows = (share, pair_cols)
        thin = (pl.BlockSpec(own_rows, lambda i, *_: (0, 0)), own_rows, F32)
        dw_inner, side_mine, side_sent, dw_step = run(
            close_kernel,
            one_step,
            [whole(block) for sum_ in (sum_a, sum_b, sum_s) for block in (sum_.kept, sum_.got)],
            [
                (pl.BlockSpec((share, inner), lambda i, *_: (0, 0)), (share, inner), F32), thin, thin,
                (pl.BlockSpec((share, LANES), lambda i, *_: (0, 0)), (share, LANES), F32),
            ],
            ids=swap_id,
            us=3,
        )
    else:
        dw_out, dw_gate, dw_inner, rest = [
            lax.psum_scatter(block, "seq", scatter_dimension=0, tiled=True).astype(F32)
            for block in (
                out_first,
                held["first"],
                jnp.concatenate([first_a, first_b], 1),
                jnp.concatenate([rest_first, rest_second], 0),
            )
        ]
        dw_out = jnp.transpose(dw_out)
        left, right = rest[:, :pair_cols], rest[:, pair_cols : 2 * pair_cols]
        side_mine, side_sent = jnp.where(swap, right, left), jnp.where(swap, left, right)
        dw_step = rest[:, LANES:]
    side_got = flip(side_sent, "head", 2)
    bit = 8
    while bit < seq_count:
        norm_sum = norm_sum + norm_got
        norm_got = flip(norm_sum, "seq", bit)
        bit *= 2
    shapes = [
        (1, quarter), (4, inner), (1, inner), (4, pair_cols), (1, pair_cols), (1, heads), (1, heads), (1, heads),
        (1, inner), side_mine.shape,
    ]
    outs = run(
        unpack_kernel,
        one_step,
        [whole(a) for a in (small, pair_mine, pair_got, norm_sum, norm_got, side_mine, side_got)],
        [(pl.BlockSpec(shape, lambda i: (0, 0)), shape, F32) for shape in shapes],
        us=1,
    )
    norm_sum, taps_sum, bias_sum, pair_taps, pair_bias, step_sum, decay_sum, skip_sum, gain_sum, dw_pair = outs
    return (
        result,
        grad_tokens,
        norm_sum.reshape(-1),
        dw_gate,
        dw_inner,
        dw_pair,
        dw_step[:, :heads],
        taps_sum,
        pair_taps,
        bias_sum.reshape(-1),
        pair_bias.reshape(-1),
        step_sum.reshape(-1),
        decay_sum.reshape(-1),
        skip_sum.reshape(-1),
        gain_sum.reshape(-1),
        dw_out,
    )


def solution(mesh):
    return jax.shard_map(
        body,
        mesh=mesh,
        in_specs=(
            P("seq", None),
            P("seq"),
            P(),
            P(None, "head"),
            P(None, "head"),
            P(None, "head"),
            P(None, "head"),
            P(None, "head"),
            P(None, "head"),
            P("head"),
            P("head"),
            P("head"),
            P("head"),
            P("head"),
            P("head"),
            P("head", None),
            P("seq", None),
        ),
        out_specs=(
            P("seq", "head"),
            P("seq", "head"),
            P("head"),
            P("seq", "head"),
            P("seq", "head"),
            P("seq", "head"),
            P("seq", "head"),
            P(None, "head"),
            P(None, "head"),
            P("head"),
            P("head"),
            P("head"),
            P("head"),
            P("head"),
            P("head"),
            P("head", "seq"),
        ),
        check_vma=False,
    )
```

```python
import functools

import jax
import jax.numpy as jnp
import numpy as np
from jax import lax
from jax.experimental import pallas as pl
from jax.experimental.pallas import tpu as pltpu
from jax.sharding import PartitionSpec as P

N = 128
HP = 64
DI = 4096
EPS = 1e-05
L = 128
LANES = 128
HALO = 16
F32 = jnp.float32
BF = jnp.bfloat16
VMEM_LIMIT = 64 * 1024 * 1024 - 65536
FIRST = (((0,), (0,)), ((), ()))
LAST = (((1,), (1,)), ((), ()))


def dot(a, b):
    return jnp.dot(a, b, preferred_element_type=F32)


def dotg(a, b, dims):
    return lax.dot_general(a, b, dims, preferred_element_type=F32)


def split2(v):
    hi = v.astype(BF)
    return hi, (v - hi.astype(F32)).astype(BF)


def split3(v):
    hi = v.astype(BF)
    rest = v - hi.astype(F32)
    mid = rest.astype(BF)
    return hi, mid, (rest - mid.astype(F32)).astype(BF)


def exact_sum(tri, v):
    hi, mid, lo = split3(v)
    return dot(tri, hi) + dot(tri, mid) + dot(tri, lo)


def expand(v, spread2):
    hi, lo = split2(v)
    return dot(jnp.concatenate([hi, lo], 1), spread2)


def fold8(v):
    return jnp.sum(v.reshape(v.shape[0] // 8, 8, v.shape[1]), axis=0)


def stacked_pair(v, left):
    zero = jnp.zeros_like(v)
    return jnp.concatenate([jnp.where(left, v, zero), jnp.where(left, zero, v)], 0)


def lane_is_left(shape):
    return lax.broadcasted_iota(jnp.int32, shape, 1) < HP


def columns(slab):
    pad = LANES - slab.shape[0]
    return jnp.concatenate([slab, jnp.zeros((pad, L), F32)], 0).T


def mask_of(info, seg_row):
    rows = lax.broadcasted_iota(jnp.int32, (L, L), 0)
    cols = lax.broadcasted_iota(jnp.int32, (L, L), 1)
    linked = (info[:, 0:1] == seg_row) & (rows >= cols)
    return jnp.where(linked, 0.0, -1e30).astype(F32)


def turned(v):
    return v.astype(F32).T.astype(BF)


def sigmoid(v):
    return 0.5 * jnp.tanh(0.5 * v) + 0.5


class Place:
    def __init__(self, u, at):
        self.u, self.at = u, at


def chunk_spec(width, place):
    return pl.BlockSpec((place.u * L, width), lambda c: (place.at(c), 0))


def slab_spec(rows, width, place):
    return pl.BlockSpec((place.u, rows, width), lambda c: (place.at(c), 0, 0))


class Turn:
    def __init__(self, i, sub, u):
        self.i, self.sub, self.u = i, sub, u

    def first(self, work):
        if self.i == 0:
            pl.when(pl.program_id(0) == 0)(work)

    def last(self, work):
        if self.i == self.u - 1:
            pl.when(pl.program_id(0) == pl.num_programs(0) - 1)(work)


def chunked(kernel, kinds, reverse, u):
    def run_all(*refs):
        for i in range(u):
            sub = u - 1 - i if reverse else i
            views = []
            for n, ref in enumerate(refs):
                kind = kinds[n] if n < len(kinds) else "-"
                if kind == "r":
                    ref = ref.at[pl.ds(sub * L, L), :]
                elif kind == "s":
                    ref = ref.at[pl.ds(sub, 1)]
                views.append(ref)
            kernel(Turn(i, sub, u), *views)

    return run_all


def whole_spec(shape):
    return pl.BlockSpec(shape, lambda c: (0,) * len(shape))


ANY = pl.BlockSpec(memory_space=pl.ANY)


class Chain:
    def __init__(self):
        self.last = None
        self.factor = 1.0

    def run(self, kernel, grid, ins, outs, after=(), scratch=(), ids=None, aliases=None, us=5.0):
        given = [array for array, _ in ins]
        after = [a for a in list(after) + [self.last] if a is not None and not any(a is g for g in given)]
        lead = 0 if ids is None else 1
        keep_in = lead + len(ins)

        def inner(*refs):
            kernel(*refs[:keep_in], *refs[keep_in + len(after) :])

        result = pl.pallas_call(
            inner,
            grid_spec=pltpu.PrefetchScalarGridSpec(
                num_scalar_prefetch=lead,
                grid=grid,
                in_specs=[spec for _, spec in ins] + [ANY] * len(after),
                out_specs=[spec for spec, _, _ in outs],
                scratch_shapes=list(scratch),
            ),
            out_shape=[jax.ShapeDtypeStruct(shape, dtype) for _, shape, dtype in outs],
            input_output_aliases={lead + i: o for i, o in (aliases or {}).items()},
            compiler_params=pltpu.CompilerParams(
                dimension_semantics=("arbitrary",) * len(grid), vmem_limit_bytes=VMEM_LIMIT
            ),
            cost_estimate=pl.CostEstimate(flops=int(us * self.factor * 1.15e9), bytes_accessed=10**4, transcendentals=0),
        )(*(() if ids is None else (ids,)), *given, *after)
        self.last = min(result, key=lambda r: r.size)
        return result


def whole(array):
    zeros = (0,) * array.ndim
    return array, pl.BlockSpec(array.shape, lambda *_: zeros)


def norm_rows(block, gain):
    t = block.astype(F32)
    scale = lax.rsqrt(jnp.mean(t * t, axis=-1, keepdims=True) + EPS)
    return scale, (t * scale * gain).astype(BF)


def proj_kernel(tokens_ref, gain_ref, w_ref, normed_ref, scale_ref, inner_ref):
    scale, normed = norm_rows(tokens_ref[...], gain_ref[...])
    scale_ref[...] = scale
    normed_ref[...] = normed
    inner_ref[...] = dot(normed, w_ref[...]).astype(BF)


def along(v, k):
    zero = jnp.zeros((1, v.shape[1]), v.dtype)
    if k > 0:
        other = jnp.concatenate([zero, v[:-1]], 0)
        return jnp.concatenate([other[:, L - k :], v[:, : L - k]], 1)
    other = jnp.concatenate([v[1:], zero], 0)
    return jnp.concatenate([v[:, -k:], other[:, :-k]], 1)


def prep_kernel(
    starts_ref, upper_ref, tokens_ref, step_bias_ref, decay_ref, skip_ref, gate_gain_ref, spread_ref,
    info_ref, sent_ref, keep_ref, head_ref, gains_ref,
):
    starts = starts_ref[...].astype(F32)
    seg = dot(starts.astype(BF), upper_ref[...])
    m1 = 1.0 - starts
    m2 = m1 * (1.0 - along(starts, 1))
    m3 = m2 * (1.0 - along(starts, 2))
    seg_last = jnp.broadcast_to(seg[:, L - 1 :], seg.shape)
    one = jnp.ones_like(seg)
    zero = jnp.zeros_like(seg)
    fields = [
        seg, jnp.where(seg == 0, one, zero), jnp.where(seg == seg_last, one, zero), m1, m2, m3,
        along(m1, -1), along(m2, -2), along(m3, -3), jnp.where(seg_last == 0, one, zero),
    ]
    for i in range(16):
        info_ref[:, i, :] = fields[i] if i < len(fields) else zero
    rows = lax.broadcasted_iota(jnp.int32, (HALO, L), 0)
    lanes = lax.broadcasted_iota(jnp.int32, (HALO, L), 1)
    last = jnp.broadcast_to(starts[starts.shape[0] - 1 :, :], (HALO, L))
    later = jnp.sum(jnp.where(lanes > rows + L - HALO, last, 0.0), axis=1, keepdims=True)
    place = lax.broadcasted_iota(jnp.int32, (HALO, 1), 0)
    keep = jnp.where((later == 0) & (place >= HALO - 3), 1.0, 0.0)
    keep_ref[...] = keep
    sent_ref[...] = (tokens_ref[...].astype(F32) * keep).astype(BF)
    heads = step_bias_ref.shape[1]
    head_ref[...] = jnp.zeros_like(head_ref)
    head_ref[0:1, 0:heads] = step_bias_ref[...]
    head_ref[1:2, 0:heads] = -jnp.exp(decay_ref[...])
    head_ref[2:3, 0:heads] = skip_ref[...]
    gains_ref[...] = expand(jnp.broadcast_to(head_ref[2:3, :], (8, LANES)), spread_ref[...])
    gains_ref[1:2, :] = gate_gain_ref[...]


def side_kernel(
    swap_ref, normed_ref, own_ref, one_ref, two_ref, three_ref, w_step_ref, halo_ref, gain_ref, w_ref,
    conv_ref, bias_ref,
    side_ref, halo_out_ref, w_side_ref, taps_ref,
):
    @pl.when(pl.program_id(0) == 0)
    def _():
        width, inner = w_ref.shape
        near = jnp.concatenate([own_ref[...], one_ref[...]], 0)
        far = jnp.concatenate([two_ref[...], three_ref[...]], 0)
        swap = swap_ref[0] != 0
        first = jnp.where(swap, far, near)
        second = jnp.where(swap, near, far)
        w_side_ref[0:N, :] = first[:, :width]
        w_side_ref[N : 2 * N, :] = second[:, :width]
        heads = w_step_ref.shape[0]
        w_side_ref[2 * N : 2 * N + heads, :] = w_step_ref[...]
        w_side_ref[2 * N + heads :, :] = jnp.zeros((LANES - heads, width), BF)
        taps_ref[0:4, :inner] = conv_ref[...]
        taps_ref[4:5, :inner] = bias_ref[...]
        taps_ref[5:8, :inner] = jnp.zeros((3, inner), F32)
        for i, part in enumerate((first, second)):
            extra = part[:, width:].astype(F32).T
            taps_ref[:, inner + i * N : inner + (i + 1) * N] = extra[0:8] + extra[8:16] + extra[16:24]
        _, halo = norm_rows(halo_ref[...], gain_ref[...])
        halo_out_ref[:, :inner] = dot(halo, w_ref[...])
        halo_out_ref[:, inner:] = dotg(halo, w_side_ref[...], LAST)

    side_ref[...] = dotg(normed_ref[...], w_side_ref[...], LAST)


def combine_kernel(
    reverse, first, known, final,
    follows_ref, arrived_ref, state_ref, rows_ref, *rest,
):
    rest = list(rest)
    before_ref = None if first else rest.pop(0)
    factor_ref = rest.pop(0) if known else None
    follows = follows_ref[0] != 0
    n = state_ref.shape[0]
    other = arrived_ref[0:n, :].astype(F32)
    if known:
        factor = factor_ref[2:3, :]
    else:
        extra = arrived_ref[n : n + 3, :].astype(F32)
        factor = extra[0:1] + extra[1:2] + extra[2:3]
    through = rows_ref[0:1, :]
    past = jnp.ones_like(through) if first else rows_ref[1:2, :]
    before = jnp.zeros_like(other) if first else before_ref[...]
    rest.pop(0)[...] = jnp.where(follows, before + past * other, before)
    new_rows = rest.pop(0)
    if first:
        new_rows[...] = jnp.zeros_like(new_rows)
    else:
        new_rows[...] = rows_ref[...]
    product = through * factor
    new_rows[0:1, :] = product
    new_rows[1:2, :] = jnp.where(follows, past * factor, past)
    new_rows[2:3, :] = factor
    if not final:
        state = state_ref[...]
        state = jnp.where(follows, state + through * other, other + factor * state)
        rest.pop(0)[...] = state
        low_ref = rest.pop(0)
        low_ref[0:n, :] = state.astype(BF)
        if not known:
            low_ref[n:, :] = factor_rows(product)


def factor_rows(row):
    hi, mid, lo = split3(row)
    return jnp.concatenate([hi, mid, lo, jnp.zeros((HALO - 3, row.shape[1]), BF)], 0)


def split_kernel(count, _, *refs):
    sent, kept = refs[4 * count :]
    at = 0
    for i in range(count):
        sent_kept, sent_got, kept_kept, kept_got = refs[4 * i : 4 * i + 4]
        cols = slice(at, at + sent_kept.shape[1])
        at = cols.stop
        sent[:, cols] = (sent_kept[...].astype(F32) + sent_got[...].astype(F32)).astype(BF)
        kept[:, cols] = kept_kept[...].astype(F32) + kept_got[...].astype(F32)


def end_kernel(kept, got, *rest):
    total = kept[...] + got[...].astype(F32)
    rest[-1][...] = total.T if rest[-1].shape != total.shape else total


def add_kernel(count, *refs):
    for i in range(count):
        refs[2 * count + i][...] = refs[2 * i][...] + refs[2 * i + 1][...]


def share_kernel(swap_ref, kept_ref, got_ref, mine_ref, sent_ref):
    total = kept_ref[...].astype(F32) + got_ref[...].astype(F32)
    half = total.shape[1] // 2
    left, right = total[:, :half], total[:, half:]
    swap = swap_ref[0] != 0
    mine_ref[...] = jnp.where(swap, right, left)
    sent_ref[...] = jnp.where(swap, left, right).astype(sent_ref.dtype)


def join_kernel(kept_ref, got_ref, step_ref, first_ref, second_ref):
    def write(out_ref):
        out_ref[:, :LANES] = (kept_ref[...].astype(F32) + got_ref[...].astype(F32)).astype(BF)
        out_ref[:, LANES:] = step_ref[...]

    pl.when(pl.program_id(0) == 0)(lambda: write(first_ref))
    pl.when(pl.program_id(0) == 1)(lambda: write(second_ref))


def close_kernel(
    swap_ref, kept_a, got_a, kept_b, got_b, kept_s, got_s, inner_ref, mine_ref, sent_ref, step_ref
):
    half = kept_a.shape[1]
    inner_ref[:, :half] = kept_a[...] + got_a[...].astype(F32)
    inner_ref[:, half:] = kept_b[...] + got_b[...].astype(F32)
    rest = kept_s[...] + got_s[...].astype(F32)
    left, right = rest[:, : LANES // 2], rest[:, LANES // 2 : LANES]
    swap = swap_ref[0] != 0
    mine_ref[...] = jnp.where(swap, right, left)
    sent_ref[...] = jnp.where(swap, left, right)
    step_ref[...] = rest[:, LANES:].T


def unpack_kernel(
    small_ref, pair_ref, pair_got, norm_ref, norm_got, side_ref, side_got,
    norm_out, taps_out, bias_out, pair_taps_out, pair_bias_out, step_out, decay_out, skip_out, gain_out, side_out,
):
    inner = taps_out.shape[1]
    heads = step_out.shape[1]
    pair = pair_ref[...] + pair_got[...]
    norm_out[...] = jnp.sum(norm_ref[...] + norm_got[...], axis=0, keepdims=True)
    taps_out[...] = small_ref[0:4, :inner]
    bias_out[...] = small_ref[4:5, :inner]
    gain_out[...] = small_ref[5:6, :inner]
    pair_taps_out[...] = pair[0:4]
    pair_bias_out[...] = pair[4:5]
    skip_out[...] = small_ref[6:7, 0:heads]
    step_out[...] = small_ref[6:7, LANES : LANES + heads]
    decay_out[...] = small_ref[6:7, 2 * LANES : 2 * LANES + heads]
    side_out[...] = (side_ref[...] + side_got[...]).T


def result_kernel(_, tokens_ref, scale_ref, mine_ref, away_ref, out_ref):
    branch = mine_ref[...] + away_ref[...].astype(F32)
    out_ref[...] = (tokens_ref[...].astype(F32) + scale_ref[...] * branch).astype(BF)


def final_kernel(
    _, tokens_ref, cot_ref, scale_ref, stat_ref, gain_ref, mine_ref, away_ref, grad_ref, norm_ref
):
    scale = scale_ref[...]
    scaled = (mine_ref[...] + away_ref[...].astype(F32)) * scale
    tokens = tokens_ref[...].astype(F32)
    factor = scale * scale * stat_ref[...] * (1.0 / (mine_ref.shape[1] * lax.axis_size("head")))
    grad_ref[...] = cot_ref[...].astype(F32) + scaled * gain_ref[...] - tokens * factor

    @pl.when(pl.program_id(0) == 0)
    def _():
        norm_ref[...] = jnp.zeros_like(norm_ref)

    norm_ref[...] += fold8(scaled * tokens)


def fix_kernel(
    raw_ref, side_ref, keep_ref, back_ref, small_ref, small_got_ref, d_in, dside_in, stat_in,
    d_ref, dside_ref, stat_ref, small_out_ref,
):
    small_out_ref[...] = small_ref[...] + small_got_ref[...]
    inner = raw_ref.shape[1]
    pair = 2 * N
    back = jnp.concatenate([jnp.zeros((HALO - 8, inner + pair), F32), back_ref[...]], 0) * keep_ref[...]
    d_ref[...] = (d_in[...].astype(F32) + back[:, :inner]).astype(BF)
    dside_ref[...] = dside_in[...]
    dside_ref[:, :pair] = (dside_in[:, :pair].astype(F32) + back[:, inner:]).astype(BF)
    row = jnp.sum(back[:, :inner] * raw_ref[...].astype(F32), axis=1, keepdims=True)
    row = row + jnp.sum(back[:, inner:] * side_ref[:, :pair].astype(BF).astype(F32), axis=1, keepdims=True)
    tall = jnp.concatenate([jnp.zeros((L - HALO, LANES), F32), jnp.broadcast_to(row, (HALO, LANES))], 0)
    stat_ref[...] = stat_in[...]
    stat_ref[0] += tall.T[0:8, :]


def nn_kernel(x_ref, w_ref, *rest):
    rest[-1][...] = dot(x_ref[...], w_ref[...]).astype(BF)


def nt_kernel(x_ref, w_ref, *rest):
    rest[-1][...] = dotg(x_ref[...], w_ref[...], LAST).astype(BF)


def cols_kernel(_, x_ref, w_ref, out_ref):
    out_ref[...] = dot(x_ref[...], w_ref[...]).astype(out_ref.dtype)


def cols_add_kernel(_, x_ref, w_ref, got_ref, out_ref):
    out_ref[...] = (dot(x_ref[...], w_ref[...]) + got_ref[...].astype(F32)).astype(out_ref.dtype)


def gate_back_kernel(_, x_ref, w_ref, out_ref):
    out_ref[0] = dotg(x_ref[...], w_ref[...], LAST).astype(BF)


def weight_kernel(scaled, count, grown, _, x_ref, *rest):
    x = x_ref[...]
    if scaled:
        x = (x.astype(F32) * rest[0][...]).astype(BF)
        rest = rest[1:]
    outs = rest[count + grown :]
    for y_ref, out_ref in zip(rest[:count], outs):
        total = dotg(x, y_ref[...], FIRST)
        if len(outs) > count and y_ref is rest[count - 1]:
            half = N // 2
            out_ref[...] = jnp.concatenate([total[:, half:N], total[:, N + half : 2 * N]], 1).astype(BF)
            outs[-2][...] = jnp.concatenate([total[:, :half], total[:, N : N + half]], 1).astype(BF)
            outs[-1][...] = total[:, 2 * N :].astype(BF)
        else:
            out_ref[...] = total.astype(BF)


def twin_kernel(lead, blocks, adds, _, *refs):
    refs = list(refs)
    x_ref, d_ref, side_ref, w_ref, v_ref, base_ref = refs[:6]
    got = refs[6 : 6 + adds]
    outs = refs[-2 - (5 if lead else 0) :]
    step = pl.program_id(0)
    if lead:

        @pl.when(step < lead)
        def _():
            x = x_ref[...]
            half = N // 2
            cols = outs[0].shape[1]
            outs[0][...] = dotg(x, d_ref[:, :cols], FIRST).astype(BF)
            outs[1][...] = dotg(x, d_ref[:, cols:], FIRST).astype(BF)
            total = dotg(x, side_ref[...], FIRST)
            outs[2][...] = jnp.concatenate([total[:, half:N], total[:, N + half : 2 * N]], 1).astype(BF)
            outs[3][...] = jnp.concatenate([total[:, :half], total[:, N : N + half]], 1).astype(BF)
            outs[4][...] = total[:, 2 * N :].astype(BF)

    for which in (0, 1):

        @pl.when((step >= lead + which * blocks) & (step < lead + (which + 1) * blocks))
        def _():
            big = base_ref.shape[1]
            rows = pl.ds(pl.multiple_of((step - lead - which * blocks) * big, big), big)
            total = dotg(d_ref[rows, :], w_ref[...], LAST) + dot(side_ref[rows, :], v_ref[...])
            total = total + base_ref[0].astype(F32)
            if adds:
                total = total + got[which][...].astype(F32)
            out = outs[which - 2]
            out[...] = total.astype(out.dtype)


def conv_kernel(
    turn, raw_ref, side_ref, info_ref, halo_ref, taps_ref, head_ref, tri_ref, spread_ref,
    act_ref, pact_ref, dt_ref, cs_ref, state_ref, low_ref, rows_ref, buf, total_ref,
):
    inner = raw_ref.shape[1]
    groups = inner // LANES
    pair = pact_ref.shape[1]
    pair_groups = pair // LANES

    @turn.first
    def _():
        buf[0:8, :] = halo_ref[HALO - 8 :, : inner + pair].astype(BF).astype(F32)
        state_ref[...] = jnp.zeros_like(state_ref)
        total_ref[0:1, :] = jnp.zeros((1, LANES), F32)
        total_ref[1:8, :] = jnp.ones((7, LANES), F32)

    info = columns(info_ref[0])
    masks = [None] + [jnp.broadcast_to(info[:, 2 + k : 3 + k], (L, LANES)) for k in (1, 2, 3)]
    dt = jax.nn.softplus(side_ref[:, pair:] + head_ref[0:1, :])
    dt_ref[...] = dt
    cs = exact_sum(tri_ref[...], dt * head_ref[1:2, :])
    cs_ref[...] = cs
    closing = cs[L - 1 :, :]
    total_ref[0:1, :] += closing
    total_ref[1:2, :] = total_ref[1:2, :] * info[0:1, 9:10]
    tail = jnp.exp(closing - cs) * info[:, 2:3] * dt
    tail_wide = expand(tail, spread_ref[...])
    keep = jnp.exp(closing) * info[0:1, 9:10]
    keep_wide = expand(jnp.broadcast_to(keep, (8, LANES)), spread_ref[...])[0:1, :]
    acts = []
    for j in range(groups + pair_groups):
        cols = slice(j * LANES, (j + 1) * LANES)
        if j < groups:
            raw = raw_ref[:, cols].astype(F32)
        else:
            raw = side_ref[:, (j - groups) * LANES : (j - groups + 1) * LANES].astype(BF).astype(F32)
        buf[8 : 8 + L, cols] = raw
        pre = taps_ref[4:5, cols] + taps_ref[0:1, cols] * raw
        for k in (1, 2, 3):
            pre = pre + taps_ref[k : k + 1, cols] * buf[8 - k : 8 - k + L, cols] * masks[k]
        act = (pre * sigmoid(pre)).astype(BF)
        buf[0:8, cols] = raw[L - 8 :, :]
        if j < groups:
            act_ref[:, cols] = act
        else:
            pact_ref[:, (j - groups) * LANES : (j - groups + 1) * LANES] = act
    key_turned = turned(pact_ref[:, :N])
    for j in range(groups):
        cols = slice(j * LANES, (j + 1) * LANES)
        weighted = (act_ref[:, cols].astype(F32) * tail_wide[:, cols]).astype(BF)
        state_ref[:, cols] = keep_wide[:, cols] * state_ref[:, cols] + dot(key_turned, weighted)

    @turn.last
    def _():
        through = jnp.exp(total_ref[0:1, :]) * total_ref[1:2, :]
        rows_ref[...] = expand(jnp.broadcast_to(through, (8, LANES)), spread_ref[...])
        low_ref[0:N, :] = state_ref[...].astype(BF)
        low_ref[N:, :] = factor_rows(rows_ref[0:1, :])


def out_kernel(
    turn, act_ref, pact_ref, dt_ref, cs_ref, info_ref, gate_ref, dgn_ref, state_in_ref,
    gains_ref, spread_ref,
    mixed_ref, gg_ref, sums_ref, entry_ref, state,
):
    inner = act_ref.shape[1]
    groups = inner // LANES

    @turn.first
    def _():
        state[...] = state_in_ref[...]

    info = columns(info_ref[0])
    mask = mask_of(info, info_ref[0, 0:1, :])
    key = pact_ref[:, :N]
    key_turned = turned(key)
    query = pact_ref[:, N:]
    scores = dotg(query, key, LAST)
    dt = dt_ref[...]
    cs = cs_ref[...]
    cs_rows = cs.T
    closing = cs[L - 1 :, :]
    spread = spread_ref[...]
    dt_wide = expand(dt, spread)
    open_wide = expand(jnp.exp(cs) * info[:, 1:2], spread)
    tail_wide = expand(jnp.exp(closing - cs) * info[:, 2:3], spread)
    keep = jnp.exp(closing) * info[0:1, 9:10]
    keep_wide = expand(jnp.broadcast_to(keep, (8, LANES)), spread)[0:1, :]
    left = lane_is_left((L, LANES))
    square = jnp.zeros((L, LANES), F32)
    cross = jnp.zeros((L, LANES), F32)
    for j in range(groups):
        cols = slice(j * LANES, (j + 1) * LANES)
        x = act_ref[:, cols].astype(F32)
        xd = x * dt_wide[:, cols]
        xd_low = xd.astype(BF)
        weights = []
        for h in (2 * j, 2 * j + 1):
            factor = jnp.exp(cs[:, h : h + 1] - cs_rows[h : h + 1, :] + mask)
            weights.append((scores * factor).astype(BF))
        entry = state[:, cols].astype(BF)
        entry_ref[0, :, cols] = entry
        y = dot(jnp.concatenate(weights, 1), stacked_pair(xd_low, left))
        y = y + open_wide[:, cols] * dot(query, entry)
        mixed = y + gains_ref[0:1, cols] * x
        mixed_ref[:, cols] = mixed.astype(BF)
        gate = gate_ref[:, cols].astype(F32)
        gated = mixed * (gate * sigmoid(gate))
        gg = gated * gains_ref[1:2, cols]
        gg_ref[:, cols] = gg.astype(BF)
        square = square + gated * gated
        cross = cross + gg * dgn_ref[:, cols].astype(F32)
        weighted = (xd * tail_wide[:, cols]).astype(BF)
        state[:, cols] = keep_wide[:, cols] * state[:, cols] + dot(key_turned, weighted)
    lane = lax.broadcasted_iota(jnp.int32, (L, LANES), 1)
    both = jnp.where(
        lane == 0,
        jnp.sum(square, axis=1, keepdims=True),
        jnp.sum(cross, axis=1, keepdims=True),
    )
    sums_ref[0] = both.T[0:2, :]


def gate_kernel(
    turn, mixed_ref, gate_ref, dgn_ref, act_ref, pact_ref, cs_ref, info_ref, near_ref, far_ref, gains_ref, spread_ref,
    dmix_ref, dgate_ref, stat_ref, dstate_ref, low_ref, dgain_ref, dskip_ref,
):
    inner = act_ref.shape[1]
    groups = inner // LANES

    @turn.first
    def _():
        dstate_ref[...] = jnp.zeros_like(dstate_ref)
        dgain_ref[...] = jnp.zeros_like(dgain_ref)
        dskip_ref[...] = jnp.zeros_like(dskip_ref)

    info = columns(info_ref[0])
    both = near_ref[0] + far_ref[0]
    scale_row = lax.rsqrt(both[0:1, :] / DI + EPS)
    coef_row = scale_row * scale_row * scale_row * both[1:2, :] / DI
    stats = columns(jnp.concatenate([scale_row, coef_row, jnp.zeros((6, L), F32)], 0))
    scale = jnp.broadcast_to(stats[:, 0:1], (L, LANES))
    coef = jnp.broadcast_to(stats[:, 1:2], (L, LANES))
    cs = cs_ref[...]
    spread = spread_ref[...]
    open_wide = expand(jnp.exp(cs) * info[:, 1:2], spread)
    keep = jnp.exp(cs[L - 1 :, :]) * info[0:1, 9:10]
    keep_wide = expand(jnp.broadcast_to(keep, (8, LANES)), spread)[0:1, :]
    query_turned = turned(pact_ref[:, N:])
    row = jnp.zeros((L, LANES), F32)
    for j in range(groups):
        cols = slice(j * LANES, (j + 1) * LANES)
        mixed = mixed_ref[:, cols].astype(F32)
        gate = gate_ref[:, cols].astype(F32)
        dgn = dgn_ref[:, cols].astype(F32)
        x = act_ref[:, cols].astype(F32)
        sig = sigmoid(gate)
        act = gate * sig
        gated = mixed * act
        scaled = dgn * scale
        dgain_ref[:, cols] += fold8(scaled * gated)
        dgated = scaled * gains_ref[1:2, cols] - gated * coef
        dmix = dgated * act
        dgate = dgated * mixed * (sig + act * (1.0 - sig))
        dskip_ref[:, cols] += fold8(dmix * x)
        row = row + dgate * gate
        dgate_ref[:, cols] = dgate.astype(BF)
        low = dmix.astype(BF)
        dmix_ref[:, cols] = low
        opened = (low.astype(F32) * open_wide[:, cols]).astype(BF)
        dstate_ref[:, cols] = keep_wide[:, cols] * dstate_ref[:, cols] + dot(query_turned, opened)
    stat_ref[0] = jnp.broadcast_to(jnp.sum(row, axis=1, keepdims=True), (L, LANES)).T[0:8, :]

    @turn.last
    def _():
        low_ref[...] = dstate_ref[...].astype(BF)


def back_kernel(
    grown, final, turn,
    act_ref, pact_ref, dt_ref, cs_ref, info_ref, dmix_ref, entry_ref,
    raw_ref, side_ref, raw_prev_ref, side_prev_ref, halo_ref,
    taps_ref, head_ref, gains_ref, tri_ref, spread_ref, gather_ref,
    dstate_in_ref, carried_in_ref, dtaps_in_ref, dhead_in_ref, dgain_ref, dskip_ref, stat_in_ref, *rest,
):
    rest = list(rest[grown:])
    d_ref, dside_ref, stat_ref, dstate, carried_ref, dtaps_ref, dhead_ref = rest[:7]
    small_ref, dhalo_ref = rest[7:9] if final else (None, None)
    buf, dbuf = rest[-2:]
    inner = act_ref.shape[1]
    groups = inner // LANES
    pair = 2 * N
    wide = inner + pair

    @turn.first
    def _():
        dstate[...] = dstate_in_ref[...]
        dbuf[L:, :] = carried_in_ref[...]
        dtaps_ref[...] = dtaps_in_ref[...]
        dhead_ref[...] = dhead_in_ref[...]

    if turn.sub:
        whole_raw, whole_side = rest[-4], rest[-3]
        start = turn.sub * L - HALO
        buf[0:8, :inner] = whole_raw[start + HALO - 8 : start + HALO, :].astype(F32)
        buf[0:8, inner:] = whole_side[start + HALO - 8 : start + HALO, :pair].astype(BF).astype(F32)
    else:
        near_inner = raw_prev_ref[HALO - 8 :, :].astype(F32)
        near_side = side_prev_ref[HALO - 8 :, :pair].astype(BF).astype(F32)
        if final:
            start = pl.program_id(0) == pl.num_programs(0) - 1
            halo = halo_ref[HALO - 8 :, :wide].astype(BF).astype(F32)
            near_inner = jnp.where(start, halo[:, :inner], near_inner)
            near_side = jnp.where(start, halo[:, inner:], near_side)
        buf[0:8, :inner] = near_inner
        buf[0:8, inner:] = near_side

    info = columns(info_ref[0])
    masks = [None] + [jnp.broadcast_to(info[:, 2 + k : 3 + k], (L, LANES)) for k in (1, 2, 3)]
    afters = [None] + [jnp.broadcast_to(info[:, 5 + k : 6 + k], (L, LANES)) for k in (1, 2, 3)]
    mask = mask_of(info, info_ref[0, 0:1, :])
    key = pact_ref[:, :N]
    query = pact_ref[:, N:]
    query_turned = turned(query)
    scores = dotg(query, key, LAST)
    dt = dt_ref[...]
    cs = cs_ref[...]
    cs_rows = cs.T
    closing = cs[L - 1 :, :]
    spread = spread_ref[...]
    dt_wide = expand(dt, spread)
    open_wide = expand(jnp.exp(cs) * info[:, 1:2], spread)
    tail_wide = expand(jnp.exp(closing - cs) * info[:, 2:3], spread)
    keep = jnp.exp(closing) * info[0:1, 9:10]
    keep_wide = expand(jnp.broadcast_to(keep, (8, LANES)), spread)[0:1, :]
    left = lane_is_left((L, LANES))

    def conv_back(j, raw, dact):
        cols = slice(j * LANES, (j + 1) * LANES)
        buf[8 : 8 + L, cols] = raw
        pre = taps_ref[4:5, cols] + taps_ref[0:1, cols] * raw
        moved = [raw]
        for k in (1, 2, 3):
            moved.append(buf[8 - k : 8 - k + L, cols] * masks[k])
            pre = pre + taps_ref[k : k + 1, cols] * moved[k]
        sig = sigmoid(pre)
        dpre = dact * (sig * (1.0 + pre * (1.0 - sig)))
        for k in range(4):
            dtaps_ref[8 * k : 8 * k + 8, cols] += fold8(dpre * moved[k])
        dtaps_ref[32:40, cols] += fold8(dpre)
        dbuf[0:L, cols] = dpre
        draw = taps_ref[0:1, cols] * dpre
        for k in (1, 2, 3):
            draw = draw + taps_ref[k : k + 1, cols] * dbuf[k : k + L, cols] * afters[k]
        dbuf[L : L + 8, cols] = dpre[0:8, :]
        if j < groups:
            d_ref[:, cols] = draw.astype(BF)
        else:
            dside_ref[:, (j - groups) * LANES : (j - groups + 1) * LANES] = draw.astype(BF)
        return draw * raw

    row = jnp.zeros((L, LANES), F32)
    dscores = jnp.zeros((L, L), F32)
    dkey = jnp.zeros((L, N), F32)
    dquery = jnp.zeros((L, N), F32)
    dcs = jnp.zeros((L, LANES), F32)
    ddt = jnp.zeros((L, LANES), F32)
    dclose = jnp.zeros((8, LANES), F32)
    for j in range(groups):
        cols = slice(j * LANES, (j + 1) * LANES)
        x = act_ref[:, cols].astype(F32)
        xd = (x * dt_wide[:, cols]).astype(BF)
        dm = dmix_ref[:, cols]
        dmf = dm.astype(F32)
        xdf = xd.astype(F32)
        factors = []
        weights = []
        for h in (2 * j, 2 * j + 1):
            factor = jnp.exp(cs[:, h : h + 1] - cs_rows[h : h + 1, :] + mask)
            factors.append(factor)
            weights.append((scores * factor).astype(BF))
        pair_x = stacked_pair(xd, left)
        pair_d = stacked_pair(dm, left)
        dweights = dotg(dm, pair_x, LAST)
        dscores = dscores + dweights[:, :L] * factors[0] + dweights[:, L:] * factors[1]
        y = dot(jnp.concatenate(weights, 1), pair_x)
        dxd = dotg(jnp.concatenate(weights, 0), pair_d, FIRST)
        entry = entry_ref[0, :, cols]
        dst = dstate[:, cols]
        dst_low = dst.astype(BF)
        opened = (dmf * open_wide[:, cols]).astype(BF)
        tailed = (xdf * tail_wide[:, cols]).astype(BF)
        from_state = dot(query, entry)
        to_state = dot(key, dst_low)
        out_part = tailed.astype(F32) * to_state
        diff = dmf * y + opened.astype(F32) * from_state - xdf * dxd - out_part
        dxd = dxd + to_state * tail_wide[:, cols]
        hi, lo = split2(diff)
        gather = gather_ref[cols, :]
        dcs = dcs + dot(hi, gather) + dot(lo, gather)
        ddt = ddt + dot((dxd * x).astype(BF), gather)
        close = fold8(out_part) + keep_wide[:, cols] * fold8(dst * entry.astype(F32))
        hi, lo = split2(close)
        dclose = dclose + dot(hi, gather) + dot(lo, gather)
        dquery = dquery + dotg(opened, entry, LAST)
        dkey = dkey + dotg(tailed, dst_low, LAST)
        dstate[:, cols] = keep_wide[:, cols] * dst + dot(query_turned, opened)
        dx = dxd * dt_wide[:, cols] + gains_ref[0:1, cols] * dmf
        row = row + conv_back(j, raw_ref[:, cols].astype(F32), dx)
    dscores = dscores.astype(BF)
    dquery = dquery + dot(dscores, key)
    dkey = dkey + dotg(dscores, query, FIRST)
    row = row + conv_back(groups, side_ref[:, :N].astype(BF).astype(F32), dkey)
    row = row + conv_back(groups + 1, side_ref[:, N:pair].astype(BF).astype(F32), dquery)
    later = dcs
    hi, mid, lo = split3(later)
    tri = tri_ref[...]
    da = dotg(tri, hi, FIRST) + dotg(tri, mid, FIRST) + dotg(tri, lo, FIRST)
    da = da + jnp.sum(dclose, axis=0, keepdims=True)
    ddt = ddt + head_ref[1:2, :] * da
    step = side_ref[:, pair:]
    dstep = ddt * sigmoid(step + head_ref[0:1, :])
    dhead_ref[0:8, :] += fold8(dstep)
    dhead_ref[8:16, :] += fold8(dt * da)
    dside_ref[:, pair:] = dstep.astype(BF)
    row = row + dstep * step
    stat_ref[0] = stat_in_ref[0] + jnp.broadcast_to(jnp.sum(row, axis=1, keepdims=True), (L, LANES)).T[0:8, :]

    @turn.last
    def _():
        carried_ref[...] = dbuf[L:, :]

    if final:

        @turn.last
        def _():
            for k in range(5):
                small_ref[k : k + 1, :] = jnp.sum(dtaps_ref[8 * k : 8 * k + 8, :], axis=0, keepdims=True)
            small_ref[5:8, :] = jnp.zeros((3, wide), F32)
            small_ref[5:6, :inner] = jnp.sum(dgain_ref[...], axis=0, keepdims=True)
            skip = jnp.broadcast_to(jnp.sum(dskip_ref[...], axis=0, keepdims=True), (8, inner))
            hi, lo = split2(skip)
            skip = dot(hi, gather_ref[...]) + dot(lo, gather_ref[...])
            small_ref[6:7, 0:LANES] = skip[0:1, :]
            small_ref[6:7, LANES : 2 * LANES] = jnp.sum(dhead_ref[0:8, :], axis=0, keepdims=True)
            small_ref[6:7, 2 * LANES : 3 * LANES] = (
                jnp.sum(dhead_ref[8:16, :], axis=0, keepdims=True) * head_ref[1:2, :]
            )
            dhalo_ref[...] = jnp.zeros((8, wide), F32)
            for j in range(groups + 2):
                cols = slice(j * LANES, (j + 1) * LANES)
                for k in (1, 2, 3):
                    reach = dbuf[L : L + 8, cols] * masks[k][0:8, :] * taps_ref[k : k + 1, cols]
                    dhalo_ref[8 - k :, cols] += reach[0:k, :]


def flip(block, axis, bit):
    count = lax.axis_size(axis)
    route = [(i, i ^ bit) for i in range(count)]
    return jax.tree.map(lambda a: lax.ppermute(a, axis, route), block)


def sum_over(block, axis):
    bit = 1
    while bit < lax.axis_size(axis):
        block = block + flip(block, axis, bit)
        bit *= 2
    return block


def shift_over(block, axis, distance):
    devices = range(lax.axis_size(axis))
    route = [(i, i + distance) for i in devices if i + distance in devices]
    return lax.ppermute(block, axis, route)


def body(
    tokens, boundary, norm_gain, w_gate, w_inner, w_pair, w_step, conv_inner, conv_pair,
    bias_inner, bias_pair, step_bias, decay_log, skip_gain, gate_gain, w_output, cotangent,
):
    rows, width = tokens.shape
    inner = w_gate.shape[1]
    heads = w_step.shape[1]
    head_count = lax.axis_size("head")
    place = lax.axis_index("head")
    quarter = width // head_count
    pair_cols = w_pair.shape[1]
    pair = pair_cols * head_count
    wide = inner + pair
    side = pair + LANES
    steps = rows // L
    chain = Chain()
    run = chain.run

    many = 2 if steps % 2 == 0 else 1
    few = 2 if steps % 2 == 0 else 1
    ahead_many = Place(many, lambda c: c)
    ahead_few = Place(few, lambda c: c)
    behind_many = Place(many, lambda c: steps // many - 1 - c)

    def row_of(v):
        return v.reshape(1, -1)

    head_of = np.arange(inner)[None, :] // HP == np.arange(LANES)[:, None]
    spread2 = jnp.asarray(np.concatenate([head_of, head_of], 0), BF)
    gather = jnp.asarray(head_of.T, BF)
    lower = jnp.asarray(np.tril(np.ones((L, L))), BF)
    upper = jnp.asarray(np.triu(np.ones((L, L))), BF)

    def split_low(v):
        hi, mid, lo = split3(v)
        return [hi, mid, lo]

    swap = (place & 2) != 0

    pair_small = jnp.concatenate([conv_pair, row_of(bias_pair), jnp.zeros((3, pair_cols), F32)], 0).T
    pair_own = jnp.concatenate([w_pair.T, *split_low(pair_small), jnp.zeros((pair_cols, LANES - 24), BF)], 1)
    pair_pieces = [pair_own] + [flip(pair_own, "head", d) for d in (1, 2, 3)]
    gain_row = row_of(norm_gain)

    one_step = (1,)
    info, sent, keep_tail, head_rows, gains = run(
        prep_kernel,
        one_step,
        [
            whole(boundary.reshape(steps, L)), whole(upper),
            (tokens, pl.BlockSpec((HALO, width), lambda c: (rows // HALO - 1, 0))),
            whole(row_of(step_bias)), whole(row_of(decay_log)), whole(row_of(skip_gain)), whole(row_of(gate_gain)),
            whole(spread2),
        ],
        [
            (whole_spec((steps, 16, L)), (steps, 16, L), F32), (whole_spec((HALO, width)), (HALO, width), BF),
            (whole_spec((HALO, 1)), (HALO, 1), F32), (whole_spec((8, LANES)), (8, LANES), F32),
            (whole_spec((8, inner)), (8, inner), F32),
        ],
        us=2,
    )
    token_halo = shift_over(sent, "seq", 1)

    big = 512
    blocks = rows // big

    def rows_spec(cols, start=0, size=big):
        return pl.BlockSpec((size, cols), lambda i, *_: (i + start, 0))

    def fixed(shape):
        return pl.BlockSpec(shape, lambda i, *_: (0,) * len(shape))

    normed, scale_in, inner_raw = run(
        proj_kernel,
        (blocks,),
        [(tokens, rows_spec(width)), whole(gain_row), whole(w_inner)],
        [
            (rows_spec(width), (rows, width), BF),
            (rows_spec(1), (rows, 1), F32),
            (rows_spec(inner), (rows, inner), BF),
        ],
        us=12,
    )
    halo_shape = (HALO, inner + side)
    side_raw, halo, w_side, taps = run(
        side_kernel,
        (blocks,),
        [(normed, rows_spec(width))]
        + [whole(p) for p in pair_pieces]
        + [whole(w_step.T), whole(token_halo), whole(gain_row), whole(w_inner), whole(conv_inner), whole(row_of(bias_inner))],
        [
            (rows_spec(side), (rows, side), F32),
            (fixed(halo_shape), halo_shape, F32),
            (fixed((side, width)), (side, width), BF),
            (fixed((8, wide)), (8, wide), F32),
        ],
        ids=swap.astype(jnp.int32).reshape(1),
        us=10,
    )

    low_rows = N + HALO
    act, pact, dt, cs, closing, closing_low, through = run(
        chunked(conv_kernel, "rrs-----rrrr", False, many),
        (steps // many,),
        [
            (inner_raw, chunk_spec(inner, ahead_many)), (side_raw, chunk_spec(side, ahead_many)), (info, slab_spec(16, L, ahead_many)),
            whole(halo), whole(taps), whole(head_rows), whole(lower), whole(spread2),
        ],
        [
            (chunk_spec(inner, ahead_many), (rows, inner), BF), (chunk_spec(pair, ahead_many), (rows, pair), BF),
            (chunk_spec(LANES, ahead_many), (rows, LANES), F32), (chunk_spec(LANES, ahead_many), (rows, LANES), F32),
            (whole_spec((N, inner)), (N, inner), F32), (whole_spec((low_rows, inner)), (low_rows, inner), BF),
            (whole_spec((8, inner)), (8, inner), F32),
        ],
        scratch=[pltpu.VMEM((8 + L, wide), F32), pltpu.VMEM((8, LANES), F32)],
        us=17,
    )

    seq_count = lax.axis_size("seq")
    seq_place = lax.axis_index("seq")

    def exchange(state, low, rows0, known, reverse, between):
        before, row, factors = None, rows0, []
        bit = 1
        while bit < seq_count:
            arrived = flip(low, "seq", bit)
            if between:
                between.pop(0)()
            follows = (seq_place & bit) != 0
            if reverse:
                follows = jnp.logical_not(follows)
            final = bit * 2 >= seq_count
            has = known is not None
            ins = [whole(arrived), whole(state), whole(row)]
            if before is not None:
                ins.append(whole(before))
            if has:
                ins.append(whole(known[len(factors)]))
            big_out = (fixed((N, inner)), (N, inner), F32)
            outs = [big_out, (fixed((8, inner)), (8, inner), F32)]
            if not final:
                height = N if has else low_rows
                outs += [big_out, (fixed((height, inner)), (height, inner), BF)]
            got = run(
                functools.partial(combine_kernel, reverse, before is None, has, final),
                one_step,
                ins,
                outs,
                ids=follows.astype(jnp.int32).reshape(1),
                us=2,
            )
            before, row = got[0], got[1]
            factors.append(row)
            if not final:
                state, low = got[2], got[3]
            bit *= 2
        for work in between:
            work()
        return before, factors

    def product(kernel, x, w, start, size, into):
        out = [] if into is None else [(into, ANY)]
        return run(
            kernel,
            (size,),
            [(x, rows_spec(x.shape[1], start)), whole(w)] + out,
            [(rows_spec(inner, start), (rows, inner), BF)],
            aliases={2: 0} if out else None,
            us=2.9 * size,
        )[0]

    third = max(blocks // 3, 1)
    held = {}

    def gate_one():
        held["gate"] = product(nn_kernel, normed, w_gate, 0, blocks - third, None)

    def gate_two():
        held["gate"] = product(nn_kernel, normed, w_gate, blocks - third, third, held["gate"])
        held["dgn"] = product(nt_kernel, cotangent, w_output, 0, third, None)

    def gate_three():
        held["dgn"] = product(nt_kernel, cotangent, w_output, third, blocks - third, held["dgn"])

    state_in, factors = exchange(closing, closing_low, through, None, False, [gate_one, gate_two, gate_three])
    gate_pre, dgn = held["gate"], held["dgn"]

    mixed, gg, sums, entries = run(
        chunked(out_kernel, "rrrrsrr---rrss", False, few),
        (steps // few,),
        [
            (act, chunk_spec(inner, ahead_few)), (pact, chunk_spec(pair, ahead_few)), (dt, chunk_spec(LANES, ahead_few)),
            (cs, chunk_spec(LANES, ahead_few)), (info, slab_spec(16, L, ahead_few)),
            (gate_pre, chunk_spec(inner, ahead_few)), (dgn, chunk_spec(inner, ahead_few)),
            whole(state_in), whole(gains), whole(spread2),
        ],
        [
            (chunk_spec(inner, ahead_few), (rows, inner), BF), (chunk_spec(inner, ahead_few), (rows, inner), BF),
            (slab_spec(2, L, ahead_few), (steps, 2, L), F32), (slab_spec(N, inner, ahead_few), (steps, N, inner), BF),
        ],
        scratch=[pltpu.VMEM((N, inner), F32)],
        us=18,
    )

    order = [place ^ 3, place ^ 1, place ^ 2, place]

    def quarter_spec():
        return pl.BlockSpec((big, quarter), lambda i, ids: (i, 0))

    def out_quarter(which, got, dtype, after=()):
        ins = [
            (gg, pl.BlockSpec((big, inner), lambda i, ids: (i, 0))),
            (w_output, pl.BlockSpec((inner, quarter), lambda i, ids: (0, ids[0]))),
        ]
        if got is not None:
            ins.append((got, quarter_spec()))
        return run(
            cols_kernel if got is None else cols_add_kernel,
            (blocks,),
            ins,
            [(quarter_spec(), (rows, quarter), dtype)],
            after=after,
            ids=order[which].reshape(1),
            us=5,
        )[0]

    sums_core = flip(sums, "head", 1)
    out_a = out_quarter(0, None, BF)
    sums = sums + sums_core
    got_a = flip(out_a, "head", 1)
    sums_x = flip(sums, "head", 2)
    out_b = out_quarter(1, None, BF, [sums_core])
    got_b = flip(out_b, "head", 1)
    scale_out = lax.rsqrt((sums + sums_x)[:, 0, :] / DI + EPS).reshape(rows, 1)

    share = width // seq_count
    manual = seq_count == 8
    half = seq_count // 2
    seq_core = seq_place % 2
    if manual:
        row_ids = [jnp.arange(half) * 2 + (1 - seq_core), jnp.arange(half) * 2 + seq_core]
    else:
        share = 256
        row_ids = [jnp.arange(width // share)]

    def weight_rows(which, x, ys, scale=None, into=()):
        ids = row_ids[which].astype(jnp.int32)
        count = ids.shape[0]
        ins = [(x, pl.BlockSpec((rows, share), lambda i, ids: (0, ids[i])))]
        if scale is not None:
            ins.append(whole(scale))
        outs = []
        lead = count * which
        for y, cols, at in ys:
            ins.append((y, pl.BlockSpec((rows, cols), lambda i, ids, at=at: (0, at))))
            if cols == side:
                spec = pl.BlockSpec((share, LANES), lambda i, ids: (i + lead, 0))
                outs += [(spec, (width, LANES), BF)] * 3
            else:
                outs.append((pl.BlockSpec((share, cols), lambda i, ids: (i, 0)), (count * share, cols), BF))
        aliases = {len(ins) + k: len(outs) - 3 + k for k in range(len(into))}
        return run(
            functools.partial(weight_kernel, scale is not None, len(ys), len(into)),
            (count,),
            ins + [(a, ANY) for a in into],
            outs,
            ids=ids,
            aliases=aliases,
            us=8,
        )

    z = seq_place // 2

    class Halving:
        def __init__(self, pieces):
            low = z % 2
            ids = jnp.stack([1 - low, 3 - low, low, 2 + low]).astype(jnp.int32)
            ins = []
            for kept, got in pieces:
                cols = kept.shape[1]
                for first in (0, 2):
                    spec = pl.BlockSpec((share, cols), lambda i, ids, f=first: (ids[f + i], 0))
                    ins += [(kept, spec), (got, spec)]
            self.cols = sum(kept.shape[1] for kept, _ in pieces)
            self.count = len(pieces)
            out = pl.BlockSpec((share, self.cols), lambda i, ids: (i, 0))
            sent, self.kept = run(
                functools.partial(split_kernel, self.count),
                (2,),
                ins,
                [(out, (2 * share, self.cols), BF), (out, (2 * share, self.cols), F32)],
                ids=ids,
                us=3,
            )
            self.got = flip(sent, "seq", 2)

        def middle(self):
            high = z // 2
            ids = jnp.stack([1 - high, high]).astype(jnp.int32)
            part = share // 2
            ins = []
            for w in (0, 1):
                spec = pl.BlockSpec((part, self.cols), lambda i, ids, w=w: (ids[w] * 2 + i, 0))
                ins += [(self.kept, spec), (self.got, spec)]
            out = pl.BlockSpec((part, self.cols), lambda i, ids: (i, 0))
            sent, self.kept = run(
                functools.partial(split_kernel, 1),
                (2,),
                ins,
                [(out, (share, self.cols), BF), (out, (share, self.cols), F32)],
                ids=ids,
                us=2,
            )
            self.got = flip(sent, "seq", 4)

        def end(self, into=None, place=0, total=1, turned=False):
            if turned:
                shape = block = (self.cols, share)
            else:
                shape, block = (share, self.cols * total), (share, self.cols)
            ins = [whole(self.kept), whole(self.got)] + ([] if into is None else [(into, ANY)])
            return run(
                end_kernel,
                one_step,
                ins,
                [(pl.BlockSpec(block, lambda i: (0, place)), shape, F32)],
                aliases=None if into is None else {2: 0},
                us=2,
            )[0]

    (out_first,) = weight_rows(0, cotangent, [(gg, inner, 0)], scale_out)
    if manual:
        out_got = flip(out_first, "seq", 1)
    away = out_quarter(2, got_a, BF)
    away_got = flip(away, "head", 2)
    mine = out_quarter(3, got_b, F32)
    if manual:
        (out_second,) = weight_rows(1, cotangent, [(gg, inner, 0)], scale_out)

    dmix, dgate, stat, dstate_local, dstate_low, dgain, dskip = run(
        chunked(gate_kernel, "rrrrrrsss--" + "rrs", True, many),
        (steps // many,),
        [
            (mixed, chunk_spec(inner, behind_many)), (gate_pre, chunk_spec(inner, behind_many)), (dgn, chunk_spec(inner, behind_many)),
            (act, chunk_spec(inner, behind_many)), (pact, chunk_spec(pair, behind_many)), (cs, chunk_spec(LANES, behind_many)),
            (info, slab_spec(16, L, behind_many)), (sums, slab_spec(2, L, behind_many)), (sums_x, slab_spec(2, L, behind_many)),
            whole(gains), whole(spread2),
        ],
        [
            (chunk_spec(inner, behind_many), (rows, inner), BF), (chunk_spec(inner, behind_many), (rows, inner), BF),
            (slab_spec(8, L, behind_many), (steps, 8, L), F32), (whole_spec((N, inner)), (N, inner), F32),
            (whole_spec((N, inner)), (N, inner), BF),
            (whole_spec((8, inner)), (8, inner), F32), (whole_spec((8, inner)), (8, inner), F32),
        ],
        us=17,
    )

    order_ids = jnp.stack(order).astype(jnp.int32)

    def gate_first():
        held["first"] = weight_rows(0, normed, [(dgate, inner, 0)])[0]

    def gate_second():
        if manual:
            held["got"] = flip(held["first"], "seq", 1)
            held["second"] = weight_rows(1, normed, [(dgate, inner, 0)])[0]

    def gate_third():
        held["dn"] = run(
            gate_back_kernel,
            (4, blocks),
            [
                (dgate, pl.BlockSpec((big, inner), lambda n, i, ids: (i, 0))),
                (w_gate, pl.BlockSpec((quarter, inner), lambda n, i, ids: (ids[n], 0))),
            ],
            [(pl.BlockSpec((1, big, quarter), lambda n, i, ids: (n, i, 0)), (4, rows, quarter), BF)],
            ids=order_ids,
            us=17,
        )[0]

    dstate, _ = exchange(
        dstate_local, dstate_low, through, factors, True, [gate_first, gate_second, gate_third]
    )
    dn_gate = held["dn"]

    def back_chunks(count, final):
        kinds = "rrrrsrsrr" + "-" * 15 + "s" + "-" * count + "rrs"
        kernel = functools.partial(back_kernel, count, final)

        def run_all(*refs):
            chunked(lambda turn, *views: kernel(turn, *views[:-2], refs[7], refs[8], *views[-2:]), kinds, True, 1)(*refs)

        return run_all

    parts = 3 if steps % 3 == 0 else 1
    each = steps // parts
    carried = jnp.zeros((8, wide), F32)
    dtaps = jnp.zeros((40, wide), F32)
    dhead = jnp.zeros((16, LANES), F32)
    d_inner = d_side = small = dhalo = None
    if manual:
        out_sum = Halving([(out_second, out_got)])
    for part in range(parts):
        first = steps - 1 - part * each
        at = Place(1, lambda c, first=first: first - c)

        def near_end(c, at=at):
            return jnp.maximum(at.at(c) * (L // HALO) - 1, 0)

        final = part == parts - 1
        if manual and part == 1:
            out_sum.middle()
        if manual and part == 2:
            dw_out = out_sum.end(turned=True)
            gate_sum = Halving([(held["second"], held["got"])])
        grown = [] if d_inner is None else [(d_inner, ANY), (d_side, ANY)]
        state_specs = [
            (whole_spec((N, inner)), (N, inner), F32), (whole_spec((8, wide)), (8, wide), F32),
            (whole_spec((40, wide)), (40, wide), F32), (whole_spec((16, LANES)), (16, LANES), F32),
        ]
        if final:
            state_specs += [(whole_spec((8, wide)), (8, wide), F32)] * 2
        ins = [
            (act, chunk_spec(inner, at)), (pact, chunk_spec(pair, at)), (dt, chunk_spec(LANES, at)),
            (cs, chunk_spec(LANES, at)), (info, slab_spec(16, L, at)),
            (dmix, chunk_spec(inner, at)), (entries, slab_spec(N, inner, at)),
            (inner_raw, chunk_spec(inner, at)), (side_raw, chunk_spec(side, at)),
            (inner_raw, pl.BlockSpec((HALO, inner), lambda c, p=near_end: (p(c), 0))),
            (side_raw, pl.BlockSpec((HALO, side), lambda c, p=near_end: (p(c), 0))),
            whole(halo), whole(taps), whole(head_rows), whole(gains), whole(lower), whole(spread2), whole(gather),
            whole(dstate), whole(carried), whole(dtaps), whole(dhead), whole(dgain), whole(dskip),
            (stat, slab_spec(8, L, at)), *grown,
        ]
        aliases = {24: 2}
        if grown:
            aliases.update({25: 0, 26: 1})
        got = run(
            back_chunks(len(grown), final),
            (each,),
            ins,
            [
                (chunk_spec(inner, at), (rows, inner), BF), (chunk_spec(side, at), (rows, side), BF),
                (slab_spec(8, L, at), (steps, 8, L), F32), *state_specs,
            ],
            after=[away_got] if part == min(1, parts - 1) else [],
            scratch=[pltpu.VMEM((8 + L, wide), F32), pltpu.VMEM((L + 8, wide), F32)],
            aliases=aliases,
            us=64 / parts,
        )
        d_inner, d_side, stat, dstate, carried, dtaps, dhead = got[:7]
        if final:
            small, dhalo = got[7:]

    if manual:
        gate_sum.middle()
    returned = shift_over(dhalo, "seq", -1)
    small_got = flip(small, "seq", 1)

    def last_rows(cols):
        return pl.BlockSpec((HALO, cols), lambda c: (rows // HALO - 1, 0))

    last_slab = slab_spec(8, L, Place(1, lambda c: steps - 1))
    d_inner, d_side, stat, small = run(
        fix_kernel,
        one_step,
        [
            (inner_raw, last_rows(inner)), (side_raw, last_rows(side)), whole(keep_tail), whole(returned),
            whole(small), whole(small_got),
            (d_inner, last_rows(inner)), (d_side, last_rows(side)), (stat, last_slab),
        ],
        [
            (last_rows(inner), (rows, inner), BF), (last_rows(side), (rows, side), BF), (last_slab, (steps, 8, L), F32),
            (whole_spec((8, wide)), (8, wide), F32),
        ],
        aliases={6: 0, 7: 1, 8: 2},
        us=2,
    )

    def add(pairs):
        return run(
            functools.partial(add_kernel, len(pairs)),
            one_step,
            [whole(a) for pair_ in pairs for a in pair_],
            [(pl.BlockSpec(a.shape, lambda i, n=a.ndim: (0,) * n), a.shape, a.dtype) for a, _ in pairs],
            us=1,
        )

    half_inner = inner // 2
    swap_id = swap.astype(jnp.int32).reshape(1)
    inner_parts = [(d_inner, half_inner, 0), (d_inner, half_inner, 1), (d_side, side, 0)]

    swap_id = swap.astype(jnp.int32).reshape(1)
    stat = stat[:, 0, :]

    def twin(pair_at, got, dtypes, into=None):
        lead = half if into is not None else 0
        ids = [order[pair_at], order[pair_at + 1]]
        ids = jnp.concatenate([jnp.stack(ids)] + ([row_ids[1]] if lead else [])).astype(jnp.int32)

        def which(s):
            return jnp.clip((s - lead) // blocks, 0, 1)

        def row(s):
            return jnp.where(s < lead, 0, (s - lead) % blocks)

        def x_at(s, ids):
            return (0, ids[2 + jnp.minimum(s, lead - 1)]) if lead else (0, 0)

        def out_at(s, w):
            return jnp.clip(s - lead - w * blocks, 0, blocks - 1)

        ins = [
            (normed, pl.BlockSpec((rows if lead else 256, 256), x_at)),
            whole(d_inner), whole(d_side),
            (w_inner, pl.BlockSpec((quarter, inner), lambda s, ids: (ids[which(s)], 0))),
            (w_side, pl.BlockSpec((side, quarter), lambda s, ids: (0, ids[which(s)]))),
            (dn_gate, pl.BlockSpec((1, big, quarter), lambda s, ids: (pair_at + which(s), row(s), 0))),
        ]
        for w, block in enumerate(got):
            ins.append((block, pl.BlockSpec((big, quarter), lambda s, ids, w=w: (out_at(s, w), 0))))
        aliases = {}
        outs = []
        if lead:
            last = lead - 1
            aliases = {len(ins) + k: 2 + k for k in range(3)}
            ins += [(a, ANY) for a in into]
            wide_spec = pl.BlockSpec((share, inner // 2), lambda s, ids: (jnp.minimum(s, last), 0))
            side_spec = pl.BlockSpec((share, LANES), lambda s, ids: (lead + jnp.minimum(s, last), 0))
            outs += [(wide_spec, (lead * share, inner // 2), BF)] * 2 + [(side_spec, (width, LANES), BF)] * 3
        for w in (0, 1):
            spec = pl.BlockSpec((big, quarter), lambda s, ids, w=w: (out_at(s, w), 0))
            outs.append((spec, (rows, quarter), dtypes[w]))
        return run(
            functools.partial(twin_kernel, lead, blocks, len(got)),
            (lead + 2 * blocks,),
            ins,
            outs,
            ids=ids,
            aliases=aliases,
            us=22 if lead else 14,
        )

    first_a, first_b, sent, kept, step = weight_rows(0, normed, inner_parts)
    here = place.astype(jnp.int32).reshape(1)
    own_spec = pl.BlockSpec((big, quarter), lambda i, ids: (i, ids[0]))
    column = pl.BlockSpec((big, 1), lambda i, ids: (i, 0))
    result = run(
        result_kernel,
        (blocks,),
        [(tokens, own_spec), (scale_out, column), (mine, quarter_spec()), (away_got, quarter_spec())],
        [(quarter_spec(), (rows, quarter), BF)],
        ids=here,
        us=4,
    )[0]
    if manual:
        dw_gate = gate_sum.end()
    tall = pl.BlockSpec((1024, LANES), lambda i, *_: (i, 0))
    stat_got = flip(stat, "head", 1)
    small_got = flip(small, "seq", 2)
    if manual:
        got_a = flip(first_a, "seq", 1)
        got_b = flip(first_b, "seq", 1)
        second_a, second_b, sent, kept, step, dn_a, dn_b = twin(0, [], [BF, BF], [sent, kept, step])
    else:
        dn_a, dn_b = twin(0, [], [BF, BF])
    side_got = flip(sent, "head", 1)
    dn_got_a = flip(dn_a, "head", 1)
    dn_got_b = flip(dn_b, "head", 1)
    if manual:
        sum_a = Halving([(second_a, got_a)])
    stat, small = add([(stat, stat_got), (small, small_got)])
    stat_got = flip(stat, "head", 2)
    small_got = flip(small, "seq", 4)
    (stat,) = add([(stat, stat_got)])
    dn_away, dn_mine = twin(2, [dn_got_a, dn_got_b], [BF, F32])
    dn_away_got = flip(dn_away, "head", 2)
    if manual:
        sum_a.middle()
    joined = (pl.BlockSpec((width // 2, 2 * LANES), lambda i: (0, 0)), (width // 2, 2 * LANES), BF)
    rest_first, rest_second = run(
        join_kernel,
        (2,),
        [(kept, tall), (side_got, tall), (step, tall)],
        [joined, joined],
        us=3,
    )
    if manual:
        rest_got = flip(rest_first, "seq", 1)
        sum_b = Halving([(second_b, got_b)])
        sum_s = Halving([(rest_second, rest_got)])
    (small,) = add([(small, small_got)])
    bit = 8
    while bit < seq_count:
        small = small + flip(small, "seq", bit)
        bit *= 2
    if manual:
        sum_b.middle()
    small_pair = small[:, inner:]
    low_half, high_half = small_pair[:, : N // 2], small_pair[:, N // 2 : N]
    pair_kept = jnp.concatenate([low_half, small_pair[:, N : N + N // 2]], 1)
    pair_sent = jnp.concatenate([high_half, small_pair[:, N + N // 2 :]], 1)
    pair_got = flip(pair_sent, "head", 1)
    grad_tokens, norm_sum = run(
        final_kernel,
        (blocks,),
        [
            (tokens, own_spec), (cotangent, own_spec), (scale_in, column), (stat.reshape(rows, 1), column),
            (gain_row, pl.BlockSpec((1, quarter), lambda i, ids: (0, ids[0]))),
            (dn_mine, quarter_spec()), (dn_away_got, quarter_spec()),
        ],
        [
            (quarter_spec(), (rows, quarter), F32),
            (pl.BlockSpec((8, quarter), lambda i, ids: (0, 0)), (8, quarter), F32),
        ],
        ids=here,
        us=6,
    )
    norm_got = flip(norm_sum, "seq", 1)
    if manual:
        sum_s.middle()
    norm_sum = add([(norm_sum, norm_got)])[0]
    norm_got = flip(norm_sum, "seq", 2)
    pair_half = pl.BlockSpec((8, pair_cols), lambda i, *_: (0, 0))
    pair_full = pl.BlockSpec((8, N), lambda i, *_: (0, 0))
    pair_mine, pair_away = run(
        share_kernel,
        one_step,
        [(pair_kept, pair_full), (pair_got, pair_full)],
        [(pair_half, (8, pair_cols), F32)] * 2,
        ids=swap_id,
        us=1,
    )
    pair_got = flip(pair_away, "head", 2)
    norm_sum = add([(norm_sum, norm_got)])[0]
    norm_got = flip(norm_sum, "seq", 4)
    if manual:
        own_rows = (share, pair_cols)
        thin = (pl.BlockSpec(own_rows, lambda i, *_: (0, 0)), own_rows, F32)
        dw_inner, side_mine, side_sent, dw_step = run(
            close_kernel,
            one_step,
            [whole(block) for sum_ in (sum_a, sum_b, sum_s) for block in (sum_.kept, sum_.got)],
            [
                (pl.BlockSpec((share, inner), lambda i, *_: (0, 0)), (share, inner), F32), thin, thin,
                (pl.BlockSpec((LANES, share), lambda i, *_: (0, 0)), (LANES, share), F32),
            ],
            ids=swap_id,
            us=3,
        )
    else:
        dw_out, dw_gate, dw_inner, rest = [
            lax.psum_scatter(block, "seq", scatter_dimension=0, tiled=True).astype(F32)
            for block in (
                out_first,
                held["first"],
                jnp.concatenate([first_a, first_b], 1),
                jnp.concatenate([rest_first, rest_second], 0),
            )
        ]
        dw_out = jnp.transpose(dw_out)
        left, right = rest[:, :pair_cols], rest[:, pair_cols : 2 * pair_cols]
        side_mine, side_sent = jnp.where(swap, right, left), jnp.where(swap, left, right)
        dw_step = rest[:, LANES:].T
    side_got = flip(side_sent, "head", 2)
    bit = 8
    while bit < seq_count:
        norm_sum = norm_sum + norm_got
        norm_got = flip(norm_sum, "seq", bit)
        bit *= 2
    shapes = [
        (1, quarter), (4, inner), (1, inner), (4, pair_cols), (1, pair_cols), (1, heads), (1, heads), (1, heads),
        (1, inner), side_mine.shape[::-1],
    ]
    outs = run(
        unpack_kernel,
        one_step,
        [whole(a) for a in (small, pair_mine, pair_got, norm_sum, norm_got, side_mine, side_got)],
        [(pl.BlockSpec(shape, lambda i: (0, 0)), shape, F32) for shape in shapes],
        us=1,
    )
    norm_sum, taps_sum, bias_sum, pair_taps, pair_bias, step_sum, decay_sum, skip_sum, gain_sum, dw_pair = outs
    return (
        result,
        grad_tokens,
        norm_sum.reshape(-1),
        dw_gate,
        dw_inner,
        dw_pair.T,
        dw_step[:heads].T,
        taps_sum,
        pair_taps,
        bias_sum.reshape(-1),
        pair_bias.reshape(-1),
        step_sum.reshape(-1),
        decay_sum.reshape(-1),
        skip_sum.reshape(-1),
        gain_sum.reshape(-1),
        dw_out,
    )


def solution(mesh):
    return jax.shard_map(
        body,
        mesh=mesh,
        in_specs=(
            P("seq", None),
            P("seq"),
            P(),
            P(None, "head"),
            P(None, "head"),
            P(None, "head"),
            P(None, "head"),
            P(None, "head"),
            P(None, "head"),
            P("head"),
            P("head"),
            P("head"),
            P("head"),
            P("head"),
            P("head"),
            P("head", None),
            P("seq", None),
        ),
        out_specs=(
            P("seq", "head"),
            P("seq", "head"),
            P("head"),
            P("seq", "head"),
            P("seq", "head"),
            P("seq", "head"),
            P("seq", "head"),
            P(None, "head"),
            P(None, "head"),
            P("head"),
            P("head"),
            P("head"),
            P("head"),
            P("head"),
            P("head"),
            P("head", "seq"),
        ),
        check_vma=False,
    )
```

```python
import functools

import jax
import jax.numpy as jnp
import numpy as np
from jax import lax
from jax.experimental import pallas as pl
from jax.experimental.pallas import tpu as pltpu
from jax.sharding import PartitionSpec as P

N = 128
HP = 64
DI = 4096
EPS = 1e-05
L = 128
LANES = 128
HALO = 16
F32 = jnp.float32
BF = jnp.bfloat16
VMEM_LIMIT = 64 * 1024 * 1024 - 65536
FIRST = (((0,), (0,)), ((), ()))
LAST = (((1,), (1,)), ((), ()))


def dot(a, b):
    return jnp.dot(a, b, preferred_element_type=F32)


def dotg(a, b, dims):
    return lax.dot_general(a, b, dims, preferred_element_type=F32)


def split2(v):
    hi = v.astype(BF)
    return hi, (v - hi.astype(F32)).astype(BF)


def split3(v):
    hi = v.astype(BF)
    rest = v - hi.astype(F32)
    mid = rest.astype(BF)
    return hi, mid, (rest - mid.astype(F32)).astype(BF)


def exact_sum(tri, v):
    hi, mid, lo = split3(v)
    return dot(tri, hi) + dot(tri, mid) + dot(tri, lo)


def expand(v, spread2):
    hi, lo = split2(v)
    return dot(jnp.concatenate([hi, lo], 1), spread2)


def fold8(v):
    return jnp.sum(v.reshape(v.shape[0] // 8, 8, v.shape[1]), axis=0)


def stacked_pair(v, left):
    zero = jnp.zeros_like(v)
    return jnp.concatenate([jnp.where(left, v, zero), jnp.where(left, zero, v)], 0)


def lane_is_left(shape):
    return lax.broadcasted_iota(jnp.int32, shape, 1) < HP


def columns(slab):
    pad = LANES - slab.shape[0]
    return jnp.concatenate([slab, jnp.zeros((pad, L), F32)], 0).T


def mask_of(info, seg_row):
    rows = lax.broadcasted_iota(jnp.int32, (L, L), 0)
    cols = lax.broadcasted_iota(jnp.int32, (L, L), 1)
    linked = (info[:, 0:1] == seg_row) & (rows >= cols)
    return jnp.where(linked, 0.0, -1e30).astype(F32)


def turned(v):
    return v.astype(F32).T.astype(BF)


def sigmoid(v):
    return 0.5 * jnp.tanh(0.5 * v) + 0.5


class Place:
    def __init__(self, u, at):
        self.u, self.at = u, at


def chunk_spec(width, place):
    return pl.BlockSpec((place.u * L, width), lambda c: (place.at(c), 0))


def slab_spec(rows, width, place):
    return pl.BlockSpec((place.u, rows, width), lambda c: (place.at(c), 0, 0))


class Turn:
    def __init__(self, i, sub, u):
        self.i, self.sub, self.u = i, sub, u

    def first(self, work):
        if self.i == 0:
            pl.when(pl.program_id(0) == 0)(work)

    def last(self, work):
        if self.i == self.u - 1:
            pl.when(pl.program_id(0) == pl.num_programs(0) - 1)(work)


def chunked(kernel, kinds, reverse, u):
    def run_all(*refs):
        for i in range(u):
            sub = u - 1 - i if reverse else i
            views = []
            for n, ref in enumerate(refs):
                kind = kinds[n] if n < len(kinds) else "-"
                if kind == "r":
                    ref = ref.at[pl.ds(sub * L, L), :]
                elif kind == "s":
                    ref = ref.at[pl.ds(sub, 1)]
                views.append(ref)
            kernel(Turn(i, sub, u), *views)

    return run_all


def whole_spec(shape):
    return pl.BlockSpec(shape, lambda c: (0,) * len(shape))


ANY = pl.BlockSpec(memory_space=pl.ANY)


class Shifted:
    def __init__(self, ref, start):
        self.ref, self.start = ref, start

    def __getitem__(self, i):
        return self.ref[self.start + i]


def shifted_spec(spec, start):
    if spec.block_shape is None:
        return spec
    old = spec.index_map
    return pl.BlockSpec(spec.block_shape, lambda *args: old(*args[:-1], Shifted(args[-1], start)))


class Chain:
    def __init__(self):
        self.last = None
        self.factor = 1.0

    def run(self, kernel, grid, ins, outs, after=(), scratch=(), ids=None, aliases=None, us=5.0):
        start = None
        if ids is not None:
            start, ids = self.starts[ids], self.table
            ins = [(array, shifted_spec(spec, start)) for array, spec in ins]
            outs = [(shifted_spec(spec, start), shape, dtype) for spec, shape, dtype in outs]
        given = [array for array, _ in ins]
        after = [a for a in list(after) + [self.last] if a is not None and not any(a is g for g in given)]
        lead = 0 if ids is None else 1
        keep_in = lead + len(ins)

        def inner(*refs):
            refs = list(refs)
            if lead:
                refs[0] = Shifted(refs[0], start)
            kernel(*refs[:keep_in], *refs[keep_in + len(after) :])

        result = pl.pallas_call(
            inner,
            grid_spec=pltpu.PrefetchScalarGridSpec(
                num_scalar_prefetch=lead,
                grid=grid,
                in_specs=[spec for _, spec in ins] + [ANY] * len(after),
                out_specs=[spec for spec, _, _ in outs],
                scratch_shapes=list(scratch),
            ),
            out_shape=[jax.ShapeDtypeStruct(shape, dtype) for _, shape, dtype in outs],
            input_output_aliases={lead + i: o for i, o in (aliases or {}).items()},
            compiler_params=pltpu.CompilerParams(
                dimension_semantics=("arbitrary",) * len(grid), vmem_limit_bytes=VMEM_LIMIT
            ),
            cost_estimate=pl.CostEstimate(flops=int(us * self.factor * 1.15e9), bytes_accessed=10**4, transcendentals=0),
        )(*(() if ids is None else (ids,)), *given, *after)
        self.last = min(result, key=lambda r: r.size)
        return result


def whole(array):
    zeros = (0,) * array.ndim
    return array, pl.BlockSpec(array.shape, lambda *_: zeros)


def norm_rows(block, gain):
    t = block.astype(F32)
    scale = lax.rsqrt(jnp.mean(t * t, axis=-1, keepdims=True) + EPS)
    return scale, (t * scale * gain).astype(BF)


def proj_kernel(tokens_ref, gain_ref, w_ref, normed_ref, scale_ref, inner_ref):
    scale, normed = norm_rows(tokens_ref[...], gain_ref[...])
    scale_ref[...] = scale
    normed_ref[...] = normed
    inner_ref[...] = dot(normed, w_ref[...]).astype(BF)


def along(v, k):
    zero = jnp.zeros((1, v.shape[1]), v.dtype)
    if k > 0:
        other = jnp.concatenate([zero, v[:-1]], 0)
        return jnp.concatenate([other[:, L - k :], v[:, : L - k]], 1)
    other = jnp.concatenate([v[1:], zero], 0)
    return jnp.concatenate([v[:, -k:], other[:, :-k]], 1)


def prep_kernel(
    starts_ref, upper_ref, tokens_ref, step_bias_ref, decay_ref, skip_ref, gate_gain_ref, spread_ref,
    info_ref, sent_ref, keep_ref, head_ref, gains_ref,
):
    starts = starts_ref[...].astype(F32)
    seg = dot(starts.astype(BF), upper_ref[...])
    m1 = 1.0 - starts
    m2 = m1 * (1.0 - along(starts, 1))
    m3 = m2 * (1.0 - along(starts, 2))
    seg_last = jnp.broadcast_to(seg[:, L - 1 :], seg.shape)
    one = jnp.ones_like(seg)
    zero = jnp.zeros_like(seg)
    fields = [
        seg, jnp.where(seg == 0, one, zero), jnp.where(seg == seg_last, one, zero), m1, m2, m3,
        along(m1, -1), along(m2, -2), along(m3, -3), jnp.where(seg_last == 0, one, zero),
    ]
    for i in range(16):
        info_ref[:, i, :] = fields[i] if i < len(fields) else zero
    rows = lax.broadcasted_iota(jnp.int32, (HALO, L), 0)
    lanes = lax.broadcasted_iota(jnp.int32, (HALO, L), 1)
    last = jnp.broadcast_to(starts[starts.shape[0] - 1 :, :], (HALO, L))
    later = jnp.sum(jnp.where(lanes > rows + L - HALO, last, 0.0), axis=1, keepdims=True)
    place = lax.broadcasted_iota(jnp.int32, (HALO, 1), 0)
    keep = jnp.where((later == 0) & (place >= HALO - 3), 1.0, 0.0)
    keep_ref[...] = keep
    sent_ref[...] = (tokens_ref[...].astype(F32) * keep).astype(BF)
    heads = step_bias_ref.shape[1]
    head_ref[...] = jnp.zeros_like(head_ref)
    head_ref[0:1, 0:heads] = step_bias_ref[...]
    head_ref[1:2, 0:heads] = -jnp.exp(decay_ref[...])
    head_ref[2:3, 0:heads] = skip_ref[...]
    gains_ref[...] = expand(jnp.broadcast_to(head_ref[2:3, :], (8, LANES)), spread_ref[...])
    gains_ref[1:2, :] = gate_gain_ref[...]


def side_kernel(
    swap_ref, normed_ref, own_ref, one_ref, two_ref, three_ref, w_step_ref, halo_ref, gain_ref, w_ref,
    conv_ref, bias_ref,
    side_ref, halo_out_ref, w_side_ref, taps_ref,
):
    @pl.when(pl.program_id(0) == 0)
    def _():
        width, inner = w_ref.shape
        near = jnp.concatenate([own_ref[...], one_ref[...]], 0)
        far = jnp.concatenate([two_ref[...], three_ref[...]], 0)
        swap = swap_ref[0] != 0
        first = jnp.where(swap, far, near)
        second = jnp.where(swap, near, far)
        w_side_ref[0:N, :] = first[:, :width]
        w_side_ref[N : 2 * N, :] = second[:, :width]
        heads = w_step_ref.shape[0]
        w_side_ref[2 * N : 2 * N + heads, :] = w_step_ref[...]
        w_side_ref[2 * N + heads :, :] = jnp.zeros((LANES - heads, width), BF)
        taps_ref[0:4, :inner] = conv_ref[...]
        taps_ref[4:5, :inner] = bias_ref[...]
        taps_ref[5:8, :inner] = jnp.zeros((3, inner), F32)
        for i, part in enumerate((first, second)):
            extra = part[:, width:].astype(F32).T
            taps_ref[:, inner + i * N : inner + (i + 1) * N] = extra[0:8] + extra[8:16] + extra[16:24]
        _, halo = norm_rows(halo_ref[...], gain_ref[...])
        halo_out_ref[:, :inner] = dot(halo, w_ref[...])
        halo_out_ref[:, inner:] = dotg(halo, w_side_ref[...], LAST)

    side_ref[...] = dotg(normed_ref[...], w_side_ref[...], LAST)


def combine_kernel(
    reverse, first, known, final,
    follows_ref, arrived_ref, state_ref, rows_ref, *rest,
):
    rest = list(rest)
    before_ref = None if first else rest.pop(0)
    factor_ref = rest.pop(0) if known else None
    follows = follows_ref[0] != 0
    n = state_ref.shape[0]
    other = arrived_ref[0:n, :].astype(F32)
    if known:
        factor = factor_ref[2:3, :]
    else:
        extra = arrived_ref[n : n + 3, :].astype(F32)
        factor = extra[0:1] + extra[1:2] + extra[2:3]
    through = rows_ref[0:1, :]
    past = jnp.ones_like(through) if first else rows_ref[1:2, :]
    before = jnp.zeros_like(other) if first else before_ref[...]
    rest.pop(0)[...] = jnp.where(follows, before + past * other, before)
    new_rows = rest.pop(0)
    if first:
        new_rows[...] = jnp.zeros_like(new_rows)
    else:
        new_rows[...] = rows_ref[...]
    product = through * factor
    new_rows[0:1, :] = product
    new_rows[1:2, :] = jnp.where(follows, past * factor, past)
    new_rows[2:3, :] = factor
    if not final:
        state = state_ref[...]
        state = jnp.where(follows, state + through * other, other + factor * state)
        rest.pop(0)[...] = state
        low_ref = rest.pop(0)
        low_ref[0:n, :] = state.astype(BF)
        if not known:
            low_ref[n:, :] = factor_rows(product)


def factor_rows(row):
    hi, mid, lo = split3(row)
    return jnp.concatenate([hi, mid, lo, jnp.zeros((HALO - 3, row.shape[1]), BF)], 0)


def split_kernel(count, _, *refs):
    sent, kept = refs[4 * count :]
    at = 0
    for i in range(count):
        sent_kept, sent_got, kept_kept, kept_got = refs[4 * i : 4 * i + 4]
        cols = slice(at, at + sent_kept.shape[1])
        at = cols.stop
        sent[:, cols] = (sent_kept[...].astype(F32) + sent_got[...].astype(F32)).astype(BF)
        kept[:, cols] = kept_kept[...].astype(F32) + kept_got[...].astype(F32)


def end_kernel(kept, got, *rest):
    total = kept[...] + got[...].astype(F32)
    rest[-1][...] = total.T if rest[-1].shape != total.shape else total


def add_kernel(count, *refs):
    for i in range(count):
        refs[2 * count + i][...] = refs[2 * i][...] + refs[2 * i + 1][...]


def share_kernel(swap_ref, kept_ref, got_ref, mine_ref, sent_ref):
    total = kept_ref[...].astype(F32) + got_ref[...].astype(F32)
    half = total.shape[1] // 2
    left, right = total[:, :half], total[:, half:]
    swap = swap_ref[0] != 0
    mine_ref[...] = jnp.where(swap, right, left)
    sent_ref[...] = jnp.where(swap, left, right).astype(sent_ref.dtype)


def join_kernel(kept_ref, got_ref, step_ref, first_ref, second_ref):
    def write(out_ref):
        out_ref[:, :LANES] = (kept_ref[...].astype(F32) + got_ref[...].astype(F32)).astype(BF)
        out_ref[:, LANES:] = step_ref[...]

    pl.when(pl.program_id(0) == 0)(lambda: write(first_ref))
    pl.when(pl.program_id(0) == 1)(lambda: write(second_ref))


def close_kernel(
    swap_ref, kept_a, got_a, kept_b, got_b, kept_s, got_s, inner_ref, mine_ref, sent_ref, step_ref
):
    half = kept_a.shape[1]
    inner_ref[:, :half] = kept_a[...] + got_a[...].astype(F32)
    inner_ref[:, half:] = kept_b[...] + got_b[...].astype(F32)
    rest = kept_s[...] + got_s[...].astype(F32)
    left, right = rest[:, : LANES // 2], rest[:, LANES // 2 : LANES]
    swap = swap_ref[0] != 0
    mine_ref[...] = jnp.where(swap, right, left)
    sent_ref[...] = jnp.where(swap, left, right)
    step_ref[...] = rest[:, LANES:].T


def unpack_kernel(
    small_ref, pair_ref, pair_got, norm_ref, norm_got, side_ref, side_got,
    norm_out, taps_out, bias_out, pair_taps_out, pair_bias_out, step_out, decay_out, skip_out, gain_out, side_out,
):
    inner = taps_out.shape[1]
    heads = step_out.shape[1]
    pair = pair_ref[...] + pair_got[...]
    norm_out[...] = jnp.sum(norm_ref[...] + norm_got[...], axis=0, keepdims=True)
    taps_out[...] = small_ref[0:4, :inner]
    bias_out[...] = small_ref[4:5, :inner]
    gain_out[...] = small_ref[5:6, :inner]
    pair_taps_out[...] = pair[0:4]
    pair_bias_out[...] = pair[4:5]
    skip_out[...] = small_ref[6:7, 0:heads]
    step_out[...] = small_ref[6:7, LANES : LANES + heads]
    decay_out[...] = small_ref[6:7, 2 * LANES : 2 * LANES + heads]
    side_out[...] = (side_ref[...] + side_got[...]).T


def result_kernel(_, tokens_ref, scale_ref, mine_ref, away_ref, out_ref):
    branch = mine_ref[...] + away_ref[...].astype(F32)
    out_ref[...] = (tokens_ref[...].astype(F32) + scale_ref[...] * branch).astype(BF)


def final_kernel(
    _, tokens_ref, cot_ref, scale_ref, stat_ref, gain_ref, mine_ref, away_ref, grad_ref, norm_ref
):
    scale = scale_ref[...]
    scaled = (mine_ref[...] + away_ref[...].astype(F32)) * scale
    tokens = tokens_ref[...].astype(F32)
    factor = scale * scale * stat_ref[...] * (1.0 / (mine_ref.shape[1] * lax.axis_size("head")))
    grad_ref[...] = cot_ref[...].astype(F32) + scaled * gain_ref[...] - tokens * factor

    @pl.when(pl.program_id(0) == 0)
    def _():
        norm_ref[...] = jnp.zeros_like(norm_ref)

    norm_ref[...] += fold8(scaled * tokens)


def fix_kernel(
    raw_ref, side_ref, keep_ref, back_ref, small_ref, small_got_ref, d_in, dside_in, stat_in,
    d_ref, dside_ref, stat_ref, small_out_ref,
):
    small_out_ref[...] = small_ref[...] + small_got_ref[...]
    inner = raw_ref.shape[1]
    pair = 2 * N
    back = jnp.concatenate([jnp.zeros((HALO - 8, inner + pair), F32), back_ref[...]], 0) * keep_ref[...]
    d_ref[...] = (d_in[...].astype(F32) + back[:, :inner]).astype(BF)
    dside_ref[...] = dside_in[...]
    dside_ref[:, :pair] = (dside_in[:, :pair].astype(F32) + back[:, inner:]).astype(BF)
    row = jnp.sum(back[:, :inner] * raw_ref[...].astype(F32), axis=1, keepdims=True)
    row = row + jnp.sum(back[:, inner:] * side_ref[:, :pair].astype(BF).astype(F32), axis=1, keepdims=True)
    tall = jnp.concatenate([jnp.zeros((L - HALO, LANES), F32), jnp.broadcast_to(row, (HALO, LANES))], 0)
    stat_ref[...] = stat_in[...]
    stat_ref[0] += tall.T[0:8, :]


def nn_kernel(x_ref, w_ref, *rest):
    rest[-1][...] = dot(x_ref[...], w_ref[...]).astype(BF)


def nt_kernel(x_ref, w_ref, *rest):
    rest[-1][...] = dotg(x_ref[...], w_ref[...], LAST).astype(BF)


def cols_kernel(_, x_ref, w_ref, out_ref):
    out_ref[...] = dot(x_ref[...], w_ref[...]).astype(out_ref.dtype)


def cols_add_kernel(_, x_ref, w_ref, got_ref, out_ref):
    out_ref[...] = (dot(x_ref[...], w_ref[...]) + got_ref[...].astype(F32)).astype(out_ref.dtype)


def gate_back_kernel(_, x_ref, w_ref, out_ref):
    out_ref[0] = dotg(x_ref[...], w_ref[...], LAST).astype(BF)


def weight_kernel(scaled, count, grown, _, x_ref, *rest):
    x = x_ref[...]
    if scaled:
        x = (x.astype(F32) * rest[0][...]).astype(BF)
        rest = rest[1:]
    outs = rest[count + grown :]
    for y_ref, out_ref in zip(rest[:count], outs):
        total = dotg(x, y_ref[...], FIRST)
        if len(outs) > count and y_ref is rest[count - 1]:
            half = N // 2
            out_ref[...] = jnp.concatenate([total[:, half:N], total[:, N + half : 2 * N]], 1).astype(BF)
            outs[-2][...] = jnp.concatenate([total[:, :half], total[:, N : N + half]], 1).astype(BF)
            outs[-1][...] = total[:, 2 * N :].astype(BF)
        else:
            out_ref[...] = total.astype(BF)


def twin_kernel(lead, blocks, adds, _, *refs):
    refs = list(refs)
    x_ref, d_ref, side_ref, w_ref, v_ref, base_ref = refs[:6]
    got = refs[6 : 6 + adds]
    outs = refs[-2 - (5 if lead else 0) :]
    step = pl.program_id(0)
    if lead:

        @pl.when(step < lead)
        def _():
            x = x_ref[...]
            half = N // 2
            cols = outs[0].shape[1]
            outs[0][...] = dotg(x, d_ref[:, :cols], FIRST).astype(BF)
            outs[1][...] = dotg(x, d_ref[:, cols:], FIRST).astype(BF)
            total = dotg(x, side_ref[...], FIRST)
            outs[2][...] = jnp.concatenate([total[:, half:N], total[:, N + half : 2 * N]], 1).astype(BF)
            outs[3][...] = jnp.concatenate([total[:, :half], total[:, N : N + half]], 1).astype(BF)
            outs[4][...] = total[:, 2 * N :].astype(BF)

    for which in (0, 1):

        @pl.when((step >= lead + which * blocks) & (step < lead + (which + 1) * blocks))
        def _():
            big = base_ref.shape[1]
            rows = pl.ds(pl.multiple_of((step - lead - which * blocks) * big, big), big)
            total = dotg(d_ref[rows, :], w_ref[...], LAST) + dot(side_ref[rows, :], v_ref[...])
            total = total + base_ref[0].astype(F32)
            if adds:
                total = total + got[which][...].astype(F32)
            out = outs[which - 2]
            out[...] = total.astype(out.dtype)


def conv_kernel(
    turn, raw_ref, side_ref, info_ref, halo_ref, taps_ref, head_ref, tri_ref, spread_ref,
    act_ref, pact_ref, dt_ref, cs_ref, state_ref, low_ref, rows_ref, buf, total_ref,
):
    inner = raw_ref.shape[1]
    groups = inner // LANES
    pair = pact_ref.shape[1]
    pair_groups = pair // LANES

    @turn.first
    def _():
        buf[0:8, :] = halo_ref[HALO - 8 :, : inner + pair].astype(BF).astype(F32)
        state_ref[...] = jnp.zeros_like(state_ref)
        total_ref[0:1, :] = jnp.zeros((1, LANES), F32)
        total_ref[1:8, :] = jnp.ones((7, LANES), F32)

    info = columns(info_ref[0])
    masks = [None] + [jnp.broadcast_to(info[:, 2 + k : 3 + k], (L, LANES)) for k in (1, 2, 3)]
    dt = jax.nn.softplus(side_ref[:, pair:] + head_ref[0:1, :])
    dt_ref[...] = dt
    cs = exact_sum(tri_ref[...], dt * head_ref[1:2, :])
    cs_ref[...] = cs
    closing = cs[L - 1 :, :]
    total_ref[0:1, :] += closing
    total_ref[1:2, :] = total_ref[1:2, :] * info[0:1, 9:10]
    tail = jnp.exp(closing - cs) * info[:, 2:3] * dt
    tail_wide = expand(tail, spread_ref[...])
    keep = jnp.exp(closing) * info[0:1, 9:10]
    keep_wide = expand(jnp.broadcast_to(keep, (8, LANES)), spread_ref[...])[0:1, :]
    acts = []
    for j in range(groups + pair_groups):
        cols = slice(j * LANES, (j + 1) * LANES)
        if j < groups:
            raw = raw_ref[:, cols].astype(F32)
        else:
            raw = side_ref[:, (j - groups) * LANES : (j - groups + 1) * LANES].astype(BF).astype(F32)
        buf[8 : 8 + L, cols] = raw
        pre = taps_ref[4:5, cols] + taps_ref[0:1, cols] * raw
        for k in (1, 2, 3):
            pre = pre + taps_ref[k : k + 1, cols] * buf[8 - k : 8 - k + L, cols] * masks[k]
        act = (pre * sigmoid(pre)).astype(BF)
        buf[0:8, cols] = raw[L - 8 :, :]
        if j < groups:
            act_ref[:, cols] = act
        else:
            pact_ref[:, (j - groups) * LANES : (j - groups + 1) * LANES] = act
    key_turned = turned(pact_ref[:, :N])
    for j in range(groups):
        cols = slice(j * LANES, (j + 1) * LANES)
        weighted = (act_ref[:, cols].astype(F32) * tail_wide[:, cols]).astype(BF)
        state_ref[:, cols] = keep_wide[:, cols] * state_ref[:, cols] + dot(key_turned, weighted)

    @turn.last
    def _():
        through = jnp.exp(total_ref[0:1, :]) * total_ref[1:2, :]
        rows_ref[...] = expand(jnp.broadcast_to(through, (8, LANES)), spread_ref[...])
        low_ref[0:N, :] = state_ref[...].astype(BF)
        low_ref[N:, :] = factor_rows(rows_ref[0:1, :])


def out_kernel(
    turn, act_ref, pact_ref, dt_ref, cs_ref, info_ref, gate_ref, dgn_ref, state_in_ref,
    gains_ref, spread_ref,
    mixed_ref, gg_ref, sums_ref, entry_ref, state,
):
    inner = act_ref.shape[1]
    groups = inner // LANES

    @turn.first
    def _():
        state[...] = state_in_ref[...]

    info = columns(info_ref[0])
    mask = mask_of(info, info_ref[0, 0:1, :])
    key = pact_ref[:, :N]
    key_turned = turned(key)
    query = pact_ref[:, N:]
    scores = dotg(query, key, LAST)
    dt = dt_ref[...]
    cs = cs_ref[...]
    cs_rows = cs.T
    closing = cs[L - 1 :, :]
    spread = spread_ref[...]
    dt_wide = expand(dt, spread)
    open_wide = expand(jnp.exp(cs) * info[:, 1:2], spread)
    tail_wide = expand(jnp.exp(closing - cs) * info[:, 2:3], spread)
    keep = jnp.exp(closing) * info[0:1, 9:10]
    keep_wide = expand(jnp.broadcast_to(keep, (8, LANES)), spread)[0:1, :]
    left = lane_is_left((L, LANES))
    square = jnp.zeros((L, LANES), F32)
    cross = jnp.zeros((L, LANES), F32)
    for j in range(groups):
        cols = slice(j * LANES, (j + 1) * LANES)
        x = act_ref[:, cols].astype(F32)
        xd = x * dt_wide[:, cols]
        xd_low = xd.astype(BF)
        weights = []
        for h in (2 * j, 2 * j + 1):
            factor = jnp.exp(cs[:, h : h + 1] - cs_rows[h : h + 1, :] + mask)
            weights.append((scores * factor).astype(BF))
        entry = state[:, cols].astype(BF)
        entry_ref[0, :, cols] = entry
        y = dot(jnp.concatenate(weights, 1), stacked_pair(xd_low, left))
        y = y + open_wide[:, cols] * dot(query, entry)
        mixed = y + gains_ref[0:1, cols] * x
        mixed_ref[:, cols] = mixed.astype(BF)
        gate = gate_ref[:, cols].astype(F32)
        gated = mixed * (gate * sigmoid(gate))
        gg = gated * gains_ref[1:2, cols]
        gg_ref[:, cols] = gg.astype(BF)
        square = square + gated * gated
        cross = cross + gg * dgn_ref[:, cols].astype(F32)
        weighted = (xd * tail_wide[:, cols]).astype(BF)
        state[:, cols] = keep_wide[:, cols] * state[:, cols] + dot(key_turned, weighted)
    lane = lax.broadcasted_iota(jnp.int32, (L, LANES), 1)
    both = jnp.where(
        lane == 0,
        jnp.sum(square, axis=1, keepdims=True),
        jnp.sum(cross, axis=1, keepdims=True),
    )
    sums_ref[0] = both.T[0:2, :]


def gate_kernel(
    turn, mixed_ref, gate_ref, dgn_ref, act_ref, pact_ref, cs_ref, info_ref, near_ref, far_ref, gains_ref, spread_ref,
    dmix_ref, dgate_ref, stat_ref, dstate_ref, low_ref, dgain_ref, dskip_ref,
):
    inner = act_ref.shape[1]
    groups = inner // LANES

    @turn.first
    def _():
        dstate_ref[...] = jnp.zeros_like(dstate_ref)
        dgain_ref[...] = jnp.zeros_like(dgain_ref)
        dskip_ref[...] = jnp.zeros_like(dskip_ref)

    info = columns(info_ref[0])
    both = near_ref[0] + far_ref[0]
    scale_row = lax.rsqrt(both[0:1, :] / DI + EPS)
    coef_row = scale_row * scale_row * scale_row * both[1:2, :] / DI
    stats = columns(jnp.concatenate([scale_row, coef_row, jnp.zeros((6, L), F32)], 0))
    scale = jnp.broadcast_to(stats[:, 0:1], (L, LANES))
    coef = jnp.broadcast_to(stats[:, 1:2], (L, LANES))
    cs = cs_ref[...]
    spread = spread_ref[...]
    open_wide = expand(jnp.exp(cs) * info[:, 1:2], spread)
    keep = jnp.exp(cs[L - 1 :, :]) * info[0:1, 9:10]
    keep_wide = expand(jnp.broadcast_to(keep, (8, LANES)), spread)[0:1, :]
    query_turned = turned(pact_ref[:, N:])
    row = jnp.zeros((L, LANES), F32)
    for j in range(groups):
        cols = slice(j * LANES, (j + 1) * LANES)
        mixed = mixed_ref[:, cols].astype(F32)
        gate = gate_ref[:, cols].astype(F32)
        dgn = dgn_ref[:, cols].astype(F32)
        x = act_ref[:, cols].astype(F32)
        sig = sigmoid(gate)
        act = gate * sig
        gated = mixed * act
        scaled = dgn * scale
        dgain_ref[:, cols] += fold8(scaled * gated)
        dgated = scaled * gains_ref[1:2, cols] - gated * coef
        dmix = dgated * act
        dgate = dgated * mixed * (sig + act * (1.0 - sig))
        dskip_ref[:, cols] += fold8(dmix * x)
        row = row + dgate * gate
        dgate_ref[:, cols] = dgate.astype(BF)
        low = dmix.astype(BF)
        dmix_ref[:, cols] = low
        opened = (low.astype(F32) * open_wide[:, cols]).astype(BF)
        dstate_ref[:, cols] = keep_wide[:, cols] * dstate_ref[:, cols] + dot(query_turned, opened)
    stat_ref[0] = jnp.broadcast_to(jnp.sum(row, axis=1, keepdims=True), (L, LANES)).T[0:8, :]

    @turn.last
    def _():
        low_ref[...] = dstate_ref[...].astype(BF)


def back_kernel(
    grown, final, turn,
    act_ref, pact_ref, dt_ref, cs_ref, info_ref, dmix_ref, entry_ref,
    raw_ref, side_ref, raw_prev_ref, side_prev_ref, halo_ref,
    taps_ref, head_ref, gains_ref, tri_ref, spread_ref, gather_ref,
    dstate_in_ref, carried_in_ref, dtaps_in_ref, dhead_in_ref, dgain_ref, dskip_ref, stat_in_ref, *rest,
):
    rest = list(rest[grown:])
    d_ref, dside_ref, stat_ref, dstate, carried_ref, dtaps_ref, dhead_ref = rest[:7]
    small_ref, dhalo_ref = rest[7:9] if final else (None, None)
    buf, dbuf = rest[-2:]
    inner = act_ref.shape[1]
    groups = inner // LANES
    pair = 2 * N
    wide = inner + pair

    @turn.first
    def _():
        dstate[...] = dstate_in_ref[...]
        dbuf[L:, :] = carried_in_ref[...]
        dtaps_ref[...] = dtaps_in_ref[...]
        dhead_ref[...] = dhead_in_ref[...]

    if turn.sub:
        whole_raw, whole_side = rest[-4], rest[-3]
        start = turn.sub * L - HALO
        buf[0:8, :inner] = whole_raw[start + HALO - 8 : start + HALO, :].astype(F32)
        buf[0:8, inner:] = whole_side[start + HALO - 8 : start + HALO, :pair].astype(BF).astype(F32)
    else:
        near_inner = raw_prev_ref[HALO - 8 :, :].astype(F32)
        near_side = side_prev_ref[HALO - 8 :, :pair].astype(BF).astype(F32)
        if final:
            start = pl.program_id(0) == pl.num_programs(0) - 1
            halo = halo_ref[HALO - 8 :, :wide].astype(BF).astype(F32)
            near_inner = jnp.where(start, halo[:, :inner], near_inner)
            near_side = jnp.where(start, halo[:, inner:], near_side)
        buf[0:8, :inner] = near_inner
        buf[0:8, inner:] = near_side

    info = columns(info_ref[0])
    masks = [None] + [jnp.broadcast_to(info[:, 2 + k : 3 + k], (L, LANES)) for k in (1, 2, 3)]
    afters = [None] + [jnp.broadcast_to(info[:, 5 + k : 6 + k], (L, LANES)) for k in (1, 2, 3)]
    mask = mask_of(info, info_ref[0, 0:1, :])
    key = pact_ref[:, :N]
    query = pact_ref[:, N:]
    query_turned = turned(query)
    scores = dotg(query, key, LAST)
    dt = dt_ref[...]
    cs = cs_ref[...]
    cs_rows = cs.T
    closing = cs[L - 1 :, :]
    spread = spread_ref[...]
    dt_wide = expand(dt, spread)
    open_wide = expand(jnp.exp(cs) * info[:, 1:2], spread)
    tail_wide = expand(jnp.exp(closing - cs) * info[:, 2:3], spread)
    keep = jnp.exp(closing) * info[0:1, 9:10]
    keep_wide = expand(jnp.broadcast_to(keep, (8, LANES)), spread)[0:1, :]
    left = lane_is_left((L, LANES))

    def conv_back(j, raw, dact):
        cols = slice(j * LANES, (j + 1) * LANES)
        buf[8 : 8 + L, cols] = raw
        pre = taps_ref[4:5, cols] + taps_ref[0:1, cols] * raw
        moved = [raw]
        for k in (1, 2, 3):
            moved.append(buf[8 - k : 8 - k + L, cols] * masks[k])
            pre = pre + taps_ref[k : k + 1, cols] * moved[k]
        sig = sigmoid(pre)
        dpre = dact * (sig * (1.0 + pre * (1.0 - sig)))
        for k in range(4):
            dtaps_ref[8 * k : 8 * k + 8, cols] += fold8(dpre * moved[k])
        dtaps_ref[32:40, cols] += fold8(dpre)
        dbuf[0:L, cols] = dpre
        draw = taps_ref[0:1, cols] * dpre
        for k in (1, 2, 3):
            draw = draw + taps_ref[k : k + 1, cols] * dbuf[k : k + L, cols] * afters[k]
        dbuf[L : L + 8, cols] = dpre[0:8, :]
        if j < groups:
            d_ref[:, cols] = draw.astype(BF)
        else:
            dside_ref[:, (j - groups) * LANES : (j - groups + 1) * LANES] = draw.astype(BF)
        return draw * raw

    row = jnp.zeros((L, LANES), F32)
    dscores = jnp.zeros((L, L), F32)
    dkey = jnp.zeros((L, N), F32)
    dquery = jnp.zeros((L, N), F32)
    dcs = jnp.zeros((L, LANES), F32)
    ddt = jnp.zeros((L, LANES), F32)
    dclose = jnp.zeros((8, LANES), F32)
    for j in range(groups):
        cols = slice(j * LANES, (j + 1) * LANES)
        x = act_ref[:, cols].astype(F32)
        xd = (x * dt_wide[:, cols]).astype(BF)
        dm = dmix_ref[:, cols]
        dmf = dm.astype(F32)
        xdf = xd.astype(F32)
        factors = []
        weights = []
        for h in (2 * j, 2 * j + 1):
            factor = jnp.exp(cs[:, h : h + 1] - cs_rows[h : h + 1, :] + mask)
            factors.append(factor)
            weights.append((scores * factor).astype(BF))
        pair_x = stacked_pair(xd, left)
        pair_d = stacked_pair(dm, left)
        dweights = dotg(dm, pair_x, LAST)
        dscores = dscores + dweights[:, :L] * factors[0] + dweights[:, L:] * factors[1]
        y = dot(jnp.concatenate(weights, 1), pair_x)
        dxd = dotg(jnp.concatenate(weights, 0), pair_d, FIRST)
        entry = entry_ref[0, :, cols]
        dst = dstate[:, cols]
        dst_low = dst.astype(BF)
        opened = (dmf * open_wide[:, cols]).astype(BF)
        tailed = (xdf * tail_wide[:, cols]).astype(BF)
        from_state = dot(query, entry)
        to_state = dot(key, dst_low)
        out_part = tailed.astype(F32) * to_state
        diff = dmf * y + opened.astype(F32) * from_state - xdf * dxd - out_part
        dxd = dxd + to_state * tail_wide[:, cols]
        hi, lo = split2(diff)
        gather = gather_ref[cols, :]
        dcs = dcs + dot(hi, gather) + dot(lo, gather)
        ddt = ddt + dot((dxd * x).astype(BF), gather)
        close = fold8(out_part) + keep_wide[:, cols] * fold8(dst * entry.astype(F32))
        hi, lo = split2(close)
        dclose = dclose + dot(hi, gather) + dot(lo, gather)
        dquery = dquery + dotg(opened, entry, LAST)
        dkey = dkey + dotg(tailed, dst_low, LAST)
        dstate[:, cols] = keep_wide[:, cols] * dst + dot(query_turned, opened)
        dx = dxd * dt_wide[:, cols] + gains_ref[0:1, cols] * dmf
        row = row + conv_back(j, raw_ref[:, cols].astype(F32), dx)
    dscores = dscores.astype(BF)
    dquery = dquery + dot(dscores, key)
    dkey = dkey + dotg(dscores, query, FIRST)
    row = row + conv_back(groups, side_ref[:, :N].astype(BF).astype(F32), dkey)
    row = row + conv_back(groups + 1, side_ref[:, N:pair].astype(BF).astype(F32), dquery)
    later = dcs
    hi, mid, lo = split3(later)
    tri = tri_ref[...]
    da = dotg(tri, hi, FIRST) + dotg(tri, mid, FIRST) + dotg(tri, lo, FIRST)
    da = da + jnp.sum(dclose, axis=0, keepdims=True)
    ddt = ddt + head_ref[1:2, :] * da
    step = side_ref[:, pair:]
    dstep = ddt * sigmoid(step + head_ref[0:1, :])
    dhead_ref[0:8, :] += fold8(dstep)
    dhead_ref[8:16, :] += fold8(dt * da)
    dside_ref[:, pair:] = dstep.astype(BF)
    row = row + dstep * step
    stat_ref[0] = stat_in_ref[0] + jnp.broadcast_to(jnp.sum(row, axis=1, keepdims=True), (L, LANES)).T[0:8, :]

    @turn.last
    def _():
        carried_ref[...] = dbuf[L:, :]

    if final:

        @turn.last
        def _():
            for k in range(5):
                small_ref[k : k + 1, :] = jnp.sum(dtaps_ref[8 * k : 8 * k + 8, :], axis=0, keepdims=True)
            small_ref[5:8, :] = jnp.zeros((3, wide), F32)
            small_ref[5:6, :inner] = jnp.sum(dgain_ref[...], axis=0, keepdims=True)
            skip = jnp.broadcast_to(jnp.sum(dskip_ref[...], axis=0, keepdims=True), (8, inner))
            hi, lo = split2(skip)
            skip = dot(hi, gather_ref[...]) + dot(lo, gather_ref[...])
            small_ref[6:7, 0:LANES] = skip[0:1, :]
            small_ref[6:7, LANES : 2 * LANES] = jnp.sum(dhead_ref[0:8, :], axis=0, keepdims=True)
            small_ref[6:7, 2 * LANES : 3 * LANES] = (
                jnp.sum(dhead_ref[8:16, :], axis=0, keepdims=True) * head_ref[1:2, :]
            )
            dhalo_ref[...] = jnp.zeros((8, wide), F32)
            for j in range(groups + 2):
                cols = slice(j * LANES, (j + 1) * LANES)
                for k in (1, 2, 3):
                    reach = dbuf[L : L + 8, cols] * masks[k][0:8, :] * taps_ref[k : k + 1, cols]
                    dhalo_ref[8 - k :, cols] += reach[0:k, :]


def flip(block, axis, bit):
    count = lax.axis_size(axis)
    route = [(i, i ^ bit) for i in range(count)]
    return jax.tree.map(lambda a: lax.ppermute(a, axis, route), block)


def sum_over(block, axis):
    bit = 1
    while bit < lax.axis_size(axis):
        block = block + flip(block, axis, bit)
        bit *= 2
    return block


def shift_over(block, axis, distance):
    devices = range(lax.axis_size(axis))
    route = [(i, i + distance) for i in devices if i + distance in devices]
    return lax.ppermute(block, axis, route)


def body(
    tokens, boundary, norm_gain, w_gate, w_inner, w_pair, w_step, conv_inner, conv_pair,
    bias_inner, bias_pair, step_bias, decay_log, skip_gain, gate_gain, w_output, cotangent,
):
    rows, width = tokens.shape
    inner = w_gate.shape[1]
    heads = w_step.shape[1]
    head_count = lax.axis_size("head")
    place = lax.axis_index("head")
    quarter = width // head_count
    pair_cols = w_pair.shape[1]
    pair = pair_cols * head_count
    wide = inner + pair
    side = pair + LANES
    steps = rows // L
    chain = Chain()
    run = chain.run

    many = 2 if steps % 2 == 0 else 1
    few = 2 if steps % 2 == 0 else 1
    ahead_many = Place(many, lambda c: c)
    ahead_few = Place(few, lambda c: c)
    behind_many = Place(many, lambda c: steps // many - 1 - c)

    seq_count = lax.axis_size("seq")
    seq_place = lax.axis_index("seq")
    manual = seq_count == 8
    half = seq_count // 2
    swap = (place & 2) != 0
    order = [place ^ 3, place ^ 1, place ^ 2, place]
    z = seq_place // 2
    seq_core, low, high = seq_place % 2, z % 2, z // 2
    if manual:
        row_ids = [[2 * i + 1 - seq_core for i in range(half)], [2 * i + seq_core for i in range(half)]]
    else:
        row_ids = [list(range(width // 256))]
    entries = {
        "swap": [swap], "place": [place], "order": order, "rows0": row_ids[0], "rows1": row_ids[-1],
        "twin0": order[:2] + (row_ids[1] if manual else []), "twin2": order[2:],
        "split": [1 - low, 3 - low, low, 2 + low], "middle": [1 - high, high],
    }
    for i in range(4):
        entries["order%d" % i] = [order[i]]
    bit = 1
    while bit < seq_count:
        later = (seq_place & bit) != 0
        entries["fwd%d" % bit] = [later]
        entries["rev%d" % bit] = [jnp.logical_not(later)]
        bit *= 2
    flat = []
    chain.starts = {}
    for name, values in entries.items():
        chain.starts[name] = len(flat)
        flat += values
    chain.table = jnp.stack([jnp.asarray(v).astype(jnp.int32) for v in flat])

    def row_of(v):
        return v.reshape(1, -1)

    head_of = np.arange(inner)[None, :] // HP == np.arange(LANES)[:, None]
    spread2 = jnp.asarray(np.concatenate([head_of, head_of], 0), BF)
    gather = jnp.asarray(head_of.T, BF)
    lower = jnp.asarray(np.tril(np.ones((L, L))), BF)
    upper = jnp.asarray(np.triu(np.ones((L, L))), BF)

    def split_low(v):
        hi, mid, lo = split3(v)
        return [hi, mid, lo]

    swap = (place & 2) != 0

    pair_small = jnp.concatenate([conv_pair, row_of(bias_pair), jnp.zeros((3, pair_cols), F32)], 0).T
    pair_own = jnp.concatenate([w_pair.T, *split_low(pair_small), jnp.zeros((pair_cols, LANES - 24), BF)], 1)
    pair_pieces = [pair_own] + [flip(pair_own, "head", d) for d in (1, 2, 3)]
    gain_row = row_of(norm_gain)

    one_step = (1,)
    info, sent, keep_tail, head_rows, gains = run(
        prep_kernel,
        one_step,
        [
            whole(boundary.reshape(steps, L)), whole(upper),
            (tokens, pl.BlockSpec((HALO, width), lambda c: (rows // HALO - 1, 0))),
            whole(row_of(step_bias)), whole(row_of(decay_log)), whole(row_of(skip_gain)), whole(row_of(gate_gain)),
            whole(spread2),
        ],
        [
            (whole_spec((steps, 16, L)), (steps, 16, L), F32), (whole_spec((HALO, width)), (HALO, width), BF),
            (whole_spec((HALO, 1)), (HALO, 1), F32), (whole_spec((8, LANES)), (8, LANES), F32),
            (whole_spec((8, inner)), (8, inner), F32),
        ],
        us=2,
    )
    token_halo = shift_over(sent, "seq", 1)

    big = 512
    blocks = rows // big

    def rows_spec(cols, start=0, size=big):
        return pl.BlockSpec((size, cols), lambda i, *_: (i + start, 0))

    def fixed(shape):
        return pl.BlockSpec(shape, lambda i, *_: (0,) * len(shape))

    normed, scale_in, inner_raw = run(
        proj_kernel,
        (blocks,),
        [(tokens, rows_spec(width)), whole(gain_row), whole(w_inner)],
        [
            (rows_spec(width), (rows, width), BF),
            (rows_spec(1), (rows, 1), F32),
            (rows_spec(inner), (rows, inner), BF),
        ],
        us=12,
    )
    halo_shape = (HALO, inner + side)
    side_raw, halo, w_side, taps = run(
        side_kernel,
        (blocks,),
        [(normed, rows_spec(width))]
        + [whole(p) for p in pair_pieces]
        + [whole(w_step.T), whole(token_halo), whole(gain_row), whole(w_inner), whole(conv_inner), whole(row_of(bias_inner))],
        [
            (rows_spec(side), (rows, side), F32),
            (fixed(halo_shape), halo_shape, F32),
            (fixed((side, width)), (side, width), BF),
            (fixed((8, wide)), (8, wide), F32),
        ],
        ids="swap",
        us=10,
    )

    low_rows = N + HALO
    act, pact, dt, cs, closing, closing_low, through = run(
        chunked(conv_kernel, "rrs-----rrrr", False, many),
        (steps // many,),
        [
            (inner_raw, chunk_spec(inner, ahead_many)), (side_raw, chunk_spec(side, ahead_many)), (info, slab_spec(16, L, ahead_many)),
            whole(halo), whole(taps), whole(head_rows), whole(lower), whole(spread2),
        ],
        [
            (chunk_spec(inner, ahead_many), (rows, inner), BF), (chunk_spec(pair, ahead_many), (rows, pair), BF),
            (chunk_spec(LANES, ahead_many), (rows, LANES), F32), (chunk_spec(LANES, ahead_many), (rows, LANES), F32),
            (whole_spec((N, inner)), (N, inner), F32), (whole_spec((low_rows, inner)), (low_rows, inner), BF),
            (whole_spec((8, inner)), (8, inner), F32),
        ],
        scratch=[pltpu.VMEM((8 + L, wide), F32), pltpu.VMEM((8, LANES), F32)],
        us=17,
    )

    seq_count = lax.axis_size("seq")
    seq_place = lax.axis_index("seq")

    def exchange(state, low, rows0, known, reverse, between):
        before, row, factors = None, rows0, []
        bit = 1
        while bit < seq_count:
            arrived = flip(low, "seq", bit)
            if between:
                between.pop(0)()
            final = bit * 2 >= seq_count
            has = known is not None
            ins = [whole(arrived), whole(state), whole(row)]
            if before is not None:
                ins.append(whole(before))
            if has:
                ins.append(whole(known[len(factors)]))
            big_out = (fixed((N, inner)), (N, inner), F32)
            outs = [big_out, (fixed((8, inner)), (8, inner), F32)]
            if not final:
                height = N if has else low_rows
                outs += [big_out, (fixed((height, inner)), (height, inner), BF)]
            got = run(
                functools.partial(combine_kernel, reverse, before is None, has, final),
                one_step,
                ins,
                outs,
                ids=("rev%d" if reverse else "fwd%d") % bit,
                us=2,
            )
            before, row = got[0], got[1]
            factors.append(row)
            if not final:
                state, low = got[2], got[3]
            bit *= 2
        for work in between:
            work()
        return before, factors

    def product(kernel, x, w, start, size, into):
        out = [] if into is None else [(into, ANY)]
        return run(
            kernel,
            (size,),
            [(x, rows_spec(x.shape[1], start)), whole(w)] + out,
            [(rows_spec(inner, start), (rows, inner), BF)],
            aliases={2: 0} if out else None,
            us=2.9 * size,
        )[0]

    third = max(blocks // 3, 1)
    held = {}

    def gate_one():
        held["gate"] = product(nn_kernel, normed, w_gate, 0, blocks - third, None)

    def gate_two():
        held["gate"] = product(nn_kernel, normed, w_gate, blocks - third, third, held["gate"])
        held["dgn"] = product(nt_kernel, cotangent, w_output, 0, third, None)

    def gate_three():
        held["dgn"] = product(nt_kernel, cotangent, w_output, third, blocks - third, held["dgn"])

    state_in, factors = exchange(closing, closing_low, through, None, False, [gate_one, gate_two, gate_three])
    gate_pre, dgn = held["gate"], held["dgn"]

    mixed, gg, sums, entries = run(
        chunked(out_kernel, "rrrrsrr---rrss", False, few),
        (steps // few,),
        [
            (act, chunk_spec(inner, ahead_few)), (pact, chunk_spec(pair, ahead_few)), (dt, chunk_spec(LANES, ahead_few)),
            (cs, chunk_spec(LANES, ahead_few)), (info, slab_spec(16, L, ahead_few)),
            (gate_pre, chunk_spec(inner, ahead_few)), (dgn, chunk_spec(inner, ahead_few)),
            whole(state_in), whole(gains), whole(spread2),
        ],
        [
            (chunk_spec(inner, ahead_few), (rows, inner), BF), (chunk_spec(inner, ahead_few), (rows, inner), BF),
            (slab_spec(2, L, ahead_few), (steps, 2, L), F32), (slab_spec(N, inner, ahead_few), (steps, N, inner), BF),
        ],
        scratch=[pltpu.VMEM((N, inner), F32)],
        us=18,
    )

    order = [place ^ 3, place ^ 1, place ^ 2, place]

    def quarter_spec():
        return pl.BlockSpec((big, quarter), lambda i, ids: (i, 0))

    def out_quarter(which, got, dtype, after=()):
        ins = [
            (gg, pl.BlockSpec((big, inner), lambda i, ids: (i, 0))),
            (w_output, pl.BlockSpec((inner, quarter), lambda i, ids: (0, ids[0]))),
        ]
        if got is not None:
            ins.append((got, quarter_spec()))
        return run(
            cols_kernel if got is None else cols_add_kernel,
            (blocks,),
            ins,
            [(quarter_spec(), (rows, quarter), dtype)],
            after=after,
            ids="order%d" % which,
            us=5,
        )[0]

    sums_core = flip(sums, "head", 1)
    out_a = out_quarter(0, None, BF)
    sums = sums + sums_core
    got_a = flip(out_a, "head", 1)
    sums_x = flip(sums, "head", 2)
    out_b = out_quarter(1, None, BF, [sums_core])
    got_b = flip(out_b, "head", 1)
    scale_out = lax.rsqrt((sums + sums_x)[:, 0, :] / DI + EPS).reshape(rows, 1)

    share = width // seq_count
    manual = seq_count == 8
    half = seq_count // 2
    seq_core = seq_place % 2
    if not manual:
        share = 256

    def weight_rows(which, x, ys, scale=None, into=()):
        count = len(row_ids[which])
        ins = [(x, pl.BlockSpec((rows, share), lambda i, ids: (0, ids[i])))]
        if scale is not None:
            ins.append(whole(scale))
        outs = []
        lead = count * which
        for y, cols, at in ys:
            ins.append((y, pl.BlockSpec((rows, cols), lambda i, ids, at=at: (0, at))))
            if cols == side:
                spec = pl.BlockSpec((share, LANES), lambda i, ids: (i + lead, 0))
                outs += [(spec, (width, LANES), BF)] * 3
            else:
                outs.append((pl.BlockSpec((share, cols), lambda i, ids: (i, 0)), (count * share, cols), BF))
        aliases = {len(ins) + k: len(outs) - 3 + k for k in range(len(into))}
        return run(
            functools.partial(weight_kernel, scale is not None, len(ys), len(into)),
            (count,),
            ins + [(a, ANY) for a in into],
            outs,
            ids="rows%d" % which,
            aliases=aliases,
            us=8,
        )

    z = seq_place // 2

    class Halving:
        def __init__(self, pieces):
            ins = []
            for kept, got in pieces:
                cols = kept.shape[1]
                for first in (0, 2):
                    spec = pl.BlockSpec((share, cols), lambda i, ids, f=first: (ids[f + i], 0))
                    ins += [(kept, spec), (got, spec)]
            self.cols = sum(kept.shape[1] for kept, _ in pieces)
            self.count = len(pieces)
            out = pl.BlockSpec((share, self.cols), lambda i, ids: (i, 0))
            sent, self.kept = run(
                functools.partial(split_kernel, self.count),
                (2,),
                ins,
                [(out, (2 * share, self.cols), BF), (out, (2 * share, self.cols), F32)],
                ids="split",
                us=3,
            )
            self.got = flip(sent, "seq", 2)

        def middle(self):
            part = share // 2
            ins = []
            for w in (0, 1):
                spec = pl.BlockSpec((part, self.cols), lambda i, ids, w=w: (ids[w] * 2 + i, 0))
                ins += [(self.kept, spec), (self.got, spec)]
            out = pl.BlockSpec((part, self.cols), lambda i, ids: (i, 0))
            sent, self.kept = run(
                functools.partial(split_kernel, 1),
                (2,),
                ins,
                [(out, (share, self.cols), BF), (out, (share, self.cols), F32)],
                ids="middle",
                us=2,
            )
            self.got = flip(sent, "seq", 4)

        def end(self, into=None, place=0, total=1, turned=False):
            if turned:
                shape = block = (self.cols, share)
            else:
                shape, block = (share, self.cols * total), (share, self.cols)
            ins = [whole(self.kept), whole(self.got)] + ([] if into is None else [(into, ANY)])
            return run(
                end_kernel,
                one_step,
                ins,
                [(pl.BlockSpec(block, lambda i: (0, place)), shape, F32)],
                aliases=None if into is None else {2: 0},
                us=2,
            )[0]

    (out_first,) = weight_rows(0, cotangent, [(gg, inner, 0)], scale_out)
    if manual:
        out_got = flip(out_first, "seq", 1)
    away = out_quarter(2, got_a, BF)
    away_got = flip(away, "head", 2)
    mine = out_quarter(3, got_b, F32)
    if manual:
        (out_second,) = weight_rows(1, cotangent, [(gg, inner, 0)], scale_out)

    dmix, dgate, stat, dstate_local, dstate_low, dgain, dskip = run(
        chunked(gate_kernel, "rrrrrrsss--" + "rrs", True, many),
        (steps // many,),
        [
            (mixed, chunk_spec(inner, behind_many)), (gate_pre, chunk_spec(inner, behind_many)), (dgn, chunk_spec(inner, behind_many)),
            (act, chunk_spec(inner, behind_many)), (pact, chunk_spec(pair, behind_many)), (cs, chunk_spec(LANES, behind_many)),
            (info, slab_spec(16, L, behind_many)), (sums, slab_spec(2, L, behind_many)), (sums_x, slab_spec(2, L, behind_many)),
            whole(gains), whole(spread2),
        ],
        [
            (chunk_spec(inner, behind_many), (rows, inner), BF), (chunk_spec(inner, behind_many), (rows, inner), BF),
            (slab_spec(8, L, behind_many), (steps, 8, L), F32), (whole_spec((N, inner)), (N, inner), F32),
            (whole_spec((N, inner)), (N, inner), BF),
            (whole_spec((8, inner)), (8, inner), F32), (whole_spec((8, inner)), (8, inner), F32),
        ],
        us=17,
    )

    order_ids = jnp.stack(order).astype(jnp.int32)

    def gate_first():
        held["first"] = weight_rows(0, normed, [(dgate, inner, 0)])[0]

    def gate_second():
        if manual:
            held["got"] = flip(held["first"], "seq", 1)
            held["second"] = weight_rows(1, normed, [(dgate, inner, 0)])[0]

    def gate_third():
        held["dn"] = run(
            gate_back_kernel,
            (4, blocks),
            [
                (dgate, pl.BlockSpec((big, inner), lambda n, i, ids: (i, 0))),
                (w_gate, pl.BlockSpec((quarter, inner), lambda n, i, ids: (ids[n], 0))),
            ],
            [(pl.BlockSpec((1, big, quarter), lambda n, i, ids: (n, i, 0)), (4, rows, quarter), BF)],
            ids="order",
            us=17,
        )[0]

    dstate, _ = exchange(
        dstate_local, dstate_low, through, factors, True, [gate_first, gate_second, gate_third]
    )
    dn_gate = held["dn"]

    def back_chunks(count, final):
        kinds = "rrrrsrsrr" + "-" * 15 + "s" + "-" * count + "rrs"
        kernel = functools.partial(back_kernel, count, final)

        def run_all(*refs):
            chunked(lambda turn, *views: kernel(turn, *views[:-2], refs[7], refs[8], *views[-2:]), kinds, True, 1)(*refs)

        return run_all

    parts = 3 if steps % 3 == 0 else 1
    each = steps // parts
    carried = jnp.zeros((8, wide), F32)
    dtaps = jnp.zeros((40, wide), F32)
    dhead = jnp.zeros((16, LANES), F32)
    d_inner = d_side = small = dhalo = None
    if manual:
        out_sum = Halving([(out_second, out_got)])
    for part in range(parts):
        first = steps - 1 - part * each
        at = Place(1, lambda c, first=first: first - c)

        def near_end(c, at=at):
            return jnp.maximum(at.at(c) * (L // HALO) - 1, 0)

        final = part == parts - 1
        if manual and part == 1:
            out_sum.middle()
        if manual and part == 2:
            dw_out = out_sum.end(turned=True)
            gate_sum = Halving([(held["second"], held["got"])])
        grown = [] if d_inner is None else [(d_inner, ANY), (d_side, ANY)]
        state_specs = [
            (whole_spec((N, inner)), (N, inner), F32), (whole_spec((8, wide)), (8, wide), F32),
            (whole_spec((40, wide)), (40, wide), F32), (whole_spec((16, LANES)), (16, LANES), F32),
        ]
        if final:
            state_specs += [(whole_spec((8, wide)), (8, wide), F32)] * 2
        ins = [
            (act, chunk_spec(inner, at)), (pact, chunk_spec(pair, at)), (dt, chunk_spec(LANES, at)),
            (cs, chunk_spec(LANES, at)), (info, slab_spec(16, L, at)),
            (dmix, chunk_spec(inner, at)), (entries, slab_spec(N, inner, at)),
            (inner_raw, chunk_spec(inner, at)), (side_raw, chunk_spec(side, at)),
            (inner_raw, pl.BlockSpec((HALO, inner), lambda c, p=near_end: (p(c), 0))),
            (side_raw, pl.BlockSpec((HALO, side), lambda c, p=near_end: (p(c), 0))),
            whole(halo), whole(taps), whole(head_rows), whole(gains), whole(lower), whole(spread2), whole(gather),
            whole(dstate), whole(carried), whole(dtaps), whole(dhead), whole(dgain), whole(dskip),
            (stat, slab_spec(8, L, at)), *grown,
        ]
        aliases = {24: 2}
        if grown:
            aliases.update({25: 0, 26: 1})
        got = run(
            back_chunks(len(grown), final),
            (each,),
            ins,
            [
                (chunk_spec(inner, at), (rows, inner), BF), (chunk_spec(side, at), (rows, side), BF),
                (slab_spec(8, L, at), (steps, 8, L), F32), *state_specs,
            ],
            after=[away_got] if part == min(1, parts - 1) else [],
            scratch=[pltpu.VMEM((8 + L, wide), F32), pltpu.VMEM((L + 8, wide), F32)],
            aliases=aliases,
            us=64 / parts,
        )
        d_inner, d_side, stat, dstate, carried, dtaps, dhead = got[:7]
        if final:
            small, dhalo = got[7:]

    if manual:
        gate_sum.middle()
    returned = shift_over(dhalo, "seq", -1)
    small_got = flip(small, "seq", 1)

    def last_rows(cols):
        return pl.BlockSpec((HALO, cols), lambda c: (rows // HALO - 1, 0))

    last_slab = slab_spec(8, L, Place(1, lambda c: steps - 1))
    d_inner, d_side, stat, small = run(
        fix_kernel,
        one_step,
        [
            (inner_raw, last_rows(inner)), (side_raw, last_rows(side)), whole(keep_tail), whole(returned),
            whole(small), whole(small_got),
            (d_inner, last_rows(inner)), (d_side, last_rows(side)), (stat, last_slab),
        ],
        [
            (last_rows(inner), (rows, inner), BF), (last_rows(side), (rows, side), BF), (last_slab, (steps, 8, L), F32),
            (whole_spec((8, wide)), (8, wide), F32),
        ],
        aliases={6: 0, 7: 1, 8: 2},
        us=2,
    )

    def add(pairs):
        return run(
            functools.partial(add_kernel, len(pairs)),
            one_step,
            [whole(a) for pair_ in pairs for a in pair_],
            [(pl.BlockSpec(a.shape, lambda i, n=a.ndim: (0,) * n), a.shape, a.dtype) for a, _ in pairs],
            us=1,
        )

    half_inner = inner // 2
    swap_id = swap.astype(jnp.int32).reshape(1)
    inner_parts = [(d_inner, half_inner, 0), (d_inner, half_inner, 1), (d_side, side, 0)]

    swap_id = swap.astype(jnp.int32).reshape(1)
    stat = stat[:, 0, :]

    def twin(pair_at, got, dtypes, into=None):
        lead = half if into is not None else 0

        def which(s):
            return jnp.clip((s - lead) // blocks, 0, 1)

        def row(s):
            return jnp.where(s < lead, 0, (s - lead) % blocks)

        def x_at(s, ids):
            return (0, ids[2 + jnp.minimum(s, lead - 1)]) if lead else (0, 0)

        def out_at(s, w):
            return jnp.clip(s - lead - w * blocks, 0, blocks - 1)

        ins = [
            (normed, pl.BlockSpec((rows if lead else 256, 256), x_at)),
            whole(d_inner), whole(d_side),
            (w_inner, pl.BlockSpec((quarter, inner), lambda s, ids: (ids[which(s)], 0))),
            (w_side, pl.BlockSpec((side, quarter), lambda s, ids: (0, ids[which(s)]))),
            (dn_gate, pl.BlockSpec((1, big, quarter), lambda s, ids: (pair_at + which(s), row(s), 0))),
        ]
        for w, block in enumerate(got):
            ins.append((block, pl.BlockSpec((big, quarter), lambda s, ids, w=w: (out_at(s, w), 0))))
        aliases = {}
        outs = []
        if lead:
            last = lead - 1
            aliases = {len(ins) + k: 2 + k for k in range(3)}
            ins += [(a, ANY) for a in into]
            wide_spec = pl.BlockSpec((share, inner // 2), lambda s, ids: (jnp.minimum(s, last), 0))
            side_spec = pl.BlockSpec((share, LANES), lambda s, ids: (lead + jnp.minimum(s, last), 0))
            outs += [(wide_spec, (lead * share, inner // 2), BF)] * 2 + [(side_spec, (width, LANES), BF)] * 3
        for w in (0, 1):
            spec = pl.BlockSpec((big, quarter), lambda s, ids, w=w: (out_at(s, w), 0))
            outs.append((spec, (rows, quarter), dtypes[w]))
        return run(
            functools.partial(twin_kernel, lead, blocks, len(got)),
            (lead + 2 * blocks,),
            ins,
            outs,
            ids="twin%d" % pair_at,
            aliases=aliases,
            us=22 if lead else 14,
        )

    first_a, first_b, sent, kept, step = weight_rows(0, normed, inner_parts)
    here = place.astype(jnp.int32).reshape(1)
    own_spec = pl.BlockSpec((big, quarter), lambda i, ids: (i, ids[0]))
    column = pl.BlockSpec((big, 1), lambda i, ids: (i, 0))
    result = run(
        result_kernel,
        (blocks,),
        [(tokens, own_spec), (scale_out, column), (mine, quarter_spec()), (away_got, quarter_spec())],
        [(quarter_spec(), (rows, quarter), BF)],
        ids="place",
        us=4,
    )[0]
    if manual:
        dw_gate = gate_sum.end()
    tall = pl.BlockSpec((1024, LANES), lambda i, *_: (i, 0))
    stat_got = flip(stat, "head", 1)
    small_got = flip(small, "seq", 2)
    if manual:
        got_a = flip(first_a, "seq", 1)
        got_b = flip(first_b, "seq", 1)
        second_a, second_b, sent, kept, step, dn_a, dn_b = twin(0, [], [BF, BF], [sent, kept, step])
    else:
        dn_a, dn_b = twin(0, [], [BF, BF])
    side_got = flip(sent, "head", 1)
    dn_got_a = flip(dn_a, "head", 1)
    dn_got_b = flip(dn_b, "head", 1)
    if manual:
        sum_a = Halving([(second_a, got_a)])
    stat, small = add([(stat, stat_got), (small, small_got)])
    stat_got = flip(stat, "head", 2)
    small_got = flip(small, "seq", 4)
    (stat,) = add([(stat, stat_got)])
    dn_away, dn_mine = twin(2, [dn_got_a, dn_got_b], [BF, F32])
    dn_away_got = flip(dn_away, "head", 2)
    if manual:
        sum_a.middle()
    joined = (pl.BlockSpec((width // 2, 2 * LANES), lambda i: (0, 0)), (width // 2, 2 * LANES), BF)
    rest_first, rest_second = run(
        join_kernel,
        (2,),
        [(kept, tall), (side_got, tall), (step, tall)],
        [joined, joined],
        us=3,
    )
    if manual:
        rest_got = flip(rest_first, "seq", 1)
        sum_b = Halving([(second_b, got_b)])
        sum_s = Halving([(rest_second, rest_got)])
    (small,) = add([(small, small_got)])
    bit = 8
    while bit < seq_count:
        small = small + flip(small, "seq", bit)
        bit *= 2
    if manual:
        sum_b.middle()
    small_pair = small[:, inner:]
    low_half, high_half = small_pair[:, : N // 2], small_pair[:, N // 2 : N]
    pair_kept = jnp.concatenate([low_half, small_pair[:, N : N + N // 2]], 1)
    pair_sent = jnp.concatenate([high_half, small_pair[:, N + N // 2 :]], 1)
    pair_got = flip(pair_sent, "head", 1)
    grad_tokens, norm_sum = run(
        final_kernel,
        (blocks,),
        [
            (tokens, own_spec), (cotangent, own_spec), (scale_in, column), (stat.reshape(rows, 1), column),
            (gain_row, pl.BlockSpec((1, quarter), lambda i, ids: (0, ids[0]))),
            (dn_mine, quarter_spec()), (dn_away_got, quarter_spec()),
        ],
        [
            (quarter_spec(), (rows, quarter), F32),
            (pl.BlockSpec((8, quarter), lambda i, ids: (0, 0)), (8, quarter), F32),
        ],
        ids="place",
        us=6,
    )
    norm_got = flip(norm_sum, "seq", 1)
    if manual:
        sum_s.middle()
    norm_sum = add([(norm_sum, norm_got)])[0]
    norm_got = flip(norm_sum, "seq", 2)
    pair_half = pl.BlockSpec((8, pair_cols), lambda i, *_: (0, 0))
    pair_full = pl.BlockSpec((8, N), lambda i, *_: (0, 0))
    pair_mine, pair_away = run(
        share_kernel,
        one_step,
        [(pair_kept, pair_full), (pair_got, pair_full)],
        [(pair_half, (8, pair_cols), F32)] * 2,
        ids="swap",
        us=1,
    )
    pair_got = flip(pair_away, "head", 2)
    norm_sum = add([(norm_sum, norm_got)])[0]
    norm_got = flip(norm_sum, "seq", 4)
    if manual:
        own_rows = (share, pair_cols)
        thin = (pl.BlockSpec(own_rows, lambda i, *_: (0, 0)), own_rows, F32)
        dw_inner, side_mine, side_sent, dw_step = run(
            close_kernel,
            one_step,
            [whole(block) for sum_ in (sum_a, sum_b, sum_s) for block in (sum_.kept, sum_.got)],
            [
                (pl.BlockSpec((share, inner), lambda i, *_: (0, 0)), (share, inner), F32), thin, thin,
                (pl.BlockSpec((LANES, share), lambda i, *_: (0, 0)), (LANES, share), F32),
            ],
            ids="swap",
            us=3,
        )
    else:
        dw_out, dw_gate, dw_inner, rest = [
            lax.psum_scatter(block, "seq", scatter_dimension=0, tiled=True).astype(F32)
            for block in (
                out_first,
                held["first"],
                jnp.concatenate([first_a, first_b], 1),
                jnp.concatenate([rest_first, rest_second], 0),
            )
        ]
        dw_out = jnp.transpose(dw_out)
        left, right = rest[:, :pair_cols], rest[:, pair_cols : 2 * pair_cols]
        side_mine, side_sent = jnp.where(swap, right, left), jnp.where(swap, left, right)
        dw_step = rest[:, LANES:].T
    side_got = flip(side_sent, "head", 2)
    bit = 8
    while bit < seq_count:
        norm_sum = norm_sum + norm_got
        norm_got = flip(norm_sum, "seq", bit)
        bit *= 2
    shapes = [
        (1, quarter), (4, inner), (1, inner), (4, pair_cols), (1, pair_cols), (1, heads), (1, heads), (1, heads),
        (1, inner), side_mine.shape[::-1],
    ]
    outs = run(
        unpack_kernel,
        one_step,
        [whole(a) for a in (small, pair_mine, pair_got, norm_sum, norm_got, side_mine, side_got)],
        [(pl.BlockSpec(shape, lambda i: (0, 0)), shape, F32) for shape in shapes],
        us=1,
    )
    norm_sum, taps_sum, bias_sum, pair_taps, pair_bias, step_sum, decay_sum, skip_sum, gain_sum, dw_pair = outs
    return (
        result,
        grad_tokens,
        norm_sum.reshape(-1),
        dw_gate,
        dw_inner,
        dw_pair.T,
        dw_step[:heads].T,
        taps_sum,
        pair_taps,
        bias_sum.reshape(-1),
        pair_bias.reshape(-1),
        step_sum.reshape(-1),
        decay_sum.reshape(-1),
        skip_sum.reshape(-1),
        gain_sum.reshape(-1),
        dw_out,
    )


def solution(mesh):
    return jax.shard_map(
        body,
        mesh=mesh,
        in_specs=(
            P("seq", None),
            P("seq"),
            P(),
            P(None, "head"),
            P(None, "head"),
            P(None, "head"),
            P(None, "head"),
            P(None, "head"),
            P(None, "head"),
            P("head"),
            P("head"),
            P("head"),
            P("head"),
            P("head"),
            P("head"),
            P("head", None),
            P("seq", None),
        ),
        out_specs=(
            P("seq", "head"),
            P("seq", "head"),
            P("head"),
            P("seq", "head"),
            P("seq", "head"),
            P("seq", "head"),
            P("seq", "head"),
            P(None, "head"),
            P(None, "head"),
            P("head"),
            P("head"),
            P("head"),
            P("head"),
            P("head"),
            P("head"),
            P("head", "seq"),
        ),
        check_vma=False,
    )
```

```python
import functools

import jax
import jax.numpy as jnp
import numpy as np
from jax import lax
from jax.experimental import pallas as pl
from jax.experimental.pallas import tpu as pltpu
from jax.sharding import PartitionSpec as P

N = 128
HP = 64
DI = 4096
EPS = 1e-05
L = 128
LANES = 128
HALO = 16
F32 = jnp.float32
BF = jnp.bfloat16
VMEM_LIMIT = 64 * 1024 * 1024 - 65536
FIRST = (((0,), (0,)), ((), ()))
LAST = (((1,), (1,)), ((), ()))


def dot(a, b):
    return jnp.dot(a, b, preferred_element_type=F32)


def dotg(a, b, dims):
    return lax.dot_general(a, b, dims, preferred_element_type=F32)


def split2(v):
    hi = v.astype(BF)
    return hi, (v - hi.astype(F32)).astype(BF)


def split3(v):
    hi = v.astype(BF)
    rest = v - hi.astype(F32)
    mid = rest.astype(BF)
    return hi, mid, (rest - mid.astype(F32)).astype(BF)


def exact_sum(tri, v):
    hi, mid, lo = split3(v)
    return dot(tri, hi) + dot(tri, mid) + dot(tri, lo)


def expand(v, spread2):
    hi, lo = split2(v)
    return dot(jnp.concatenate([hi, lo], 1), spread2)


def fold8(v):
    return jnp.sum(v.reshape(v.shape[0] // 8, 8, v.shape[1]), axis=0)


def stacked_pair(v, left):
    zero = jnp.zeros_like(v)
    return jnp.concatenate([jnp.where(left, v, zero), jnp.where(left, zero, v)], 0)


def lane_is_left(shape):
    return lax.broadcasted_iota(jnp.int32, shape, 1) < HP


def columns(slab):
    pad = LANES - slab.shape[0]
    return jnp.concatenate([slab, jnp.zeros((pad, L), F32)], 0).T


def mask_of(info, seg_row):
    rows = lax.broadcasted_iota(jnp.int32, (L, L), 0)
    cols = lax.broadcasted_iota(jnp.int32, (L, L), 1)
    linked = (info[:, 0:1] == seg_row) & (rows >= cols)
    return jnp.where(linked, 0.0, -1e30).astype(F32)


def turned(v):
    return v.astype(F32).T.astype(BF)


def sigmoid(v):
    return 0.5 * jnp.tanh(0.5 * v) + 0.5


class Place:
    def __init__(self, u, at):
        self.u, self.at = u, at


def chunk_spec(width, place):
    return pl.BlockSpec((place.u * L, width), lambda c: (place.at(c), 0))


def slab_spec(rows, width, place):
    return pl.BlockSpec((place.u, rows, width), lambda c: (place.at(c), 0, 0))


class Turn:
    def __init__(self, i, sub, u):
        self.i, self.sub, self.u = i, sub, u

    def first(self, work):
        if self.i == 0:
            pl.when(pl.program_id(0) == 0)(work)

    def last(self, work):
        if self.i == self.u - 1:
            pl.when(pl.program_id(0) == pl.num_programs(0) - 1)(work)


def chunked(kernel, kinds, reverse, u):
    def run_all(*refs):
        for i in range(u):
            sub = u - 1 - i if reverse else i
            views = []
            for n, ref in enumerate(refs):
                kind = kinds[n] if n < len(kinds) else "-"
                if kind == "r":
                    ref = ref.at[pl.ds(sub * L, L), :]
                elif kind == "s":
                    ref = ref.at[pl.ds(sub, 1)]
                views.append(ref)
            kernel(Turn(i, sub, u), *views)

    return run_all


def whole_spec(shape):
    return pl.BlockSpec(shape, lambda c: (0,) * len(shape))


ANY = pl.BlockSpec(memory_space=pl.ANY)


class Chain:
    def __init__(self):
        self.last = None
        self.factor = 1.0

    def run(self, kernel, grid, ins, outs, after=(), scratch=(), ids=None, aliases=None, us=5.0):
        given = [array for array, _ in ins]
        after = [a for a in list(after) + [self.last] if a is not None and not any(a is g for g in given)]
        lead = 0 if ids is None else 1
        keep_in = lead + len(ins)

        def inner(*refs):
            kernel(*refs[:keep_in], *refs[keep_in + len(after) :])

        result = pl.pallas_call(
            inner,
            grid_spec=pltpu.PrefetchScalarGridSpec(
                num_scalar_prefetch=lead,
                grid=grid,
                in_specs=[spec for _, spec in ins] + [ANY] * len(after),
                out_specs=[spec for spec, _, _ in outs],
                scratch_shapes=list(scratch),
            ),
            out_shape=[jax.ShapeDtypeStruct(shape, dtype) for _, shape, dtype in outs],
            input_output_aliases={lead + i: o for i, o in (aliases or {}).items()},
            compiler_params=pltpu.CompilerParams(
                dimension_semantics=("arbitrary",) * len(grid), vmem_limit_bytes=VMEM_LIMIT
            ),
            cost_estimate=pl.CostEstimate(flops=int(us * self.factor * 1.15e9), bytes_accessed=10**4, transcendentals=0),
        )(*(() if ids is None else (ids,)), *given, *after)
        self.last = min(result, key=lambda r: r.size)
        return result


def whole(array):
    zeros = (0,) * array.ndim
    return array, pl.BlockSpec(array.shape, lambda *_: zeros)


def norm_rows(block, gain):
    t = block.astype(F32)
    scale = lax.rsqrt(jnp.mean(t * t, axis=-1, keepdims=True) + EPS)
    return scale, (t * scale * gain).astype(BF)


def proj_kernel(tokens_ref, gain_ref, w_ref, normed_ref, scale_ref, inner_ref):
    scale, normed = norm_rows(tokens_ref[...], gain_ref[...])
    scale_ref[...] = scale
    normed_ref[...] = normed
    inner_ref[...] = dot(normed, w_ref[...]).astype(BF)


def along(v, k):
    zero = jnp.zeros((1, v.shape[1]), v.dtype)
    if k > 0:
        other = jnp.concatenate([zero, v[:-1]], 0)
        return jnp.concatenate([other[:, L - k :], v[:, : L - k]], 1)
    other = jnp.concatenate([v[1:], zero], 0)
    return jnp.concatenate([v[:, -k:], other[:, :-k]], 1)


def prep_kernel(
    starts_ref, upper_ref, tokens_ref, step_bias_ref, decay_ref, skip_ref, gate_gain_ref, spread_ref,
    info_ref, sent_ref, keep_ref, head_ref, gains_ref,
):
    starts = starts_ref[...].astype(F32)
    seg = dot(starts.astype(BF), upper_ref[...])
    m1 = 1.0 - starts
    m2 = m1 * (1.0 - along(starts, 1))
    m3 = m2 * (1.0 - along(starts, 2))
    seg_last = jnp.broadcast_to(seg[:, L - 1 :], seg.shape)
    one = jnp.ones_like(seg)
    zero = jnp.zeros_like(seg)
    fields = [
        seg, jnp.where(seg == 0, one, zero), jnp.where(seg == seg_last, one, zero), m1, m2, m3,
        along(m1, -1), along(m2, -2), along(m3, -3), jnp.where(seg_last == 0, one, zero),
    ]
    for i in range(16):
        info_ref[:, i, :] = fields[i] if i < len(fields) else zero
    rows = lax.broadcasted_iota(jnp.int32, (HALO, L), 0)
    lanes = lax.broadcasted_iota(jnp.int32, (HALO, L), 1)
    last = jnp.broadcast_to(starts[starts.shape[0] - 1 :, :], (HALO, L))
    later = jnp.sum(jnp.where(lanes > rows + L - HALO, last, 0.0), axis=1, keepdims=True)
    place = lax.broadcasted_iota(jnp.int32, (HALO, 1), 0)
    keep = jnp.where((later == 0) & (place >= HALO - 3), 1.0, 0.0)
    keep_ref[...] = keep
    sent_ref[...] = (tokens_ref[...].astype(F32) * keep).astype(BF)
    heads = step_bias_ref.shape[1]
    head_ref[...] = jnp.zeros_like(head_ref)
    head_ref[0:1, 0:heads] = step_bias_ref[...]
    head_ref[1:2, 0:heads] = -jnp.exp(decay_ref[...])
    head_ref[2:3, 0:heads] = skip_ref[...]
    gains_ref[...] = expand(jnp.broadcast_to(head_ref[2:3, :], (8, LANES)), spread_ref[...])
    gains_ref[1:2, :] = gate_gain_ref[...]


def side_kernel(
    swap_ref, normed_ref, own_ref, one_ref, two_ref, three_ref, w_step_ref, halo_ref, gain_ref, w_ref,
    conv_ref, bias_ref,
    side_ref, halo_out_ref, w_side_ref, taps_ref,
):
    @pl.when(pl.program_id(0) == 0)
    def _():
        width, inner = w_ref.shape
        near = jnp.concatenate([own_ref[...], one_ref[...]], 0)
        far = jnp.concatenate([two_ref[...], three_ref[...]], 0)
        swap = swap_ref[0] != 0
        first = jnp.where(swap, far, near)
        second = jnp.where(swap, near, far)
        w_side_ref[0:N, :] = first[:, :width]
        w_side_ref[N : 2 * N, :] = second[:, :width]
        heads = w_step_ref.shape[0]
        w_side_ref[2 * N : 2 * N + heads, :] = w_step_ref[...]
        w_side_ref[2 * N + heads :, :] = jnp.zeros((LANES - heads, width), BF)
        taps_ref[0:4, :inner] = conv_ref[...]
        taps_ref[4:5, :inner] = bias_ref[...]
        taps_ref[5:8, :inner] = jnp.zeros((3, inner), F32)
        for i, part in enumerate((first, second)):
            extra = part[:, width:].astype(F32).T
            taps_ref[:, inner + i * N : inner + (i + 1) * N] = extra[0:8] + extra[8:16] + extra[16:24]
        _, halo = norm_rows(halo_ref[...], gain_ref[...])
        halo_out_ref[:, :inner] = dot(halo, w_ref[...])
        halo_out_ref[:, inner:] = dotg(halo, w_side_ref[...], LAST)

    side_ref[...] = dotg(normed_ref[...], w_side_ref[...], LAST)


def combine_kernel(
    reverse, first, known, final,
    follows_ref, arrived_ref, state_ref, rows_ref, *rest,
):
    rest = list(rest)
    before_ref = None if first else rest.pop(0)
    factor_ref = rest.pop(0) if known else None
    follows = follows_ref[0] != 0
    n = state_ref.shape[0]
    other = arrived_ref[0:n, :].astype(F32)
    if known:
        factor = factor_ref[2:3, :]
    else:
        extra = arrived_ref[n : n + 3, :].astype(F32)
        factor = extra[0:1] + extra[1:2] + extra[2:3]
    through = rows_ref[0:1, :]
    past = jnp.ones_like(through) if first else rows_ref[1:2, :]
    before = jnp.zeros_like(other) if first else before_ref[...]
    rest.pop(0)[...] = jnp.where(follows, before + past * other, before)
    new_rows = rest.pop(0)
    if first:
        new_rows[...] = jnp.zeros_like(new_rows)
    else:
        new_rows[...] = rows_ref[...]
    product = through * factor
    new_rows[0:1, :] = product
    new_rows[1:2, :] = jnp.where(follows, past * factor, past)
    new_rows[2:3, :] = factor
    if not final:
        state = state_ref[...]
        state = jnp.where(follows, state + through * other, other + factor * state)
        rest.pop(0)[...] = state
        low_ref = rest.pop(0)
        low_ref[0:n, :] = state.astype(BF)
        if not known:
            low_ref[n:, :] = factor_rows(product)


def factor_rows(row):
    hi, mid, lo = split3(row)
    return jnp.concatenate([hi, mid, lo, jnp.zeros((HALO - 3, row.shape[1]), BF)], 0)


def split_kernel(count, _, *refs):
    sent, kept = refs[4 * count :]
    at = 0
    for i in range(count):
        sent_kept, sent_got, kept_kept, kept_got = refs[4 * i : 4 * i + 4]
        cols = slice(at, at + sent_kept.shape[1])
        at = cols.stop
        sent[:, cols] = (sent_kept[...].astype(F32) + sent_got[...].astype(F32)).astype(BF)
        kept[:, cols] = kept_kept[...].astype(F32) + kept_got[...].astype(F32)


def end_kernel(kept, got, *rest):
    total = kept[...] + got[...].astype(F32)
    rest[-1][...] = total.T if rest[-1].shape != total.shape else total


def add_kernel(count, *refs):
    for i in range(count):
        refs[2 * count + i][...] = refs[2 * i][...] + refs[2 * i + 1][...]


def share_kernel(swap_ref, kept_ref, got_ref, mine_ref, sent_ref):
    total = kept_ref[...].astype(F32) + got_ref[...].astype(F32)
    half = total.shape[1] // 2
    left, right = total[:, :half], total[:, half:]
    swap = swap_ref[0] != 0
    mine_ref[...] = jnp.where(swap, right, left)
    sent_ref[...] = jnp.where(swap, left, right).astype(sent_ref.dtype)


def join_kernel(kept_ref, got_ref, step_ref, first_ref, second_ref):
    def write(out_ref):
        out_ref[:, :LANES] = (kept_ref[...].astype(F32) + got_ref[...].astype(F32)).astype(BF)
        out_ref[:, LANES:] = step_ref[...]

    pl.when(pl.program_id(0) == 0)(lambda: write(first_ref))
    pl.when(pl.program_id(0) == 1)(lambda: write(second_ref))


def close_kernel(
    swap_ref, kept_a, got_a, kept_b, got_b, kept_s, got_s, inner_ref, mine_ref, sent_ref, step_ref
):
    half = kept_a.shape[1]
    inner_ref[:, :half] = kept_a[...] + got_a[...].astype(F32)
    inner_ref[:, half:] = kept_b[...] + got_b[...].astype(F32)
    rest = kept_s[...] + got_s[...].astype(F32)
    left, right = rest[:, : LANES // 2], rest[:, LANES // 2 : LANES]
    swap = swap_ref[0] != 0
    mine_ref[...] = jnp.where(swap, right, left)
    sent_ref[...] = jnp.where(swap, left, right)
    step_ref[...] = rest[:, LANES:].T


def unpack_kernel(
    small_ref, pair_ref, pair_got, norm_ref, norm_got, side_ref, side_got,
    norm_out, taps_out, bias_out, pair_taps_out, pair_bias_out, step_out, decay_out, skip_out, gain_out, side_out,
):
    inner = taps_out.shape[1]
    heads = step_out.shape[1]
    pair = pair_ref[...] + pair_got[...]
    norm_out[...] = jnp.sum(norm_ref[...] + norm_got[...], axis=0, keepdims=True)
    taps_out[...] = small_ref[0:4, :inner]
    bias_out[...] = small_ref[4:5, :inner]
    gain_out[...] = small_ref[5:6, :inner]
    pair_taps_out[...] = pair[0:4]
    pair_bias_out[...] = pair[4:5]
    skip_out[...] = small_ref[6:7, 0:heads]
    step_out[...] = small_ref[6:7, LANES : LANES + heads]
    decay_out[...] = small_ref[6:7, 2 * LANES : 2 * LANES + heads]
    side_out[...] = (side_ref[...] + side_got[...]).T


def result_kernel(_, tokens_ref, scale_ref, mine_ref, away_ref, out_ref):
    branch = mine_ref[...] + away_ref[...].astype(F32)
    out_ref[...] = (tokens_ref[...].astype(F32) + scale_ref[...] * branch).astype(BF)


def final_kernel(
    _, tokens_ref, cot_ref, scale_ref, stat_ref, gain_ref, mine_ref, away_ref, grad_ref, norm_ref
):
    scale = scale_ref[...]
    scaled = (mine_ref[...] + away_ref[...].astype(F32)) * scale
    tokens = tokens_ref[...].astype(F32)
    factor = scale * scale * stat_ref[...] * (1.0 / (mine_ref.shape[1] * lax.axis_size("head")))
    grad_ref[...] = cot_ref[...].astype(F32) + scaled * gain_ref[...] - tokens * factor

    @pl.when(pl.program_id(0) == 0)
    def _():
        norm_ref[...] = jnp.zeros_like(norm_ref)

    norm_ref[...] += fold8(scaled * tokens)


def fix_kernel(
    raw_ref, side_ref, keep_ref, back_ref, small_ref, small_got_ref, d_in, dside_in, stat_in,
    d_ref, dside_ref, stat_ref, small_out_ref,
):
    small_out_ref[...] = small_ref[...] + small_got_ref[...]
    inner = raw_ref.shape[1]
    pair = 2 * N
    back = jnp.concatenate([jnp.zeros((HALO - 8, inner + pair), F32), back_ref[...]], 0) * keep_ref[...]
    d_ref[...] = (d_in[...].astype(F32) + back[:, :inner]).astype(BF)
    dside_ref[...] = dside_in[...]
    dside_ref[:, :pair] = (dside_in[:, :pair].astype(F32) + back[:, inner:]).astype(BF)
    row = jnp.sum(back[:, :inner] * raw_ref[...].astype(F32), axis=1, keepdims=True)
    row = row + jnp.sum(back[:, inner:] * side_ref[:, :pair].astype(BF).astype(F32), axis=1, keepdims=True)
    tall = jnp.concatenate([jnp.zeros((L - HALO, LANES), F32), jnp.broadcast_to(row, (HALO, LANES))], 0)
    stat_ref[...] = stat_in[...]
    stat_ref[0] += tall.T[0:8, :]


def nn_kernel(x_ref, w_ref, *rest):
    rest[-1][...] = dot(x_ref[...], w_ref[...]).astype(BF)


def nt_kernel(x_ref, w_ref, *rest):
    rest[-1][...] = dotg(x_ref[...], w_ref[...], LAST).astype(BF)


def cols_kernel(_, x_ref, w_ref, out_ref):
    out_ref[...] = dot(x_ref[...], w_ref[...]).astype(out_ref.dtype)


def cols_add_kernel(_, x_ref, w_ref, got_ref, out_ref):
    out_ref[...] = (dot(x_ref[...], w_ref[...]) + got_ref[...].astype(F32)).astype(out_ref.dtype)


def gate_back_kernel(_, x_ref, w_ref, out_ref):
    out_ref[0] = dotg(x_ref[...], w_ref[...], LAST).astype(BF)


def weight_kernel(scaled, count, grown, _, x_ref, *rest):
    x = x_ref[...]
    if scaled:
        x = (x.astype(F32) * rest[0][...]).astype(BF)
        rest = rest[1:]
    outs = rest[count + grown :]
    for y_ref, out_ref in zip(rest[:count], outs):
        total = dotg(x, y_ref[...], FIRST)
        if len(outs) > count and y_ref is rest[count - 1]:
            half = N // 2
            out_ref[...] = jnp.concatenate([total[:, half:N], total[:, N + half : 2 * N]], 1).astype(BF)
            outs[-2][...] = jnp.concatenate([total[:, :half], total[:, N : N + half]], 1).astype(BF)
            outs[-1][...] = total[:, 2 * N :].astype(BF)
        else:
            out_ref[...] = total.astype(BF)


def twin_kernel(lead, blocks, adds, _, *refs):
    refs = list(refs)
    x_ref, d_ref, side_ref, w_ref, v_ref, base_ref = refs[:6]
    got = refs[6 : 6 + adds]
    outs = refs[-2 - (5 if lead else 0) :]
    step = pl.program_id(0)
    if lead:

        @pl.when(step < lead)
        def _():
            x = x_ref[...]
            half = N // 2
            cols = outs[0].shape[1]
            outs[0][...] = dotg(x, d_ref[:, :cols], FIRST).astype(BF)
            outs[1][...] = dotg(x, d_ref[:, cols:], FIRST).astype(BF)
            total = dotg(x, side_ref[...], FIRST)
            outs[2][...] = jnp.concatenate([total[:, half:N], total[:, N + half : 2 * N]], 1).astype(BF)
            outs[3][...] = jnp.concatenate([total[:, :half], total[:, N : N + half]], 1).astype(BF)
            outs[4][...] = total[:, 2 * N :].astype(BF)

    for which in (0, 1):

        @pl.when((step >= lead + which * blocks) & (step < lead + (which + 1) * blocks))
        def _():
            big = base_ref.shape[1]
            rows = pl.ds(pl.multiple_of((step - lead - which * blocks) * big, big), big)
            total = dotg(d_ref[rows, :], w_ref[...], LAST) + dot(side_ref[rows, :], v_ref[...])
            total = total + base_ref[0].astype(F32)
            if adds:
                total = total + got[which][...].astype(F32)
            out = outs[which - 2]
            out[...] = total.astype(out.dtype)


def conv_kernel(
    turn, raw_ref, side_ref, info_ref, halo_ref, taps_ref, head_ref, tri_ref, spread_ref,
    act_ref, pact_ref, dt_ref, cs_ref, state_ref, low_ref, rows_ref, buf, total_ref,
):
    inner = raw_ref.shape[1]
    groups = inner // LANES
    pair = pact_ref.shape[1]
    pair_groups = pair // LANES

    @turn.first
    def _():
        buf[0:8, :] = halo_ref[HALO - 8 :, : inner + pair].astype(BF).astype(F32)
        state_ref[...] = jnp.zeros_like(state_ref)
        total_ref[0:1, :] = jnp.zeros((1, LANES), F32)
        total_ref[1:8, :] = jnp.ones((7, LANES), F32)

    info = columns(info_ref[0])
    masks = [None] + [jnp.broadcast_to(info[:, 2 + k : 3 + k], (L, LANES)) for k in (1, 2, 3)]
    dt = jax.nn.softplus(side_ref[:, pair:] + head_ref[0:1, :])
    dt_ref[...] = dt
    cs = exact_sum(tri_ref[...], dt * head_ref[1:2, :])
    cs_ref[...] = cs
    closing = cs[L - 1 :, :]
    total_ref[0:1, :] += closing
    total_ref[1:2, :] = total_ref[1:2, :] * info[0:1, 9:10]
    tail = jnp.exp(closing - cs) * info[:, 2:3] * dt
    tail_wide = expand(tail, spread_ref[...])
    keep = jnp.exp(closing) * info[0:1, 9:10]
    keep_wide = expand(jnp.broadcast_to(keep, (8, LANES)), spread_ref[...])[0:1, :]
    acts = []
    for j in range(groups + pair_groups):
        cols = slice(j * LANES, (j + 1) * LANES)
        if j < groups:
            raw = raw_ref[:, cols].astype(F32)
        else:
            raw = side_ref[:, (j - groups) * LANES : (j - groups + 1) * LANES].astype(BF).astype(F32)
        buf[8 : 8 + L, cols] = raw
        pre = taps_ref[4:5, cols] + taps_ref[0:1, cols] * raw
        for k in (1, 2, 3):
            pre = pre + taps_ref[k : k + 1, cols] * buf[8 - k : 8 - k + L, cols] * masks[k]
        act = (pre * sigmoid(pre)).astype(BF)
        buf[0:8, cols] = raw[L - 8 :, :]
        if j < groups:
            act_ref[:, cols] = act
        else:
            pact_ref[:, (j - groups) * LANES : (j - groups + 1) * LANES] = act
    key_turned = turned(pact_ref[:, :N])
    for j in range(groups):
        cols = slice(j * LANES, (j + 1) * LANES)
        weighted = (act_ref[:, cols].astype(F32) * tail_wide[:, cols]).astype(BF)
        state_ref[:, cols] = keep_wide[:, cols] * state_ref[:, cols] + dot(key_turned, weighted)

    @turn.last
    def _():
        through = jnp.exp(total_ref[0:1, :]) * total_ref[1:2, :]
        rows_ref[...] = expand(jnp.broadcast_to(through, (8, LANES)), spread_ref[...])
        low_ref[0:N, :] = state_ref[...].astype(BF)
        low_ref[N:, :] = factor_rows(rows_ref[0:1, :])


def out_kernel(
    turn, act_ref, pact_ref, dt_ref, cs_ref, info_ref, gate_ref, dgn_ref, state_in_ref,
    gains_ref, spread_ref,
    mixed_ref, gg_ref, sums_ref, entry_ref, state,
):
    inner = act_ref.shape[1]
    groups = inner // LANES

    @turn.first
    def _():
        state[...] = state_in_ref[...]

    info = columns(info_ref[0])
    mask = mask_of(info, info_ref[0, 0:1, :])
    key = pact_ref[:, :N]
    key_turned = turned(key)
    query = pact_ref[:, N:]
    scores = dotg(query, key, LAST)
    dt = dt_ref[...]
    cs = cs_ref[...]
    cs_rows = cs.T
    closing = cs[L - 1 :, :]
    spread = spread_ref[...]
    dt_wide = expand(dt, spread)
    open_wide = expand(jnp.exp(cs) * info[:, 1:2], spread)
    tail_wide = expand(jnp.exp(closing - cs) * info[:, 2:3], spread)
    keep = jnp.exp(closing) * info[0:1, 9:10]
    keep_wide = expand(jnp.broadcast_to(keep, (8, LANES)), spread)[0:1, :]
    left = lane_is_left((L, LANES))
    square = jnp.zeros((L, LANES), F32)
    cross = jnp.zeros((L, LANES), F32)
    for j in range(groups):
        cols = slice(j * LANES, (j + 1) * LANES)
        x = act_ref[:, cols].astype(F32)
        xd = x * dt_wide[:, cols]
        xd_low = xd.astype(BF)
        weights = []
        for h in (2 * j, 2 * j + 1):
            factor = jnp.exp(cs[:, h : h + 1] - cs_rows[h : h + 1, :] + mask)
            weights.append((scores * factor).astype(BF))
        entry = state[:, cols].astype(BF)
        entry_ref[0, :, cols] = entry
        y = dot(jnp.concatenate(weights, 1), stacked_pair(xd_low, left))
        y = y + open_wide[:, cols] * dot(query, entry)
        mixed = y + gains_ref[0:1, cols] * x
        mixed_ref[:, cols] = mixed.astype(BF)
        gate = gate_ref[:, cols].astype(F32)
        gated = mixed * (gate * sigmoid(gate))
        gg = gated * gains_ref[1:2, cols]
        gg_ref[:, cols] = gg.astype(BF)
        square = square + gated * gated
        cross = cross + gg * dgn_ref[:, cols].astype(F32)
        weighted = (xd * tail_wide[:, cols]).astype(BF)
        state[:, cols] = keep_wide[:, cols] * state[:, cols] + dot(key_turned, weighted)
    lane = lax.broadcasted_iota(jnp.int32, (L, LANES), 1)
    both = jnp.where(
        lane == 0,
        jnp.sum(square, axis=1, keepdims=True),
        jnp.sum(cross, axis=1, keepdims=True),
    )
    sums_ref[0] = both.T[0:2, :]


def gate_kernel(
    turn, mixed_ref, gate_ref, dgn_ref, act_ref, pact_ref, cs_ref, info_ref, near_ref, far_ref, gains_ref, spread_ref,
    dmix_ref, dgate_ref, stat_ref, dstate_ref, low_ref, dgain_ref, dskip_ref,
):
    inner = act_ref.shape[1]
    groups = inner // LANES

    @turn.first
    def _():
        dstate_ref[...] = jnp.zeros_like(dstate_ref)
        dgain_ref[...] = jnp.zeros_like(dgain_ref)
        dskip_ref[...] = jnp.zeros_like(dskip_ref)

    info = columns(info_ref[0])
    both = near_ref[0] + far_ref[0]
    scale_row = lax.rsqrt(both[0:1, :] / DI + EPS)
    coef_row = scale_row * scale_row * scale_row * both[1:2, :] / DI
    stats = columns(jnp.concatenate([scale_row, coef_row, jnp.zeros((6, L), F32)], 0))
    scale = jnp.broadcast_to(stats[:, 0:1], (L, LANES))
    coef = jnp.broadcast_to(stats[:, 1:2], (L, LANES))
    cs = cs_ref[...]
    spread = spread_ref[...]
    open_wide = expand(jnp.exp(cs) * info[:, 1:2], spread)
    keep = jnp.exp(cs[L - 1 :, :]) * info[0:1, 9:10]
    keep_wide = expand(jnp.broadcast_to(keep, (8, LANES)), spread)[0:1, :]
    query_turned = turned(pact_ref[:, N:])
    row = jnp.zeros((L, LANES), F32)
    for j in range(groups):
        cols = slice(j * LANES, (j + 1) * LANES)
        mixed = mixed_ref[:, cols].astype(F32)
        gate = gate_ref[:, cols].astype(F32)
        dgn = dgn_ref[:, cols].astype(F32)
        x = act_ref[:, cols].astype(F32)
        sig = sigmoid(gate)
        act = gate * sig
        gated = mixed * act
        scaled = dgn * scale
        dgain_ref[:, cols] += fold8(scaled * gated)
        dgated = scaled * gains_ref[1:2, cols] - gated * coef
        dmix = dgated * act
        dgate = dgated * mixed * (sig + act * (1.0 - sig))
        dskip_ref[:, cols] += fold8(dmix * x)
        row = row + dgate * gate
        dgate_ref[:, cols] = dgate.astype(BF)
        low = dmix.astype(BF)
        dmix_ref[:, cols] = low
        opened = (low.astype(F32) * open_wide[:, cols]).astype(BF)
        dstate_ref[:, cols] = keep_wide[:, cols] * dstate_ref[:, cols] + dot(query_turned, opened)
    stat_ref[0] = jnp.broadcast_to(jnp.sum(row, axis=1, keepdims=True), (L, LANES)).T[0:8, :]

    @turn.last
    def _():
        low_ref[...] = dstate_ref[...].astype(BF)


def back_kernel(
    grown, final, turn,
    act_ref, pact_ref, dt_ref, cs_ref, info_ref, dmix_ref, entry_ref,
    raw_ref, side_ref, raw_prev_ref, side_prev_ref, halo_ref,
    taps_ref, head_ref, gains_ref, tri_ref, spread_ref, gather_ref,
    dstate_in_ref, carried_in_ref, dtaps_in_ref, dhead_in_ref, dgain_ref, dskip_ref, stat_in_ref, *rest,
):
    rest = list(rest[grown:])
    d_ref, dside_ref, stat_ref, dstate, carried_ref, dtaps_ref, dhead_ref = rest[:7]
    small_ref, dhalo_ref = rest[7:9] if final else (None, None)
    buf, dbuf = rest[-2:]
    inner = act_ref.shape[1]
    groups = inner // LANES
    pair = 2 * N
    wide = inner + pair

    @turn.first
    def _():
        dstate[...] = dstate_in_ref[...]
        if grown:
            dbuf[L:, :] = carried_in_ref[...]
            dtaps_ref[...] = dtaps_in_ref[...]
            dhead_ref[...] = dhead_in_ref[...]
        else:
            dbuf[L:, :] = jnp.zeros((8, wide), F32)
            dtaps_ref[...] = jnp.zeros_like(dtaps_ref)
            dhead_ref[...] = jnp.zeros_like(dhead_ref)

    if turn.sub:
        whole_raw, whole_side = rest[-4], rest[-3]
        start = turn.sub * L - HALO
        buf[0:8, :inner] = whole_raw[start + HALO - 8 : start + HALO, :].astype(F32)
        buf[0:8, inner:] = whole_side[start + HALO - 8 : start + HALO, :pair].astype(BF).astype(F32)
    else:
        near_inner = raw_prev_ref[HALO - 8 :, :].astype(F32)
        near_side = side_prev_ref[HALO - 8 :, :pair].astype(BF).astype(F32)
        if final:
            start = pl.program_id(0) == pl.num_programs(0) - 1
            halo = halo_ref[HALO - 8 :, :wide].astype(BF).astype(F32)
            near_inner = jnp.where(start, halo[:, :inner], near_inner)
            near_side = jnp.where(start, halo[:, inner:], near_side)
        buf[0:8, :inner] = near_inner
        buf[0:8, inner:] = near_side

    info = columns(info_ref[0])
    masks = [None] + [jnp.broadcast_to(info[:, 2 + k : 3 + k], (L, LANES)) for k in (1, 2, 3)]
    afters = [None] + [jnp.broadcast_to(info[:, 5 + k : 6 + k], (L, LANES)) for k in (1, 2, 3)]
    mask = mask_of(info, info_ref[0, 0:1, :])
    key = pact_ref[:, :N]
    query = pact_ref[:, N:]
    query_turned = turned(query)
    scores = dotg(query, key, LAST)
    dt = dt_ref[...]
    cs = cs_ref[...]
    cs_rows = cs.T
    closing = cs[L - 1 :, :]
    spread = spread_ref[...]
    dt_wide = expand(dt, spread)
    open_wide = expand(jnp.exp(cs) * info[:, 1:2], spread)
    tail_wide = expand(jnp.exp(closing - cs) * info[:, 2:3], spread)
    keep = jnp.exp(closing) * info[0:1, 9:10]
    keep_wide = expand(jnp.broadcast_to(keep, (8, LANES)), spread)[0:1, :]
    left = lane_is_left((L, LANES))

    def conv_back(j, raw, dact):
        cols = slice(j * LANES, (j + 1) * LANES)
        buf[8 : 8 + L, cols] = raw
        pre = taps_ref[4:5, cols] + taps_ref[0:1, cols] * raw
        moved = [raw]
        for k in (1, 2, 3):
            moved.append(buf[8 - k : 8 - k + L, cols] * masks[k])
            pre = pre + taps_ref[k : k + 1, cols] * moved[k]
        sig = sigmoid(pre)
        dpre = dact * (sig * (1.0 + pre * (1.0 - sig)))
        for k in range(4):
            dtaps_ref[8 * k : 8 * k + 8, cols] += fold8(dpre * moved[k])
        dtaps_ref[32:40, cols] += fold8(dpre)
        dbuf[0:L, cols] = dpre
        draw = taps_ref[0:1, cols] * dpre
        for k in (1, 2, 3):
            draw = draw + taps_ref[k : k + 1, cols] * dbuf[k : k + L, cols] * afters[k]
        dbuf[L : L + 8, cols] = dpre[0:8, :]
        if j < groups:
            d_ref[:, cols] = draw.astype(BF)
        else:
            dside_ref[:, (j - groups) * LANES : (j - groups + 1) * LANES] = draw.astype(BF)
        return draw * raw

    row = jnp.zeros((L, LANES), F32)
    dscores = jnp.zeros((L, L), F32)
    dkey = jnp.zeros((L, N), F32)
    dquery = jnp.zeros((L, N), F32)
    dcs = jnp.zeros((L, LANES), F32)
    ddt = jnp.zeros((L, LANES), F32)
    dclose = jnp.zeros((8, LANES), F32)
    for j in range(groups):
        cols = slice(j * LANES, (j + 1) * LANES)
        x = act_ref[:, cols].astype(F32)
        xd = (x * dt_wide[:, cols]).astype(BF)
        dm = dmix_ref[:, cols]
        dmf = dm.astype(F32)
        xdf = xd.astype(F32)
        factors = []
        weights = []
        for h in (2 * j, 2 * j + 1):
            factor = jnp.exp(cs[:, h : h + 1] - cs_rows[h : h + 1, :] + mask)
            factors.append(factor)
            weights.append((scores * factor).astype(BF))
        pair_x = stacked_pair(xd, left)
        pair_d = stacked_pair(dm, left)
        dweights = dotg(dm, pair_x, LAST)
        dscores = dscores + dweights[:, :L] * factors[0] + dweights[:, L:] * factors[1]
        y = dot(jnp.concatenate(weights, 1), pair_x)
        dxd = dotg(jnp.concatenate(weights, 0), pair_d, FIRST)
        entry = entry_ref[0, :, cols]
        dst = dstate[:, cols]
        dst_low = dst.astype(BF)
        opened = (dmf * open_wide[:, cols]).astype(BF)
        tailed = (xdf * tail_wide[:, cols]).astype(BF)
        from_state = dot(query, entry)
        to_state = dot(key, dst_low)
        out_part = tailed.astype(F32) * to_state
        diff = dmf * y + opened.astype(F32) * from_state - xdf * dxd - out_part
        dxd = dxd + to_state * tail_wide[:, cols]
        hi, lo = split2(diff)
        gather = gather_ref[cols, :]
        dcs = dcs + dot(hi, gather) + dot(lo, gather)
        ddt = ddt + dot((dxd * x).astype(BF), gather)
        close = fold8(out_part) + keep_wide[:, cols] * fold8(dst * entry.astype(F32))
        hi, lo = split2(close)
        dclose = dclose + dot(hi, gather) + dot(lo, gather)
        dquery = dquery + dotg(opened, entry, LAST)
        dkey = dkey + dotg(tailed, dst_low, LAST)
        dstate[:, cols] = keep_wide[:, cols] * dst + dot(query_turned, opened)
        dx = dxd * dt_wide[:, cols] + gains_ref[0:1, cols] * dmf
        row = row + conv_back(j, raw_ref[:, cols].astype(F32), dx)
    dscores = dscores.astype(BF)
    dquery = dquery + dot(dscores, key)
    dkey = dkey + dotg(dscores, query, FIRST)
    row = row + conv_back(groups, side_ref[:, :N].astype(BF).astype(F32), dkey)
    row = row + conv_back(groups + 1, side_ref[:, N:pair].astype(BF).astype(F32), dquery)
    later = dcs
    hi, mid, lo = split3(later)
    tri = tri_ref[...]
    da = dotg(tri, hi, FIRST) + dotg(tri, mid, FIRST) + dotg(tri, lo, FIRST)
    da = da + jnp.sum(dclose, axis=0, keepdims=True)
    ddt = ddt + head_ref[1:2, :] * da
    step = side_ref[:, pair:]
    dstep = ddt * sigmoid(step + head_ref[0:1, :])
    dhead_ref[0:8, :] += fold8(dstep)
    dhead_ref[8:16, :] += fold8(dt * da)
    dside_ref[:, pair:] = dstep.astype(BF)
    row = row + dstep * step
    stat_ref[0] = stat_in_ref[0] + jnp.broadcast_to(jnp.sum(row, axis=1, keepdims=True), (L, LANES)).T[0:8, :]

    @turn.last
    def _():
        carried_ref[...] = dbuf[L:, :]

    if final:

        @turn.last
        def _():
            for k in range(5):
                small_ref[k : k + 1, :] = jnp.sum(dtaps_ref[8 * k : 8 * k + 8, :], axis=0, keepdims=True)
            small_ref[5:8, :] = jnp.zeros((3, wide), F32)
            small_ref[5:6, :inner] = jnp.sum(dgain_ref[...], axis=0, keepdims=True)
            skip = jnp.broadcast_to(jnp.sum(dskip_ref[...], axis=0, keepdims=True), (8, inner))
            hi, lo = split2(skip)
            skip = dot(hi, gather_ref[...]) + dot(lo, gather_ref[...])
            small_ref[6:7, 0:LANES] = skip[0:1, :]
            small_ref[6:7, LANES : 2 * LANES] = jnp.sum(dhead_ref[0:8, :], axis=0, keepdims=True)
            small_ref[6:7, 2 * LANES : 3 * LANES] = (
                jnp.sum(dhead_ref[8:16, :], axis=0, keepdims=True) * head_ref[1:2, :]
            )
            dhalo_ref[...] = jnp.zeros((8, wide), F32)
            for j in range(groups + 2):
                cols = slice(j * LANES, (j + 1) * LANES)
                for k in (1, 2, 3):
                    reach = dbuf[L : L + 8, cols] * masks[k][0:8, :] * taps_ref[k : k + 1, cols]
                    dhalo_ref[8 - k :, cols] += reach[0:k, :]


def flip(block, axis, bit):
    count = lax.axis_size(axis)
    route = [(i, i ^ bit) for i in range(count)]
    return jax.tree.map(lambda a: lax.ppermute(a, axis, route), block)


def sum_over(block, axis):
    bit = 1
    while bit < lax.axis_size(axis):
        block = block + flip(block, axis, bit)
        bit *= 2
    return block


def shift_over(block, axis, distance):
    devices = range(lax.axis_size(axis))
    route = [(i, i + distance) for i in devices if i + distance in devices]
    return lax.ppermute(block, axis, route)


def body(
    tokens, boundary, norm_gain, w_gate, w_inner, w_pair, w_step, conv_inner, conv_pair,
    bias_inner, bias_pair, step_bias, decay_log, skip_gain, gate_gain, w_output, cotangent,
):
    rows, width = tokens.shape
    inner = w_gate.shape[1]
    heads = w_step.shape[1]
    head_count = lax.axis_size("head")
    place = lax.axis_index("head")
    quarter = width // head_count
    pair_cols = w_pair.shape[1]
    pair = pair_cols * head_count
    wide = inner + pair
    side = pair + LANES
    steps = rows // L
    chain = Chain()
    run = chain.run

    many = 2 if steps % 2 == 0 else 1
    few = 2 if steps % 2 == 0 else 1
    ahead_many = Place(many, lambda c: c)
    ahead_few = Place(few, lambda c: c)
    behind_many = Place(many, lambda c: steps // many - 1 - c)

    def row_of(v):
        return v.reshape(1, -1)

    head_of = np.arange(inner)[None, :] // HP == np.arange(LANES)[:, None]
    spread2 = jnp.asarray(np.concatenate([head_of, head_of], 0), BF)
    gather = jnp.asarray(head_of.T, BF)
    lower = jnp.asarray(np.tril(np.ones((L, L))), BF)
    upper = jnp.asarray(np.triu(np.ones((L, L))), BF)

    def split_low(v):
        hi, mid, lo = split3(v)
        return [hi, mid, lo]

    swap = (place & 2) != 0

    pair_small = jnp.concatenate([conv_pair, row_of(bias_pair), jnp.zeros((3, pair_cols), F32)], 0).T
    pair_own = jnp.concatenate([w_pair.T, *split_low(pair_small), jnp.zeros((pair_cols, LANES - 24), BF)], 1)
    pair_pieces = [pair_own] + [flip(pair_own, "head", d) for d in (1, 2, 3)]
    gain_row = row_of(norm_gain)

    one_step = (1,)
    info, sent, keep_tail, head_rows, gains = run(
        prep_kernel,
        one_step,
        [
            whole(boundary.reshape(steps, L)), whole(upper),
            (tokens, pl.BlockSpec((HALO, width), lambda c: (rows // HALO - 1, 0))),
            whole(row_of(step_bias)), whole(row_of(decay_log)), whole(row_of(skip_gain)), whole(row_of(gate_gain)),
            whole(spread2),
        ],
        [
            (whole_spec((steps, 16, L)), (steps, 16, L), F32), (whole_spec((HALO, width)), (HALO, width), BF),
            (whole_spec((HALO, 1)), (HALO, 1), F32), (whole_spec((8, LANES)), (8, LANES), F32),
            (whole_spec((8, inner)), (8, inner), F32),
        ],
        us=2,
    )
    token_halo = shift_over(sent, "seq", 1)

    big = 512
    blocks = rows // big

    def rows_spec(cols, start=0, size=big):
        return pl.BlockSpec((size, cols), lambda i, *_: (i + start, 0))

    def fixed(shape):
        return pl.BlockSpec(shape, lambda i, *_: (0,) * len(shape))

    normed, scale_in, inner_raw = run(
        proj_kernel,
        (blocks,),
        [(tokens, rows_spec(width)), whole(gain_row), whole(w_inner)],
        [
            (rows_spec(width), (rows, width), BF),
            (rows_spec(1), (rows, 1), F32),
            (rows_spec(inner), (rows, inner), BF),
        ],
        us=12,
    )
    halo_shape = (HALO, inner + side)
    side_raw, halo, w_side, taps = run(
        side_kernel,
        (blocks,),
        [(normed, rows_spec(width))]
        + [whole(p) for p in pair_pieces]
        + [whole(w_step.T), whole(token_halo), whole(gain_row), whole(w_inner), whole(conv_inner), whole(row_of(bias_inner))],
        [
            (rows_spec(side), (rows, side), F32),
            (fixed(halo_shape), halo_shape, F32),
            (fixed((side, width)), (side, width), BF),
            (fixed((8, wide)), (8, wide), F32),
        ],
        ids=swap.astype(jnp.int32).reshape(1),
        us=10,
    )

    low_rows = N + HALO
    act, pact, dt, cs, closing, closing_low, through = run(
        chunked(conv_kernel, "rrs-----rrrr", False, many),
        (steps // many,),
        [
            (inner_raw, chunk_spec(inner, ahead_many)), (side_raw, chunk_spec(side, ahead_many)), (info, slab_spec(16, L, ahead_many)),
            whole(halo), whole(taps), whole(head_rows), whole(lower), whole(spread2),
        ],
        [
            (chunk_spec(inner, ahead_many), (rows, inner), BF), (chunk_spec(pair, ahead_many), (rows, pair), BF),
            (chunk_spec(LANES, ahead_many), (rows, LANES), F32), (chunk_spec(LANES, ahead_many), (rows, LANES), F32),
            (whole_spec((N, inner)), (N, inner), F32), (whole_spec((low_rows, inner)), (low_rows, inner), BF),
            (whole_spec((8, inner)), (8, inner), F32),
        ],
        scratch=[pltpu.VMEM((8 + L, wide), F32), pltpu.VMEM((8, LANES), F32)],
        us=17,
    )

    seq_count = lax.axis_size("seq")
    seq_place = lax.axis_index("seq")

    def exchange(state, low, rows0, known, reverse, between):
        before, row, factors = None, rows0, []
        bit = 1
        while bit < seq_count:
            arrived = flip(low, "seq", bit)
            if between:
                between.pop(0)()
            follows = (seq_place & bit) != 0
            if reverse:
                follows = jnp.logical_not(follows)
            final = bit * 2 >= seq_count
            has = known is not None
            ins = [whole(arrived), whole(state), whole(row)]
            if before is not None:
                ins.append(whole(before))
            if has:
                ins.append(whole(known[len(factors)]))
            big_out = (fixed((N, inner)), (N, inner), F32)
            outs = [big_out, (fixed((8, inner)), (8, inner), F32)]
            if not final:
                height = N if has else low_rows
                outs += [big_out, (fixed((height, inner)), (height, inner), BF)]
            got = run(
                functools.partial(combine_kernel, reverse, before is None, has, final),
                one_step,
                ins,
                outs,
                ids=follows.astype(jnp.int32).reshape(1),
                us=2,
            )
            before, row = got[0], got[1]
            factors.append(row)
            if not final:
                state, low = got[2], got[3]
            bit *= 2
        for work in between:
            work()
        return before, factors

    def product(kernel, x, w, start, size, into):
        out = [] if into is None else [(into, ANY)]
        return run(
            kernel,
            (size,),
            [(x, rows_spec(x.shape[1], start)), whole(w)] + out,
            [(rows_spec(inner, start), (rows, inner), BF)],
            aliases={2: 0} if out else None,
            us=2.9 * size,
        )[0]

    third = max(blocks // 3, 1)
    held = {}

    def gate_one():
        held["gate"] = product(nn_kernel, normed, w_gate, 0, blocks - third, None)

    def gate_two():
        held["gate"] = product(nn_kernel, normed, w_gate, blocks - third, third, held["gate"])
        held["dgn"] = product(nt_kernel, cotangent, w_output, 0, third, None)

    def gate_three():
        held["dgn"] = product(nt_kernel, cotangent, w_output, third, blocks - third, held["dgn"])

    state_in, factors = exchange(closing, closing_low, through, None, False, [gate_one, gate_two, gate_three])
    gate_pre, dgn = held["gate"], held["dgn"]

    mixed, gg, sums, entries = run(
        chunked(out_kernel, "rrrrsrr---rrss", False, few),
        (steps // few,),
        [
            (act, chunk_spec(inner, ahead_few)), (pact, chunk_spec(pair, ahead_few)), (dt, chunk_spec(LANES, ahead_few)),
            (cs, chunk_spec(LANES, ahead_few)), (info, slab_spec(16, L, ahead_few)),
            (gate_pre, chunk_spec(inner, ahead_few)), (dgn, chunk_spec(inner, ahead_few)),
            whole(state_in), whole(gains), whole(spread2),
        ],
        [
            (chunk_spec(inner, ahead_few), (rows, inner), BF), (chunk_spec(inner, ahead_few), (rows, inner), BF),
            (slab_spec(2, L, ahead_few), (steps, 2, L), F32), (slab_spec(N, inner, ahead_few), (steps, N, inner), BF),
        ],
        scratch=[pltpu.VMEM((N, inner), F32)],
        us=18,
    )

    order = [place ^ 3, place ^ 1, place ^ 2, place]

    def quarter_spec():
        return pl.BlockSpec((big, quarter), lambda i, ids: (i, 0))

    def out_quarter(which, got, dtype, after=()):
        ins = [
            (gg, pl.BlockSpec((big, inner), lambda i, ids: (i, 0))),
            (w_output, pl.BlockSpec((inner, quarter), lambda i, ids: (0, ids[0]))),
        ]
        if got is not None:
            ins.append((got, quarter_spec()))
        return run(
            cols_kernel if got is None else cols_add_kernel,
            (blocks,),
            ins,
            [(quarter_spec(), (rows, quarter), dtype)],
            after=after,
            ids=order[which].reshape(1),
            us=5,
        )[0]

    sums_core = flip(sums, "head", 1)
    out_a = out_quarter(0, None, BF)
    sums = sums + sums_core
    got_a = flip(out_a, "head", 1)
    sums_x = flip(sums, "head", 2)
    out_b = out_quarter(1, None, BF, [sums_core])
    got_b = flip(out_b, "head", 1)
    scale_out = lax.rsqrt((sums + sums_x)[:, 0, :] / DI + EPS).reshape(rows, 1)

    share = width // seq_count
    manual = seq_count == 8
    half = seq_count // 2
    seq_core = seq_place % 2
    if manual:
        row_ids = [jnp.arange(half) * 2 + (1 - seq_core), jnp.arange(half) * 2 + seq_core]
    else:
        share = 256
        row_ids = [jnp.arange(width // share)]

    def weight_rows(which, x, ys, scale=None, into=()):
        ids = row_ids[which].astype(jnp.int32)
        count = ids.shape[0]
        ins = [(x, pl.BlockSpec((rows, share), lambda i, ids: (0, ids[i])))]
        if scale is not None:
            ins.append(whole(scale))
        outs = []
        lead = count * which
        for y, cols, at in ys:
            ins.append((y, pl.BlockSpec((rows, cols), lambda i, ids, at=at: (0, at))))
            if cols == side:
                spec = pl.BlockSpec((share, LANES), lambda i, ids: (i + lead, 0))
                outs += [(spec, (width, LANES), BF)] * 3
            else:
                outs.append((pl.BlockSpec((share, cols), lambda i, ids: (i, 0)), (count * share, cols), BF))
        aliases = {len(ins) + k: len(outs) - 3 + k for k in range(len(into))}
        return run(
            functools.partial(weight_kernel, scale is not None, len(ys), len(into)),
            (count,),
            ins + [(a, ANY) for a in into],
            outs,
            ids=ids,
            aliases=aliases,
            us=8,
        )

    z = seq_place // 2

    class Halving:
        def __init__(self, pieces):
            low = z % 2
            ids = jnp.stack([1 - low, 3 - low, low, 2 + low]).astype(jnp.int32)
            ins = []
            for kept, got in pieces:
                cols = kept.shape[1]
                for first in (0, 2):
                    spec = pl.BlockSpec((share, cols), lambda i, ids, f=first: (ids[f + i], 0))
                    ins += [(kept, spec), (got, spec)]
            self.cols = sum(kept.shape[1] for kept, _ in pieces)
            self.count = len(pieces)
            out = pl.BlockSpec((share, self.cols), lambda i, ids: (i, 0))
            sent, self.kept = run(
                functools.partial(split_kernel, self.count),
                (2,),
                ins,
                [(out, (2 * share, self.cols), BF), (out, (2 * share, self.cols), F32)],
                ids=ids,
                us=3,
            )
            self.got = flip(sent, "seq", 2)

        def middle(self):
            high = z // 2
            ids = jnp.stack([1 - high, high]).astype(jnp.int32)
            part = share // 2
            ins = []
            for w in (0, 1):
                spec = pl.BlockSpec((part, self.cols), lambda i, ids, w=w: (ids[w] * 2 + i, 0))
                ins += [(self.kept, spec), (self.got, spec)]
            out = pl.BlockSpec((part, self.cols), lambda i, ids: (i, 0))
            sent, self.kept = run(
                functools.partial(split_kernel, 1),
                (2,),
                ins,
                [(out, (share, self.cols), BF), (out, (share, self.cols), F32)],
                ids=ids,
                us=2,
            )
            self.got = flip(sent, "seq", 4)

        def end(self, into=None, place=0, total=1, turned=False):
            if turned:
                shape = block = (self.cols, share)
            else:
                shape, block = (share, self.cols * total), (share, self.cols)
            ins = [whole(self.kept), whole(self.got)] + ([] if into is None else [(into, ANY)])
            return run(
                end_kernel,
                one_step,
                ins,
                [(pl.BlockSpec(block, lambda i: (0, place)), shape, F32)],
                aliases=None if into is None else {2: 0},
                us=2,
            )[0]

    (out_first,) = weight_rows(0, cotangent, [(gg, inner, 0)], scale_out)
    if manual:
        out_got = flip(out_first, "seq", 1)
    away = out_quarter(2, got_a, BF)
    away_got = flip(away, "head", 2)
    mine = out_quarter(3, got_b, F32)
    if manual:
        (out_second,) = weight_rows(1, cotangent, [(gg, inner, 0)], scale_out)

    dmix, dgate, stat, dstate_local, dstate_low, dgain, dskip = run(
        chunked(gate_kernel, "rrrrrrsss--" + "rrs", True, many),
        (steps // many,),
        [
            (mixed, chunk_spec(inner, behind_many)), (gate_pre, chunk_spec(inner, behind_many)), (dgn, chunk_spec(inner, behind_many)),
            (act, chunk_spec(inner, behind_many)), (pact, chunk_spec(pair, behind_many)), (cs, chunk_spec(LANES, behind_many)),
            (info, slab_spec(16, L, behind_many)), (sums, slab_spec(2, L, behind_many)), (sums_x, slab_spec(2, L, behind_many)),
            whole(gains), whole(spread2),
        ],
        [
            (chunk_spec(inner, behind_many), (rows, inner), BF), (chunk_spec(inner, behind_many), (rows, inner), BF),
            (slab_spec(8, L, behind_many), (steps, 8, L), F32), (whole_spec((N, inner)), (N, inner), F32),
            (whole_spec((N, inner)), (N, inner), BF),
            (whole_spec((8, inner)), (8, inner), F32), (whole_spec((8, inner)), (8, inner), F32),
        ],
        us=17,
    )

    order_ids = jnp.stack(order).astype(jnp.int32)

    def gate_first():
        held["first"] = weight_rows(0, normed, [(dgate, inner, 0)])[0]

    def gate_second():
        if manual:
            held["got"] = flip(held["first"], "seq", 1)
            held["second"] = weight_rows(1, normed, [(dgate, inner, 0)])[0]

    def gate_third():
        held["dn"] = run(
            gate_back_kernel,
            (4, blocks),
            [
                (dgate, pl.BlockSpec((big, inner), lambda n, i, ids: (i, 0))),
                (w_gate, pl.BlockSpec((quarter, inner), lambda n, i, ids: (ids[n], 0))),
            ],
            [(pl.BlockSpec((1, big, quarter), lambda n, i, ids: (n, i, 0)), (4, rows, quarter), BF)],
            ids=order_ids,
            us=17,
        )[0]

    dstate, _ = exchange(
        dstate_local, dstate_low, through, factors, True, [gate_first, gate_second, gate_third]
    )
    dn_gate = held["dn"]

    def back_chunks(count, final):
        kinds = "rrrrsrsrr" + "-" * 15 + "s" + "-" * count + "rrs"
        kernel = functools.partial(back_kernel, count, final)

        def run_all(*refs):
            chunked(lambda turn, *views: kernel(turn, *views[:-2], refs[7], refs[8], *views[-2:]), kinds, True, 1)(*refs)

        return run_all

    parts = 3 if steps % 3 == 0 else 1
    each = steps // parts
    carried = dtaps = dhead = head_rows
    d_inner = d_side = small = dhalo = None
    if manual:
        out_sum = Halving([(out_second, out_got)])
    for part in range(parts):
        first = steps - 1 - part * each
        at = Place(1, lambda c, first=first: first - c)

        def near_end(c, at=at):
            return jnp.maximum(at.at(c) * (L // HALO) - 1, 0)

        final = part == parts - 1
        if manual and part == 1:
            out_sum.middle()
        if manual and part == 2:
            dw_out = out_sum.end(turned=True)
            gate_sum = Halving([(held["second"], held["got"])])
        grown = [] if d_inner is None else [(d_inner, ANY), (d_side, ANY)]
        state_specs = [
            (whole_spec((N, inner)), (N, inner), F32), (whole_spec((8, wide)), (8, wide), F32),
            (whole_spec((40, wide)), (40, wide), F32), (whole_spec((16, LANES)), (16, LANES), F32),
        ]
        if final:
            state_specs += [(whole_spec((8, wide)), (8, wide), F32)] * 2
        ins = [
            (act, chunk_spec(inner, at)), (pact, chunk_spec(pair, at)), (dt, chunk_spec(LANES, at)),
            (cs, chunk_spec(LANES, at)), (info, slab_spec(16, L, at)),
            (dmix, chunk_spec(inner, at)), (entries, slab_spec(N, inner, at)),
            (inner_raw, chunk_spec(inner, at)), (side_raw, chunk_spec(side, at)),
            (inner_raw, pl.BlockSpec((HALO, inner), lambda c, p=near_end: (p(c), 0))),
            (side_raw, pl.BlockSpec((HALO, side), lambda c, p=near_end: (p(c), 0))),
            whole(halo), whole(taps), whole(head_rows), whole(gains), whole(lower), whole(spread2), whole(gather),
            whole(dstate), whole(carried), whole(dtaps), whole(dhead), whole(dgain), whole(dskip),
            (stat, slab_spec(8, L, at)), *grown,
        ]
        aliases = {24: 2}
        if grown:
            aliases.update({25: 0, 26: 1})
        got = run(
            back_chunks(len(grown), final),
            (each,),
            ins,
            [
                (chunk_spec(inner, at), (rows, inner), BF), (chunk_spec(side, at), (rows, side), BF),
                (slab_spec(8, L, at), (steps, 8, L), F32), *state_specs,
            ],
            after=[away_got] if part == min(1, parts - 1) else [],
            scratch=[pltpu.VMEM((8 + L, wide), F32), pltpu.VMEM((L + 8, wide), F32)],
            aliases=aliases,
            us=64 / parts,
        )
        d_inner, d_side, stat, dstate, carried, dtaps, dhead = got[:7]
        if final:
            small, dhalo = got[7:]

    if manual:
        gate_sum.middle()
    returned = shift_over(dhalo, "seq", -1)
    small_got = flip(small, "seq", 1)

    def last_rows(cols):
        return pl.BlockSpec((HALO, cols), lambda c: (rows // HALO - 1, 0))

    last_slab = slab_spec(8, L, Place(1, lambda c: steps - 1))
    d_inner, d_side, stat, small = run(
        fix_kernel,
        one_step,
        [
            (inner_raw, last_rows(inner)), (side_raw, last_rows(side)), whole(keep_tail), whole(returned),
            whole(small), whole(small_got),
            (d_inner, last_rows(inner)), (d_side, last_rows(side)), (stat, last_slab),
        ],
        [
            (last_rows(inner), (rows, inner), BF), (last_rows(side), (rows, side), BF), (last_slab, (steps, 8, L), F32),
            (whole_spec((8, wide)), (8, wide), F32),
        ],
        aliases={6: 0, 7: 1, 8: 2},
        us=2,
    )

    def add(pairs):
        return run(
            functools.partial(add_kernel, len(pairs)),
            one_step,
            [whole(a) for pair_ in pairs for a in pair_],
            [(pl.BlockSpec(a.shape, lambda i, n=a.ndim: (0,) * n), a.shape, a.dtype) for a, _ in pairs],
            us=1,
        )

    half_inner = inner // 2
    swap_id = swap.astype(jnp.int32).reshape(1)
    inner_parts = [(d_inner, half_inner, 0), (d_inner, half_inner, 1), (d_side, side, 0)]

    swap_id = swap.astype(jnp.int32).reshape(1)
    stat = stat[:, 0, :]

    def twin(pair_at, got, dtypes, into=None):
        lead = half if into is not None else 0
        ids = [order[pair_at], order[pair_at + 1]]
        ids = jnp.concatenate([jnp.stack(ids)] + ([row_ids[1]] if lead else [])).astype(jnp.int32)

        def which(s):
            return jnp.clip((s - lead) // blocks, 0, 1)

        def row(s):
            return jnp.where(s < lead, 0, (s - lead) % blocks)

        def x_at(s, ids):
            return (0, ids[2 + jnp.minimum(s, lead - 1)]) if lead else (0, 0)

        def out_at(s, w):
            return jnp.clip(s - lead - w * blocks, 0, blocks - 1)

        ins = [
            (normed, pl.BlockSpec((rows if lead else 256, 256), x_at)),
            whole(d_inner), whole(d_side),
            (w_inner, pl.BlockSpec((quarter, inner), lambda s, ids: (ids[which(s)], 0))),
            (w_side, pl.BlockSpec((side, quarter), lambda s, ids: (0, ids[which(s)]))),
            (dn_gate, pl.BlockSpec((1, big, quarter), lambda s, ids: (pair_at + which(s), row(s), 0))),
        ]
        for w, block in enumerate(got):
            ins.append((block, pl.BlockSpec((big, quarter), lambda s, ids, w=w: (out_at(s, w), 0))))
        aliases = {}
        outs = []
        if lead:
            last = lead - 1
            aliases = {len(ins) + k: 2 + k for k in range(3)}
            ins += [(a, ANY) for a in into]
            wide_spec = pl.BlockSpec((share, inner // 2), lambda s, ids: (jnp.minimum(s, last), 0))
            side_spec = pl.BlockSpec((share, LANES), lambda s, ids: (lead + jnp.minimum(s, last), 0))
            outs += [(wide_spec, (lead * share, inner // 2), BF)] * 2 + [(side_spec, (width, LANES), BF)] * 3
        for w in (0, 1):
            spec = pl.BlockSpec((big, quarter), lambda s, ids, w=w: (out_at(s, w), 0))
            outs.append((spec, (rows, quarter), dtypes[w]))
        return run(
            functools.partial(twin_kernel, lead, blocks, len(got)),
            (lead + 2 * blocks,),
            ins,
            outs,
            ids=ids,
            aliases=aliases,
            us=22 if lead else 14,
        )

    first_a, first_b, sent, kept, step = weight_rows(0, normed, inner_parts)
    here = place.astype(jnp.int32).reshape(1)
    own_spec = pl.BlockSpec((big, quarter), lambda i, ids: (i, ids[0]))
    column = pl.BlockSpec((big, 1), lambda i, ids: (i, 0))
    result = run(
        result_kernel,
        (blocks,),
        [(tokens, own_spec), (scale_out, column), (mine, quarter_spec()), (away_got, quarter_spec())],
        [(quarter_spec(), (rows, quarter), BF)],
        ids=here,
        us=4,
    )[0]
    if manual:
        dw_gate = gate_sum.end()
    tall = pl.BlockSpec((1024, LANES), lambda i, *_: (i, 0))
    stat_got = flip(stat, "head", 1)
    small_got = flip(small, "seq", 2)
    if manual:
        got_a = flip(first_a, "seq", 1)
        got_b = flip(first_b, "seq", 1)
        second_a, second_b, sent, kept, step, dn_a, dn_b = twin(0, [], [BF, BF], [sent, kept, step])
    else:
        dn_a, dn_b = twin(0, [], [BF, BF])
    side_got = flip(sent, "head", 1)
    dn_got_a = flip(dn_a, "head", 1)
    dn_got_b = flip(dn_b, "head", 1)
    if manual:
        sum_a = Halving([(second_a, got_a)])
    stat, small = add([(stat, stat_got), (small, small_got)])
    stat_got = flip(stat, "head", 2)
    small_got = flip(small, "seq", 4)
    (stat,) = add([(stat, stat_got)])
    dn_away, dn_mine = twin(2, [dn_got_a, dn_got_b], [BF, F32])
    dn_away_got = flip(dn_away, "head", 2)
    if manual:
        sum_a.middle()
    joined = (pl.BlockSpec((width // 2, 2 * LANES), lambda i: (0, 0)), (width // 2, 2 * LANES), BF)
    rest_first, rest_second = run(
        join_kernel,
        (2,),
        [(kept, tall), (side_got, tall), (step, tall)],
        [joined, joined],
        us=3,
    )
    if manual:
        rest_got = flip(rest_first, "seq", 1)
        sum_b = Halving([(second_b, got_b)])
        sum_s = Halving([(rest_second, rest_got)])
    (small,) = add([(small, small_got)])
    bit = 8
    while bit < seq_count:
        small = small + flip(small, "seq", bit)
        bit *= 2
    if manual:
        sum_b.middle()
    small_pair = small[:, inner:]
    low_half, high_half = small_pair[:, : N // 2], small_pair[:, N // 2 : N]
    pair_kept = jnp.concatenate([low_half, small_pair[:, N : N + N // 2]], 1)
    pair_sent = jnp.concatenate([high_half, small_pair[:, N + N // 2 :]], 1)
    pair_got = flip(pair_sent, "head", 1)
    grad_tokens, norm_sum = run(
        final_kernel,
        (blocks,),
        [
            (tokens, own_spec), (cotangent, own_spec), (scale_in, column), (stat.reshape(rows, 1), column),
            (gain_row, pl.BlockSpec((1, quarter), lambda i, ids: (0, ids[0]))),
            (dn_mine, quarter_spec()), (dn_away_got, quarter_spec()),
        ],
        [
            (quarter_spec(), (rows, quarter), F32),
            (pl.BlockSpec((8, quarter), lambda i, ids: (0, 0)), (8, quarter), F32),
        ],
        ids=here,
        us=6,
    )
    norm_got = flip(norm_sum, "seq", 1)
    if manual:
        sum_s.middle()
    norm_sum = add([(norm_sum, norm_got)])[0]
    norm_got = flip(norm_sum, "seq", 2)
    pair_half = pl.BlockSpec((8, pair_cols), lambda i, *_: (0, 0))
    pair_full = pl.BlockSpec((8, N), lambda i, *_: (0, 0))
    pair_mine, pair_away = run(
        share_kernel,
        one_step,
        [(pair_kept, pair_full), (pair_got, pair_full)],
        [(pair_half, (8, pair_cols), F32)] * 2,
        ids=swap_id,
        us=1,
    )
    pair_got = flip(pair_away, "head", 2)
    norm_sum = add([(norm_sum, norm_got)])[0]
    norm_got = flip(norm_sum, "seq", 4)
    if manual:
        own_rows = (share, pair_cols)
        thin = (pl.BlockSpec(own_rows, lambda i, *_: (0, 0)), own_rows, F32)
        dw_inner, side_mine, side_sent, dw_step = run(
            close_kernel,
            one_step,
            [whole(block) for sum_ in (sum_a, sum_b, sum_s) for block in (sum_.kept, sum_.got)],
            [
                (pl.BlockSpec((share, inner), lambda i, *_: (0, 0)), (share, inner), F32), thin, thin,
                (pl.BlockSpec((LANES, share), lambda i, *_: (0, 0)), (LANES, share), F32),
            ],
            ids=swap_id,
            us=3,
        )
    else:
        dw_out, dw_gate, dw_inner, rest = [
            lax.psum_scatter(block, "seq", scatter_dimension=0, tiled=True).astype(F32)
            for block in (
                out_first,
                held["first"],
                jnp.concatenate([first_a, first_b], 1),
                jnp.concatenate([rest_first, rest_second], 0),
            )
        ]
        dw_out = jnp.transpose(dw_out)
        left, right = rest[:, :pair_cols], rest[:, pair_cols : 2 * pair_cols]
        side_mine, side_sent = jnp.where(swap, right, left), jnp.where(swap, left, right)
        dw_step = rest[:, LANES:].T
    side_got = flip(side_sent, "head", 2)
    bit = 8
    while bit < seq_count:
        norm_sum = norm_sum + norm_got
        norm_got = flip(norm_sum, "seq", bit)
        bit *= 2
    shapes = [
        (1, quarter), (4, inner), (1, inner), (4, pair_cols), (1, pair_cols), (1, heads), (1, heads), (1, heads),
        (1, inner), side_mine.shape[::-1],
    ]
    outs = run(
        unpack_kernel,
        one_step,
        [whole(a) for a in (small, pair_mine, pair_got, norm_sum, norm_got, side_mine, side_got)],
        [(pl.BlockSpec(shape, lambda i: (0, 0)), shape, F32) for shape in shapes],
        us=1,
    )
    norm_sum, taps_sum, bias_sum, pair_taps, pair_bias, step_sum, decay_sum, skip_sum, gain_sum, dw_pair = outs
    return (
        result,
        grad_tokens,
        norm_sum.reshape(-1),
        dw_gate,
        dw_inner,
        dw_pair.T,
        dw_step[:heads].T,
        taps_sum,
        pair_taps,
        bias_sum.reshape(-1),
        pair_bias.reshape(-1),
        step_sum.reshape(-1),
        decay_sum.reshape(-1),
        skip_sum.reshape(-1),
        gain_sum.reshape(-1),
        dw_out,
    )


def solution(mesh):
    return jax.shard_map(
        body,
        mesh=mesh,
        in_specs=(
            P("seq", None),
            P("seq"),
            P(),
            P(None, "head"),
            P(None, "head"),
            P(None, "head"),
            P(None, "head"),
            P(None, "head"),
            P(None, "head"),
            P("head"),
            P("head"),
            P("head"),
            P("head"),
            P("head"),
            P("head"),
            P("head", None),
            P("seq", None),
        ),
        out_specs=(
            P("seq", "head"),
            P("seq", "head"),
            P("head"),
            P("seq", "head"),
            P("seq", "head"),
            P("seq", "head"),
            P("seq", "head"),
            P(None, "head"),
            P(None, "head"),
            P("head"),
            P("head"),
            P("head"),
            P("head"),
            P("head"),
            P("head"),
            P("head", "seq"),
        ),
        check_vma=False,
    )
```
